32 devices in a mesh: dp: 8 (over y, x, core), tensor: 4 (over z).
Axes of the slice: x: 2, y: 2, z: 4, core: 2. Of those that a mesh axis runs over, the one named last changes fastest.
Arguments:
- inputs: bfloat16 [8, 1024, 768], P('dp'), may hold values from -8 to 8
- doc_ids: int32 [8, 8], P('dp'), may hold values from 0 to 3, never falling along the last dimension, each value on 1 to 4 neighbouring positions
- qkv_weight: bfloat16 [2, 3, 768, 768], P(None, None, None, 'tensor'), may hold values from -0.21875 to 0.21875
- out_weight: bfloat16 [2, 768, 768], P(None, 'tensor'), may hold values from -1.25 to 1.25
- up_weight: bfloat16 [2, 768, 3072], P(None, None, 'tensor'), may hold values from -0.21875 to 0.21875
- down_weight: bfloat16 [2, 3072, 768], P(None, 'tensor'), may hold values from -0.109375 to 0.109375
- norm_gain: float32 [2, 2, 768], replicated, may hold values from 0.5 to 1.5
- norm_shift: float32 [2, 2, 768], replicated, may hold values from -3 to 3
- cotangent: bfloat16 [8, 1024, 768], P('dp'), may hold values from -6 to 6
Outputs:
- outputs: bfloat16 [8, 1024, 768], P('dp', 'tensor')
- input_grad: bfloat16 [8, 1024, 768], P('dp', 'tensor')
- qkv_grad: float32 [2, 3, 768, 768], P(None, None, 'dp', 'tensor')
- out_grad: float32 [2, 768, 768], P(None, 'tensor', 'dp')
- up_grad: float32 [2, 768, 3072], P(None, 'dp', 'tensor')
- down_grad: float32 [2, 3072, 768], P(None, 'tensor', 'dp')
- gain_grad: float32 [2, 768], P(None, 'dp')
- shift_grad: float32 [2, 768], P(None, 'dp')
- cross_norm_grad: float32 [2, 2, 768], P(None, None, 'dp')
The draws below stay inside these ranges and needn't reach their ends.
Inputs may be any that keep to these rules, and one draw needn't show every extreme that they name: `doc_ids`: document ids of a sequence never fall along its segments; a document spans 1 to 4 consecutive segments.
All inputs are finite; a program needn't handle non-finite values.
Results may differ from the reference program's by a relative error of at most 0.022.
Values may be sent and summed in bfloat16 or wider, within the bound.
A program may use at most 128 MiB of HBM per device.

```python
import math
import jax
import jax.numpy as jnp
import numpy as np
from jax import lax

D = 768
HEADS = 12
HEAD_DIM = 64
FF = 3072
SEG = 128
SEGS_SEQ = 8
SEQ_LEN = 1024
SEQS = 8
N_TENSOR = 4


def with_spikes(values, key, source, target, parts, factor):
    def block_of(dim):
        return (jnp.arange(values.shape[dim]) // (values.shape[dim] // parts)).reshape((-1,) + (1,) * (values.ndim - 1 - dim))

    first = jax.random.permutation(key, parts)[block_of(target)]
    second = (block_of(target) + parts // 2) % parts
    return jnp.where((block_of(source) == first) | (block_of(source) == second), factor * values, values)


def block_levels(rng, shape, split, low, top_value):
    def one(position, shards_of):
        steps = jax.random.uniform(jax.random.fold_in(jax.random.fold_in(rng, 6), position), (shards_of,), jnp.float32, low / len(split), top_value / len(split))
        return jnp.repeat(jnp.exp(steps), shape[position] // shards_of).reshape((-1,) + (1,) * (len(shape) - position - 1))

    gain = one(*split[0])
    for cut in split[1:]:
        gain = gain * one(*cut)
    return gain


def split_up(amount, total, limit, slope):
    loads = [(1 << 20) // math.isqrt(grade ** slope) + 1 for grade in range(2, amount + 1)]
    surplus, counts = total - limit - (amount - 1), [1] * (amount - 1)
    while surplus > 0:
        candidates = [i for i in range(amount - 1) if counts[i] < limit]
        mass, budget = sum([loads[i] for i in candidates]), surplus
        for i in candidates:
            extra = min(limit - counts[i], max(1, budget * loads[i] // mass), surplus)
            counts[i] = counts[i] + extra
            surplus = surplus - extra
    return np.array([limit] + counts)


def ragged(rng, amount, total, most, slope):
    if amount == 2:
        one = jax.random.randint(rng, (), max(1, total - most), min(most, total - 1) + 1)
        return jnp.stack([one, total - one])
    sizes = jnp.asarray(split_up(amount, total, most, slope), jnp.int32)
    pairs = (amount - 1) // 2
    donor, taker = sizes[1:1 + 2 * pairs:2], sizes[2:2 + 2 * pairs:2]
    room = jnp.minimum(donor - 1, most - taker)
    moved = jax.random.randint(jax.random.fold_in(rng, 1), (pairs,), 0, 1 << 20) % (room + 1)
    sizes = sizes.at[1:1 + 2 * pairs:2].set(donor - moved).at[2:2 + 2 * pairs:2].set(taker + moved)
    return sizes[jax.random.permutation(jax.random.fold_in(rng, 2), amount)]


def gaussian(rng, shape, width, reach, shards=(), held_as=jnp.bfloat16):
    values = width * jax.random.normal(rng, shape, jnp.float32)
    if shards:
        values = values * block_levels(rng, shape, shards, -0.22, 0.18)
    return jnp.clip(values, -reach, reach).astype(held_as)


def noise_with(rng, dims, deviation, most, cuts, heavy, dtype=jnp.bfloat16):
    values = deviation * jax.random.normal(rng, dims, jnp.float32)
    if cuts:
        values = values * block_levels(rng, dims, cuts, -0.22, 0.18)
    return jnp.clip(with_spikes(values, jax.random.fold_in(rng, 3), *heavy), -most, most).astype(dtype)


def setup_inputs(seed: int = 0) -> dict:
    seeds = jax.random.split(jax.random.key(seed), 10)
    return {
        "inputs": noise_with(seeds[0], (SEQS, SEQ_LEN, D), 1.0, 8.0, ((0, 8),), (0, 2, 8, 2.0)),
        "doc_ids": jax.vmap(lambda own: jnp.searchsorted(jnp.cumsum(ragged(own, SEGS_SEQ // 2, SEGS_SEQ, SEGS_SEQ // 2, 0)), jnp.arange(SEGS_SEQ), side="right"))(jax.random.split(seeds[1], SEQS)).reshape((SEQS, SEGS_SEQ)).astype(jnp.int32),
        "qkv_weight": gaussian(seeds[2], (2, 3, D, D), D ** -0.5, 0.21875, ((3, 4),)),
        "out_weight": gaussian(seeds[3], (2, D, D), (D // 32) ** -0.5, 1.25, ((1, 4),)),
        "up_weight": gaussian(seeds[4], (2, D, FF), D ** -0.5, 0.21875, ((2, 4),)),
        "down_weight": gaussian(seeds[5], (2, FF, D), FF ** -0.5, 0.109375, ((1, 4),)),
        "norm_gain": jnp.clip(1.0 + 0.1 * jax.random.normal(seeds[6], (2, 2, D), jnp.float32), 0.5, 1.5),
        "norm_shift": gaussian(seeds[7], (2, 2, D), 0.5, 3.0, (), jnp.float32),
        "cotangent": gaussian(seeds[8], (SEQS, SEQ_LEN, D), 1.0, 6.0, ((0, 8),)),
    }


EPSILON = 1e-05
MASK_FILL = -1000000000.0
PRECISE = lax.Precision.HIGHEST

@jax.custom_vjp
def low(v):
    return lax.optimization_barrier(v.astype(jnp.bfloat16)).astype(jnp.float32)

@jax.custom_vjp
def low_back(v):
    return v

def low_keep(v):
    return (low(v), None)

def low_pass(kept, grad):
    return (grad,)

def back_keep(v):
    return (v, None)

def back_low(kept, grad):
    return (low(grad),)
low.defvjp(low_keep, low_pass)
low_back.defvjp(back_keep, back_low)

def layer_norm(values, gain_row, shift_row):
    center = lax.optimization_barrier(jnp.mean(values, axis=-1, keepdims=True))
    offset = values - center
    spread = lax.optimization_barrier(jnp.mean(offset * offset, axis=-1, keepdims=True))
    return offset * lax.rsqrt(spread + EPSILON) * gain_row + shift_row

def block_layer(rows_in, allowed, qkv_matrix, out_matrix, up_matrix, down_matrix, gains, shifts):
    batch_count, length, model_width = rows_in.shape
    groups = N_TENSOR
    rows_low = low(rows_in)
    project = jnp.einsum('brd,cde->cbre', rows_low, qkv_matrix, precision=PRECISE)
    project = low(low_back(project))
    head_split = project.reshape(3, batch_count, length, HEADS, HEAD_DIM)
    scores = jnp.einsum('bqhe,bkhe->bhqk', head_split[0], head_split[1], precision=PRECISE) * (1.0 / math.sqrt(HEAD_DIM))
    if allowed is not None:
        scores = jnp.where(allowed, scores, MASK_FILL)
    scores = low_back(scores)
    softmax_weights = jax.nn.softmax(scores, axis=-1)
    mixture = jnp.einsum('bhqk,bkhe->bqhe', low(softmax_weights), head_split[2], precision=PRECISE)
    mixture = low(low_back(mixture)).reshape(batch_count, length, groups, model_width // groups)
    pieces = jnp.einsum('brgf,gfd->gbrd', mixture, out_matrix.reshape(groups, model_width // groups, model_width), precision=PRECISE)
    attended = low_back(lax.optimization_barrier(jnp.sum(low(pieces), axis=0)))
    first_norm = layer_norm(rows_in + attended, gains[0], shifts[0])
    upward = jnp.einsum('brd,df->brf', low(first_norm), up_matrix, precision=PRECISE)
    active = low(jax.nn.gelu(low_back(upward), approximate=False))
    hidden_units = up_matrix.shape[1]
    fed_pieces = jnp.einsum('brgf,gfd->gbrd', active.reshape(batch_count, length, groups, hidden_units // groups), down_matrix.reshape(groups, hidden_units // groups, model_width), precision=PRECISE)
    fed = low_back(lax.optimization_barrier(jnp.sum(low(fed_pieces), axis=0)))
    return layer_norm(first_norm + fed, gains[1], shifts[1])

def sequence_output(tokens_in, doc_row, params_in):
    qkv_all, out_all, up_all, down_all, gain_all, shift_all = params_in
    segmented = tokens_in.reshape(SEGS_SEQ, SEG, D)
    lower = block_layer(segmented, None, qkv_all[0], out_all[0], up_all[0], down_all[0], gain_all[0], shift_all[0])
    same_doc = (doc_row[:, None] == doc_row[None, :])[None, None]
    upper = block_layer(lower[:, 0, :][None], same_doc, qkv_all[1], out_all[1], up_all[1], down_all[1], gain_all[1], shift_all[1])
    joined = lower.at[:, 0, :].set(upper[0])
    return joined.reshape(SEQ_LEN, D)

def reference(inputs, doc_ids, qkv_weight, out_weight, up_weight, down_weight, norm_gain, norm_shift, cotangent):
    params = (qkv_weight.astype(jnp.float32), out_weight.astype(jnp.float32), up_weight.astype(jnp.float32), down_weight.astype(jnp.float32), norm_gain.astype(jnp.float32), norm_shift.astype(jnp.float32))

    def one_sequence(totals, packed):
        tokens, doc_row, seed_grad = packed

        def forward(tokens_in, params_in):
            return sequence_output(tokens_in, doc_row, params_in)
        result, pullback = jax.vjp(forward, tokens, params)
        token_grad, param_grads = pullback(seed_grad)
        totals = jax.tree.map(lambda running, update: running + update, totals, param_grads)
        return (totals, (result, token_grad))
    start_grads = jax.tree.map(jnp.zeros_like, params)
    totals, stacked = lax.scan(one_sequence, start_grads, (inputs.astype(jnp.float32), doc_ids, cotangent.astype(jnp.float32)))
    results, token_grads = stacked
    cross_norm = jnp.stack([totals[4][1], totals[5][1]])
    return (results.astype(jnp.bfloat16), token_grads.astype(jnp.bfloat16), totals[0], totals[1], totals[2], totals[3], totals[4][0], totals[5][0], cross_norm)
```

```python
from functools import partial
import math

import jax
import jax.numpy as jnp
from jax import lax
from jax.experimental import pallas as pl
from jax.experimental.pallas import tpu as pltpu
from jax.sharding import PartitionSpec as P

HEAD_DIM = 64
SEG = 128


EPSILON = 1e-05
MASK_FILL = -1000000000.0


def layer_norm(values, gain_row, shift_row):
    center = jnp.mean(values, axis=-1, keepdims=True)
    offset = values - center
    spread = jnp.mean(offset * offset, axis=-1, keepdims=True)
    inverse = lax.rsqrt(spread + EPSILON)
    scaled = offset * inverse
    return (scaled * gain_row + shift_row, (scaled, inverse))


def norm_back(grad_out, saved, gain_row):
    scaled, inverse = saved
    weighted = grad_out * gain_row
    mean_one = jnp.mean(weighted, axis=-1, keepdims=True)
    mean_two = jnp.mean(weighted * scaled, axis=-1, keepdims=True)
    grad_in = inverse * (weighted - mean_one - scaled * mean_two)
    return (grad_in, jnp.sum(grad_out * scaled, axis=(0, 1)), jnp.sum(grad_out, axis=(0, 1)))


def score_block(head_split, allowed):
    scores = jnp.einsum(
        "bqhe,bkhe->bhqk", head_split[0], head_split[1], preferred_element_type=jnp.float32
    ) * (1.0 / math.sqrt(HEAD_DIM))
    if allowed is not None:
        scores = jnp.where(allowed, scores, MASK_FILL)
    return scores


def attend_forward(rows_low, qkv_local, allowed):
    batch_count = rows_low.shape[0]
    length = rows_low.shape[1]
    project = jnp.einsum(
        "brd,cde->cbre", rows_low, qkv_local, preferred_element_type=jnp.float32
    ).astype(jnp.bfloat16)
    head_split = project.reshape(3, batch_count, length, -1, HEAD_DIM)
    scores = score_block(head_split, allowed)
    log_total = jax.nn.logsumexp(scores, axis=-1)
    soft_low = jnp.exp(scores - log_total[..., None]).astype(jnp.bfloat16)
    mixture = jnp.einsum(
        "bhqk,bkhe->bqhe", soft_low, head_split[2], preferred_element_type=jnp.float32
    )
    return (project, log_total, mixture.astype(jnp.bfloat16).reshape(batch_count, length, -1))


def attend_backward(rows_low, qkv_local, out_local, project, log_total, mixture, grad_low, allowed):
    batch_count = rows_low.shape[0]
    length = rows_low.shape[1]
    head_split = project.reshape(3, batch_count, length, -1, HEAD_DIM)
    grad_mixture = jnp.einsum(
        "brd,fd->brf", grad_low, out_local, preferred_element_type=jnp.float32
    ).astype(jnp.bfloat16)
    out_local_grad = jnp.einsum(
        "brf,brd->fd", mixture, grad_low, preferred_element_type=jnp.float32
    )
    grad_heads = grad_mixture.reshape(batch_count, length, -1, HEAD_DIM)
    scores = score_block(head_split, allowed)
    soft_full = jnp.exp(scores - log_total[..., None])
    grad_soft = jnp.einsum(
        "bqhe,bkhe->bhqk", grad_heads, head_split[2], preferred_element_type=jnp.float32
    )
    row_inner = jnp.sum(grad_soft * soft_full, axis=-1, keepdims=True)
    grad_scores = (soft_full * (grad_soft - row_inner)).astype(jnp.bfloat16)
    scale_factor = 1.0 / math.sqrt(HEAD_DIM)
    grad_query = (
        jnp.einsum(
            "bhqk,bkhe->bqhe", grad_scores, head_split[1], preferred_element_type=jnp.float32
        )
        * scale_factor
    )
    grad_key = (
        jnp.einsum(
            "bhqk,bqhe->bkhe", grad_scores, head_split[0], preferred_element_type=jnp.float32
        )
        * scale_factor
    )
    grad_value = jnp.einsum(
        "bhqk,bqhe->bkhe",
        soft_full.astype(jnp.bfloat16),
        grad_heads,
        preferred_element_type=jnp.float32,
    )
    grad_project = (
        jnp.stack([grad_query, grad_key, grad_value])
        .reshape(3, batch_count, length, -1)
        .astype(jnp.bfloat16)
    )
    qkv_local_grad = jnp.einsum(
        "brd,cbre->cde", rows_low, grad_project, preferred_element_type=jnp.float32
    )
    input_part = jnp.einsum(
        "cbre,cde->brd", grad_project, qkv_local, preferred_element_type=jnp.float32
    )
    return (input_part, qkv_local_grad, out_local_grad)


def expand_forward(rows_low, up_local, down_local):
    upward = jnp.einsum("brd,df->brf", rows_low, up_local, preferred_element_type=jnp.float32)
    active = jax.nn.gelu(upward, approximate=False).astype(jnp.bfloat16)
    return (
        upward,
        active,
        jnp.einsum("brf,fd->brd", active, down_local, preferred_element_type=jnp.float32),
    )


def expand_backward(rows_low, up_local, down_local, upward, active, grad_low):
    grad_active = jnp.einsum(
        "brd,fd->brf", grad_low, down_local, preferred_element_type=jnp.float32
    )
    down_local_grad = jnp.einsum(
        "brf,brd->fd", active, grad_low, preferred_element_type=jnp.float32
    )
    gelu_pull = jax.vjp(partial(jax.nn.gelu, approximate=False), upward)[1]
    grad_upward = gelu_pull(grad_active)[0].astype(jnp.bfloat16)
    up_local_grad = jnp.einsum(
        "brd,brf->df", rows_low, grad_upward, preferred_element_type=jnp.float32
    )
    input_part = jnp.einsum(
        "brf,df->brd", grad_upward, up_local, preferred_element_type=jnp.float32
    )
    return (input_part, up_local_grad, down_local_grad)


def body(
    inputs,
    doc_ids,
    qkv_weight,
    out_weight,
    up_weight,
    down_weight,
    norm_gain,
    norm_shift,
    cotangent,
):
    groups = lax.axis_size("tensor")
    position = lax.axis_index("tensor")
    model_width = inputs.shape[2]
    segment_count = inputs.shape[1] // SEG
    own_count = segment_count // groups
    row_start = position * own_count

    def final_rows(values):
        return lax.dynamic_slice_in_dim(values, row_start, own_count, 0)

    def forward_sum(partial_term):
        return lax.psum(partial_term.astype(jnp.bfloat16), "tensor").astype(jnp.float32)

    def backward_sum(partial_term):
        return lax.psum(partial_term.astype(jnp.bfloat16), "tensor").astype(jnp.float32)

    def cross_sum(partial_term):
        return lax.psum(partial_term.astype(jnp.bfloat16), "tensor").astype(jnp.float32)

    def cross_grad_sum(partial_term):
        return lax.psum(partial_term, "tensor")

    tokens = inputs[0].reshape(segment_count, SEG, model_width)
    tokens_wide = tokens.astype(jnp.float32)
    lower_proj, lower_total, lower_mix = attend_forward(tokens, qkv_weight[0], None)
    attended = forward_sum(
        jnp.einsum("brf,fd->brd", lower_mix, out_weight[0], preferred_element_type=jnp.float32)
    )
    first_norm, first_saved = layer_norm(tokens_wide + attended, norm_gain[0, 0], norm_shift[0, 0])
    first_low = first_norm.astype(jnp.bfloat16)
    lower_up, lower_active, fed_term = expand_forward(first_low, up_weight[0], down_weight[0])
    second, second_saved = layer_norm(
        first_norm + forward_sum(fed_term), norm_gain[0, 1], norm_shift[0, 1]
    )
    summary = second[:, 0, :]
    summary = summary[None]
    same_doc = (doc_ids[0][:, None] == doc_ids[0][None, :])[None, None]
    summary_low = summary.astype(jnp.bfloat16)
    upper_proj, upper_total, upper_mix = attend_forward(summary_low, qkv_weight[1], same_doc)
    upper_att = cross_sum(
        jnp.einsum("brf,fd->brd", upper_mix, out_weight[1], preferred_element_type=jnp.float32)
    )
    upper_first, upper_saved_one = layer_norm(
        summary + upper_att, norm_gain[1, 0], norm_shift[1, 0]
    )
    upper_first_low = upper_first.astype(jnp.bfloat16)
    upper_up, upper_active, upper_fed = expand_forward(
        upper_first_low, up_weight[1], down_weight[1]
    )
    upper_out, upper_saved_two = layer_norm(
        upper_first + cross_sum(upper_fed), norm_gain[1, 1], norm_shift[1, 1]
    )
    joined = second.at[:, 0, :].set(upper_out[0])
    outputs_own = final_rows(joined).reshape(1, -1, model_width).astype(jnp.bfloat16)
    grad_full = cotangent[0].reshape(segment_count, SEG, model_width).astype(jnp.float32)
    grad_top = grad_full[:, 0, :][None]
    grad_upper_fed, gain_cross_two, shift_cross_two = norm_back(
        grad_top, upper_saved_two, norm_gain[1, 1]
    )
    cross_part, up_cross, down_cross = expand_backward(
        upper_first_low,
        up_weight[1],
        down_weight[1],
        upper_up,
        upper_active,
        grad_upper_fed.astype(jnp.bfloat16),
    )
    grad_upper_first = grad_upper_fed + cross_grad_sum(cross_part)
    grad_upper_att, gain_cross_one, shift_cross_one = norm_back(
        grad_upper_first, upper_saved_one, norm_gain[1, 0]
    )
    cross_input_part, qkv_cross, out_cross = attend_backward(
        summary_low,
        qkv_weight[1],
        out_weight[1],
        upper_proj,
        upper_total,
        upper_mix,
        grad_upper_att.astype(jnp.bfloat16),
        same_doc,
    )
    grad_summary = grad_upper_att + cross_grad_sum(cross_input_part)
    grad_second = grad_full.at[:, 0, :].set(grad_summary[0])
    grad_fed, gain_seg_two, shift_seg_two = norm_back(grad_second, second_saved, norm_gain[0, 1])
    fed_low = grad_fed.astype(jnp.bfloat16)
    seg_part, up_seg, down_seg = expand_backward(
        first_low, up_weight[0], down_weight[0], lower_up, lower_active, fed_low
    )
    grad_first = grad_fed + backward_sum(seg_part)
    grad_att, gain_seg_one, shift_seg_one = norm_back(grad_first, first_saved, norm_gain[0, 0])
    att_low = grad_att.astype(jnp.bfloat16)
    seg_input_part, qkv_seg, out_seg = attend_backward(
        tokens, qkv_weight[0], out_weight[0], lower_proj, lower_total, lower_mix, att_low, None
    )
    input_full = grad_att + backward_sum(seg_input_part)
    input_own = final_rows(input_full).reshape(1, -1, model_width).astype(jnp.bfloat16)
    seg_gain = jnp.stack([gain_seg_one, gain_seg_two])
    seg_shift = jnp.stack([shift_seg_one, shift_seg_two])
    cross_norm = jnp.stack(
        [jnp.stack([gain_cross_one, gain_cross_two]), jnp.stack([shift_cross_one, shift_cross_two])]
    )
    qkv_all = jnp.stack([qkv_seg, qkv_cross])
    out_all = jnp.stack([out_seg, out_cross])
    up_all = jnp.stack([up_seg, up_cross])
    down_all = jnp.stack([down_seg, down_cross])
    summed = (
        lax.psum_scatter(qkv_all, "dp", scatter_dimension=2, tiled=True),
        lax.psum_scatter(out_all, "dp", scatter_dimension=2, tiled=True),
        lax.psum_scatter(up_all, "dp", scatter_dimension=1, tiled=True),
        lax.psum_scatter(down_all, "dp", scatter_dimension=2, tiled=True),
        lax.psum_scatter(seg_gain, "dp", scatter_dimension=1, tiled=True),
        lax.psum_scatter(seg_shift, "dp", scatter_dimension=1, tiled=True),
        lax.psum_scatter(cross_norm, "dp", scatter_dimension=2, tiled=True),
    )
    return (
        outputs_own,
        input_own,
        summed[0],
        summed[1],
        summed[2],
        summed[3],
        summed[4],
        summed[5],
        summed[6],
    )


MESH = pl.DeviceIdType.MESH
F32 = jnp.float32
BF16 = jnp.bfloat16
SCALE = 1.0 / math.sqrt(HEAD_DIM)
ATT, UP, DOWN = 0, 1, 2
BLK = 96
HALF = 48


def mm(a, b):
    return lax.dot_general(a, b, (((1,), (0,)), ((), ())), preferred_element_type=F32)


def mm_nt(a, b):
    return lax.dot_general(a, b, (((1,), (1,)), ((), ())), preferred_element_type=F32)


def mm_tn(a, b):
    return lax.dot_general(a, b, (((0,), (0,)), ((), ())), preferred_element_type=F32)


def normalize(values):
    center = jnp.mean(values, axis=-1, keepdims=True)
    offset = values - center
    spread = jnp.mean(offset * offset, axis=-1, keepdims=True)
    inverse = lax.rsqrt(spread + EPSILON)
    return offset * inverse, inverse


def normalize_back(grad_out, scaled, inverse, gain_row):
    weighted = grad_out * gain_row
    mean_one = jnp.mean(weighted, axis=-1, keepdims=True)
    mean_two = jnp.mean(weighted * scaled, axis=-1, keepdims=True)
    return inverse * (weighted - mean_one - scaled * mean_two)


def gelu_pair(upward):
    cdf = 0.5 * (1.0 + lax.erf(upward * math.sqrt(0.5)))
    pdf = jnp.exp(upward * upward * -0.5) * (1.0 / math.sqrt(2.0 * math.pi))
    return upward * cdf, cdf + upward * pdf


def fused_kernel(
    tokens_hbm, cot_hbm, cot_seg, allowed_ref, wa_hbm, wu_hbm, wd_hbm, gain_ref, shift_ref,
    out_ref, ing_ref, qkvg_ref, outg_ref, upg_ref, downg_ref, gaing_ref, shiftg_ref, crossg_ref,
    W, G, RC, RA1, RB1, RA2, RB2, RZ, L1, X, COT, QKV, PR, MIX, ACT, DG, GU, GQ, ACC, SC1, SC2, GF,
    FL, FLT, FDL, FDLT, XT, GM, C8, INV1, INV2, FAC, LT, EL, ER, E, NV, SV, RSV,
    sem_local, ag_s, ag_r, rs_s, rs_r, e_s, e_r, f_s, f_r, v_s, v_r,
):
    dp = lax.axis_index("dp")
    z = lax.axis_index("tensor")
    c = dp % 2
    x = (dp // 2) % 2
    y = dp // 4
    nc, nx, ny = 1 - c, 1 - x, 1 - y
    core_peer = (dp + 1 - 2 * c, z)
    x_peer = (dp + 2 - 4 * x, z)
    y_peer = (dp + 4 - 8 * y, z)
    z_peer = [None, (dp, z + 1 - 2 * (z % 2)), (dp, z + 2 - 4 * (z // 2)), (dp, 3 - z)]
    z_of = [z, z + 1 - 2 * (z % 2), z + 2 - 4 * (z // 2), 3 - z]

    def plane_index(m):
        ty = y if m // 4 == 0 else ny
        tx = x if (m // 2) % 2 == 0 else nx
        tc = c if m % 2 == 0 else nc
        return ty * 4 + tx * 2 + tc

    sends = []
    waited = []

    def remote(src, dst, ssem, rsem, target):
        copy = pltpu.make_async_remote_copy(
            src_ref=src, dst_ref=dst, send_sem=ssem, recv_sem=rsem, device_id=target, device_id_type=MESH
        )
        copy.start()
        sends.append(copy)
        return copy

    loads = {}

    def load(name, index, src, dst):
        copy = pltpu.make_async_copy(src, dst, sem_local.at[index])
        copy.start()
        loads[name] = copy

    load("x", 0, tokens_hbm.at[0, pl.ds(pl.multiple_of(z * 256, 256), 256)], X)
    load("wa", 1, wa_hbm.at[0], W.at[ATT, 0])
    load("wu", 2, wu_hbm.at[0], W.at[UP, 0])
    load("wd", 3, wd_hbm.at[0], W.at[DOWN, 0])
    load("cot", 4, cot_hbm.at[0, pl.ds(pl.multiple_of(z * 256, 256), 256)], COT)
    load("l1a", 5, wa_hbm.at[1], L1.at[ATT])
    load("l1u", 6, wu_hbm.at[1], L1.at[UP])
    load("l1d", 7, wd_hbm.at[1], L1.at[DOWN])
    load("c8", 8, cot_seg.at[:, pl.ds(0, 16)], C8)

    barrier = pltpu.get_barrier_semaphore()
    for m in range(1, 8):
        pl.semaphore_signal(barrier, inc=1, device_id=(plane_index(m), z), device_id_type=MESH)
    for r in range(1, 4):
        pl.semaphore_signal(barrier, inc=1, device_id=z_peer[r], device_id_type=MESH)
    pl.semaphore_wait(barrier, 10)

    own_hbm = [wa_hbm.at[0], wu_hbm.at[0], wd_hbm.at[0]]
    units = [(ATT, 1), (ATT, 2), (ATT, 3), (UP, 1), (DOWN, 1), (UP, 2), (DOWN, 2), (UP, 3), (DOWN, 3)]
    zc, a1, b1, a2, b2, cc = {}, {}, {}, {}, {}, {}
    for i, (k, r) in enumerate(units):
        zc[i] = remote(
            own_hbm[k].at[y, x, c], W.at[k, r, y, x, c], ag_s.at[0, i], ag_r.at[0, i], z_peer[r]
        )

    def gather_tick(t):
        i = t
        if 0 <= i < 9:
            k, r = units[i]
            zc[i].wait_recv()
            part = W.at[k, r, y, x, c, pl.ds(0, HALF)]
            a1[i] = remote(part, part, ag_s.at[1, i], ag_r.at[1, i], x_peer)
            part = W.at[k, r, y, x, c, pl.ds(HALF, HALF)]
            b1[i] = remote(part, part, ag_s.at[2, i], ag_r.at[2, i], y_peer)
        i = t - 1
        if 0 <= i < 9:
            k, r = units[i]
            a1[i].wait_recv()
            part = W.at[k, r, y, :, c, pl.ds(0, HALF)]
            a2[i] = remote(part, part, ag_s.at[3, i], ag_r.at[3, i], y_peer)
            b1[i].wait_recv()
            part = W.at[k, r, :, x, c, pl.ds(HALF, HALF)]
            b2[i] = remote(part, part, ag_s.at[4, i], ag_r.at[4, i], x_peer)
        i = t - 2
        if 0 <= i < 9:
            k, r = units[i]
            a2[i].wait_recv()
            b2[i].wait_recv()
            part = W.at[k, r, :, :, c]
            cc[i] = remote(part, part, ag_s.at[5, i], ag_r.at[5, i], core_peer)
        i = t - 3
        if 0 <= i < 9:
            cc[i].wait_recv()

    def unit_value(ref):
        return ref[...].reshape(768, ref.shape[-1])

    def cols(k, r, start, size):
        return unit_value(W.at[k, r, :, :, :, :, pl.ds(start, size)])

    def accumulate(first, value):
        if first:
            ACC[...] = value
        else:
            ACC[...] += value

    def attn_forward(r):
        QKV[r] = mm(X[...], cols(ATT, r, 0, 576)).astype(BF16)

        def segment(s, carry):
            rows = pl.ds(pl.multiple_of(s * SEG, SEG), SEG)
            qkv = QKV[r, rows, :]
            mixes = []
            for h in range(3):
                q = qkv[:, h * 64 : h * 64 + 64]
                key = qkv[:, 192 + h * 64 : 256 + h * 64]
                val = qkv[:, 384 + h * 64 : 448 + h * 64]
                scores = mm_nt(q, key) * SCALE
                top = jnp.max(scores, axis=-1, keepdims=True)
                expd = jnp.exp(scores - top)
                prob = expd * (1.0 / jnp.sum(expd, axis=-1, keepdims=True))
                PR[r, h, rows, :] = prob
                mixes.append(mm(prob.astype(BF16), val))
            MIX[r, rows, :] = jnp.concatenate(mixes, axis=-1).astype(BF16)
            return carry

        lax.fori_loop(0, 2, segment, 0)
        accumulate(r == 0, mm_nt(MIX[r], cols(ATT, r, 576, 192)))

    def row_chunks(body, init=0):
        def one(i, carry):
            return body(i, pl.ds(pl.multiple_of(i * 64, 64), 64), carry)

        return lax.fori_loop(0, 4, one, init)

    g00, g01 = gain_ref[0, 0:1, :], gain_ref[0, 1:2, :]
    b00, b01 = shift_ref[0, 0:1, :], shift_ref[0, 1:2, :]
    g10, g11 = gain_ref[1, 0:1, :], gain_ref[1, 1:2, :]
    b10, b11 = shift_ref[1, 0:1, :], shift_ref[1, 1:2, :]

    def norm_one():
        def chunk(i, rows, carry):
            scaled, inverse = normalize(X[rows, :].astype(F32) + ACC[rows, :])
            SC1[rows, :] = scaled
            INV1[rows, :] = jnp.broadcast_to(inverse, (64, 128))
            FL[rows, :] = (scaled * g00 + b00).astype(BF16)
            return carry

        row_chunks(chunk)

    def ffn_forward(r):
        def block(n, carry):
            part = pl.ds(pl.multiple_of(n * 256, 256), 256)
            upward = mm(FL[...], unit_value(W.at[UP, r, :, :, :, :, part]))
            active, slope = gelu_pair(upward)
            ACT[r, :, part] = active.astype(BF16)
            DG[r, :, part] = slope.astype(DG.dtype)
            return carry

        lax.fori_loop(0, 3, block, 0)

    def ffn_down(r):
        accumulate(r == 0, mm(ACT[r], cols(DOWN, r, 0, 768)))

    def norm_two():
        def chunk(i, rows, carry):
            first = SC1[rows, :] * g00 + b00
            scaled, inverse = normalize(first + ACC[rows, :])
            SC2[rows, :] = scaled
            INV2[rows, :] = jnp.broadcast_to(inverse, (64, 128))
            out_ref[0, rows, :] = (scaled * g01 + b01).astype(BF16)
            return carry

        row_chunks(chunk)

    def transpose_into(dst, src):
        for i in range(2):
            dst[:, i * 128 : i * 128 + 128] = src[i * 128 : i * 128 + 128, :].T

    loads["x"].wait()
    loads["wa"].wait()
    attn_forward(0)
    gather_tick(0)
    gather_tick(1)
    transpose_into(XT, X)
    gather_tick(2)
    gather_tick(3)
    attn_forward(1)
    gather_tick(4)
    attn_forward(2)
    gather_tick(5)
    attn_forward(3)
    norm_one()
    loads["wu"].wait()
    loads["wd"].wait()
    gather_tick(6)
    ffn_forward(0)
    ffn_down(0)
    gather_tick(7)
    ffn_forward(1)
    ffn_down(1)
    gather_tick(8)
    transpose_into(FLT, FL)
    gather_tick(9)
    ffn_forward(2)
    ffn_down(2)
    gather_tick(10)
    ffn_forward(3)
    gather_tick(11)
    ffn_down(3)
    norm_two()

    exch = {}

    def exchange(e, value):
        E[e, 0] = value
        for r in range(1, 4):
            exch[e, r] = remote(E.at[e, 0], E.at[e, r], e_s.at[e, r - 1], e_r.at[e, r - 1], z_peer[r])

    def exchange_wait(e):
        for r in range(1, 4):
            exch[e, r].wait_recv()

    def exchange_sum(e):
        exchange_wait(e)
        return (E[e, 0] + E[e, 1]) + (E[e, 2] + E[e, 3])

    row_of = lax.broadcasted_iota(jnp.int32, (8, 768), 0)
    pair_of = row_of // 2

    def assemble(e, start):
        total = None
        for r in range(4):
            two = E[e, r][start : start + 2, :]
            four = jnp.concatenate([two, two, two, two], axis=0)
            part = jnp.where(pair_of == z_of[r], four, 0.0)
            total = part if total is None else total + part
        return total

    def own_row(value, j):
        return jnp.sum(jnp.where(row_of == 2 * z + j, value, 0.0), axis=0, keepdims=True)

    def two_rows(ref):
        return jnp.concatenate([ref[0:1, :], ref[128:129, :]], axis=0)

    inv_two = jnp.broadcast_to(two_rows(INV2)[:, 0:1], (2, 768))
    first_two = two_rows(SC1) * g00 + b00
    exchange(0, jnp.concatenate([two_rows(SC2), first_two, inv_two, inv_two], axis=0))

    loads["cot"].wait()

    def norm_two_back():
        def chunk(i, rows, carry):
            gains, shifts = carry
            which = lax.broadcasted_iota(jnp.int32, (64, 768), 0) + i * 64
            grad = jnp.where(which % SEG == 0, 0.0, COT[rows, :].astype(F32))
            scaled = SC2[rows, :]
            fed = normalize_back(grad, scaled, INV2[rows, 0:1], g01)
            GF[rows, :] = fed
            FDL[rows, :] = fed.astype(BF16)
            return (
                gains + jnp.sum(grad * scaled, axis=0, keepdims=True),
                shifts + jnp.sum(grad, axis=0, keepdims=True),
            )

        zero = jnp.zeros((1, 768), F32)
        gains, shifts = row_chunks(chunk, (zero, zero))
        NV[1:2, :] = gains
        NV[3:4, :] = shifts

    norm_two_back()
    transpose_into(FDLT, FDL)

    def grad_unit(k, r):
        return W.at[UP, r] if k == ATT else G.at[k - 1, r]

    order = [(DOWN, 1), (UP, 1), (DOWN, 2), (UP, 2), (DOWN, 3), (UP, 3), (DOWN, 0), (UP, 0)]
    order += [(ATT, 1), (ATT, 2), (ATT, 3), (ATT, 0)]
    s0, sa1, sb1, sa2, sb2, sz = {}, {}, {}, {}, {}, {}

    def sum_start(i):
        k, r = order[i]
        g = grad_unit(k, r)
        s0[i] = remote(g.at[:, :, nc], RC.at[i], rs_s.at[0, i], rs_r.at[0, i], core_peer)

    def add_low(a, b):
        return (a.astype(F32) + b.astype(F32)).astype(BF16)

    def sum_one(i):
        if not 0 <= i < 12:
            return
        k, r = order[i]
        g = grad_unit(k, r)
        s0[i].wait_recv()

        def block(j, carry):
            jy, jx = j // 2, j % 2
            g[jy, jx, c] = add_low(g[jy, jx, c], RC[i, jy, jx])
            return carry

        lax.fori_loop(0, 4, block, 0)
        sa1[i] = remote(g.at[:, nx, c, pl.ds(0, HALF)], RA1.at[i], rs_s.at[1, i], rs_r.at[1, i], x_peer)
        sb1[i] = remote(g.at[ny, :, c, pl.ds(HALF, HALF)], RB1.at[i], rs_s.at[2, i], rs_r.at[2, i], y_peer)

    def sum_two(i):
        if not 0 <= i < 12:
            return
        k, r = order[i]
        g = grad_unit(k, r)
        sa1[i].wait_recv()
        for j in range(2):
            g[j, x, c, 0:HALF, :] = add_low(g[j, x, c, 0:HALF, :], RA1[i, j])
        sa2[i] = remote(g.at[ny, x, c, pl.ds(0, HALF)], RA2.at[i], rs_s.at[3, i], rs_r.at[3, i], y_peer)
        sb1[i].wait_recv()
        for j in range(2):
            g[y, j, c, HALF:BLK, :] = add_low(g[y, j, c, HALF:BLK, :], RB1[i, j])
        sb2[i] = remote(g.at[y, nx, c, pl.ds(HALF, HALF)], RB2.at[i], rs_s.at[4, i], rs_r.at[4, i], x_peer)

    def sum_three(i):
        if not 0 <= i < 12:
            return
        k, r = order[i]
        g = grad_unit(k, r)
        sa2[i].wait_recv()
        g[y, x, c, 0:HALF, :] = add_low(g[y, x, c, 0:HALF, :], RA2[i])
        sb2[i].wait_recv()
        g[y, x, c, HALF:BLK, :] = add_low(g[y, x, c, HALF:BLK, :], RB2[i])
        if r:
            sz[k, r] = remote(g.at[y, x, c], RZ.at[k, r - 1], rs_s.at[5, i], rs_r.at[5, i], z_peer[r])

    def pump(i):
        sum_one(i)
        sum_two(i - 1)
        sum_three(i - 2)

    def sum_final(k):
        for r in range(1, 4):
            sz[k, r].wait_recv()
        g = grad_unit(k, 0)
        own = g[y, x, c].astype(F32) + RZ[k, 0].astype(F32)
        return own + (RZ[k, 1].astype(F32) + RZ[k, 2].astype(F32))

    def store_unit(ref, parts):
        for start, size, value in parts:
            ref[:, :, :, :, start : start + size] = value().astype(BF16).reshape(2, 2, 2, BLK, size)

    def store_ffn(k, r, lhs_t, rhs, extra=None):
        ref = grad_unit(k, r)

        def block(n, carry):
            part = pl.ds(pl.multiple_of(n * 256, 256), 256)
            value = mm(lhs_t[...], rhs[:, part])
            if extra is not None:
                value = value + mm(extra[0][...], extra[1][:, part])
            ref[:, :, :, :, part] = value.astype(BF16).reshape(2, 2, 2, BLK, 256)
            return carry

        lax.fori_loop(0, 3, block, 0)

    def ffn_back_one(r):
        ga = mm_nt(FDL[...], cols(DOWN, r, 0, 768))
        GU[...] = (ga * DG[r].astype(F32)).astype(BF16)

    def ffn_back_two(r, first):
        accumulate(first, mm_nt(GU[...], cols(UP, r, 0, 768)))

    def l1(k, start, size):
        return unit_value(L1.at[k, :, :, :, :, pl.ds(start, size)])

    live = {}

    def cross_one():
        exchange_wait(0)
        live["sc2"] = assemble(0, 0)
        first8 = assemble(0, 2)
        live["inv2"] = assemble(0, 4)[:, 0:1]
        summary = live["sc2"] * g01 + b01
        live["summary"] = summary
        live["summary_low"] = summary.astype(BF16)
        live["first8_low"] = first8.astype(BF16)
        loads["l1a"].wait()
        qkv = mm(live["summary_low"], l1(ATT, 0, 576)).astype(BF16).astype(F32)
        pad = jnp.zeros((120, 64), F32)
        keep = allowed_ref[...] > 0.5
        mixes = []
        for h in range(3):
            q = qkv[:, h * 64 : h * 64 + 64].astype(BF16)
            key = jnp.concatenate([qkv[:, 192 + h * 64 : 256 + h * 64], pad], axis=0).astype(BF16)
            val = jnp.concatenate([qkv[:, 384 + h * 64 : 448 + h * 64], pad], axis=0).astype(BF16)
            scores = jnp.where(keep, mm_nt(q, key) * SCALE, MASK_FILL)
            top = jnp.max(scores, axis=-1, keepdims=True)
            expd = jnp.exp(scores - top)
            prob = expd * (1.0 / jnp.sum(expd, axis=-1, keepdims=True))
            live["prob", h], live["q", h], live["key", h], live["val", h] = prob, q, key, val
            mixes.append(mm(prob.astype(BF16), val))
        mix = jnp.concatenate(mixes, axis=-1).astype(BF16)
        live["mix"] = mix
        exchange(1, mm_nt(mix, l1(ATT, 576, 192)))

    def cross_two():
        attended = exchange_sum(1)
        live["xs1"], live["xi1"] = normalize(live["summary"] + attended)
        first = live["xs1"] * g10 + b10
        live["xfirst"] = first
        live["xfirst_low"] = first.astype(BF16)
        loads["l1u"].wait()
        loads["l1d"].wait()
        active, live["xdg"] = gelu_pair(mm(live["xfirst_low"], l1(UP, 0, 768)))
        live["xact"] = active.astype(BF16)
        exchange(2, mm(live["xact"], l1(DOWN, 0, 768)))

    def cross_three():
        fed = exchange_sum(2)
        xs2, xi2 = normalize(live["xfirst"] + fed)
        upper = xs2 * g11 + b11
        for j in range(2):
            out_ref[0, j * 128 : j * 128 + 1, :] = own_row(upper, j).astype(BF16)
        loads["c8"].wait()
        grad_top = C8[...].astype(F32)[:, 0, :]
        live["xs2"], live["xi2"] = xs2, xi2
        grad_fed = normalize_back(grad_top, live["xs2"], live["xi2"], g11)
        NV[5:6, :] = jnp.sum(grad_top * live["xs2"], axis=0, keepdims=True)
        NV[7:8, :] = jnp.sum(grad_top, axis=0, keepdims=True)
        live["xgf"] = grad_fed
        live["xfed_low"] = grad_fed.astype(BF16)
        ga = mm_nt(live["xfed_low"], l1(DOWN, 0, 768))
        live["xgu"] = (ga * live["xdg"]).astype(BF16)
        exchange(3, mm_nt(live["xgu"], l1(UP, 0, 768)))

    def cross_four():
        grad_first = live["xgf"] + exchange_sum(3)
        grad_att = normalize_back(grad_first, live["xs1"], live["xi1"], g10)
        NV[4:5, :] = jnp.sum(grad_first * live["xs1"], axis=0, keepdims=True)
        NV[6:7, :] = jnp.sum(grad_first, axis=0, keepdims=True)
        live["xga"] = grad_att
        att_low = grad_att.astype(BF16)
        live["xatt_low"] = att_low
        gm = mm(att_low, l1(ATT, 576, 192)).astype(BF16)
        gqs, gks, gvs = [], [], []
        for h in range(3):
            gmh = gm[:, h * 64 : h * 64 + 64]
            prob = live["prob", h]
            gp = mm_nt(gmh, live["val", h])
            inner = jnp.sum(gp * prob, axis=-1, keepdims=True)
            gs = (prob * (gp - inner)).astype(BF16)
            gqs.append(mm(gs, live["key", h]) * SCALE)
            gks.append(mm_tn(gs, live["q", h])[0:8, :] * SCALE)
            gvs.append(mm_tn(prob.astype(BF16), gmh)[0:8, :])
        gqkv = jnp.concatenate(gqs + gks + gvs, axis=-1).astype(BF16)
        live["xgqkv"] = gqkv
        exchange(4, mm_nt(gqkv, l1(ATT, 0, 576)))

    def cross_five():
        grad_summary = live["xga"] + exchange_sum(4)
        mine = jnp.where(pair_of == z, grad_summary, 0.0)
        NV[1:2, :] += jnp.sum(mine * live["sc2"], axis=0, keepdims=True)
        NV[3:4, :] += jnp.sum(mine, axis=0, keepdims=True)
        gfed8 = normalize_back(grad_summary, live["sc2"], live["inv2"], g01)
        live["gfed8"] = gfed8
        fed8_low = gfed8.astype(BF16)
        live["fed8_low"] = fed8_low
        active, slope = gelu_pair(mm(live["first8_low"], cols(UP, 0, 0, 768)))
        live["act8"] = active.astype(BF16)
        ga = mm_nt(fed8_low, cols(DOWN, 0, 0, 768))
        live["gu8"] = (ga * slope).astype(BF16)
        exchange(5, mm_nt(live["gu8"], cols(UP, 0, 0, 768)))

    def cross_six():
        part = exchange_sum(5)
        for j in range(2):
            GF[j * 128 : j * 128 + 1, :] = own_row(live["gfed8"], j)
            ACC[j * 128 : j * 128 + 1, :] = own_row(part, j)

    def norm_one_back():
        def chunk(i, rows, carry):
            gains, shifts = carry
            grad = GF[rows, :] + ACC[rows, :]
            scaled = SC1[rows, :]
            att = normalize_back(grad, scaled, INV1[rows, 0:1], g00)
            GF[rows, :] = att
            FDL[rows, :] = att.astype(BF16)
            return (
                gains + jnp.sum(grad * scaled, axis=0, keepdims=True),
                shifts + jnp.sum(grad, axis=0, keepdims=True),
            )

        zero = jnp.zeros((1, 768), F32)
        gains, shifts = row_chunks(chunk, (zero, zero))
        NV[0:1, :] = gains
        NV[2:3, :] = shifts

    def attn_backward(r, first):
        GM[...] = mm(FDL[...], cols(ATT, r, 576, 192)).astype(BF16)

        def segment(s, carry):
            rows = pl.ds(pl.multiple_of(s * SEG, SEG), SEG)
            qkv = QKV[r, rows, :]
            gm = GM[rows, :]
            gqs, gks, gvs = [], [], []
            for h in range(3):
                q = qkv[:, h * 64 : h * 64 + 64]
                key = qkv[:, 192 + h * 64 : 256 + h * 64]
                val = qkv[:, 384 + h * 64 : 448 + h * 64]
                gmh = gm[:, h * 64 : h * 64 + 64]
                prob = PR[r, h, rows, :]
                gp = mm_nt(gmh, val)
                inner = jnp.sum(gp * prob, axis=-1, keepdims=True)
                gs = (prob * (gp - inner)).astype(BF16)
                gqs.append(mm(gs, key) * SCALE)
                gks.append(mm_tn(gs, q) * SCALE)
                gvs.append(mm_tn(prob.astype(BF16), gmh))
            GQ[rows, :] = jnp.concatenate(gqs + gks + gvs, axis=-1).astype(BF16)
            return carry

        lax.fori_loop(0, 2, segment, 0)
        store_unit(
            grad_unit(ATT, r),
            [
                (0, 576, lambda: mm(XT[...], GQ[...])),
                (576, 192, lambda: mm(FDLT[...], MIX[r])),
            ],
        )
        accumulate(first, mm_nt(GQ[...], cols(ATT, r, 0, 576)))

    fac = {}

    def factor_start():
        wide = lambda v: v.astype(F32)
        zero_a, zero_b = jnp.zeros((8, 192), F32), jnp.zeros((8, 576), F32)
        att_left = jnp.concatenate([wide(live["xgqkv"]), zero_a], axis=-1)
        att_right = jnp.concatenate([zero_b, wide(live["mix"])], axis=-1)
        right = jnp.concatenate([wide(live["xact"]), wide(live["xgu"]), att_left, att_right], axis=0)
        left = jnp.concatenate(
            [wide(live["xfed_low"]), wide(live["xfirst_low"]), wide(live["summary_low"]), wide(live["xatt_low"])],
            axis=0,
        )
        FAC[y, x, c, 0:32, :] = right.astype(BF16)
        FAC[y, x, c, 32:64, :] = left.astype(BF16)
        part = FAC.at[y, x, c]
        fac[0] = remote(part, part, f_s.at[0], f_r.at[0], x_peer)

    def factor_two():
        fac[0].wait_recv()
        part = FAC.at[y, :, c]
        fac[1] = remote(part, part, f_s.at[1], f_r.at[1], y_peer)

    def factor_three():
        fac[1].wait_recv()
        part = FAC.at[:, :, c]
        fac[2] = remote(part, part, f_s.at[2], f_r.at[2], core_peer)

    def turn_rows(value):
        rows = value.shape[0]
        full = jnp.concatenate([value, jnp.zeros((128 - rows, value.shape[1]), F32)], axis=0)
        return full.T[:, 0:rows]

    def write_unit(layer, k, value):
        if k == ATT:
            for i in range(3):
                qkvg_ref[layer, i] = value[:, i * 192 : i * 192 + 192]
            outg_ref[layer] = turn_rows(value[:, 576:768])
        elif k == UP:
            upg_ref[layer] = value
        else:
            downg_ref[layer] = turn_rows(value)

    def factor_final():
        fac[2].wait_recv()
        left = FAC[:, :, :, 32:64, :].reshape(256, 768)
        for i in range(2):
            LT[:, i * 128 : i * 128 + 128] = left[i * 128 : i * 128 + 128, :].T
        mine = LT[pl.ds(pl.multiple_of(dp * BLK, BLK), BLK), :].astype(F32)
        kind = (lax.broadcasted_iota(jnp.int32, (BLK, 256), 1) // 8) % 4
        right = FAC[:, :, :, 0:32, :].reshape(256, 768)
        write_unit(1, DOWN, mm(jnp.where(kind == 0, mine, 0.0).astype(BF16), right))
        write_unit(1, UP, mm(jnp.where(kind == 1, mine, 0.0).astype(BF16), right))
        write_unit(1, ATT, mm(jnp.where(kind >= 2, mine, 0.0).astype(BF16), right))

    vec = {}

    def norm_grads_start():
        exchange(6, NV[...])

    def norm_grads_two():
        total = jnp.where(row_of < 4, exchange_sum(6), NV[...])
        pad = jnp.zeros((8, 32), F32)
        for p in range(8):
            SV[p // 4, (p // 2) % 2, p % 2] = jnp.concatenate([total[:, p * BLK : p * BLK + BLK], pad], axis=-1)
        for m in range(1, 8):
            ty = y if m // 4 == 0 else ny
            tx = x if (m // 2) % 2 == 0 else nx
            tc = c if m % 2 == 0 else nc
            vec[m] = remote(
                SV.at[ty, tx, tc], RSV.at[m - 1], v_s.at[m - 1], v_r.at[m - 1], (plane_index(m), z)
            )

    def norm_grads_final():
        total = SV[y, x, c]
        for m in range(1, 8):
            vec[m].wait_recv()
            total = total + RSV[m - 1]
        gaing_ref[...] = total[0:2, 0:BLK]
        shiftg_ref[...] = total[2:4, 0:BLK]
        crossg_ref[0] = total[4:6, 0:BLK]
        crossg_ref[1] = total[6:8, 0:BLK]

    def eight_turned(dst, value):
        full = jnp.concatenate([value.astype(F32), jnp.zeros((120, 768), F32)], axis=0)
        dst[...] = full.T.astype(BF16)

    def eight_rows(dst, value):
        dst[...] = jnp.concatenate([value.astype(F32), jnp.zeros((120, 768), F32)], axis=0).astype(BF16)

    cross_one()
    ffn_back_one(1)
    store_ffn(DOWN, 1, FDLT, ACT.at[1])
    sum_start(0)
    store_ffn(UP, 1, FLT, GU)
    sum_start(1)
    ffn_back_two(1, True)
    cross_two()
    pump(0)
    ffn_back_one(2)
    store_ffn(DOWN, 2, FDLT, ACT.at[2])
    sum_start(2)
    store_ffn(UP, 2, FLT, GU)
    sum_start(3)
    ffn_back_two(2, False)
    cross_three()
    pump(1)
    ffn_back_one(3)
    store_ffn(DOWN, 3, FDLT, ACT.at[3])
    sum_start(4)
    store_ffn(UP, 3, FLT, GU)
    sum_start(5)
    ffn_back_two(3, False)
    cross_four()
    factor_start()
    pump(2)
    cross_five()
    pump(3)
    ffn_back_one(0)
    eight_turned(EL, live["fed8_low"])
    eight_rows(ER, live["act8"])
    store_ffn(DOWN, 0, FDLT, ACT.at[0], (EL, ER))
    sum_start(6)
    eight_turned(EL, live["first8_low"])
    eight_rows(ER, live["gu8"])
    store_ffn(UP, 0, FLT, GU, (EL, ER))
    sum_start(7)
    ffn_back_two(0, False)
    cross_six()
    norm_one_back()
    norm_grads_start()
    transpose_into(FDLT, FDL)
    for table in (a1, b1, a2, b2, cc):
        for i in range(9):
            table[i].wait_send()
            waited.append(id(table[i]))
    pump(4)
    factor_two()
    attn_backward(1, True)
    sum_start(8)
    pump(5)
    factor_three()
    norm_grads_two()
    attn_backward(2, False)
    sum_start(9)
    pump(6)
    attn_backward(3, False)
    sum_start(10)
    pump(7)
    attn_backward(0, False)
    sum_start(11)
    ing_ref[0] = (GF[...] + ACC[...]).astype(BF16)
    pump(8)
    factor_final()
    pump(9)
    norm_grads_final()
    pump(10)
    write_unit(0, DOWN, sum_final(DOWN))
    pump(11)
    write_unit(0, UP, sum_final(UP))
    pump(12)
    pump(13)
    write_unit(0, ATT, sum_final(ATT))
    for copy in sends:
        if id(copy) not in waited:
            copy.wait_send()


def fused_body(
    inputs, doc_ids, qkv_weight, out_weight, up_weight, down_weight, norm_gain, norm_shift, cotangent
):
    qkv_rows = qkv_weight.transpose(0, 2, 1, 3).reshape(2, 768, 576)
    wa = jnp.concatenate([qkv_rows, out_weight.transpose(0, 2, 1)], axis=-1).reshape(2, 2, 2, 2, BLK, 768)
    wu = up_weight.reshape(2, 2, 2, 2, BLK, 768)
    wd = down_weight.reshape(2, 2, 2, 2, BLK, 768)
    same = doc_ids[0][:, None] == doc_ids[0][None, :]
    allowed = jnp.pad(same.astype(F32), ((0, 0), (0, 120)))
    whole = pl.BlockSpec(memory_space=pl.ANY)
    vmem = pl.BlockSpec(memory_space=pltpu.VMEM)
    blocks = (2, 2, 2, BLK, 768)
    sem = pltpu.SemaphoreType.DMA
    return pl.pallas_call(
        fused_kernel,
        out_shape=(
            jax.ShapeDtypeStruct((1, 256, 768), BF16),
            jax.ShapeDtypeStruct((1, 256, 768), BF16),
            jax.ShapeDtypeStruct((2, 3, BLK, 192), F32),
            jax.ShapeDtypeStruct((2, 192, BLK), F32),
            jax.ShapeDtypeStruct((2, BLK, 768), F32),
            jax.ShapeDtypeStruct((2, 768, BLK), F32),
            jax.ShapeDtypeStruct((2, BLK), F32),
            jax.ShapeDtypeStruct((2, BLK), F32),
            jax.ShapeDtypeStruct((2, 2, BLK), F32),
        ),
        in_specs=[whole, whole, whole, vmem, whole, whole, whole, vmem, vmem],
        out_specs=(vmem,) * 9,
        scratch_shapes=[
            pltpu.VMEM((3, 4) + blocks, BF16),
            pltpu.VMEM((2, 4) + blocks, BF16),
            pltpu.VMEM((12, 2, 2, BLK, 768), BF16),
            pltpu.VMEM((12, 2, HALF, 768), BF16),
            pltpu.VMEM((12, 2, HALF, 768), BF16),
            pltpu.VMEM((12, HALF, 768), BF16),
            pltpu.VMEM((12, HALF, 768), BF16),
            pltpu.VMEM((3, 3, BLK, 768), BF16),
            pltpu.VMEM((3,) + blocks, BF16),
            pltpu.VMEM((256, 768), BF16),
            pltpu.VMEM((256, 768), BF16),
            pltpu.VMEM((4, 256, 576), BF16),
            pltpu.VMEM((4, 3, 256, 128), F32),
            pltpu.VMEM((4, 256, 192), BF16),
            pltpu.VMEM((4, 256, 768), BF16),
            pltpu.VMEM((4, 256, 768), BF16),
            pltpu.VMEM((256, 768), BF16),
            pltpu.VMEM((256, 576), BF16),
            pltpu.VMEM((256, 768), F32),
            pltpu.VMEM((256, 768), F32),
            pltpu.VMEM((256, 768), F32),
            pltpu.VMEM((256, 768), F32),
            pltpu.VMEM((256, 768), BF16),
            pltpu.VMEM((768, 256), BF16),
            pltpu.VMEM((256, 768), BF16),
            pltpu.VMEM((768, 256), BF16),
            pltpu.VMEM((768, 256), BF16),
            pltpu.VMEM((256, 192), BF16),
            pltpu.VMEM((8, 16, 768), BF16),
            pltpu.VMEM((256, 128), F32),
            pltpu.VMEM((256, 128), F32),
            pltpu.VMEM((2, 2, 2, 64, 768), BF16),
            pltpu.VMEM((768, 256), BF16),
            pltpu.VMEM((768, 128), BF16),
            pltpu.VMEM((128, 768), BF16),
            pltpu.VMEM((7, 4, 8, 768), F32),
            pltpu.VMEM((8, 768), F32),
            pltpu.VMEM((2, 2, 2, 8, 128), F32),
            pltpu.VMEM((7, 8, 128), F32),
            sem((9,)),
            sem((6, 9)),
            sem((6, 9)),
            sem((6, 12)),
            sem((6, 12)),
            sem((7, 3)),
            sem((7, 3)),
            sem((3,)),
            sem((3,)),
            sem((7,)),
            sem((7,)),
        ],
        compiler_params=pltpu.CompilerParams(
            collective_id=0, has_side_effects=True, vmem_limit_bytes=63 * 2**20
        ),
    )(
        inputs, cotangent, cotangent.reshape(8, SEG, 768), allowed, wa, wu, wd, norm_gain, norm_shift
    )


def solution(mesh):
    in_specs = (
        P("dp", None, None),
        P("dp", None),
        P(None, None, None, "tensor"),
        P(None, "tensor", None),
        P(None, None, "tensor"),
        P(None, "tensor", None),
        P(),
        P(),
        P("dp", None, None),
    )
    out_specs = (
        P("dp", "tensor", None),
        P("dp", "tensor", None),
        P(None, None, "dp", "tensor"),
        P(None, "tensor", "dp"),
        P(None, "dp", "tensor"),
        P(None, "tensor", "dp"),
        P(None, "dp"),
        P(None, "dp"),
        P(None, None, "dp"),
    )
    fits = dict(mesh.shape) == {"dp": 8, "tensor": 4}
    chosen = fused_body if fits else body
    return jax.shard_map(chosen, mesh=mesh, in_specs=in_specs, out_specs=out_specs, check_vma=False)
```

```python
from functools import partial
import math

import jax
import jax.numpy as jnp
from jax import lax
from jax.experimental import pallas as pl
from jax.experimental.pallas import tpu as pltpu
from jax.sharding import PartitionSpec as P

HEAD_DIM = 64
SEG = 128


EPSILON = 1e-05
MASK_FILL = -1000000000.0


def layer_norm(values, gain_row, shift_row):
    center = jnp.mean(values, axis=-1, keepdims=True)
    offset = values - center
    spread = jnp.mean(offset * offset, axis=-1, keepdims=True)
    inverse = lax.rsqrt(spread + EPSILON)
    scaled = offset * inverse
    return (scaled * gain_row + shift_row, (scaled, inverse))


def norm_back(grad_out, saved, gain_row):
    scaled, inverse = saved
    weighted = grad_out * gain_row
    mean_one = jnp.mean(weighted, axis=-1, keepdims=True)
    mean_two = jnp.mean(weighted * scaled, axis=-1, keepdims=True)
    grad_in = inverse * (weighted - mean_one - scaled * mean_two)
    return (grad_in, jnp.sum(grad_out * scaled, axis=(0, 1)), jnp.sum(grad_out, axis=(0, 1)))


def score_block(head_split, allowed):
    scores = jnp.einsum(
        "bqhe,bkhe->bhqk", head_split[0], head_split[1], preferred_element_type=jnp.float32
    ) * (1.0 / math.sqrt(HEAD_DIM))
    if allowed is not None:
        scores = jnp.where(allowed, scores, MASK_FILL)
    return scores


def attend_forward(rows_low, qkv_local, allowed):
    batch_count = rows_low.shape[0]
    length = rows_low.shape[1]
    project = jnp.einsum(
        "brd,cde->cbre", rows_low, qkv_local, preferred_element_type=jnp.float32
    ).astype(jnp.bfloat16)
    head_split = project.reshape(3, batch_count, length, -1, HEAD_DIM)
    scores = score_block(head_split, allowed)
    log_total = jax.nn.logsumexp(scores, axis=-1)
    soft_low = jnp.exp(scores - log_total[..., None]).astype(jnp.bfloat16)
    mixture = jnp.einsum(
        "bhqk,bkhe->bqhe", soft_low, head_split[2], preferred_element_type=jnp.float32
    )
    return (project, log_total, mixture.astype(jnp.bfloat16).reshape(batch_count, length, -1))


def attend_backward(rows_low, qkv_local, out_local, project, log_total, mixture, grad_low, allowed):
    batch_count = rows_low.shape[0]
    length = rows_low.shape[1]
    head_split = project.reshape(3, batch_count, length, -1, HEAD_DIM)
    grad_mixture = jnp.einsum(
        "brd,fd->brf", grad_low, out_local, preferred_element_type=jnp.float32
    ).astype(jnp.bfloat16)
    out_local_grad = jnp.einsum(
        "brf,brd->fd", mixture, grad_low, preferred_element_type=jnp.float32
    )
    grad_heads = grad_mixture.reshape(batch_count, length, -1, HEAD_DIM)
    scores = score_block(head_split, allowed)
    soft_full = jnp.exp(scores - log_total[..., None])
    grad_soft = jnp.einsum(
        "bqhe,bkhe->bhqk", grad_heads, head_split[2], preferred_element_type=jnp.float32
    )
    row_inner = jnp.sum(grad_soft * soft_full, axis=-1, keepdims=True)
    grad_scores = (soft_full * (grad_soft - row_inner)).astype(jnp.bfloat16)
    scale_factor = 1.0 / math.sqrt(HEAD_DIM)
    grad_query = (
        jnp.einsum(
            "bhqk,bkhe->bqhe", grad_scores, head_split[1], preferred_element_type=jnp.float32
        )
        * scale_factor
    )
    grad_key = (
        jnp.einsum(
            "bhqk,bqhe->bkhe", grad_scores, head_split[0], preferred_element_type=jnp.float32
        )
        * scale_factor
    )
    grad_value = jnp.einsum(
        "bhqk,bqhe->bkhe",
        soft_full.astype(jnp.bfloat16),
        grad_heads,
        preferred_element_type=jnp.float32,
    )
    grad_project = (
        jnp.stack([grad_query, grad_key, grad_value])
        .reshape(3, batch_count, length, -1)
        .astype(jnp.bfloat16)
    )
    qkv_local_grad = jnp.einsum(
        "brd,cbre->cde", rows_low, grad_project, preferred_element_type=jnp.float32
    )
    input_part = jnp.einsum(
        "cbre,cde->brd", grad_project, qkv_local, preferred_element_type=jnp.float32
    )
    return (input_part, qkv_local_grad, out_local_grad)


def expand_forward(rows_low, up_local, down_local):
    upward = jnp.einsum("brd,df->brf", rows_low, up_local, preferred_element_type=jnp.float32)
    active = jax.nn.gelu(upward, approximate=False).astype(jnp.bfloat16)
    return (
        upward,
        active,
        jnp.einsum("brf,fd->brd", active, down_local, preferred_element_type=jnp.float32),
    )


def expand_backward(rows_low, up_local, down_local, upward, active, grad_low):
    grad_active = jnp.einsum(
        "brd,fd->brf", grad_low, down_local, preferred_element_type=jnp.float32
    )
    down_local_grad = jnp.einsum(
        "brf,brd->fd", active, grad_low, preferred_element_type=jnp.float32
    )
    gelu_pull = jax.vjp(partial(jax.nn.gelu, approximate=False), upward)[1]
    grad_upward = gelu_pull(grad_active)[0].astype(jnp.bfloat16)
    up_local_grad = jnp.einsum(
        "brd,brf->df", rows_low, grad_upward, preferred_element_type=jnp.float32
    )
    input_part = jnp.einsum(
        "brf,df->brd", grad_upward, up_local, preferred_element_type=jnp.float32
    )
    return (input_part, up_local_grad, down_local_grad)


def body(
    inputs,
    doc_ids,
    qkv_weight,
    out_weight,
    up_weight,
    down_weight,
    norm_gain,
    norm_shift,
    cotangent,
):
    groups = lax.axis_size("tensor")
    position = lax.axis_index("tensor")
    model_width = inputs.shape[2]
    segment_count = inputs.shape[1] // SEG
    own_count = segment_count // groups
    row_start = position * own_count

    def final_rows(values):
        return lax.dynamic_slice_in_dim(values, row_start, own_count, 0)

    def forward_sum(partial_term):
        return lax.psum(partial_term.astype(jnp.bfloat16), "tensor").astype(jnp.float32)

    def backward_sum(partial_term):
        return lax.psum(partial_term.astype(jnp.bfloat16), "tensor").astype(jnp.float32)

    def cross_sum(partial_term):
        return lax.psum(partial_term.astype(jnp.bfloat16), "tensor").astype(jnp.float32)

    def cross_grad_sum(partial_term):
        return lax.psum(partial_term, "tensor")

    tokens = inputs[0].reshape(segment_count, SEG, model_width)
    tokens_wide = tokens.astype(jnp.float32)
    lower_proj, lower_total, lower_mix = attend_forward(tokens, qkv_weight[0], None)
    attended = forward_sum(
        jnp.einsum("brf,fd->brd", lower_mix, out_weight[0], preferred_element_type=jnp.float32)
    )
    first_norm, first_saved = layer_norm(tokens_wide + attended, norm_gain[0, 0], norm_shift[0, 0])
    first_low = first_norm.astype(jnp.bfloat16)
    lower_up, lower_active, fed_term = expand_forward(first_low, up_weight[0], down_weight[0])
    second, second_saved = layer_norm(
        first_norm + forward_sum(fed_term), norm_gain[0, 1], norm_shift[0, 1]
    )
    summary = second[:, 0, :]
    summary = summary[None]
    same_doc = (doc_ids[0][:, None] == doc_ids[0][None, :])[None, None]
    summary_low = summary.astype(jnp.bfloat16)
    upper_proj, upper_total, upper_mix = attend_forward(summary_low, qkv_weight[1], same_doc)
    upper_att = cross_sum(
        jnp.einsum("brf,fd->brd", upper_mix, out_weight[1], preferred_element_type=jnp.float32)
    )
    upper_first, upper_saved_one = layer_norm(
        summary + upper_att, norm_gain[1, 0], norm_shift[1, 0]
    )
    upper_first_low = upper_first.astype(jnp.bfloat16)
    upper_up, upper_active, upper_fed = expand_forward(
        upper_first_low, up_weight[1], down_weight[1]
    )
    upper_out, upper_saved_two = layer_norm(
        upper_first + cross_sum(upper_fed), norm_gain[1, 1], norm_shift[1, 1]
    )
    joined = second.at[:, 0, :].set(upper_out[0])
    outputs_own = final_rows(joined).reshape(1, -1, model_width).astype(jnp.bfloat16)
    grad_full = cotangent[0].reshape(segment_count, SEG, model_width).astype(jnp.float32)
    grad_top = grad_full[:, 0, :][None]
    grad_upper_fed, gain_cross_two, shift_cross_two = norm_back(
        grad_top, upper_saved_two, norm_gain[1, 1]
    )
    cross_part, up_cross, down_cross = expand_backward(
        upper_first_low,
        up_weight[1],
        down_weight[1],
        upper_up,
        upper_active,
        grad_upper_fed.astype(jnp.bfloat16),
    )
    grad_upper_first = grad_upper_fed + cross_grad_sum(cross_part)
    grad_upper_att, gain_cross_one, shift_cross_one = norm_back(
        grad_upper_first, upper_saved_one, norm_gain[1, 0]
    )
    cross_input_part, qkv_cross, out_cross = attend_backward(
        summary_low,
        qkv_weight[1],
        out_weight[1],
        upper_proj,
        upper_total,
        upper_mix,
        grad_upper_att.astype(jnp.bfloat16),
        same_doc,
    )
    grad_summary = grad_upper_att + cross_grad_sum(cross_input_part)
    grad_second = grad_full.at[:, 0, :].set(grad_summary[0])
    grad_fed, gain_seg_two, shift_seg_two = norm_back(grad_second, second_saved, norm_gain[0, 1])
    fed_low = grad_fed.astype(jnp.bfloat16)
    seg_part, up_seg, down_seg = expand_backward(
        first_low, up_weight[0], down_weight[0], lower_up, lower_active, fed_low
    )
    grad_first = grad_fed + backward_sum(seg_part)
    grad_att, gain_seg_one, shift_seg_one = norm_back(grad_first, first_saved, norm_gain[0, 0])
    att_low = grad_att.astype(jnp.bfloat16)
    seg_input_part, qkv_seg, out_seg = attend_backward(
        tokens, qkv_weight[0], out_weight[0], lower_proj, lower_total, lower_mix, att_low, None
    )
    input_full = grad_att + backward_sum(seg_input_part)
    input_own = final_rows(input_full).reshape(1, -1, model_width).astype(jnp.bfloat16)
    seg_gain = jnp.stack([gain_seg_one, gain_seg_two])
    seg_shift = jnp.stack([shift_seg_one, shift_seg_two])
    cross_norm = jnp.stack(
        [jnp.stack([gain_cross_one, gain_cross_two]), jnp.stack([shift_cross_one, shift_cross_two])]
    )
    qkv_all = jnp.stack([qkv_seg, qkv_cross])
    out_all = jnp.stack([out_seg, out_cross])
    up_all = jnp.stack([up_seg, up_cross])
    down_all = jnp.stack([down_seg, down_cross])
    summed = (
        lax.psum_scatter(qkv_all, "dp", scatter_dimension=2, tiled=True),
        lax.psum_scatter(out_all, "dp", scatter_dimension=2, tiled=True),
        lax.psum_scatter(up_all, "dp", scatter_dimension=1, tiled=True),
        lax.psum_scatter(down_all, "dp", scatter_dimension=2, tiled=True),
        lax.psum_scatter(seg_gain, "dp", scatter_dimension=1, tiled=True),
        lax.psum_scatter(seg_shift, "dp", scatter_dimension=1, tiled=True),
        lax.psum_scatter(cross_norm, "dp", scatter_dimension=2, tiled=True),
    )
    return (
        outputs_own,
        input_own,
        summed[0],
        summed[1],
        summed[2],
        summed[3],
        summed[4],
        summed[5],
        summed[6],
    )


MESH = pl.DeviceIdType.MESH
F32 = jnp.float32
BF16 = jnp.bfloat16
SCALE = 1.0 / math.sqrt(HEAD_DIM)
ATT, UP, DOWN = 0, 1, 2
BLK = 96
HALF = 48


def mm(a, b):
    return lax.dot_general(a, b, (((1,), (0,)), ((), ())), preferred_element_type=F32)


def mm_nt(a, b):
    return lax.dot_general(a, b, (((1,), (1,)), ((), ())), preferred_element_type=F32)


def mm_tn(a, b):
    return lax.dot_general(a, b, (((0,), (0,)), ((), ())), preferred_element_type=F32)


def normalize(values):
    center = jnp.mean(values, axis=-1, keepdims=True)
    offset = values - center
    spread = jnp.mean(offset * offset, axis=-1, keepdims=True)
    inverse = lax.rsqrt(spread + EPSILON)
    return offset * inverse, inverse


def normalize_back(grad_out, scaled, inverse, gain_row):
    weighted = grad_out * gain_row
    mean_one = jnp.mean(weighted, axis=-1, keepdims=True)
    mean_two = jnp.mean(weighted * scaled, axis=-1, keepdims=True)
    return inverse * (weighted - mean_one - scaled * mean_two)


def gelu_pair(upward):
    cdf = 0.5 * (1.0 + lax.erf(upward * math.sqrt(0.5)))
    pdf = jnp.exp(upward * upward * -0.5) * (1.0 / math.sqrt(2.0 * math.pi))
    return upward * cdf, cdf + upward * pdf


def fused_kernel(
    tokens_hbm, cot_hbm, cot_seg, doc_ref, wq_hbm, wo_hbm, wu_hbm, wd_hbm, gain_ref, shift_ref,
    out_ref, ing_ref, qkvg_ref, outg_ref, upg_ref, downg_ref, gaing_ref, shiftg_ref, crossg_ref,
    W, G, RC, RA1, RB1, RA2, RB2, RZ, L1, X, COT, QKV, PR, MIX, ACT, DG, GU, GQ, ACC, SC1, SC2, GF,
    FL, FLT, FDL, FDLT, XT, GM, C8, INV1, INV2, FAC, LT, EL, ER, E, NV, SV, RSV,
    sem_local, ag_s, ag_r, rs_s, rs_r, e_s, e_r, f_s, f_r, v_s, v_r,
):
    dp = lax.axis_index("dp")
    z = lax.axis_index("tensor")
    c = dp % 2
    x = (dp // 2) % 2
    y = dp // 4
    nc, nx, ny = 1 - c, 1 - x, 1 - y
    core_peer = (dp + 1 - 2 * c, z)
    x_peer = (dp + 2 - 4 * x, z)
    y_peer = (dp + 4 - 8 * y, z)
    z_peer = [None, (dp, z + 1 - 2 * (z % 2)), (dp, z + 2 - 4 * (z // 2)), (dp, 3 - z)]
    z_of = [z, z + 1 - 2 * (z % 2), z + 2 - 4 * (z // 2), 3 - z]

    def plane_index(m):
        ty = y if m // 4 == 0 else ny
        tx = x if (m // 2) % 2 == 0 else nx
        tc = c if m % 2 == 0 else nc
        return ty * 4 + tx * 2 + tc

    sends = []
    waited = []

    def remote(src, dst, ssem, rsem, target):
        copy = pltpu.make_async_remote_copy(
            src_ref=src, dst_ref=dst, send_sem=ssem, recv_sem=rsem, device_id=target, device_id_type=MESH
        )
        copy.start()
        sends.append(copy)
        return copy

    loads = {}

    def load(name, index, src, dst):
        copy = pltpu.make_async_copy(src, dst, sem_local.at[index])
        copy.start()
        loads[name] = copy

    load("x", 0, tokens_hbm.at[0, pl.ds(pl.multiple_of(z * 256, 256), 256)], X)
    load("wqk", 1, wq_hbm.at[0, pl.ds(0, 2)], W.at[ATT, 0, 0])
    load("wv", 9, wq_hbm.at[0, 2], W.at[ATT, 0, 1, 0])
    load("wo", 10, wo_hbm.at[0], W.at[ATT, 0, 1, 1])
    load("wu", 2, wu_hbm.at[0], W.at[UP, 0])
    load("wd", 3, wd_hbm.at[0], W.at[DOWN, 0])
    load("cot", 4, cot_hbm.at[0, pl.ds(pl.multiple_of(z * 256, 256), 256)], COT)
    load("l1qk", 5, wq_hbm.at[1, pl.ds(0, 2)], L1.at[ATT, 0])
    load("l1v", 11, wq_hbm.at[1, 2], L1.at[ATT, 1, 0])
    load("l1o", 12, wo_hbm.at[1], L1.at[ATT, 1, 1])
    load("l1u", 6, wu_hbm.at[1], L1.at[UP])
    load("l1d", 7, wd_hbm.at[1], L1.at[DOWN])
    load("c8", 8, cot_seg.at[:, pl.ds(0, 16)], C8)

    barrier = pltpu.get_barrier_semaphore()
    for m in range(1, 8):
        pl.semaphore_signal(barrier, inc=1, device_id=(plane_index(m), z), device_id_type=MESH)
    for r in range(1, 4):
        pl.semaphore_signal(barrier, inc=1, device_id=z_peer[r], device_id_type=MESH)
    pl.semaphore_wait(barrier, 10)

    own_unit = [W.at[ATT, 0], wu_hbm.at[0], wd_hbm.at[0]]
    units = [(ATT, 1), (ATT, 2), (ATT, 3), (UP, 1), (DOWN, 1), (UP, 2), (DOWN, 2), (UP, 3), (DOWN, 3)]
    zc, a1, b1, a2, b2, cc = {}, {}, {}, {}, {}, {}
    for name in ("wqk", "wv", "wo"):
        loads[name].wait()
    for i, (k, r) in enumerate(units):
        zc[i] = remote(
            own_unit[k].at[y, x, c], W.at[k, r, y, x, c], ag_s.at[0, i], ag_r.at[0, i], z_peer[r]
        )

    def gather_tick(t):
        i = t
        if 0 <= i < 9:
            k, r = units[i]
            zc[i].wait_recv()
            part = W.at[k, r, y, x, c, pl.ds(0, HALF)]
            a1[i] = remote(part, part, ag_s.at[1, i], ag_r.at[1, i], x_peer)
            part = W.at[k, r, y, x, c, pl.ds(HALF, HALF)]
            b1[i] = remote(part, part, ag_s.at[2, i], ag_r.at[2, i], y_peer)
        i = t - 1
        if 0 <= i < 9:
            k, r = units[i]
            a1[i].wait_recv()
            part = W.at[k, r, y, :, c, pl.ds(0, HALF)]
            a2[i] = remote(part, part, ag_s.at[3, i], ag_r.at[3, i], y_peer)
            b1[i].wait_recv()
            part = W.at[k, r, :, x, c, pl.ds(HALF, HALF)]
            b2[i] = remote(part, part, ag_s.at[4, i], ag_r.at[4, i], x_peer)
        i = t - 2
        if 0 <= i < 9:
            k, r = units[i]
            a2[i].wait_recv()
            b2[i].wait_recv()
            part = W.at[k, r, :, :, c]
            cc[i] = remote(part, part, ag_s.at[5, i], ag_r.at[5, i], core_peer)
        i = t - 3
        if 0 <= i < 9:
            cc[i].wait_recv()

    def unit_value(ref):
        return ref[...].reshape(768, ref.shape[-1])

    def cols(k, r, start, size):
        return unit_value(W.at[k, r, :, :, :, :, pl.ds(start, size)])

    def qkv_rows(ref):
        return jnp.concatenate([ref[0].reshape(384, 768), ref[1, 0].reshape(192, 768)], axis=0)

    def out_rows(ref):
        return ref[1, 1].reshape(192, 768)

    def accumulate(first, value):
        if first:
            ACC[...] = value
        else:
            ACC[...] += value

    def attn_forward(r):
        QKV[r] = mm_nt(X[...], qkv_rows(W.at[ATT, r])).astype(BF16)

        def segment(s, carry):
            rows = pl.ds(pl.multiple_of(s * SEG, SEG), SEG)
            qkv = QKV[r, rows, :]
            mixes = []
            for h in range(3):
                q = qkv[:, h * 64 : h * 64 + 64]
                key = qkv[:, 192 + h * 64 : 256 + h * 64]
                val = qkv[:, 384 + h * 64 : 448 + h * 64]
                scores = mm_nt(q, key) * SCALE
                top = jnp.max(scores, axis=-1, keepdims=True)
                expd = jnp.exp(scores - top)
                prob = expd * (1.0 / jnp.sum(expd, axis=-1, keepdims=True))
                PR[r, h, rows, :] = prob
                mixes.append(mm(prob.astype(BF16), val))
            MIX[r, rows, :] = jnp.concatenate(mixes, axis=-1).astype(BF16)
            return carry

        lax.fori_loop(0, 2, segment, 0)
        accumulate(r == 0, mm(MIX[r], out_rows(W.at[ATT, r])))

    def row_chunks(body, init=0):
        def one(i, carry):
            return body(i, pl.ds(pl.multiple_of(i * 64, 64), 64), carry)

        return lax.fori_loop(0, 4, one, init)

    g00, g01 = gain_ref[0, 0:1, :], gain_ref[0, 1:2, :]
    b00, b01 = shift_ref[0, 0:1, :], shift_ref[0, 1:2, :]
    g10, g11 = gain_ref[1, 0:1, :], gain_ref[1, 1:2, :]
    b10, b11 = shift_ref[1, 0:1, :], shift_ref[1, 1:2, :]

    def norm_one():
        def chunk(i, rows, carry):
            scaled, inverse = normalize(X[rows, :].astype(F32) + ACC[rows, :])
            SC1[rows, :] = scaled
            INV1[rows, :] = jnp.broadcast_to(inverse, (64, 128))
            FL[rows, :] = (scaled * g00 + b00).astype(BF16)
            return carry

        row_chunks(chunk)

    def ffn_forward(r):
        def block(n, carry):
            part = pl.ds(pl.multiple_of(n * 256, 256), 256)
            upward = mm(FL[...], unit_value(W.at[UP, r, :, :, :, :, part]))
            active, slope = gelu_pair(upward)
            ACT[r, :, part] = active.astype(BF16)
            DG[r, :, part] = slope.astype(DG.dtype)
            return carry

        lax.fori_loop(0, 3, block, 0)

    def ffn_down(r):
        accumulate(r == 0, mm(ACT[r], cols(DOWN, r, 0, 768)))

    def norm_two():
        def chunk(i, rows, carry):
            first = SC1[rows, :] * g00 + b00
            scaled, inverse = normalize(first + ACC[rows, :])
            SC2[rows, :] = scaled
            INV2[rows, :] = jnp.broadcast_to(inverse, (64, 128))
            out_ref[0, rows, :] = (scaled * g01 + b01).astype(BF16)
            return carry

        row_chunks(chunk)

    def transpose_into(dst, src):
        for i in range(2):
            dst[:, i * 128 : i * 128 + 128] = src[i * 128 : i * 128 + 128, :].T

    loads["x"].wait()
    attn_forward(0)
    gather_tick(0)
    gather_tick(1)
    transpose_into(XT, X)
    gather_tick(2)
    gather_tick(3)
    attn_forward(1)
    gather_tick(4)
    attn_forward(2)
    gather_tick(5)
    attn_forward(3)
    norm_one()
    loads["wu"].wait()
    loads["wd"].wait()
    gather_tick(6)
    ffn_forward(0)
    ffn_down(0)
    gather_tick(7)
    ffn_forward(1)
    ffn_down(1)
    gather_tick(8)
    transpose_into(FLT, FL)
    gather_tick(9)
    ffn_forward(2)
    ffn_down(2)
    gather_tick(10)
    ffn_forward(3)
    gather_tick(11)
    ffn_down(3)
    norm_two()

    exch = {}

    def exchange(e, value):
        E[e, 0] = value
        for r in range(1, 4):
            exch[e, r] = remote(E.at[e, 0], E.at[e, r], e_s.at[e, r - 1], e_r.at[e, r - 1], z_peer[r])

    def exchange_wait(e):
        for r in range(1, 4):
            exch[e, r].wait_recv()

    def exchange_sum(e):
        exchange_wait(e)
        return (E[e, 0] + E[e, 1]) + (E[e, 2] + E[e, 3])

    row_of = lax.broadcasted_iota(jnp.int32, (8, 768), 0)
    pair_of = row_of // 2

    def assemble(e, start):
        total = None
        for r in range(4):
            two = E[e, r][start : start + 2, :]
            four = jnp.concatenate([two, two, two, two], axis=0)
            part = jnp.where(pair_of == z_of[r], four, 0.0)
            total = part if total is None else total + part
        return total

    def own_row(value, j):
        return jnp.sum(jnp.where(row_of == 2 * z + j, value, 0.0), axis=0, keepdims=True)

    def two_rows(ref):
        return jnp.concatenate([ref[0:1, :], ref[128:129, :]], axis=0)

    inv_two = jnp.broadcast_to(two_rows(INV2)[:, 0:1], (2, 768))
    first_two = two_rows(SC1) * g00 + b00
    exchange(0, jnp.concatenate([two_rows(SC2), first_two, inv_two, inv_two], axis=0))

    loads["cot"].wait()

    def norm_two_back():
        def chunk(i, rows, carry):
            gains, shifts = carry
            which = lax.broadcasted_iota(jnp.int32, (64, 768), 0) + i * 64
            grad = jnp.where(which % SEG == 0, 0.0, COT[rows, :].astype(F32))
            scaled = SC2[rows, :]
            fed = normalize_back(grad, scaled, INV2[rows, 0:1], g01)
            GF[rows, :] = fed
            FDL[rows, :] = fed.astype(BF16)
            return (
                gains + jnp.sum(grad * scaled, axis=0, keepdims=True),
                shifts + jnp.sum(grad, axis=0, keepdims=True),
            )

        zero = jnp.zeros((1, 768), F32)
        gains, shifts = row_chunks(chunk, (zero, zero))
        NV[1:2, :] = gains
        NV[3:4, :] = shifts

    norm_two_back()
    transpose_into(FDLT, FDL)

    def grad_unit(k, r):
        return W.at[UP, r] if k == ATT else G.at[k - 1, r]

    order = [(DOWN, 1), (UP, 1), (DOWN, 2), (UP, 2), (DOWN, 3), (UP, 3), (DOWN, 0), (UP, 0)]
    order += [(ATT, 1), (ATT, 2), (ATT, 3), (ATT, 0)]
    s0, sa1, sb1, sa2, sb2, sz = {}, {}, {}, {}, {}, {}

    def sum_start(i):
        k, r = order[i]
        g = grad_unit(k, r)
        s0[i] = remote(g.at[:, :, nc], RC.at[i], rs_s.at[0, i], rs_r.at[0, i], core_peer)

    def add_low(a, b):
        return (a.astype(F32) + b.astype(F32)).astype(BF16)

    def sum_one(i):
        if not 0 <= i < 12:
            return
        k, r = order[i]
        g = grad_unit(k, r)
        s0[i].wait_recv()

        def block(j, carry):
            jy, jx = j // 2, j % 2
            g[jy, jx, c] = add_low(g[jy, jx, c], RC[i, jy, jx])
            return carry

        lax.fori_loop(0, 4, block, 0)
        sa1[i] = remote(g.at[:, nx, c, pl.ds(0, HALF)], RA1.at[i], rs_s.at[1, i], rs_r.at[1, i], x_peer)
        sb1[i] = remote(g.at[ny, :, c, pl.ds(HALF, HALF)], RB1.at[i], rs_s.at[2, i], rs_r.at[2, i], y_peer)

    def sum_two(i):
        if not 0 <= i < 12:
            return
        k, r = order[i]
        g = grad_unit(k, r)
        sa1[i].wait_recv()
        for j in range(2):
            g[j, x, c, 0:HALF, :] = add_low(g[j, x, c, 0:HALF, :], RA1[i, j])
        sa2[i] = remote(g.at[ny, x, c, pl.ds(0, HALF)], RA2.at[i], rs_s.at[3, i], rs_r.at[3, i], y_peer)
        sb1[i].wait_recv()
        for j in range(2):
            g[y, j, c, HALF:BLK, :] = add_low(g[y, j, c, HALF:BLK, :], RB1[i, j])
        sb2[i] = remote(g.at[y, nx, c, pl.ds(HALF, HALF)], RB2.at[i], rs_s.at[4, i], rs_r.at[4, i], x_peer)

    def sum_three(i):
        if not 0 <= i < 12:
            return
        k, r = order[i]
        g = grad_unit(k, r)
        sa2[i].wait_recv()
        g[y, x, c, 0:HALF, :] = add_low(g[y, x, c, 0:HALF, :], RA2[i])
        sb2[i].wait_recv()
        g[y, x, c, HALF:BLK, :] = add_low(g[y, x, c, HALF:BLK, :], RB2[i])
        if r:
            sz[k, r] = remote(g.at[y, x, c], RZ.at[k, r - 1], rs_s.at[5, i], rs_r.at[5, i], z_peer[r])

    def pump(i):
        sum_one(i)
        sum_two(i - 1)
        sum_three(i - 2)

    def sum_final(k):
        for r in range(1, 4):
            sz[k, r].wait_recv()
        g = grad_unit(k, 0)
        own = g[y, x, c].astype(F32) + RZ[k, 0].astype(F32)
        return own + (RZ[k, 1].astype(F32) + RZ[k, 2].astype(F32))

    def store_unit(ref, parts):
        for start, size, value in parts:
            ref[:, :, :, :, start : start + size] = value().astype(BF16).reshape(2, 2, 2, BLK, size)

    def store_ffn(k, r, lhs_t, rhs, extra=None):
        ref = grad_unit(k, r)

        def block(n, carry):
            part = pl.ds(pl.multiple_of(n * 256, 256), 256)
            value = mm(lhs_t[...], rhs[:, part])
            if extra is not None:
                value = value + mm(extra[0][...], extra[1][:, part])
            ref[:, :, :, :, part] = value.astype(BF16).reshape(2, 2, 2, BLK, 256)
            return carry

        lax.fori_loop(0, 3, block, 0)

    def ffn_back_one(r):
        ga = mm_nt(FDL[...], cols(DOWN, r, 0, 768))
        GU[...] = (ga * DG[r].astype(F32)).astype(BF16)

    def ffn_back_two(r, first):
        accumulate(first, mm_nt(GU[...], cols(UP, r, 0, 768)))

    def l1(k, start, size):
        return unit_value(L1.at[k, :, :, :, :, pl.ds(start, size)])

    live = {}

    def cross_one():
        exchange_wait(0)
        live["sc2"] = assemble(0, 0)
        first8 = assemble(0, 2)
        live["inv2"] = assemble(0, 4)[:, 0:1]
        summary = live["sc2"] * g01 + b01
        live["summary"] = summary
        live["summary_low"] = summary.astype(BF16)
        live["first8_low"] = first8.astype(BF16)
        for name in ("l1qk", "l1v", "l1o"):
            loads[name].wait()
        qkv = mm_nt(live["summary_low"], qkv_rows(L1.at[ATT])).astype(BF16).astype(F32)
        pad = jnp.zeros((120, 64), F32)
        ids = jnp.broadcast_to(doc_ref[...].astype(F32), (8, 8))
        eye = lax.broadcasted_iota(jnp.int32, (8, 8), 0) == lax.broadcasted_iota(jnp.int32, (8, 8), 1)
        same = ids == jnp.sum(jnp.where(eye, ids, 0.0), axis=1, keepdims=True)
        keep = jnp.concatenate([jnp.where(same, 1.0, 0.0), jnp.zeros((8, 120), F32)], axis=1) > 0.5
        mixes = []
        for h in range(3):
            q = qkv[:, h * 64 : h * 64 + 64].astype(BF16)
            key = jnp.concatenate([qkv[:, 192 + h * 64 : 256 + h * 64], pad], axis=0).astype(BF16)
            val = jnp.concatenate([qkv[:, 384 + h * 64 : 448 + h * 64], pad], axis=0).astype(BF16)
            scores = jnp.where(keep, mm_nt(q, key) * SCALE, MASK_FILL)
            top = jnp.max(scores, axis=-1, keepdims=True)
            expd = jnp.exp(scores - top)
            prob = expd * (1.0 / jnp.sum(expd, axis=-1, keepdims=True))
            live["prob", h], live["q", h], live["key", h], live["val", h] = prob, q, key, val
            mixes.append(mm(prob.astype(BF16), val))
        mix = jnp.concatenate(mixes, axis=-1).astype(BF16)
        live["mix"] = mix
        exchange(1, mm(mix, out_rows(L1.at[ATT])))

    def cross_two():
        attended = exchange_sum(1)
        live["xs1"], live["xi1"] = normalize(live["summary"] + attended)
        first = live["xs1"] * g10 + b10
        live["xfirst"] = first
        live["xfirst_low"] = first.astype(BF16)
        loads["l1u"].wait()
        loads["l1d"].wait()
        active, live["xdg"] = gelu_pair(mm(live["xfirst_low"], l1(UP, 0, 768)))
        live["xact"] = active.astype(BF16)
        exchange(2, mm(live["xact"], l1(DOWN, 0, 768)))

    def cross_three():
        fed = exchange_sum(2)
        xs2, xi2 = normalize(live["xfirst"] + fed)
        upper = xs2 * g11 + b11
        for j in range(2):
            out_ref[0, j * 128 : j * 128 + 1, :] = own_row(upper, j).astype(BF16)
        loads["c8"].wait()
        grad_top = C8[...].astype(F32)[:, 0, :]
        live["xs2"], live["xi2"] = xs2, xi2
        grad_fed = normalize_back(grad_top, live["xs2"], live["xi2"], g11)
        NV[5:6, :] = jnp.sum(grad_top * live["xs2"], axis=0, keepdims=True)
        NV[7:8, :] = jnp.sum(grad_top, axis=0, keepdims=True)
        live["xgf"] = grad_fed
        live["xfed_low"] = grad_fed.astype(BF16)
        ga = mm_nt(live["xfed_low"], l1(DOWN, 0, 768))
        live["xgu"] = (ga * live["xdg"]).astype(BF16)
        exchange(3, mm_nt(live["xgu"], l1(UP, 0, 768)))

    def cross_four():
        grad_first = live["xgf"] + exchange_sum(3)
        grad_att = normalize_back(grad_first, live["xs1"], live["xi1"], g10)
        NV[4:5, :] = jnp.sum(grad_first * live["xs1"], axis=0, keepdims=True)
        NV[6:7, :] = jnp.sum(grad_first, axis=0, keepdims=True)
        live["xga"] = grad_att
        att_low = grad_att.astype(BF16)
        live["xatt_low"] = att_low
        gm = mm_nt(att_low, out_rows(L1.at[ATT])).astype(BF16)
        gqs, gks, gvs = [], [], []
        for h in range(3):
            gmh = gm[:, h * 64 : h * 64 + 64]
            prob = live["prob", h]
            gp = mm_nt(gmh, live["val", h])
            inner = jnp.sum(gp * prob, axis=-1, keepdims=True)
            gs = (prob * (gp - inner)).astype(BF16)
            gqs.append(mm(gs, live["key", h]) * SCALE)
            gks.append(mm_tn(gs, live["q", h])[0:8, :] * SCALE)
            gvs.append(mm_tn(prob.astype(BF16), gmh)[0:8, :])
        gqkv = jnp.concatenate(gqs + gks + gvs, axis=-1).astype(BF16)
        live["xgqkv"] = gqkv
        exchange(4, mm(gqkv, qkv_rows(L1.at[ATT])))

    def cross_five():
        grad_summary = live["xga"] + exchange_sum(4)
        mine = jnp.where(pair_of == z, grad_summary, 0.0)
        NV[1:2, :] += jnp.sum(mine * live["sc2"], axis=0, keepdims=True)
        NV[3:4, :] += jnp.sum(mine, axis=0, keepdims=True)
        gfed8 = normalize_back(grad_summary, live["sc2"], live["inv2"], g01)
        live["gfed8"] = gfed8
        fed8_low = gfed8.astype(BF16)
        live["fed8_low"] = fed8_low
        active, slope = gelu_pair(mm(live["first8_low"], cols(UP, 0, 0, 768)))
        live["act8"] = active.astype(BF16)
        ga = mm_nt(fed8_low, cols(DOWN, 0, 0, 768))
        live["gu8"] = (ga * slope).astype(BF16)
        exchange(5, mm_nt(live["gu8"], cols(UP, 0, 0, 768)))

    def cross_six():
        part = exchange_sum(5)
        for j in range(2):
            GF[j * 128 : j * 128 + 1, :] = own_row(live["gfed8"], j)
            ACC[j * 128 : j * 128 + 1, :] = own_row(part, j)

    def norm_one_back():
        def chunk(i, rows, carry):
            gains, shifts = carry
            grad = GF[rows, :] + ACC[rows, :]
            scaled = SC1[rows, :]
            att = normalize_back(grad, scaled, INV1[rows, 0:1], g00)
            GF[rows, :] = att
            FDL[rows, :] = att.astype(BF16)
            return (
                gains + jnp.sum(grad * scaled, axis=0, keepdims=True),
                shifts + jnp.sum(grad, axis=0, keepdims=True),
            )

        zero = jnp.zeros((1, 768), F32)
        gains, shifts = row_chunks(chunk, (zero, zero))
        NV[0:1, :] = gains
        NV[2:3, :] = shifts

    def attn_backward(r, first):
        GM[...] = mm_nt(FDL[...], out_rows(W.at[ATT, r])).astype(BF16)

        def segment(s, carry):
            rows = pl.ds(pl.multiple_of(s * SEG, SEG), SEG)
            qkv = QKV[r, rows, :]
            gm = GM[rows, :]
            gqs, gks, gvs = [], [], []
            for h in range(3):
                q = qkv[:, h * 64 : h * 64 + 64]
                key = qkv[:, 192 + h * 64 : 256 + h * 64]
                val = qkv[:, 384 + h * 64 : 448 + h * 64]
                gmh = gm[:, h * 64 : h * 64 + 64]
                prob = PR[r, h, rows, :]
                gp = mm_nt(gmh, val)
                inner = jnp.sum(gp * prob, axis=-1, keepdims=True)
                gs = (prob * (gp - inner)).astype(BF16)
                gqs.append(mm(gs, key) * SCALE)
                gks.append(mm_tn(gs, q) * SCALE)
                gvs.append(mm_tn(prob.astype(BF16), gmh))
            GQ[rows, :] = jnp.concatenate(gqs + gks + gvs, axis=-1).astype(BF16)
            return carry

        lax.fori_loop(0, 2, segment, 0)
        store_unit(
            grad_unit(ATT, r),
            [
                (0, 576, lambda: mm(XT[...], GQ[...])),
                (576, 192, lambda: mm(FDLT[...], MIX[r])),
            ],
        )
        accumulate(first, mm(GQ[...], qkv_rows(W.at[ATT, r])))

    fac = {}

    def factor_start():
        wide = lambda v: v.astype(F32)
        zero_a, zero_b = jnp.zeros((8, 192), F32), jnp.zeros((8, 576), F32)
        att_left = jnp.concatenate([wide(live["xgqkv"]), zero_a], axis=-1)
        att_right = jnp.concatenate([zero_b, wide(live["mix"])], axis=-1)
        right = jnp.concatenate([wide(live["xact"]), wide(live["xgu"]), att_left, att_right], axis=0)
        left = jnp.concatenate(
            [wide(live["xfed_low"]), wide(live["xfirst_low"]), wide(live["summary_low"]), wide(live["xatt_low"])],
            axis=0,
        )
        FAC[y, x, c, 0:32, :] = right.astype(BF16)
        FAC[y, x, c, 32:64, :] = left.astype(BF16)
        part = FAC.at[y, x, c]
        fac[0] = remote(part, part, f_s.at[0], f_r.at[0], x_peer)

    def factor_two():
        fac[0].wait_recv()
        part = FAC.at[y, :, c]
        fac[1] = remote(part, part, f_s.at[1], f_r.at[1], y_peer)

    def factor_three():
        fac[1].wait_recv()
        part = FAC.at[:, :, c]
        fac[2] = remote(part, part, f_s.at[2], f_r.at[2], core_peer)

    def turn_rows(value):
        rows = value.shape[0]
        full = jnp.concatenate([value, jnp.zeros((128 - rows, value.shape[1]), F32)], axis=0)
        return full.T[:, 0:rows]

    def write_unit(layer, k, value):
        if k == ATT:
            for i in range(3):
                qkvg_ref[layer, i] = value[:, i * 192 : i * 192 + 192]
            outg_ref[layer] = turn_rows(value[:, 576:768])
        elif k == UP:
            upg_ref[layer] = value
        else:
            downg_ref[layer] = value

    def factor_final():
        fac[2].wait_recv()
        left = FAC[:, :, :, 32:64, :].reshape(256, 768)
        for i in range(2):
            LT[:, i * 128 : i * 128 + 128] = left[i * 128 : i * 128 + 128, :].T
        mine = LT[pl.ds(pl.multiple_of(dp * BLK, BLK), BLK), :].astype(F32)
        kind = (lax.broadcasted_iota(jnp.int32, (BLK, 256), 1) // 8) % 4
        right = FAC[:, :, :, 0:32, :].reshape(256, 768)
        write_unit(1, DOWN, mm(jnp.where(kind == 0, mine, 0.0).astype(BF16), right))
        write_unit(1, UP, mm(jnp.where(kind == 1, mine, 0.0).astype(BF16), right))
        write_unit(1, ATT, mm(jnp.where(kind >= 2, mine, 0.0).astype(BF16), right))

    vec = {}

    def norm_grads_start():
        exchange(6, NV[...])

    def norm_grads_two():
        total = jnp.where(row_of < 4, exchange_sum(6), NV[...])
        pad = jnp.zeros((8, 32), F32)
        for p in range(8):
            SV[p // 4, (p // 2) % 2, p % 2] = jnp.concatenate([total[:, p * BLK : p * BLK + BLK], pad], axis=-1)
        for m in range(1, 8):
            ty = y if m // 4 == 0 else ny
            tx = x if (m // 2) % 2 == 0 else nx
            tc = c if m % 2 == 0 else nc
            vec[m] = remote(
                SV.at[ty, tx, tc], RSV.at[m - 1], v_s.at[m - 1], v_r.at[m - 1], (plane_index(m), z)
            )

    def norm_grads_final():
        total = SV[y, x, c]
        for m in range(1, 8):
            vec[m].wait_recv()
            total = total + RSV[m - 1]
        gaing_ref[...] = total[0:2, 0:BLK]
        shiftg_ref[...] = total[2:4, 0:BLK]
        crossg_ref[0] = total[4:6, 0:BLK]
        crossg_ref[1] = total[6:8, 0:BLK]

    def eight_turned(dst, value):
        full = jnp.concatenate([value.astype(F32), jnp.zeros((120, 768), F32)], axis=0)
        dst[...] = full.T.astype(BF16)

    def eight_rows(dst, value):
        dst[...] = jnp.concatenate([value.astype(F32), jnp.zeros((120, 768), F32)], axis=0).astype(BF16)

    cross_one()
    ffn_back_one(1)
    store_ffn(DOWN, 1, FDLT, ACT.at[1])
    sum_start(0)
    store_ffn(UP, 1, FLT, GU)
    sum_start(1)
    ffn_back_two(1, True)
    cross_two()
    pump(0)
    ffn_back_one(2)
    store_ffn(DOWN, 2, FDLT, ACT.at[2])
    sum_start(2)
    store_ffn(UP, 2, FLT, GU)
    sum_start(3)
    ffn_back_two(2, False)
    cross_three()
    pump(1)
    ffn_back_one(3)
    store_ffn(DOWN, 3, FDLT, ACT.at[3])
    sum_start(4)
    store_ffn(UP, 3, FLT, GU)
    sum_start(5)
    ffn_back_two(3, False)
    cross_four()
    factor_start()
    pump(2)
    cross_five()
    pump(3)
    ffn_back_one(0)
    eight_turned(EL, live["fed8_low"])
    eight_rows(ER, live["act8"])
    store_ffn(DOWN, 0, FDLT, ACT.at[0], (EL, ER))
    sum_start(6)
    eight_turned(EL, live["first8_low"])
    eight_rows(ER, live["gu8"])
    store_ffn(UP, 0, FLT, GU, (EL, ER))
    sum_start(7)
    ffn_back_two(0, False)
    cross_six()
    norm_one_back()
    norm_grads_start()
    transpose_into(FDLT, FDL)
    for table in (a1, b1, a2, b2, cc):
        for i in range(9):
            table[i].wait_send()
            waited.append(id(table[i]))
    pump(4)
    factor_two()
    attn_backward(1, True)
    sum_start(8)
    pump(5)
    factor_three()
    norm_grads_two()
    attn_backward(2, False)
    sum_start(9)
    pump(6)
    attn_backward(3, False)
    sum_start(10)
    pump(7)
    attn_backward(0, False)
    sum_start(11)
    ing_ref[0] = (GF[...] + ACC[...]).astype(BF16)
    pump(8)
    factor_final()
    pump(9)
    norm_grads_final()
    pump(10)
    write_unit(0, DOWN, sum_final(DOWN))
    pump(11)
    write_unit(0, UP, sum_final(UP))
    pump(12)
    pump(13)
    write_unit(0, ATT, sum_final(ATT))
    for copy in sends:
        if id(copy) not in waited:
            copy.wait_send()


def settle_kernel(*refs):
    sources, targets, held, sems = refs[:9], refs[9:18], refs[18:27], refs[27]
    arrive = [pltpu.make_async_copy(sources[i], held[i], sems.at[0, i]) for i in range(9)]
    leave = [pltpu.make_async_copy(held[i], targets[i], sems.at[1, i]) for i in range(9)]
    for copy in arrive:
        copy.start()
    for i in range(9):
        arrive[i].wait()
        leave[i].start()
    for copy in leave:
        copy.wait()


def fused_body(
    inputs, doc_ids, qkv_weight, out_weight, up_weight, down_weight, norm_gain, norm_shift, cotangent
):
    wq = qkv_weight.swapaxes(2, 3).reshape(2, 3, 2, BLK, 768)
    wo = out_weight.reshape(2, 2, BLK, 768)
    wu = up_weight.reshape(2, 2, 2, 2, BLK, 768)
    wd = down_weight.reshape(2, 2, 2, 2, BLK, 768)
    whole = pl.BlockSpec(memory_space=pl.ANY)
    vmem = pl.BlockSpec(memory_space=pltpu.VMEM)
    blocks = (2, 2, 2, BLK, 768)
    sem = pltpu.SemaphoreType.DMA
    results = pl.pallas_call(
        fused_kernel,
        out_shape=(
            jax.ShapeDtypeStruct((1, 256, 768), BF16),
            jax.ShapeDtypeStruct((1, 256, 768), BF16),
            jax.ShapeDtypeStruct((2, 3, BLK, 192), F32),
            jax.ShapeDtypeStruct((2, 192, BLK), F32),
            jax.ShapeDtypeStruct((2, BLK, 768), F32),
            jax.ShapeDtypeStruct((2, BLK, 768), F32),
            jax.ShapeDtypeStruct((2, BLK), F32),
            jax.ShapeDtypeStruct((2, BLK), F32),
            jax.ShapeDtypeStruct((2, 2, BLK), F32),
        ),
        in_specs=[whole, whole, whole, vmem, whole, whole, whole, whole, vmem, vmem],
        out_specs=(vmem,) * 9,
        scratch_shapes=[
            pltpu.VMEM((3, 4) + blocks, BF16),
            pltpu.VMEM((2, 4) + blocks, BF16),
            pltpu.VMEM((12, 2, 2, BLK, 768), BF16),
            pltpu.VMEM((12, 2, HALF, 768), BF16),
            pltpu.VMEM((12, 2, HALF, 768), BF16),
            pltpu.VMEM((12, HALF, 768), BF16),
            pltpu.VMEM((12, HALF, 768), BF16),
            pltpu.VMEM((3, 3, BLK, 768), BF16),
            pltpu.VMEM((3,) + blocks, BF16),
            pltpu.VMEM((256, 768), BF16),
            pltpu.VMEM((256, 768), BF16),
            pltpu.VMEM((4, 256, 576), BF16),
            pltpu.VMEM((4, 3, 256, 128), F32),
            pltpu.VMEM((4, 256, 192), BF16),
            pltpu.VMEM((4, 256, 768), BF16),
            pltpu.VMEM((4, 256, 768), BF16),
            pltpu.VMEM((256, 768), BF16),
            pltpu.VMEM((256, 576), BF16),
            pltpu.VMEM((256, 768), F32),
            pltpu.VMEM((256, 768), F32),
            pltpu.VMEM((256, 768), F32),
            pltpu.VMEM((256, 768), F32),
            pltpu.VMEM((256, 768), BF16),
            pltpu.VMEM((768, 256), BF16),
            pltpu.VMEM((256, 768), BF16),
            pltpu.VMEM((768, 256), BF16),
            pltpu.VMEM((768, 256), BF16),
            pltpu.VMEM((256, 192), BF16),
            pltpu.VMEM((8, 16, 768), BF16),
            pltpu.VMEM((256, 128), F32),
            pltpu.VMEM((256, 128), F32),
            pltpu.VMEM((2, 2, 2, 64, 768), BF16),
            pltpu.VMEM((768, 256), BF16),
            pltpu.VMEM((768, 128), BF16),
            pltpu.VMEM((128, 768), BF16),
            pltpu.VMEM((7, 4, 8, 768), F32),
            pltpu.VMEM((8, 768), F32),
            pltpu.VMEM((2, 2, 2, 8, 128), F32),
            pltpu.VMEM((7, 8, 128), F32),
            sem((13,)),
            sem((6, 9)),
            sem((6, 9)),
            sem((6, 12)),
            sem((6, 12)),
            sem((7, 3)),
            sem((7, 3)),
            sem((3,)),
            sem((3,)),
            sem((7,)),
            sem((7,)),
        ],
        compiler_params=pltpu.CompilerParams(
            collective_id=0, has_side_effects=True, vmem_limit_bytes=63 * 2**20
        ),
    )(
        inputs, cotangent, cotangent.reshape(8, SEG, 768), doc_ids, wq, wo, wu, wd, norm_gain, norm_shift
    )
    final = pl.pallas_call(
        settle_kernel,
        out_shape=tuple(jax.ShapeDtypeStruct(v.shape, v.dtype) for v in results),
        in_specs=[whole] * 9,
        out_specs=(whole,) * 9,
        scratch_shapes=[pltpu.VMEM(v.shape, v.dtype) for v in results] + [sem((2, 9))],
    )(*results)
    return final[:5] + (final[5].swapaxes(1, 2),) + final[6:]


def solution(mesh):
    in_specs = (
        P("dp", None, None),
        P("dp", None),
        P(None, None, None, "tensor"),
        P(None, "tensor", None),
        P(None, None, "tensor"),
        P(None, "tensor", None),
        P(),
        P(),
        P("dp", None, None),
    )
    out_specs = (
        P("dp", "tensor", None),
        P("dp", "tensor", None),
        P(None, None, "dp", "tensor"),
        P(None, "tensor", "dp"),
        P(None, "dp", "tensor"),
        P(None, "tensor", "dp"),
        P(None, "dp"),
        P(None, "dp"),
        P(None, None, "dp"),
    )
    fits = dict(mesh.shape) == {"dp": 8, "tensor": 4}
    chosen = fused_body if fits else body
    return jax.shard_map(chosen, mesh=mesh, in_specs=in_specs, out_specs=out_specs, check_vma=False)
```

```python
from functools import partial
import math

import jax
import jax.numpy as jnp
from jax import lax
from jax.experimental import pallas as pl
from jax.experimental.pallas import tpu as pltpu
from jax.sharding import PartitionSpec as P

HEAD_DIM = 64
SEG = 128


EPSILON = 1e-05
MASK_FILL = -1000000000.0


def layer_norm(values, gain_row, shift_row):
    center = jnp.mean(values, axis=-1, keepdims=True)
    offset = values - center
    spread = jnp.mean(offset * offset, axis=-1, keepdims=True)
    inverse = lax.rsqrt(spread + EPSILON)
    scaled = offset * inverse
    return (scaled * gain_row + shift_row, (scaled, inverse))


def norm_back(grad_out, saved, gain_row):
    scaled, inverse = saved
    weighted = grad_out * gain_row
    mean_one = jnp.mean(weighted, axis=-1, keepdims=True)
    mean_two = jnp.mean(weighted * scaled, axis=-1, keepdims=True)
    grad_in = inverse * (weighted - mean_one - scaled * mean_two)
    return (grad_in, jnp.sum(grad_out * scaled, axis=(0, 1)), jnp.sum(grad_out, axis=(0, 1)))


def score_block(head_split, allowed):
    scores = jnp.einsum(
        "bqhe,bkhe->bhqk", head_split[0], head_split[1], preferred_element_type=jnp.float32
    ) * (1.0 / math.sqrt(HEAD_DIM))
    if allowed is not None:
        scores = jnp.where(allowed, scores, MASK_FILL)
    return scores


def attend_forward(rows_low, qkv_local, allowed):
    batch_count = rows_low.shape[0]
    length = rows_low.shape[1]
    project = jnp.einsum(
        "brd,cde->cbre", rows_low, qkv_local, preferred_element_type=jnp.float32
    ).astype(jnp.bfloat16)
    head_split = project.reshape(3, batch_count, length, -1, HEAD_DIM)
    scores = score_block(head_split, allowed)
    log_total = jax.nn.logsumexp(scores, axis=-1)
    soft_low = jnp.exp(scores - log_total[..., None]).astype(jnp.bfloat16)
    mixture = jnp.einsum(
        "bhqk,bkhe->bqhe", soft_low, head_split[2], preferred_element_type=jnp.float32
    )
    return (project, log_total, mixture.astype(jnp.bfloat16).reshape(batch_count, length, -1))


def attend_backward(rows_low, qkv_local, out_local, project, log_total, mixture, grad_low, allowed):
    batch_count = rows_low.shape[0]
    length = rows_low.shape[1]
    head_split = project.reshape(3, batch_count, length, -1, HEAD_DIM)
    grad_mixture = jnp.einsum(
        "brd,fd->brf", grad_low, out_local, preferred_element_type=jnp.float32
    ).astype(jnp.bfloat16)
    out_local_grad = jnp.einsum(
        "brf,brd->fd", mixture, grad_low, preferred_element_type=jnp.float32
    )
    grad_heads = grad_mixture.reshape(batch_count, length, -1, HEAD_DIM)
    scores = score_block(head_split, allowed)
    soft_full = jnp.exp(scores - log_total[..., None])
    grad_soft = jnp.einsum(
        "bqhe,bkhe->bhqk", grad_heads, head_split[2], preferred_element_type=jnp.float32
    )
    row_inner = jnp.sum(grad_soft * soft_full, axis=-1, keepdims=True)
    grad_scores = (soft_full * (grad_soft - row_inner)).astype(jnp.bfloat16)
    scale_factor = 1.0 / math.sqrt(HEAD_DIM)
    grad_query = (
        jnp.einsum(
            "bhqk,bkhe->bqhe", grad_scores, head_split[1], preferred_element_type=jnp.float32
        )
        * scale_factor
    )
    grad_key = (
        jnp.einsum(
            "bhqk,bqhe->bkhe", grad_scores, head_split[0], preferred_element_type=jnp.float32
        )
        * scale_factor
    )
    grad_value = jnp.einsum(
        "bhqk,bqhe->bkhe",
        soft_full.astype(jnp.bfloat16),
        grad_heads,
        preferred_element_type=jnp.float32,
    )
    grad_project = (
        jnp.stack([grad_query, grad_key, grad_value])
        .reshape(3, batch_count, length, -1)
        .astype(jnp.bfloat16)
    )
    qkv_local_grad = jnp.einsum(
        "brd,cbre->cde", rows_low, grad_project, preferred_element_type=jnp.float32
    )
    input_part = jnp.einsum(
        "cbre,cde->brd", grad_project, qkv_local, preferred_element_type=jnp.float32
    )
    return (input_part, qkv_local_grad, out_local_grad)


def expand_forward(rows_low, up_local, down_local):
    upward = jnp.einsum("brd,df->brf", rows_low, up_local, preferred_element_type=jnp.float32)
    active = jax.nn.gelu(upward, approximate=False).astype(jnp.bfloat16)
    return (
        upward,
        active,
        jnp.einsum("brf,fd->brd", active, down_local, preferred_element_type=jnp.float32),
    )


def expand_backward(rows_low, up_local, down_local, upward, active, grad_low):
    grad_active = jnp.einsum(
        "brd,fd->brf", grad_low, down_local, preferred_element_type=jnp.float32
    )
    down_local_grad = jnp.einsum(
        "brf,brd->fd", active, grad_low, preferred_element_type=jnp.float32
    )
    gelu_pull = jax.vjp(partial(jax.nn.gelu, approximate=False), upward)[1]
    grad_upward = gelu_pull(grad_active)[0].astype(jnp.bfloat16)
    up_local_grad = jnp.einsum(
        "brd,brf->df", rows_low, grad_upward, preferred_element_type=jnp.float32
    )
    input_part = jnp.einsum(
        "brf,df->brd", grad_upward, up_local, preferred_element_type=jnp.float32
    )
    return (input_part, up_local_grad, down_local_grad)


def body(
    inputs,
    doc_ids,
    qkv_weight,
    out_weight,
    up_weight,
    down_weight,
    norm_gain,
    norm_shift,
    cotangent,
):
    groups = lax.axis_size("tensor")
    position = lax.axis_index("tensor")
    model_width = inputs.shape[2]
    segment_count = inputs.shape[1] // SEG
    own_count = segment_count // groups
    row_start = position * own_count

    def final_rows(values):
        return lax.dynamic_slice_in_dim(values, row_start, own_count, 0)

    def forward_sum(partial_term):
        return lax.psum(partial_term.astype(jnp.bfloat16), "tensor").astype(jnp.float32)

    def backward_sum(partial_term):
        return lax.psum(partial_term.astype(jnp.bfloat16), "tensor").astype(jnp.float32)

    def cross_sum(partial_term):
        return lax.psum(partial_term.astype(jnp.bfloat16), "tensor").astype(jnp.float32)

    def cross_grad_sum(partial_term):
        return lax.psum(partial_term, "tensor")

    tokens = inputs[0].reshape(segment_count, SEG, model_width)
    tokens_wide = tokens.astype(jnp.float32)
    lower_proj, lower_total, lower_mix = attend_forward(tokens, qkv_weight[0], None)
    attended = forward_sum(
        jnp.einsum("brf,fd->brd", lower_mix, out_weight[0], preferred_element_type=jnp.float32)
    )
    first_norm, first_saved = layer_norm(tokens_wide + attended, norm_gain[0, 0], norm_shift[0, 0])
    first_low = first_norm.astype(jnp.bfloat16)
    lower_up, lower_active, fed_term = expand_forward(first_low, up_weight[0], down_weight[0])
    second, second_saved = layer_norm(
        first_norm + forward_sum(fed_term), norm_gain[0, 1], norm_shift[0, 1]
    )
    summary = second[:, 0, :]
    summary = summary[None]
    same_doc = (doc_ids[0][:, None] == doc_ids[0][None, :])[None, None]
    summary_low = summary.astype(jnp.bfloat16)
    upper_proj, upper_total, upper_mix = attend_forward(summary_low, qkv_weight[1], same_doc)
    upper_att = cross_sum(
        jnp.einsum("brf,fd->brd", upper_mix, out_weight[1], preferred_element_type=jnp.float32)
    )
    upper_first, upper_saved_one = layer_norm(
        summary + upper_att, norm_gain[1, 0], norm_shift[1, 0]
    )
    upper_first_low = upper_first.astype(jnp.bfloat16)
    upper_up, upper_active, upper_fed = expand_forward(
        upper_first_low, up_weight[1], down_weight[1]
    )
    upper_out, upper_saved_two = layer_norm(
        upper_first + cross_sum(upper_fed), norm_gain[1, 1], norm_shift[1, 1]
    )
    joined = second.at[:, 0, :].set(upper_out[0])
    outputs_own = final_rows(joined).reshape(1, -1, model_width).astype(jnp.bfloat16)
    grad_full = cotangent[0].reshape(segment_count, SEG, model_width).astype(jnp.float32)
    grad_top = grad_full[:, 0, :][None]
    grad_upper_fed, gain_cross_two, shift_cross_two = norm_back(
        grad_top, upper_saved_two, norm_gain[1, 1]
    )
    cross_part, up_cross, down_cross = expand_backward(
        upper_first_low,
        up_weight[1],
        down_weight[1],
        upper_up,
        upper_active,
        grad_upper_fed.astype(jnp.bfloat16),
    )
    grad_upper_first = grad_upper_fed + cross_grad_sum(cross_part)
    grad_upper_att, gain_cross_one, shift_cross_one = norm_back(
        grad_upper_first, upper_saved_one, norm_gain[1, 0]
    )
    cross_input_part, qkv_cross, out_cross = attend_backward(
        summary_low,
        qkv_weight[1],
        out_weight[1],
        upper_proj,
        upper_total,
        upper_mix,
        grad_upper_att.astype(jnp.bfloat16),
        same_doc,
    )
    grad_summary = grad_upper_att + cross_grad_sum(cross_input_part)
    grad_second = grad_full.at[:, 0, :].set(grad_summary[0])
    grad_fed, gain_seg_two, shift_seg_two = norm_back(grad_second, second_saved, norm_gain[0, 1])
    fed_low = grad_fed.astype(jnp.bfloat16)
    seg_part, up_seg, down_seg = expand_backward(
        first_low, up_weight[0], down_weight[0], lower_up, lower_active, fed_low
    )
    grad_first = grad_fed + backward_sum(seg_part)
    grad_att, gain_seg_one, shift_seg_one = norm_back(grad_first, first_saved, norm_gain[0, 0])
    att_low = grad_att.astype(jnp.bfloat16)
    seg_input_part, qkv_seg, out_seg = attend_backward(
        tokens, qkv_weight[0], out_weight[0], lower_proj, lower_total, lower_mix, att_low, None
    )
    input_full = grad_att + backward_sum(seg_input_part)
    input_own = final_rows(input_full).reshape(1, -1, model_width).astype(jnp.bfloat16)
    seg_gain = jnp.stack([gain_seg_one, gain_seg_two])
    seg_shift = jnp.stack([shift_seg_one, shift_seg_two])
    cross_norm = jnp.stack(
        [jnp.stack([gain_cross_one, gain_cross_two]), jnp.stack([shift_cross_one, shift_cross_two])]
    )
    qkv_all = jnp.stack([qkv_seg, qkv_cross])
    out_all = jnp.stack([out_seg, out_cross])
    up_all = jnp.stack([up_seg, up_cross])
    down_all = jnp.stack([down_seg, down_cross])
    summed = (
        lax.psum_scatter(qkv_all, "dp", scatter_dimension=2, tiled=True),
        lax.psum_scatter(out_all, "dp", scatter_dimension=2, tiled=True),
        lax.psum_scatter(up_all, "dp", scatter_dimension=1, tiled=True),
        lax.psum_scatter(down_all, "dp", scatter_dimension=2, tiled=True),
        lax.psum_scatter(seg_gain, "dp", scatter_dimension=1, tiled=True),
        lax.psum_scatter(seg_shift, "dp", scatter_dimension=1, tiled=True),
        lax.psum_scatter(cross_norm, "dp", scatter_dimension=2, tiled=True),
    )
    return (
        outputs_own,
        input_own,
        summed[0],
        summed[1],
        summed[2],
        summed[3],
        summed[4],
        summed[5],
        summed[6],
    )


MESH = pl.DeviceIdType.MESH
F32 = jnp.float32
BF16 = jnp.bfloat16
SCALE = 1.0 / math.sqrt(HEAD_DIM)
ATT, UP, DOWN = 0, 1, 2
BLK = 96
HALF = 48


def mm(a, b):
    return lax.dot_general(a, b, (((1,), (0,)), ((), ())), preferred_element_type=F32)


def mm_nt(a, b):
    return lax.dot_general(a, b, (((1,), (1,)), ((), ())), preferred_element_type=F32)


def mm_tn(a, b):
    return lax.dot_general(a, b, (((0,), (0,)), ((), ())), preferred_element_type=F32)


def normalize(values):
    center = jnp.mean(values, axis=-1, keepdims=True)
    offset = values - center
    spread = jnp.mean(offset * offset, axis=-1, keepdims=True)
    inverse = lax.rsqrt(spread + EPSILON)
    return offset * inverse, inverse


def normalize_back(grad_out, scaled, inverse, gain_row):
    weighted = grad_out * gain_row
    mean_one = jnp.mean(weighted, axis=-1, keepdims=True)
    mean_two = jnp.mean(weighted * scaled, axis=-1, keepdims=True)
    return inverse * (weighted - mean_one - scaled * mean_two)


def gelu_pair(upward):
    cdf = 0.5 * (1.0 + lax.erf(upward * math.sqrt(0.5)))
    pdf = jnp.exp(upward * upward * -0.5) * (1.0 / math.sqrt(2.0 * math.pi))
    return upward * cdf, cdf + upward * pdf


def fused_kernel(
    tokens_hbm, cot_hbm, cot_seg, doc_ref, wq_hbm, wo_hbm, wu_hbm, wd_hbm, gain_ref, shift_ref,
    out_ref, ing_ref, qkvg_ref, outg_ref, upg_ref, downg_ref, gaing_ref, shiftg_ref, crossg_ref,
    W, G, RC, RA1, RB1, RA2, RB2, RZ, L1, XA, COT, QKV, PR, MIX, ACT, DG, GU, GQ, ACC, SC1, SC2, GF,
    FL, FLT, FDL, FDLT, XT, GM, C8, INV1, INV2, FAC, LT, GS, E, NV, SV, RSV,
    sem_local, zg_s, zg_r, ag_s, ag_r, rs_s, rs_r, e_s, e_r, f_s, f_r, v_s, v_r,
):
    dp = lax.axis_index("dp")
    z = lax.axis_index("tensor")
    c = dp % 2
    x = (dp // 2) % 2
    y = dp // 4
    nc, nx, ny = 1 - c, 1 - x, 1 - y
    core_peer = (dp + 1 - 2 * c, z)
    x_peer = (dp + 2 - 4 * x, z)
    y_peer = (dp + 4 - 8 * y, z)
    left_peer, right_peer = (dp, jnp.maximum(z - 1, 0)), (dp, jnp.minimum(z + 1, 3))
    z_peer = [None, (dp, z + 1 - 2 * (z % 2)), (dp, z + 2 - 4 * (z // 2)), (dp, 3 - z)]
    z_of = [z, z + 1 - 2 * (z % 2), z + 2 - 4 * (z // 2), 3 - z]

    def plane_index(m):
        ty = y if m // 4 == 0 else ny
        tx = x if (m // 2) % 2 == 0 else nx
        tc = c if m % 2 == 0 else nc
        return ty * 4 + tx * 2 + tc

    sends = []
    waited = []

    def remote(src, dst, ssem, rsem, target):
        copy = pltpu.make_async_remote_copy(
            src_ref=src, dst_ref=dst, send_sem=ssem, recv_sem=rsem, device_id=target, device_id_type=MESH
        )
        copy.start()
        sends.append(copy)
        return copy

    loads = {}

    def load(name, index, src, dst):
        copy = pltpu.make_async_copy(src, dst, sem_local.at[index])
        copy.start()
        loads[name] = copy

    load("x", 0, tokens_hbm.at[0], XA)
    load("wqk", 1, wq_hbm.at[0, pl.ds(0, 2)], W.at[ATT, z, 0])
    load("wv", 9, wq_hbm.at[0, 2], W.at[ATT, z, 1, 0])
    load("wo", 10, wo_hbm.at[0], W.at[ATT, z, 1, 1])
    load("wu", 2, wu_hbm.at[0], W.at[UP, z])
    load("wd", 3, wd_hbm.at[0], W.at[DOWN, z])
    load("cot", 4, cot_hbm.at[0, pl.ds(pl.multiple_of(z * 256, 256), 256)], COT)
    load("l1qk", 5, wq_hbm.at[1, pl.ds(0, 2)], L1.at[ATT, 0])
    load("l1v", 11, wq_hbm.at[1, 2], L1.at[ATT, 1, 0])
    load("l1o", 12, wo_hbm.at[1], L1.at[ATT, 1, 1])
    load("l1u", 6, wu_hbm.at[1], L1.at[UP])
    load("l1d", 7, wd_hbm.at[1], L1.at[DOWN])
    load("c8", 8, cot_seg.at[:, pl.ds(0, 16)], C8)

    barrier = pltpu.get_barrier_semaphore()
    for m in range(1, 8):
        pl.semaphore_signal(barrier, inc=1, device_id=(plane_index(m), z), device_id_type=MESH)
    for r in range(1, 4):
        pl.semaphore_signal(barrier, inc=1, device_id=z_peer[r], device_id_type=MESH)
    pl.semaphore_wait(barrier, 10)

    own_unit = [W.at[ATT, z], wu_hbm.at[0], wd_hbm.at[0]]
    units = [(k, r) for k in (ATT, UP, DOWN) for r in (1, 2, 3)]
    a1, b1, a2, b2, cc = {}, {}, {}, {}, {}
    passed = []

    def z_copy(src, k, shard, side):
        return pltpu.make_async_remote_copy(
            src_ref=src,
            dst_ref=W.at[k, shard, y, x, c],
            send_sem=zg_s.at[k * 4 + shard, side],
            recv_sem=zg_r.at[k * 4 + shard],
            device_id=(left_peer, right_peer)[side],
            device_id_type=MESH,
        )

    def pass_on(condition, copy):
        @pl.when(condition)
        def _():
            copy.start()

        passed.append((condition, copy))

    def z_own(k):
        src = own_unit[k].at[y, x, c]
        pass_on(z > 0, z_copy(src, k, z, 0))
        pass_on(z < 3, z_copy(src, k, z, 1))

    def z_step(k, step):
        for side in range(2):
            shard = z - 1 - step if side else z + 1 + step
            there = shard >= 0 if side else shard <= 3
            further = jnp.logical_and(there, z < 3 if side else z > 0)
            shard = jnp.clip(shard, 0, 3)
            copy = z_copy(W.at[k, shard, y, x, c], k, shard, side)

            @pl.when(there)
            def _():
                copy.wait_recv()

            pass_on(further, copy)

    def gather_tick(t):
        i = t
        if 0 <= i < 9:
            k, r = units[i]
            z_step(k, r - 1)
            part = W.at[k, z_of[r], y, x, c, pl.ds(0, HALF)]
            a1[i] = remote(part, part, ag_s.at[0, i], ag_r.at[0, i], x_peer)
            part = W.at[k, z_of[r], y, x, c, pl.ds(HALF, HALF)]
            b1[i] = remote(part, part, ag_s.at[1, i], ag_r.at[1, i], y_peer)
        i = t - 1
        if 0 <= i < 9:
            k, r = units[i]
            a1[i].wait_recv()
            part = W.at[k, z_of[r], y, :, c, pl.ds(0, HALF)]
            a2[i] = remote(part, part, ag_s.at[2, i], ag_r.at[2, i], y_peer)
            b1[i].wait_recv()
            part = W.at[k, z_of[r], :, x, c, pl.ds(HALF, HALF)]
            b2[i] = remote(part, part, ag_s.at[3, i], ag_r.at[3, i], x_peer)
        i = t - 2
        if 0 <= i < 9:
            k, r = units[i]
            a2[i].wait_recv()
            b2[i].wait_recv()
            part = W.at[k, z_of[r], :, :, c]
            cc[i] = remote(part, part, ag_s.at[4, i], ag_r.at[4, i], core_peer)
        i = t - 3
        if 0 <= i < 9:
            cc[i].wait_recv()

    def unit_value(ref):
        return ref[...].reshape(768, ref.shape[-1])

    def cols(k, r, start, size):
        return unit_value(W.at[k, z_of[r], :, :, :, :, pl.ds(start, size)])

    def qkv_rows(ref):
        return jnp.concatenate([ref[0].reshape(384, 768), ref[1, 0].reshape(192, 768)], axis=0)

    def out_rows(ref):
        return ref[1, 1].reshape(192, 768)

    def accumulate(first, value):
        if first:
            ACC[...] = value
        else:
            ACC[...] += value

    def attn_forward(r):
        QKV[r] = mm_nt(XA[own_rows, :], qkv_rows(W.at[ATT, z_of[r]])).astype(BF16)

        def segment(s, carry):
            rows = pl.ds(pl.multiple_of(s * SEG, SEG), SEG)
            qkv = QKV[r, rows, :]
            mixes = []
            for h in range(3):
                q = qkv[:, h * 64 : h * 64 + 64]
                key = qkv[:, 192 + h * 64 : 256 + h * 64]
                val = qkv[:, 384 + h * 64 : 448 + h * 64]
                scores = mm_nt(q, key) * SCALE
                top = jnp.max(scores, axis=-1, keepdims=True)
                expd = jnp.exp(scores - top)
                prob = expd * (1.0 / jnp.sum(expd, axis=-1, keepdims=True))
                PR[r, h, rows, :] = prob
                mixes.append(mm(prob.astype(BF16), val))
            MIX[r, rows, :] = jnp.concatenate(mixes, axis=-1).astype(BF16)
            return carry

        lax.fori_loop(0, 2, segment, 0)
        accumulate(r == 0, mm(MIX[r], out_rows(W.at[ATT, z_of[r]])))

    own_rows = pl.ds(pl.multiple_of(z * 256, 256), 256)

    def row_chunks(body, init=0):
        def one(i, carry):
            return body(i, pl.ds(pl.multiple_of(i * 64, 64), 64), carry)

        return lax.fori_loop(0, 4, one, init)

    g00, g01 = gain_ref[0, 0:1, :], gain_ref[0, 1:2, :]
    b00, b01 = shift_ref[0, 0:1, :], shift_ref[0, 1:2, :]
    g10, g11 = gain_ref[1, 0:1, :], gain_ref[1, 1:2, :]
    b10, b11 = shift_ref[1, 0:1, :], shift_ref[1, 1:2, :]

    def norm_one():
        def chunk(i, rows, carry):
            mine = XA[pl.ds(pl.multiple_of(z * 256 + i * 64, 64), 64), :]
            scaled, inverse = normalize(mine.astype(F32) + ACC[rows, :])
            SC1[rows, :] = scaled
            INV1[rows, :] = jnp.broadcast_to(inverse, (64, 128))
            FL[rows, :] = (scaled * g00 + b00).astype(BF16)
            return carry

        row_chunks(chunk)

    def ffn_forward(r):
        def block(n, carry):
            part = pl.ds(pl.multiple_of(n * 256, 256), 256)
            upward = mm(FL[...], unit_value(W.at[UP, z_of[r], :, :, :, :, part]))
            active, slope = gelu_pair(upward)
            ACT[r, :, part] = active.astype(BF16)
            DG[r, :, part] = slope.astype(DG.dtype)
            return carry

        lax.fori_loop(0, 3, block, 0)

    def ffn_down(r):
        accumulate(r == 0, mm(ACT[r], cols(DOWN, r, 0, 768)))

    def norm_two():
        def chunk(i, rows, carry):
            first = SC1[rows, :] * g00 + b00
            scaled, inverse = normalize(first + ACC[rows, :])
            SC2[rows, :] = scaled
            INV2[rows, :] = jnp.broadcast_to(inverse, (64, 128))
            out_ref[0, rows, :] = (scaled * g01 + b01).astype(BF16)
            return carry

        row_chunks(chunk)

    def transpose_into(dst, src, start=0):
        for i in range(2):
            dst[:, i * 128 : i * 128 + 128] = src[pl.ds(pl.multiple_of(start + i * 128, 128), 128), :].T

    exch = {}

    def exchange(e, value):
        E[e, 0] = value
        for r in range(1, 4):
            exch[e, r] = remote(E.at[e, 0], E.at[e, r], e_s.at[e, r - 1], e_r.at[e, r - 1], z_peer[r])

    def exchange_wait(e):
        for r in range(1, 4):
            exch[e, r].wait_recv()

    def exchange_sum(e):
        exchange_wait(e)
        return (E[e, 0] + E[e, 1]) + (E[e, 2] + E[e, 3])

    row_of = lax.broadcasted_iota(jnp.int32, (8, 768), 0)
    pair_of = row_of // 2

    def own_row(value, j):
        return jnp.sum(jnp.where(row_of == 2 * z + j, value, 0.0), axis=0, keepdims=True)


    def norm_two_back():
        def chunk(i, rows, carry):
            gains, shifts = carry
            which = lax.broadcasted_iota(jnp.int32, (64, 768), 0) + i * 64
            grad = jnp.where(which % SEG == 0, GS[i // 2][0:1, :], COT[rows, :].astype(F32))
            scaled = SC2[rows, :]
            fed = normalize_back(grad, scaled, INV2[rows, 0:1], g01)
            GF[rows, :] = fed
            FDL[rows, :] = fed.astype(BF16)
            return (
                gains + jnp.sum(grad * scaled, axis=0, keepdims=True),
                shifts + jnp.sum(grad, axis=0, keepdims=True),
            )

        zero = jnp.zeros((1, 768), F32)
        gains, shifts = row_chunks(chunk, (zero, zero))
        NV[1:2, :] = gains
        NV[3:4, :] = shifts

    def grad_unit(k, r):
        return W.at[UP, r] if k == ATT else G.at[k - 1, r]

    turn = (2, 3, 1, 0)
    order = [(k, r) for r in turn for k in (DOWN, UP)] + [(ATT, r) for r in turn]
    s0, sa1, sb1, sa2, sb2, sz = {}, {}, {}, {}, {}, {}

    def sum_start(i):
        k, r = order[i]
        g = grad_unit(k, r)
        s0[i] = remote(g.at[:, :, nc], RC.at[i], rs_s.at[0, i], rs_r.at[0, i], core_peer)

    def add_low(a, b):
        return (a.astype(F32) + b.astype(F32)).astype(BF16)

    def sum_one(i):
        if not 0 <= i < 12:
            return
        k, r = order[i]
        g = grad_unit(k, r)
        s0[i].wait_recv()

        def block(j, carry):
            jy, jx = j // 2, j % 2
            g[jy, jx, c] = add_low(g[jy, jx, c], RC[i, jy, jx])
            return carry

        lax.fori_loop(0, 4, block, 0)
        sa1[i] = remote(g.at[:, nx, c, pl.ds(0, HALF)], RA1.at[i], rs_s.at[1, i], rs_r.at[1, i], x_peer)
        sb1[i] = remote(g.at[ny, :, c, pl.ds(HALF, HALF)], RB1.at[i], rs_s.at[2, i], rs_r.at[2, i], y_peer)

    def sum_two(i):
        if not 0 <= i < 12:
            return
        k, r = order[i]
        g = grad_unit(k, r)
        sa1[i].wait_recv()
        for j in range(2):
            g[j, x, c, 0:HALF, :] = add_low(g[j, x, c, 0:HALF, :], RA1[i, j])
        sa2[i] = remote(g.at[ny, x, c, pl.ds(0, HALF)], RA2.at[i], rs_s.at[3, i], rs_r.at[3, i], y_peer)
        sb1[i].wait_recv()
        for j in range(2):
            g[y, j, c, HALF:BLK, :] = add_low(g[y, j, c, HALF:BLK, :], RB1[i, j])
        sb2[i] = remote(g.at[y, nx, c, pl.ds(HALF, HALF)], RB2.at[i], rs_s.at[4, i], rs_r.at[4, i], x_peer)

    def sum_three(i):
        if not 0 <= i < 12:
            return
        k, r = order[i]
        g = grad_unit(k, r)
        sa2[i].wait_recv()
        g[y, x, c, 0:HALF, :] = add_low(g[y, x, c, 0:HALF, :], RA2[i])
        sb2[i].wait_recv()
        g[y, x, c, HALF:BLK, :] = add_low(g[y, x, c, HALF:BLK, :], RB2[i])
        if r:
            sz[k, r] = remote(g.at[y, x, c], RZ.at[k, r - 1], rs_s.at[5, i], rs_r.at[5, i], z_peer[r])

    def pump(i):
        sum_one(i)
        sum_two(i - 1)
        sum_three(i - 2)

    def sum_final(k):
        for r in range(1, 4):
            sz[k, r].wait_recv()
        g = grad_unit(k, 0)
        own = g[y, x, c].astype(F32) + RZ[k, 0].astype(F32)
        return own + (RZ[k, 1].astype(F32) + RZ[k, 2].astype(F32))

    def store_unit(ref, parts):
        for start, size, value in parts:
            ref[:, :, :, :, start : start + size] = value().astype(BF16).reshape(2, 2, 2, BLK, size)

    def store_ffn(k, r, lhs_t, rhs):
        ref = grad_unit(k, r)

        def block(n, carry):
            part = pl.ds(pl.multiple_of(n * 256, 256), 256)
            value = mm(lhs_t[...], rhs[:, part])
            ref[:, :, :, :, part] = value.astype(BF16).reshape(2, 2, 2, BLK, 256)
            return carry

        lax.fori_loop(0, 3, block, 0)

    def ffn_back_one(r):
        ga = mm_nt(FDL[...], cols(DOWN, r, 0, 768))
        GU[...] = (ga * DG[r].astype(F32)).astype(BF16)

    def ffn_back_two(r, first):
        accumulate(first, mm_nt(GU[...], cols(UP, r, 0, 768)))

    def l1(k, start, size):
        return unit_value(L1.at[k, :, :, :, :, pl.ds(start, size)])

    live = {}

    def token_one():
        unit = W.at[ATT, z]
        kv_weight = jnp.concatenate([unit[0, 1].reshape(192, 768), unit[1, 0].reshape(192, 768)], axis=0)

        def rows_of(i, carry):
            rows = pl.ds(pl.multiple_of(i * 256, 256), 256)
            ACT[i, :, 0:384] = mm_nt(XA[rows, :], kv_weight).astype(BF16)
            return carry

        lax.fori_loop(0, 4, rows_of, 0)
        x8 = jnp.concatenate([XA[i * SEG : i * SEG + 16, :].astype(F32)[0:1] for i in range(8)], axis=0)
        live["x8"] = x8
        q8 = mm_nt(x8.astype(BF16), unit[0, 0].reshape(192, 768)).astype(BF16).astype(F32)
        row = lax.broadcasted_iota(jnp.int32, (8, 1024), 0)
        keep = lax.broadcasted_iota(jnp.int32, (8, 1024), 1) // SEG == row
        mixes = []
        for h in range(3):
            q = q8[:, h * 64 : h * 64 + 64].astype(BF16)
            parts = [mm_nt(q, ACT[i, :, h * 64 : h * 64 + 64]) for i in range(4)]
            scores = jnp.where(keep, jnp.concatenate(parts, axis=1) * SCALE, -3.0e38)
            top = jnp.max(scores, axis=-1, keepdims=True)
            expd = jnp.exp(scores - top)
            prob = (expd * (1.0 / jnp.sum(expd, axis=-1, keepdims=True))).astype(BF16)
            mix = None
            for i in range(4):
                val = ACT[i, :, 192 + h * 64 : 256 + h * 64]
                part = mm(prob[:, i * 256 : i * 256 + 256], val)
                mix = part if mix is None else mix + part
            mixes.append(mix)
        exchange(0, mm(jnp.concatenate(mixes, axis=-1).astype(BF16), out_rows(unit)))

    def token_two():
        attended = exchange_sum(0)
        scaled, _ = normalize(live["x8"] + attended)
        first = scaled * g00 + b00
        live["first8"] = first
        loads["wu"].wait()
        loads["wd"].wait()
        active, _ = gelu_pair(mm(first.astype(BF16), cols(UP, 0, 0, 768)))
        exchange(1, mm(active.astype(BF16), cols(DOWN, 0, 0, 768)))

    def cross_one():
        fed = exchange_sum(1)
        scaled, _ = normalize(live["first8"] + fed)
        summary = scaled * g01 + b01
        live["summary"] = summary
        live["summary_low"] = summary.astype(BF16)
        for name in ("l1qk", "l1v", "l1o"):
            loads[name].wait()
        qkv = mm_nt(live["summary_low"], qkv_rows(L1.at[ATT])).astype(BF16).astype(F32)
        pad = jnp.zeros((120, 64), F32)
        ids = jnp.broadcast_to(doc_ref[...].astype(F32), (8, 8))
        eye = lax.broadcasted_iota(jnp.int32, (8, 8), 0) == lax.broadcasted_iota(jnp.int32, (8, 8), 1)
        same = ids == jnp.sum(jnp.where(eye, ids, 0.0), axis=1, keepdims=True)
        keep = jnp.concatenate([jnp.where(same, 1.0, 0.0), jnp.zeros((8, 120), F32)], axis=1) > 0.5
        mixes = []
        for h in range(3):
            q = qkv[:, h * 64 : h * 64 + 64].astype(BF16)
            key = jnp.concatenate([qkv[:, 192 + h * 64 : 256 + h * 64], pad], axis=0).astype(BF16)
            val = jnp.concatenate([qkv[:, 384 + h * 64 : 448 + h * 64], pad], axis=0).astype(BF16)
            scores = jnp.where(keep, mm_nt(q, key) * SCALE, MASK_FILL)
            top = jnp.max(scores, axis=-1, keepdims=True)
            expd = jnp.exp(scores - top)
            prob = expd * (1.0 / jnp.sum(expd, axis=-1, keepdims=True))
            live["prob", h], live["q", h], live["key", h], live["val", h] = prob, q, key, val
            mixes.append(mm(prob.astype(BF16), val))
        mix = jnp.concatenate(mixes, axis=-1).astype(BF16)
        live["mix"] = mix
        exchange(2, mm(mix, out_rows(L1.at[ATT])))

    def cross_two():
        attended = exchange_sum(2)
        live["xs1"], live["xi1"] = normalize(live["summary"] + attended)
        first = live["xs1"] * g10 + b10
        live["xfirst"] = first
        live["xfirst_low"] = first.astype(BF16)
        loads["l1u"].wait()
        loads["l1d"].wait()
        active, live["xdg"] = gelu_pair(mm(live["xfirst_low"], l1(UP, 0, 768)))
        live["xact"] = active.astype(BF16)
        exchange(3, mm(live["xact"], l1(DOWN, 0, 768)))

    def cross_three():
        fed = exchange_sum(3)
        xs2, xi2 = normalize(live["xfirst"] + fed)
        upper = xs2 * g11 + b11
        for j in range(2):
            GS[j, 1:2, :] = own_row(upper, j)
        loads["c8"].wait()
        grad_top = C8[...].astype(F32)[:, 0, :]
        live["xs2"], live["xi2"] = xs2, xi2
        grad_fed = normalize_back(grad_top, live["xs2"], live["xi2"], g11)
        NV[5:6, :] = jnp.sum(grad_top * live["xs2"], axis=0, keepdims=True)
        NV[7:8, :] = jnp.sum(grad_top, axis=0, keepdims=True)
        live["xgf"] = grad_fed
        live["xfed_low"] = grad_fed.astype(BF16)
        ga = mm_nt(live["xfed_low"], l1(DOWN, 0, 768))
        live["xgu"] = (ga * live["xdg"]).astype(BF16)
        exchange(4, mm_nt(live["xgu"], l1(UP, 0, 768)))

    def cross_four():
        grad_first = live["xgf"] + exchange_sum(4)
        grad_att = normalize_back(grad_first, live["xs1"], live["xi1"], g10)
        NV[4:5, :] = jnp.sum(grad_first * live["xs1"], axis=0, keepdims=True)
        NV[6:7, :] = jnp.sum(grad_first, axis=0, keepdims=True)
        live["xga"] = grad_att
        att_low = grad_att.astype(BF16)
        live["xatt_low"] = att_low
        gm = mm_nt(att_low, out_rows(L1.at[ATT])).astype(BF16)
        gqs, gks, gvs = [], [], []
        for h in range(3):
            gmh = gm[:, h * 64 : h * 64 + 64]
            prob = live["prob", h]
            gp = mm_nt(gmh, live["val", h])
            inner = jnp.sum(gp * prob, axis=-1, keepdims=True)
            gs = (prob * (gp - inner)).astype(BF16)
            gqs.append(mm(gs, live["key", h]) * SCALE)
            gks.append(mm_tn(gs, live["q", h])[0:8, :] * SCALE)
            gvs.append(mm_tn(prob.astype(BF16), gmh)[0:8, :])
        gqkv = jnp.concatenate(gqs + gks + gvs, axis=-1).astype(BF16)
        live["xgqkv"] = gqkv
        exchange(5, mm(gqkv, qkv_rows(L1.at[ATT])))

    def cross_five():
        grad_summary = live["xga"] + exchange_sum(5)
        for j in range(2):
            GS[j, 0:1, :] = own_row(grad_summary, j)

    def output_rows():
        for j in range(2):
            out_ref[0, j * 128 : j * 128 + 1, :] = GS[j, 1:2, :].astype(BF16)

    def norm_one_back():
        def chunk(i, rows, carry):
            gains, shifts = carry
            grad = GF[rows, :] + ACC[rows, :]
            scaled = SC1[rows, :]
            att = normalize_back(grad, scaled, INV1[rows, 0:1], g00)
            GF[rows, :] = att
            FDL[rows, :] = att.astype(BF16)
            return (
                gains + jnp.sum(grad * scaled, axis=0, keepdims=True),
                shifts + jnp.sum(grad, axis=0, keepdims=True),
            )

        zero = jnp.zeros((1, 768), F32)
        gains, shifts = row_chunks(chunk, (zero, zero))
        NV[0:1, :] = gains
        NV[2:3, :] = shifts

    def attn_backward(r, first):
        GM[...] = mm_nt(FDL[...], out_rows(W.at[ATT, z_of[r]])).astype(BF16)

        def segment(s, carry):
            rows = pl.ds(pl.multiple_of(s * SEG, SEG), SEG)
            qkv = QKV[r, rows, :]
            gm = GM[rows, :]
            gqs, gks, gvs = [], [], []
            for h in range(3):
                q = qkv[:, h * 64 : h * 64 + 64]
                key = qkv[:, 192 + h * 64 : 256 + h * 64]
                val = qkv[:, 384 + h * 64 : 448 + h * 64]
                gmh = gm[:, h * 64 : h * 64 + 64]
                prob = PR[r, h, rows, :]
                gp = mm_nt(gmh, val)
                inner = jnp.sum(gp * prob, axis=-1, keepdims=True)
                gs = (prob * (gp - inner)).astype(BF16)
                gqs.append(mm(gs, key) * SCALE)
                gks.append(mm_tn(gs, q) * SCALE)
                gvs.append(mm_tn(prob.astype(BF16), gmh))
            GQ[rows, :] = jnp.concatenate(gqs + gks + gvs, axis=-1).astype(BF16)
            return carry

        lax.fori_loop(0, 2, segment, 0)
        store_unit(
            grad_unit(ATT, r),
            [
                (0, 576, lambda: mm(XT[...], GQ[...])),
                (576, 192, lambda: mm(FDLT[...], MIX[r])),
            ],
        )
        accumulate(first, mm(GQ[...], qkv_rows(W.at[ATT, z_of[r]])))

    fac = {}

    def factor_start():
        wide = lambda v: v.astype(F32)
        zero_a, zero_b = jnp.zeros((8, 192), F32), jnp.zeros((8, 576), F32)
        att_left = jnp.concatenate([wide(live["xgqkv"]), zero_a], axis=-1)
        att_right = jnp.concatenate([zero_b, wide(live["mix"])], axis=-1)
        right = jnp.concatenate([wide(live["xact"]), wide(live["xgu"]), att_left, att_right], axis=0)
        left = jnp.concatenate(
            [wide(live["xfed_low"]), wide(live["xfirst_low"]), wide(live["summary_low"]), wide(live["xatt_low"])],
            axis=0,
        )
        FAC[y, x, c, 0:32, :] = right.astype(BF16)
        FAC[y, x, c, 32:64, :] = left.astype(BF16)
        part = FAC.at[y, x, c]
        fac[0] = remote(part, part, f_s.at[0], f_r.at[0], x_peer)

    def factor_two():
        fac[0].wait_recv()
        part = FAC.at[y, :, c]
        fac[1] = remote(part, part, f_s.at[1], f_r.at[1], y_peer)

    def factor_three():
        fac[1].wait_recv()
        part = FAC.at[:, :, c]
        fac[2] = remote(part, part, f_s.at[2], f_r.at[2], core_peer)

    def turn_rows(value):
        rows = value.shape[0]
        full = jnp.concatenate([value, jnp.zeros((128 - rows, value.shape[1]), F32)], axis=0)
        return full.T[:, 0:rows]

    def write_unit(layer, k, value):
        if k == ATT:
            for i in range(3):
                qkvg_ref[layer, i] = value[:, i * 192 : i * 192 + 192]
            outg_ref[layer] = turn_rows(value[:, 576:768])
        elif k == UP:
            upg_ref[layer] = value
        else:
            downg_ref[layer] = value

    def factor_final():
        fac[2].wait_recv()
        left = FAC[:, :, :, 32:64, :].reshape(256, 768)
        for i in range(2):
            LT[:, i * 128 : i * 128 + 128] = left[i * 128 : i * 128 + 128, :].T
        mine = LT[pl.ds(pl.multiple_of(dp * BLK, BLK), BLK), :].astype(F32)
        kind = (lax.broadcasted_iota(jnp.int32, (BLK, 256), 1) // 8) % 4
        right = FAC[:, :, :, 0:32, :].reshape(256, 768)
        write_unit(1, DOWN, mm(jnp.where(kind == 0, mine, 0.0).astype(BF16), right))
        write_unit(1, UP, mm(jnp.where(kind == 1, mine, 0.0).astype(BF16), right))
        write_unit(1, ATT, mm(jnp.where(kind >= 2, mine, 0.0).astype(BF16), right))

    vec = {}

    def norm_grads_start():
        exchange(6, NV[...])

    def norm_grads_two():
        total = jnp.where(row_of < 4, exchange_sum(6), NV[...])
        pad = jnp.zeros((8, 32), F32)
        for p in range(8):
            SV[p // 4, (p // 2) % 2, p % 2] = jnp.concatenate([total[:, p * BLK : p * BLK + BLK], pad], axis=-1)
        for m in range(1, 8):
            ty = y if m // 4 == 0 else ny
            tx = x if (m // 2) % 2 == 0 else nx
            tc = c if m % 2 == 0 else nc
            vec[m] = remote(
                SV.at[ty, tx, tc], RSV.at[m - 1], v_s.at[m - 1], v_r.at[m - 1], (plane_index(m), z)
            )

    def norm_grads_final():
        total = SV[y, x, c]
        for m in range(1, 8):
            vec[m].wait_recv()
            total = total + RSV[m - 1]
        gaing_ref[...] = total[0:2, 0:BLK]
        shiftg_ref[...] = total[2:4, 0:BLK]
        crossg_ref[0] = total[4:6, 0:BLK]
        crossg_ref[1] = total[6:8, 0:BLK]

    for name in ("wqk", "wv", "wo"):
        loads[name].wait()
    z_own(ATT)
    loads["x"].wait()
    token_one()
    gather_tick(0)
    z_own(UP)
    attn_forward(0)
    gather_tick(1)
    token_two()
    gather_tick(2)
    z_own(DOWN)
    cross_one()
    gather_tick(3)
    attn_forward(1)
    transpose_into(XT, XA, z * 256)
    gather_tick(4)
    cross_two()
    attn_forward(2)
    gather_tick(5)
    cross_three()
    attn_forward(3)
    norm_one()
    gather_tick(6)
    cross_four()
    ffn_forward(0)
    ffn_forward(1)
    gather_tick(7)
    cross_five()
    ffn_forward(2)
    gather_tick(8)
    ffn_forward(3)
    ffn_down(0)
    gather_tick(9)
    ffn_down(1)
    transpose_into(FLT, FL)
    gather_tick(10)
    factor_start()
    ffn_down(2)
    gather_tick(11)
    ffn_down(3)
    norm_two()
    output_rows()
    factor_two()
    loads["cot"].wait()
    norm_two_back()
    transpose_into(FDLT, FDL)

    step = 0
    for n, r in enumerate(turn):
        ffn_back_one(r)
        store_ffn(DOWN, r, FDLT, ACT.at[r])
        sum_start(2 * n)
        store_ffn(UP, r, FLT, GU)
        sum_start(2 * n + 1)
        ffn_back_two(r, n == 0)
        if n == 0:
            factor_three()
        pump(step)
        step += 1
    norm_one_back()
    norm_grads_start()
    transpose_into(FDLT, FDL)
    for table in (a1, b1, a2, b2, cc):
        for i in range(9):
            table[i].wait_send()
            waited.append(id(table[i]))
    for condition, copy in passed:

        @pl.when(condition)
        def _(copy=copy):
            copy.wait_send()

    pump(step)
    step += 1
    factor_final()
    for n, r in enumerate(turn):
        attn_backward(r, n == 0)
        sum_start(8 + n)
        pump(step)
        step += 1
        if n == 1:
            norm_grads_two()
    ing_ref[0] = (GF[...] + ACC[...]).astype(BF16)
    norm_grads_final()
    pump(9)
    write_unit(0, DOWN, sum_final(DOWN))
    pump(10)
    write_unit(0, UP, sum_final(UP))
    pump(11)
    pump(12)
    pump(13)
    write_unit(0, ATT, sum_final(ATT))
    for copy in sends:
        if id(copy) not in waited:
            copy.wait_send()


def settle_kernel(*refs):
    sources, targets, held, sems = refs[:9], refs[9:18], refs[18:27], refs[27]
    arrive = [pltpu.make_async_copy(sources[i], held[i], sems.at[0, i]) for i in range(9)]
    leave = [pltpu.make_async_copy(held[i], targets[i], sems.at[1, i]) for i in range(9)]
    for copy in arrive:
        copy.start()
    for i in range(9):
        arrive[i].wait()
        leave[i].start()
    for copy in leave:
        copy.wait()


def fused_body(
    inputs, doc_ids, qkv_weight, out_weight, up_weight, down_weight, norm_gain, norm_shift, cotangent
):
    wq = qkv_weight.swapaxes(2, 3).reshape(2, 3, 2, BLK, 768)
    wo = out_weight.reshape(2, 2, BLK, 768)
    wu = up_weight.reshape(2, 2, 2, 2, BLK, 768)
    wd = down_weight.reshape(2, 2, 2, 2, BLK, 768)
    whole = pl.BlockSpec(memory_space=pl.ANY)
    vmem = pl.BlockSpec(memory_space=pltpu.VMEM)
    blocks = (2, 2, 2, BLK, 768)
    sem = pltpu.SemaphoreType.DMA
    results = pl.pallas_call(
        fused_kernel,
        out_shape=(
            jax.ShapeDtypeStruct((1, 256, 768), BF16),
            jax.ShapeDtypeStruct((1, 256, 768), BF16),
            jax.ShapeDtypeStruct((2, 3, BLK, 192), F32),
            jax.ShapeDtypeStruct((2, 192, BLK), F32),
            jax.ShapeDtypeStruct((2, BLK, 768), F32),
            jax.ShapeDtypeStruct((2, BLK, 768), F32),
            jax.ShapeDtypeStruct((2, BLK), F32),
            jax.ShapeDtypeStruct((2, BLK), F32),
            jax.ShapeDtypeStruct((2, 2, BLK), F32),
        ),
        in_specs=[whole, whole, whole, vmem, whole, whole, whole, whole, vmem, vmem],
        out_specs=(vmem,) * 9,
        scratch_shapes=[
            pltpu.VMEM((3, 4) + blocks, BF16),
            pltpu.VMEM((2, 4) + blocks, BF16),
            pltpu.VMEM((12, 2, 2, BLK, 768), BF16),
            pltpu.VMEM((12, 2, HALF, 768), BF16),
            pltpu.VMEM((12, 2, HALF, 768), BF16),
            pltpu.VMEM((12, HALF, 768), BF16),
            pltpu.VMEM((12, HALF, 768), BF16),
            pltpu.VMEM((3, 3, BLK, 768), BF16),
            pltpu.VMEM((3,) + blocks, BF16),
            pltpu.VMEM((1024, 768), BF16),
            pltpu.VMEM((256, 768), BF16),
            pltpu.VMEM((4, 256, 576), BF16),
            pltpu.VMEM((4, 3, 256, 128), F32),
            pltpu.VMEM((4, 256, 192), BF16),
            pltpu.VMEM((4, 256, 768), BF16),
            pltpu.VMEM((4, 256, 768), BF16),
            pltpu.VMEM((256, 768), BF16),
            pltpu.VMEM((256, 576), BF16),
            pltpu.VMEM((256, 768), F32),
            pltpu.VMEM((256, 768), F32),
            pltpu.VMEM((256, 768), F32),
            pltpu.VMEM((256, 768), F32),
            pltpu.VMEM((256, 768), BF16),
            pltpu.VMEM((768, 256), BF16),
            pltpu.VMEM((256, 768), BF16),
            pltpu.VMEM((768, 256), BF16),
            pltpu.VMEM((768, 256), BF16),
            pltpu.VMEM((256, 192), BF16),
            pltpu.VMEM((8, 16, 768), BF16),
            pltpu.VMEM((256, 128), F32),
            pltpu.VMEM((256, 128), F32),
            pltpu.VMEM((2, 2, 2, 64, 768), BF16),
            pltpu.VMEM((768, 256), BF16),
            pltpu.VMEM((2, 8, 768), F32),
            pltpu.VMEM((7, 4, 8, 768), F32),
            pltpu.VMEM((8, 768), F32),
            pltpu.VMEM((2, 2, 2, 8, 128), F32),
            pltpu.VMEM((7, 8, 128), F32),
            sem((13,)),
            sem((12, 2)),
            sem((12,)),
            sem((5, 9)),
            sem((5, 9)),
            sem((6, 12)),
            sem((6, 12)),
            sem((7, 3)),
            sem((7, 3)),
            sem((3,)),
            sem((3,)),
            sem((7,)),
            sem((7,)),
        ],
        compiler_params=pltpu.CompilerParams(
            collective_id=0, has_side_effects=True, vmem_limit_bytes=63 * 2**20
        ),
    )(
        inputs, cotangent, cotangent.reshape(8, SEG, 768), doc_ids, wq, wo, wu, wd, norm_gain, norm_shift
    )
    final = pl.pallas_call(
        settle_kernel,
        out_shape=tuple(jax.ShapeDtypeStruct(v.shape, v.dtype) for v in results),
        in_specs=[whole] * 9,
        out_specs=(whole,) * 9,
        scratch_shapes=[pltpu.VMEM(v.shape, v.dtype) for v in results] + [sem((2, 9))],
    )(*results)
    return final[:5] + (final[5].swapaxes(1, 2),) + final[6:]


def solution(mesh):
    in_specs = (
        P("dp", None, None),
        P("dp", None),
        P(None, None, None, "tensor"),
        P(None, "tensor", None),
        P(None, None, "tensor"),
        P(None, "tensor", None),
        P(),
        P(),
        P("dp", None, None),
    )
    out_specs = (
        P("dp", "tensor", None),
        P("dp", "tensor", None),
        P(None, None, "dp", "tensor"),
        P(None, "tensor", "dp"),
        P(None, "dp", "tensor"),
        P(None, "tensor", "dp"),
        P(None, "dp"),
        P(None, "dp"),
        P(None, None, "dp"),
    )
    fits = dict(mesh.shape) == {"dp": 8, "tensor": 4}
    chosen = fused_body if fits else body
    return jax.shard_map(chosen, mesh=mesh, in_specs=in_specs, out_specs=out_specs, check_vma=False)
```

```python
from functools import partial
import math

import jax
import jax.numpy as jnp
from jax import lax
from jax.experimental import pallas as pl
from jax.experimental.pallas import tpu as pltpu
from jax.sharding import PartitionSpec as P

HEAD_DIM = 64
SEG = 128


EPSILON = 1e-05
MASK_FILL = -1000000000.0


def layer_norm(values, gain_row, shift_row):
    center = jnp.mean(values, axis=-1, keepdims=True)
    offset = values - center
    spread = jnp.mean(offset * offset, axis=-1, keepdims=True)
    inverse = lax.rsqrt(spread + EPSILON)
    scaled = offset * inverse
    return (scaled * gain_row + shift_row, (scaled, inverse))


def norm_back(grad_out, saved, gain_row):
    scaled, inverse = saved
    weighted = grad_out * gain_row
    mean_one = jnp.mean(weighted, axis=-1, keepdims=True)
    mean_two = jnp.mean(weighted * scaled, axis=-1, keepdims=True)
    grad_in = inverse * (weighted - mean_one - scaled * mean_two)
    return (grad_in, jnp.sum(grad_out * scaled, axis=(0, 1)), jnp.sum(grad_out, axis=(0, 1)))


def score_block(head_split, allowed):
    scores = jnp.einsum(
        "bqhe,bkhe->bhqk", head_split[0], head_split[1], preferred_element_type=jnp.float32
    ) * (1.0 / math.sqrt(HEAD_DIM))
    if allowed is not None:
        scores = jnp.where(allowed, scores, MASK_FILL)
    return scores


def attend_forward(rows_low, qkv_local, allowed):
    batch_count = rows_low.shape[0]
    length = rows_low.shape[1]
    project = jnp.einsum(
        "brd,cde->cbre", rows_low, qkv_local, preferred_element_type=jnp.float32
    ).astype(jnp.bfloat16)
    head_split = project.reshape(3, batch_count, length, -1, HEAD_DIM)
    scores = score_block(head_split, allowed)
    log_total = jax.nn.logsumexp(scores, axis=-1)
    soft_low = jnp.exp(scores - log_total[..., None]).astype(jnp.bfloat16)
    mixture = jnp.einsum(
        "bhqk,bkhe->bqhe", soft_low, head_split[2], preferred_element_type=jnp.float32
    )
    return (project, log_total, mixture.astype(jnp.bfloat16).reshape(batch_count, length, -1))


def attend_backward(rows_low, qkv_local, out_local, project, log_total, mixture, grad_low, allowed):
    batch_count = rows_low.shape[0]
    length = rows_low.shape[1]
    head_split = project.reshape(3, batch_count, length, -1, HEAD_DIM)
    grad_mixture = jnp.einsum(
        "brd,fd->brf", grad_low, out_local, preferred_element_type=jnp.float32
    ).astype(jnp.bfloat16)
    out_local_grad = jnp.einsum(
        "brf,brd->fd", mixture, grad_low, preferred_element_type=jnp.float32
    )
    grad_heads = grad_mixture.reshape(batch_count, length, -1, HEAD_DIM)
    scores = score_block(head_split, allowed)
    soft_full = jnp.exp(scores - log_total[..., None])
    grad_soft = jnp.einsum(
        "bqhe,bkhe->bhqk", grad_heads, head_split[2], preferred_element_type=jnp.float32
    )
    row_inner = jnp.sum(grad_soft * soft_full, axis=-1, keepdims=True)
    grad_scores = (soft_full * (grad_soft - row_inner)).astype(jnp.bfloat16)
    scale_factor = 1.0 / math.sqrt(HEAD_DIM)
    grad_query = (
        jnp.einsum(
            "bhqk,bkhe->bqhe", grad_scores, head_split[1], preferred_element_type=jnp.float32
        )
        * scale_factor
    )
    grad_key = (
        jnp.einsum(
            "bhqk,bqhe->bkhe", grad_scores, head_split[0], preferred_element_type=jnp.float32
        )
        * scale_factor
    )
    grad_value = jnp.einsum(
        "bhqk,bqhe->bkhe",
        soft_full.astype(jnp.bfloat16),
        grad_heads,
        preferred_element_type=jnp.float32,
    )
    grad_project = (
        jnp.stack([grad_query, grad_key, grad_value])
        .reshape(3, batch_count, length, -1)
        .astype(jnp.bfloat16)
    )
    qkv_local_grad = jnp.einsum(
        "brd,cbre->cde", rows_low, grad_project, preferred_element_type=jnp.float32
    )
    input_part = jnp.einsum(
        "cbre,cde->brd", grad_project, qkv_local, preferred_element_type=jnp.float32
    )
    return (input_part, qkv_local_grad, out_local_grad)


def expand_forward(rows_low, up_local, down_local):
    upward = jnp.einsum("brd,df->brf", rows_low, up_local, preferred_element_type=jnp.float32)
    active = jax.nn.gelu(upward, approximate=False).astype(jnp.bfloat16)
    return (
        upward,
        active,
        jnp.einsum("brf,fd->brd", active, down_local, preferred_element_type=jnp.float32),
    )


def expand_backward(rows_low, up_local, down_local, upward, active, grad_low):
    grad_active = jnp.einsum(
        "brd,fd->brf", grad_low, down_local, preferred_element_type=jnp.float32
    )
    down_local_grad = jnp.einsum(
        "brf,brd->fd", active, grad_low, preferred_element_type=jnp.float32
    )
    gelu_pull = jax.vjp(partial(jax.nn.gelu, approximate=False), upward)[1]
    grad_upward = gelu_pull(grad_active)[0].astype(jnp.bfloat16)
    up_local_grad = jnp.einsum(
        "brd,brf->df", rows_low, grad_upward, preferred_element_type=jnp.float32
    )
    input_part = jnp.einsum(
        "brf,df->brd", grad_upward, up_local, preferred_element_type=jnp.float32
    )
    return (input_part, up_local_grad, down_local_grad)


def body(
    inputs,
    doc_ids,
    qkv_weight,
    out_weight,
    up_weight,
    down_weight,
    norm_gain,
    norm_shift,
    cotangent,
):
    groups = lax.axis_size("tensor")
    position = lax.axis_index("tensor")
    model_width = inputs.shape[2]
    segment_count = inputs.shape[1] // SEG
    own_count = segment_count // groups
    row_start = position * own_count

    def final_rows(values):
        return lax.dynamic_slice_in_dim(values, row_start, own_count, 0)

    def forward_sum(partial_term):
        return lax.psum(partial_term.astype(jnp.bfloat16), "tensor").astype(jnp.float32)

    def backward_sum(partial_term):
        return lax.psum(partial_term.astype(jnp.bfloat16), "tensor").astype(jnp.float32)

    def cross_sum(partial_term):
        return lax.psum(partial_term.astype(jnp.bfloat16), "tensor").astype(jnp.float32)

    def cross_grad_sum(partial_term):
        return lax.psum(partial_term, "tensor")

    tokens = inputs[0].reshape(segment_count, SEG, model_width)
    tokens_wide = tokens.astype(jnp.float32)
    lower_proj, lower_total, lower_mix = attend_forward(tokens, qkv_weight[0], None)
    attended = forward_sum(
        jnp.einsum("brf,fd->brd", lower_mix, out_weight[0], preferred_element_type=jnp.float32)
    )
    first_norm, first_saved = layer_norm(tokens_wide + attended, norm_gain[0, 0], norm_shift[0, 0])
    first_low = first_norm.astype(jnp.bfloat16)
    lower_up, lower_active, fed_term = expand_forward(first_low, up_weight[0], down_weight[0])
    second, second_saved = layer_norm(
        first_norm + forward_sum(fed_term), norm_gain[0, 1], norm_shift[0, 1]
    )
    summary = second[:, 0, :]
    summary = summary[None]
    same_doc = (doc_ids[0][:, None] == doc_ids[0][None, :])[None, None]
    summary_low = summary.astype(jnp.bfloat16)
    upper_proj, upper_total, upper_mix = attend_forward(summary_low, qkv_weight[1], same_doc)
    upper_att = cross_sum(
        jnp.einsum("brf,fd->brd", upper_mix, out_weight[1], preferred_element_type=jnp.float32)
    )
    upper_first, upper_saved_one = layer_norm(
        summary + upper_att, norm_gain[1, 0], norm_shift[1, 0]
    )
    upper_first_low = upper_first.astype(jnp.bfloat16)
    upper_up, upper_active, upper_fed = expand_forward(
        upper_first_low, up_weight[1], down_weight[1]
    )
    upper_out, upper_saved_two = layer_norm(
        upper_first + cross_sum(upper_fed), norm_gain[1, 1], norm_shift[1, 1]
    )
    joined = second.at[:, 0, :].set(upper_out[0])
    outputs_own = final_rows(joined).reshape(1, -1, model_width).astype(jnp.bfloat16)
    grad_full = cotangent[0].reshape(segment_count, SEG, model_width).astype(jnp.float32)
    grad_top = grad_full[:, 0, :][None]
    grad_upper_fed, gain_cross_two, shift_cross_two = norm_back(
        grad_top, upper_saved_two, norm_gain[1, 1]
    )
    cross_part, up_cross, down_cross = expand_backward(
        upper_first_low,
        up_weight[1],
        down_weight[1],
        upper_up,
        upper_active,
        grad_upper_fed.astype(jnp.bfloat16),
    )
    grad_upper_first = grad_upper_fed + cross_grad_sum(cross_part)
    grad_upper_att, gain_cross_one, shift_cross_one = norm_back(
        grad_upper_first, upper_saved_one, norm_gain[1, 0]
    )
    cross_input_part, qkv_cross, out_cross = attend_backward(
        summary_low,
        qkv_weight[1],
        out_weight[1],
        upper_proj,
        upper_total,
        upper_mix,
        grad_upper_att.astype(jnp.bfloat16),
        same_doc,
    )
    grad_summary = grad_upper_att + cross_grad_sum(cross_input_part)
    grad_second = grad_full.at[:, 0, :].set(grad_summary[0])
    grad_fed, gain_seg_two, shift_seg_two = norm_back(grad_second, second_saved, norm_gain[0, 1])
    fed_low = grad_fed.astype(jnp.bfloat16)
    seg_part, up_seg, down_seg = expand_backward(
        first_low, up_weight[0], down_weight[0], lower_up, lower_active, fed_low
    )
    grad_first = grad_fed + backward_sum(seg_part)
    grad_att, gain_seg_one, shift_seg_one = norm_back(grad_first, first_saved, norm_gain[0, 0])
    att_low = grad_att.astype(jnp.bfloat16)
    seg_input_part, qkv_seg, out_seg = attend_backward(
        tokens, qkv_weight[0], out_weight[0], lower_proj, lower_total, lower_mix, att_low, None
    )
    input_full = grad_att + backward_sum(seg_input_part)
    input_own = final_rows(input_full).reshape(1, -1, model_width).astype(jnp.bfloat16)
    seg_gain = jnp.stack([gain_seg_one, gain_seg_two])
    seg_shift = jnp.stack([shift_seg_one, shift_seg_two])
    cross_norm = jnp.stack(
        [jnp.stack([gain_cross_one, gain_cross_two]), jnp.stack([shift_cross_one, shift_cross_two])]
    )
    qkv_all = jnp.stack([qkv_seg, qkv_cross])
    out_all = jnp.stack([out_seg, out_cross])
    up_all = jnp.stack([up_seg, up_cross])
    down_all = jnp.stack([down_seg, down_cross])
    summed = (
        lax.psum_scatter(qkv_all, "dp", scatter_dimension=2, tiled=True),
        lax.psum_scatter(out_all, "dp", scatter_dimension=2, tiled=True),
        lax.psum_scatter(up_all, "dp", scatter_dimension=1, tiled=True),
        lax.psum_scatter(down_all, "dp", scatter_dimension=2, tiled=True),
        lax.psum_scatter(seg_gain, "dp", scatter_dimension=1, tiled=True),
        lax.psum_scatter(seg_shift, "dp", scatter_dimension=1, tiled=True),
        lax.psum_scatter(cross_norm, "dp", scatter_dimension=2, tiled=True),
    )
    return (
        outputs_own,
        input_own,
        summed[0],
        summed[1],
        summed[2],
        summed[3],
        summed[4],
        summed[5],
        summed[6],
    )


MESH = pl.DeviceIdType.MESH
F32 = jnp.float32
BF16 = jnp.bfloat16
SCALE = 1.0 / math.sqrt(HEAD_DIM)
ATT, UP, DOWN = 0, 1, 2
BLK = 96
HALF = 48


def mm(a, b):
    return lax.dot_general(a, b, (((1,), (0,)), ((), ())), preferred_element_type=F32)


def mm_nt(a, b):
    return lax.dot_general(a, b, (((1,), (1,)), ((), ())), preferred_element_type=F32)


def mm_tn(a, b):
    return lax.dot_general(a, b, (((0,), (0,)), ((), ())), preferred_element_type=F32)


def normalize(values):
    center = jnp.mean(values, axis=-1, keepdims=True)
    offset = values - center
    spread = jnp.mean(offset * offset, axis=-1, keepdims=True)
    inverse = lax.rsqrt(spread + EPSILON)
    return offset * inverse, inverse


def normalize_back(grad_out, scaled, inverse, gain_row):
    weighted = grad_out * gain_row
    mean_one = jnp.mean(weighted, axis=-1, keepdims=True)
    mean_two = jnp.mean(weighted * scaled, axis=-1, keepdims=True)
    return inverse * (weighted - mean_one - scaled * mean_two)


def gelu_pair(upward):
    cdf = 0.5 * (1.0 + lax.erf(upward * math.sqrt(0.5)))
    pdf = jnp.exp(upward * upward * -0.5) * (1.0 / math.sqrt(2.0 * math.pi))
    return upward * cdf, cdf + upward * pdf


def fused_kernel(
    tokens_hbm, cot_hbm, cot_seg, doc_ref, wq_hbm, wo_hbm, wu_hbm, wd_hbm, gain_ref, shift_ref,
    out_ref, ing_ref, qkvg_ref, outg_ref, upg_ref, downg_ref, gaing_ref, shiftg_ref, crossg_ref,
    W, G, RC, RA1, RB1, RA2, RB2, RZ, RZF, RF, L1, XA, COT, QKV, PR, MIX, ACT, DG, GU, GQ, ACC, SC1, SC2, GF,
    FL, FLT, FDL, FDLT, XT, GM, C8, INV1, INV2, FAC, LT, GS, E, NV, SV, RSV,
    sem_local, zg_s, zg_r, ag_s, ag_r, rs_s, rs_r, e_s, e_r, f_s, f_r, v_s, v_r,
):
    dp = lax.axis_index("dp")
    z = lax.axis_index("tensor")
    c = dp % 2
    x = (dp // 2) % 2
    y = dp // 4
    nc, nx, ny = 1 - c, 1 - x, 1 - y
    core_peer = (dp + 1 - 2 * c, z)
    x_peer = (dp + 2 - 4 * x, z)
    y_peer = (dp + 4 - 8 * y, z)
    left_peer, right_peer = (dp, jnp.maximum(z - 1, 0)), (dp, jnp.minimum(z + 1, 3))
    z_peer = [None, (dp, z + 1 - 2 * (z % 2)), (dp, z + 2 - 4 * (z // 2)), (dp, 3 - z)]
    z_of = [z, z + 1 - 2 * (z % 2), z + 2 - 4 * (z // 2), 3 - z]

    def plane_index(m):
        ty = y if m // 4 == 0 else ny
        tx = x if (m // 2) % 2 == 0 else nx
        tc = c if m % 2 == 0 else nc
        return ty * 4 + tx * 2 + tc

    sends = []
    waited = []

    def remote(src, dst, ssem, rsem, target):
        copy = pltpu.make_async_remote_copy(
            src_ref=src, dst_ref=dst, send_sem=ssem, recv_sem=rsem, device_id=target, device_id_type=MESH
        )
        copy.start()
        sends.append(copy)
        return copy

    loads = {}

    def load(name, index, src, dst):
        copy = pltpu.make_async_copy(src, dst, sem_local.at[index])
        copy.start()
        loads[name] = copy

    load("x", 0, tokens_hbm.at[0], XA)
    load("wqk", 1, wq_hbm.at[0, pl.ds(0, 2)], W.at[ATT, z, 0])
    load("wv", 9, wq_hbm.at[0, 2], W.at[ATT, z, 1, 0])
    load("wo", 10, wo_hbm.at[0], W.at[ATT, z, 1, 1])
    load("wu", 2, wu_hbm.at[0], W.at[UP, z])
    load("wd", 3, wd_hbm.at[0], W.at[DOWN, z])
    load("cot", 4, cot_hbm.at[0, pl.ds(pl.multiple_of(z * 256, 256), 256)], COT)
    load("l1qk", 5, wq_hbm.at[1, pl.ds(0, 2)], L1.at[ATT, 0])
    load("l1v", 11, wq_hbm.at[1, 2], L1.at[ATT, 1, 0])
    load("l1o", 12, wo_hbm.at[1], L1.at[ATT, 1, 1])
    load("l1u", 6, wu_hbm.at[1], L1.at[UP])
    load("l1d", 7, wd_hbm.at[1], L1.at[DOWN])
    load("c8", 8, cot_seg.at[:, pl.ds(0, 16)], C8)

    barrier = pltpu.get_barrier_semaphore()
    for m in range(1, 8):
        pl.semaphore_signal(barrier, inc=1, device_id=(plane_index(m), z), device_id_type=MESH)
    for r in range(1, 4):
        pl.semaphore_signal(barrier, inc=1, device_id=z_peer[r], device_id_type=MESH)
    pl.semaphore_wait(barrier, 10)

    own_unit = [W.at[ATT, z], wu_hbm.at[0], wd_hbm.at[0]]
    units = [(ATT, 1), (UP, 1), (ATT, 2), (ATT, 3), (UP, 2), (DOWN, 1), (UP, 3), (DOWN, 2), (DOWN, 3)]
    a1, b1, a2, b2, cc = {}, {}, {}, {}, {}
    passed = []

    def z_copy(src, k, shard, side):
        return pltpu.make_async_remote_copy(
            src_ref=src,
            dst_ref=W.at[k, shard, y, x, c],
            send_sem=zg_s.at[k * 4 + shard, side],
            recv_sem=zg_r.at[k * 4 + shard],
            device_id=(left_peer, right_peer)[side],
            device_id_type=MESH,
        )

    def pass_on(condition, copy):
        @pl.when(condition)
        def _():
            copy.start()

        passed.append((condition, copy))

    def z_own(k):
        src = own_unit[k].at[y, x, c]
        pass_on(z > 0, z_copy(src, k, z, 0))
        pass_on(z < 3, z_copy(src, k, z, 1))

    def z_step(k, step):
        for side in range(2):
            shard = z - 1 - step if side else z + 1 + step
            there = shard >= 0 if side else shard <= 3
            further = jnp.logical_and(there, z < 3 if side else z > 0)
            shard = jnp.clip(shard, 0, 3)
            copy = z_copy(W.at[k, shard, y, x, c], k, shard, side)

            @pl.when(there)
            def _():
                copy.wait_recv()

            pass_on(further, copy)

    def gather_a(i):
        k, r = units[i]
        z_step(k, r - 1)
        part = W.at[k, z_of[r], y, x, c, pl.ds(0, HALF)]
        a1[i] = remote(part, part, ag_s.at[0, i], ag_r.at[0, i], x_peer)
        part = W.at[k, z_of[r], y, x, c, pl.ds(HALF, HALF)]
        b1[i] = remote(part, part, ag_s.at[1, i], ag_r.at[1, i], y_peer)

    def gather_b(i):
        k, r = units[i]
        a1[i].wait_recv()
        part = W.at[k, z_of[r], y, :, c, pl.ds(0, HALF)]
        a2[i] = remote(part, part, ag_s.at[2, i], ag_r.at[2, i], y_peer)
        b1[i].wait_recv()
        part = W.at[k, z_of[r], :, x, c, pl.ds(HALF, HALF)]
        b2[i] = remote(part, part, ag_s.at[3, i], ag_r.at[3, i], x_peer)

    def gather_c(i):
        k, r = units[i]
        a2[i].wait_recv()
        b2[i].wait_recv()
        part = W.at[k, z_of[r], :, :, c]
        cc[i] = remote(part, part, ag_s.at[4, i], ag_r.at[4, i], core_peer)

    def arrived(k, r):
        if r:
            cc[units.index((k, r))].wait_recv()

    def unit_value(ref):
        return ref[...].reshape(768, ref.shape[-1])

    def cols(k, r, start, size):
        return unit_value(W.at[k, z_of[r], :, :, :, :, pl.ds(start, size)])

    def qkv_rows(ref):
        return jnp.concatenate([ref[0].reshape(384, 768), ref[1, 0].reshape(192, 768)], axis=0)

    def out_rows(ref):
        return ref[1, 1].reshape(192, 768)

    def accumulate(first, value):
        if first:
            ACC[...] = value
        else:
            ACC[...] += value

    def attn_forward(r):
        arrived(ATT, r)
        QKV[r] = mm_nt(XA[own_rows, :], qkv_rows(W.at[ATT, z_of[r]])).astype(BF16)

        def segment(s, carry):
            rows = pl.ds(pl.multiple_of(s * SEG, SEG), SEG)
            qkv = QKV[r, rows, :]
            mixes = []
            for h in range(3):
                q = qkv[:, h * 64 : h * 64 + 64]
                key = qkv[:, 192 + h * 64 : 256 + h * 64]
                val = qkv[:, 384 + h * 64 : 448 + h * 64]
                scores = mm_nt(q, key) * SCALE
                top = jnp.max(scores, axis=-1, keepdims=True)
                expd = jnp.exp(scores - top)
                prob = expd * (1.0 / jnp.sum(expd, axis=-1, keepdims=True))
                PR[r, h, rows, :] = prob
                mixes.append(mm(prob.astype(BF16), val))
            MIX[r, rows, :] = jnp.concatenate(mixes, axis=-1).astype(BF16)
            return carry

        lax.fori_loop(0, 2, segment, 0)
        accumulate(r == 0, mm(MIX[r], out_rows(W.at[ATT, z_of[r]])))

    own_rows = pl.ds(pl.multiple_of(z * 256, 256), 256)

    def row_chunks(body, init=0):
        def one(i, carry):
            return body(i, pl.ds(pl.multiple_of(i * 64, 64), 64), carry)

        return lax.fori_loop(0, 4, one, init)

    g00, g01 = gain_ref[0, 0:1, :], gain_ref[0, 1:2, :]
    b00, b01 = shift_ref[0, 0:1, :], shift_ref[0, 1:2, :]
    g10, g11 = gain_ref[1, 0:1, :], gain_ref[1, 1:2, :]
    b10, b11 = shift_ref[1, 0:1, :], shift_ref[1, 1:2, :]

    def norm_one():
        def chunk(i, rows, carry):
            mine = XA[pl.ds(pl.multiple_of(z * 256 + i * 64, 64), 64), :]
            scaled, inverse = normalize(mine.astype(F32) + ACC[rows, :])
            SC1[rows, :] = scaled
            INV1[rows, :] = jnp.broadcast_to(inverse, (64, 128))
            FL[rows, :] = (scaled * g00 + b00).astype(BF16)
            return carry

        row_chunks(chunk)

    def ffn_forward(r):
        arrived(UP, r)
        def block(n, carry):
            part = pl.ds(pl.multiple_of(n * 256, 256), 256)
            upward = mm(FL[...], unit_value(W.at[UP, z_of[r], :, :, :, :, part]))
            active, slope = gelu_pair(upward)
            ACT[r, :, part] = active.astype(BF16)
            DG[r, :, part] = slope.astype(DG.dtype)
            return carry

        lax.fori_loop(0, 3, block, 0)

    def ffn_down(r):
        arrived(DOWN, r)
        accumulate(r == 0, mm(ACT[r], cols(DOWN, r, 0, 768)))

    def norm_two():
        def chunk(i, rows, carry):
            first = SC1[rows, :] * g00 + b00
            scaled, inverse = normalize(first + ACC[rows, :])
            SC2[rows, :] = scaled
            INV2[rows, :] = jnp.broadcast_to(inverse, (64, 128))
            out_ref[0, rows, :] = (scaled * g01 + b01).astype(BF16)
            return carry

        row_chunks(chunk)

    def transpose_into(dst, src, start=0):
        for i in range(2):
            dst[:, i * 128 : i * 128 + 128] = src[pl.ds(pl.multiple_of(start + i * 128, 128), 128), :].T

    exch = {}

    def exchange(e, value):
        E[e, 0] = value
        for r in range(1, 4):
            exch[e, r] = remote(E.at[e, 0], E.at[e, r], e_s.at[e, r - 1], e_r.at[e, r - 1], z_peer[r])

    def exchange_wait(e):
        for r in range(1, 4):
            exch[e, r].wait_recv()

    def exchange_sum(e):
        exchange_wait(e)
        return (E[e, 0] + E[e, 1]) + (E[e, 2] + E[e, 3])

    row_of = lax.broadcasted_iota(jnp.int32, (8, 768), 0)
    pair_of = row_of // 2

    def own_row(value, j):
        return jnp.sum(jnp.where(row_of == 2 * z + j, value, 0.0), axis=0, keepdims=True)


    def norm_two_back():
        def chunk(i, rows, carry):
            gains, shifts = carry
            which = lax.broadcasted_iota(jnp.int32, (64, 768), 0) + i * 64
            grad = jnp.where(which % SEG == 0, GS[i // 2][0:1, :], COT[rows, :].astype(F32))
            scaled = SC2[rows, :]
            fed = normalize_back(grad, scaled, INV2[rows, 0:1], g01)
            GF[rows, :] = fed
            FDL[rows, :] = fed.astype(BF16)
            return (
                gains + jnp.sum(grad * scaled, axis=0, keepdims=True),
                shifts + jnp.sum(grad, axis=0, keepdims=True),
            )

        zero = jnp.zeros((1, 768), F32)
        gains, shifts = row_chunks(chunk, (zero, zero))
        NV[1:2, :] = gains
        NV[3:4, :] = shifts

    def grad_unit(k, r):
        return W.at[UP, r] if k == ATT else G.at[k - 1, r]

    turn = (3, 2, 1, 0)
    order = [(k, r) for r in turn for k in (DOWN, UP)] + [(ATT, r) for r in turn]
    s0, sa1, sb1, sa2, sb2, sza, szb, sfa, sfb = {}, {}, {}, {}, {}, {}, {}, {}, {}

    def sum_start(i):
        k, r = order[i]
        g = grad_unit(k, r)
        s0[i] = remote(g.at[:, :, nc], RC.at[i], rs_s.at[0, i], rs_r.at[0, i], core_peer)

    def add_low(a, b):
        return (a.astype(F32) + b.astype(F32)).astype(BF16)

    top, low = pl.ds(0, HALF), pl.ds(HALF, HALF)

    def sum_one(i):
        k, r = order[i]
        g = grad_unit(k, r)
        s0[i].wait_recv()

        def block(j, carry):
            jy, jx = j // 2, j % 2
            g[jy, jx, c] = add_low(g[jy, jx, c], RC[i, jy, jx])
            return carry

        lax.fori_loop(0, 4, block, 0)
        if k == ATT:
            part_a, part_b = g.at[:, nx, c, top], g.at[ny, :, c, low]
            peer_a, peer_b = x_peer, y_peer
        else:
            part_a, part_b = g.at[ny, :, c, top], g.at[:, nx, c, low]
            peer_a, peer_b = y_peer, x_peer
        sa1[i] = remote(part_a, RA1.at[i], rs_s.at[1, i], rs_r.at[1, i], peer_a)
        sb1[i] = remote(part_b, RB1.at[i], rs_s.at[2, i], rs_r.at[2, i], peer_b)

    def sum_two(i):
        k, r = order[i]
        g = grad_unit(k, r)
        sa1[i].wait_recv()
        if k == ATT:
            for j in range(2):
                g[j, x, c, 0:HALF, :] = add_low(g[j, x, c, 0:HALF, :], RA1[i, j])
            sa2[i] = remote(g.at[ny, x, c, top], RA2.at[i - 8], rs_s.at[3, i], rs_r.at[3, i], y_peer)
            sb1[i].wait_recv()
            for j in range(2):
                g[y, j, c, HALF:BLK, :] = add_low(g[y, j, c, HALF:BLK, :], RB1[i, j])
            sb2[i] = remote(g.at[y, nx, c, low], RB2.at[i - 8], rs_s.at[4, i], rs_r.at[4, i], x_peer)
        else:
            sb1[i].wait_recv()
            for j in range(2):
                g[y, j, c, 0:HALF, :] = add_low(g[y, j, c, 0:HALF, :], RA1[i, j])
                g[j, x, c, HALF:BLK, :] = add_low(g[j, x, c, HALF:BLK, :], RB1[i, j])

    def sum_three(i):
        g = grad_unit(*order[i])
        sa2[i].wait_recv()
        g[y, x, c, 0:HALF, :] = add_low(g[y, x, c, 0:HALF, :], RA2[i - 8])
        sb2[i].wait_recv()
        g[y, x, c, HALF:BLK, :] = add_low(g[y, x, c, HALF:BLK, :], RB2[i - 8])

    landing = {1: 0, 3: 1, 2: 2}

    def z_wait(k, r):
        i = order.index((k, r))
        sza[i].wait_recv()
        if k != ATT:
            szb[i].wait_recv()

    def z_add(k, g, slot):
        if k == ATT:
            g[y, x, c] = add_low(g[y, x, c], RZ[slot])
        else:
            for j in range(2):
                g[y, j, c, 0:HALF, :] = add_low(g[y, j, c, 0:HALF, :], RZF[k - 1, slot, 0, j])
                g[j, x, c, HALF:BLK, :] = add_low(g[j, x, c, HALF:BLK, :], RZF[k - 1, slot, 1, j])

    def sum_z(i):
        k, r = order[i]
        g = grad_unit(k, r)
        if r == 2:
            z_wait(k, 3)
            z_add(k, g, landing[3])
        if r:
            peer = z_peer[2] if r == 2 else z_peer[1]
            if k == ATT:
                sza[i] = remote(g.at[y, x, c], RZ.at[landing[r]], rs_s.at[5, i], rs_r.at[5, i], peer)
            else:
                land = RZF.at[k - 1, landing[r]]
                sza[i] = remote(g.at[y, :, c, top], land.at[0], rs_s.at[5, i], rs_r.at[5, i], peer)
                szb[i] = remote(g.at[:, x, c, low], land.at[1], rs_s.at[6, i], rs_r.at[6, i], peer)
        else:
            z_wait(k, 1)
            z_wait(k, 2)
            if k != ATT:
                for j in range(2):
                    a, b = RZF[k - 1, 0, 0, j].astype(F32), RZF[k - 1, 2, 0, j].astype(F32)
                    g[y, j, c, 0:HALF, :] = add_low(g[y, j, c, 0:HALF, :], a + b)
                    a, b = RZF[k - 1, 0, 1, j].astype(F32), RZF[k - 1, 2, 1, j].astype(F32)
                    g[j, x, c, HALF:BLK, :] = add_low(g[j, x, c, HALF:BLK, :], a + b)
                sfa[k] = remote(g.at[y, nx, c, top], RF.at[k - 1, 0], rs_s.at[7, k], rs_r.at[7, k], x_peer)
                sfb[k] = remote(g.at[ny, x, c, low], RF.at[k - 1, 1], rs_s.at[8, k], rs_r.at[8, k], y_peer)

    def sum_final(k):
        own = grad_unit(k, 0)[y, x, c].astype(F32)
        if k == ATT:
            return own + (RZ[0].astype(F32) + RZ[2].astype(F32))
        sfa[k].wait_recv()
        sfb[k].wait_recv()
        return own + jnp.concatenate([RF[k - 1, 0], RF[k - 1, 1]], axis=0).astype(F32)

    def store_unit(ref, parts):
        for start, size, value in parts:
            ref[:, :, :, :, start : start + size] = value().astype(BF16).reshape(2, 2, 2, BLK, size)

    def store_ffn(k, r, lhs_t, rhs):
        ref = grad_unit(k, r)

        def block(n, carry):
            part = pl.ds(pl.multiple_of(n * 256, 256), 256)
            value = mm(lhs_t[...], rhs[:, part])
            ref[:, :, :, :, part] = value.astype(BF16).reshape(2, 2, 2, BLK, 256)
            return carry

        lax.fori_loop(0, 3, block, 0)

    def ffn_back_one(r):
        ga = mm_nt(FDL[...], cols(DOWN, r, 0, 768))
        GU[...] = (ga * DG[r].astype(F32)).astype(BF16)

    def ffn_back_two(r):
        accumulate(r == turn[0], mm_nt(GU[...], cols(UP, r, 0, 768)))

    def grad_down(r):
        store_ffn(DOWN, r, FDLT, ACT.at[r])
        sum_start(order.index((DOWN, r)))

    def grad_up(r):
        store_ffn(UP, r, FLT, GU)
        sum_start(order.index((UP, r)))

    def l1(k, start, size):
        return unit_value(L1.at[k, :, :, :, :, pl.ds(start, size)])

    live = {}

    def token_one():
        unit = W.at[ATT, z]
        kv_weight = jnp.concatenate([unit[0, 1].reshape(192, 768), unit[1, 0].reshape(192, 768)], axis=0)

        def rows_of(i, carry):
            rows = pl.ds(pl.multiple_of(i * 256, 256), 256)
            ACT[i, :, 0:384] = mm_nt(XA[rows, :], kv_weight).astype(BF16)
            return carry

        lax.fori_loop(0, 4, rows_of, 0)
        x8 = jnp.concatenate([XA[i * SEG : i * SEG + 16, :].astype(F32)[0:1] for i in range(8)], axis=0)
        live["x8"] = x8
        q8 = mm_nt(x8.astype(BF16), unit[0, 0].reshape(192, 768)).astype(BF16).astype(F32)
        row = lax.broadcasted_iota(jnp.int32, (8, 1024), 0)
        keep = lax.broadcasted_iota(jnp.int32, (8, 1024), 1) // SEG == row
        mixes = []
        for h in range(3):
            q = q8[:, h * 64 : h * 64 + 64].astype(BF16)
            parts = [mm_nt(q, ACT[i, :, h * 64 : h * 64 + 64]) for i in range(4)]
            scores = jnp.where(keep, jnp.concatenate(parts, axis=1) * SCALE, -3.0e38)
            top = jnp.max(scores, axis=-1, keepdims=True)
            expd = jnp.exp(scores - top)
            prob = (expd * (1.0 / jnp.sum(expd, axis=-1, keepdims=True))).astype(BF16)
            mix = None
            for i in range(4):
                val = ACT[i, :, 192 + h * 64 : 256 + h * 64]
                part = mm(prob[:, i * 256 : i * 256 + 256], val)
                mix = part if mix is None else mix + part
            mixes.append(mix)
        exchange(0, mm(jnp.concatenate(mixes, axis=-1).astype(BF16), out_rows(unit)))

    def token_two():
        attended = exchange_sum(0)
        scaled, _ = normalize(live["x8"] + attended)
        first = scaled * g00 + b00
        live["first8"] = first
        loads["wu"].wait()
        loads["wd"].wait()
        active, _ = gelu_pair(mm(first.astype(BF16), cols(UP, 0, 0, 768)))
        exchange(1, mm(active.astype(BF16), cols(DOWN, 0, 0, 768)))

    def cross_one():
        fed = exchange_sum(1)
        scaled, _ = normalize(live["first8"] + fed)
        summary = scaled * g01 + b01
        live["summary"] = summary
        live["summary_low"] = summary.astype(BF16)
        for name in ("l1qk", "l1v", "l1o"):
            loads[name].wait()
        qkv = mm_nt(live["summary_low"], qkv_rows(L1.at[ATT])).astype(BF16).astype(F32)
        pad = jnp.zeros((120, 64), F32)
        ids = jnp.broadcast_to(doc_ref[...].astype(F32), (8, 8))
        eye = lax.broadcasted_iota(jnp.int32, (8, 8), 0) == lax.broadcasted_iota(jnp.int32, (8, 8), 1)
        same = ids == jnp.sum(jnp.where(eye, ids, 0.0), axis=1, keepdims=True)
        keep = jnp.concatenate([jnp.where(same, 1.0, 0.0), jnp.zeros((8, 120), F32)], axis=1) > 0.5
        mixes = []
        for h in range(3):
            q = qkv[:, h * 64 : h * 64 + 64].astype(BF16)
            key = jnp.concatenate([qkv[:, 192 + h * 64 : 256 + h * 64], pad], axis=0).astype(BF16)
            val = jnp.concatenate([qkv[:, 384 + h * 64 : 448 + h * 64], pad], axis=0).astype(BF16)
            scores = jnp.where(keep, mm_nt(q, key) * SCALE, MASK_FILL)
            top = jnp.max(scores, axis=-1, keepdims=True)
            expd = jnp.exp(scores - top)
            prob = expd * (1.0 / jnp.sum(expd, axis=-1, keepdims=True))
            live["prob", h], live["q", h], live["key", h], live["val", h] = prob, q, key, val
            mixes.append(mm(prob.astype(BF16), val))
        mix = jnp.concatenate(mixes, axis=-1).astype(BF16)
        live["mix"] = mix
        exchange(2, mm(mix, out_rows(L1.at[ATT])))

    def cross_two():
        attended = exchange_sum(2)
        live["xs1"], live["xi1"] = normalize(live["summary"] + attended)
        first = live["xs1"] * g10 + b10
        live["xfirst"] = first
        live["xfirst_low"] = first.astype(BF16)
        loads["l1u"].wait()
        loads["l1d"].wait()
        active, live["xdg"] = gelu_pair(mm(live["xfirst_low"], l1(UP, 0, 768)))
        live["xact"] = active.astype(BF16)
        exchange(3, mm(live["xact"], l1(DOWN, 0, 768)))

    def cross_three():
        fed = exchange_sum(3)
        xs2, xi2 = normalize(live["xfirst"] + fed)
        upper = xs2 * g11 + b11
        for j in range(2):
            GS[j, 1:2, :] = own_row(upper, j)
        loads["c8"].wait()
        grad_top = C8[...].astype(F32)[:, 0, :]
        live["xs2"], live["xi2"] = xs2, xi2
        grad_fed = normalize_back(grad_top, live["xs2"], live["xi2"], g11)
        NV[5:6, :] = jnp.sum(grad_top * live["xs2"], axis=0, keepdims=True)
        NV[7:8, :] = jnp.sum(grad_top, axis=0, keepdims=True)
        live["xgf"] = grad_fed
        live["xfed_low"] = grad_fed.astype(BF16)
        ga = mm_nt(live["xfed_low"], l1(DOWN, 0, 768))
        live["xgu"] = (ga * live["xdg"]).astype(BF16)
        exchange(4, mm_nt(live["xgu"], l1(UP, 0, 768)))

    def cross_four():
        grad_first = live["xgf"] + exchange_sum(4)
        grad_att = normalize_back(grad_first, live["xs1"], live["xi1"], g10)
        NV[4:5, :] = jnp.sum(grad_first * live["xs1"], axis=0, keepdims=True)
        NV[6:7, :] = jnp.sum(grad_first, axis=0, keepdims=True)
        live["xga"] = grad_att
        att_low = grad_att.astype(BF16)
        live["xatt_low"] = att_low
        gm = mm_nt(att_low, out_rows(L1.at[ATT])).astype(BF16)
        gqs, gks, gvs = [], [], []
        for h in range(3):
            gmh = gm[:, h * 64 : h * 64 + 64]
            prob = live["prob", h]
            gp = mm_nt(gmh, live["val", h])
            inner = jnp.sum(gp * prob, axis=-1, keepdims=True)
            gs = (prob * (gp - inner)).astype(BF16)
            gqs.append(mm(gs, live["key", h]) * SCALE)
            gks.append(mm_tn(gs, live["q", h])[0:8, :] * SCALE)
            gvs.append(mm_tn(prob.astype(BF16), gmh)[0:8, :])
        gqkv = jnp.concatenate(gqs + gks + gvs, axis=-1).astype(BF16)
        live["xgqkv"] = gqkv
        exchange(5, mm(gqkv, qkv_rows(L1.at[ATT])))

    def cross_five():
        grad_summary = live["xga"] + exchange_sum(5)
        for j in range(2):
            GS[j, 0:1, :] = own_row(grad_summary, j)

    def output_rows():
        for j in range(2):
            out_ref[0, j * 128 : j * 128 + 1, :] = GS[j, 1:2, :].astype(BF16)

    def norm_one_back():
        def chunk(i, rows, carry):
            gains, shifts = carry
            grad = GF[rows, :] + ACC[rows, :]
            scaled = SC1[rows, :]
            att = normalize_back(grad, scaled, INV1[rows, 0:1], g00)
            GF[rows, :] = att
            FDL[rows, :] = att.astype(BF16)
            return (
                gains + jnp.sum(grad * scaled, axis=0, keepdims=True),
                shifts + jnp.sum(grad, axis=0, keepdims=True),
            )

        zero = jnp.zeros((1, 768), F32)
        gains, shifts = row_chunks(chunk, (zero, zero))
        NV[0:1, :] = gains
        NV[2:3, :] = shifts

    def attn_backward(r):
        GM[...] = mm_nt(FDL[...], out_rows(W.at[ATT, z_of[r]])).astype(BF16)

        def segment(s, carry):
            rows = pl.ds(pl.multiple_of(s * SEG, SEG), SEG)
            qkv = QKV[r, rows, :]
            gm = GM[rows, :]
            gqs, gks, gvs = [], [], []
            for h in range(3):
                q = qkv[:, h * 64 : h * 64 + 64]
                key = qkv[:, 192 + h * 64 : 256 + h * 64]
                val = qkv[:, 384 + h * 64 : 448 + h * 64]
                gmh = gm[:, h * 64 : h * 64 + 64]
                prob = PR[r, h, rows, :]
                gp = mm_nt(gmh, val)
                inner = jnp.sum(gp * prob, axis=-1, keepdims=True)
                gs = (prob * (gp - inner)).astype(BF16)
                gqs.append(mm(gs, key) * SCALE)
                gks.append(mm_tn(gs, q) * SCALE)
                gvs.append(mm_tn(prob.astype(BF16), gmh))
            GQ[rows, :] = jnp.concatenate(gqs + gks + gvs, axis=-1).astype(BF16)
            return carry

        lax.fori_loop(0, 2, segment, 0)
        store_unit(
            grad_unit(ATT, r),
            [
                (0, 576, lambda: mm(XT[...], GQ[...])),
                (576, 192, lambda: mm(FDLT[...], MIX[r])),
            ],
        )
        sum_start(order.index((ATT, r)))
        accumulate(r == turn[0], mm(GQ[...], qkv_rows(W.at[ATT, z_of[r]])))

    fac = {}

    def factor_start():
        wide = lambda v: v.astype(F32)
        zero_a, zero_b = jnp.zeros((8, 192), F32), jnp.zeros((8, 576), F32)
        att_left = jnp.concatenate([wide(live["xgqkv"]), zero_a], axis=-1)
        att_right = jnp.concatenate([zero_b, wide(live["mix"])], axis=-1)
        right = jnp.concatenate([wide(live["xact"]), wide(live["xgu"]), att_left, att_right], axis=0)
        left = jnp.concatenate(
            [wide(live["xfed_low"]), wide(live["xfirst_low"]), wide(live["summary_low"]), wide(live["xatt_low"])],
            axis=0,
        )
        FAC[y, x, c, 0:32, :] = right.astype(BF16)
        FAC[y, x, c, 32:64, :] = left.astype(BF16)
        part = FAC.at[y, x, c]
        fac[0] = remote(part, part, f_s.at[0], f_r.at[0], x_peer)

    def factor_two():
        fac[0].wait_recv()
        part = FAC.at[y, :, c]
        fac[1] = remote(part, part, f_s.at[1], f_r.at[1], y_peer)

    def factor_three():
        fac[1].wait_recv()
        part = FAC.at[:, :, c]
        fac[2] = remote(part, part, f_s.at[2], f_r.at[2], core_peer)

    def turn_rows(value):
        rows = value.shape[0]
        full = jnp.concatenate([value, jnp.zeros((128 - rows, value.shape[1]), F32)], axis=0)
        return full.T[:, 0:rows]

    def write_unit(layer, k, value):
        if k == ATT:
            for i in range(3):
                qkvg_ref[layer, i] = value[:, i * 192 : i * 192 + 192]
            outg_ref[layer] = turn_rows(value[:, 576:768])
        elif k == UP:
            upg_ref[layer] = value
        else:
            downg_ref[layer] = value

    def factor_final():
        fac[2].wait_recv()
        left = FAC[:, :, :, 32:64, :].reshape(256, 768)
        for i in range(2):
            LT[:, i * 128 : i * 128 + 128] = left[i * 128 : i * 128 + 128, :].T
        mine = LT[pl.ds(pl.multiple_of(dp * BLK, BLK), BLK), :].astype(F32)
        kind = (lax.broadcasted_iota(jnp.int32, (BLK, 256), 1) // 8) % 4
        right = FAC[:, :, :, 0:32, :].reshape(256, 768)
        write_unit(1, DOWN, mm(jnp.where(kind == 0, mine, 0.0).astype(BF16), right))
        write_unit(1, UP, mm(jnp.where(kind == 1, mine, 0.0).astype(BF16), right))
        write_unit(1, ATT, mm(jnp.where(kind >= 2, mine, 0.0).astype(BF16), right))

    vec = {}

    def norm_grads_start():
        exchange(6, NV[...])

    def norm_grads_two():
        total = jnp.where(row_of < 4, exchange_sum(6), NV[...])
        pad = jnp.zeros((8, 32), F32)
        for p in range(8):
            SV[p // 4, (p // 2) % 2, p % 2] = jnp.concatenate([total[:, p * BLK : p * BLK + BLK], pad], axis=-1)
        for m in range(1, 8):
            ty = y if m // 4 == 0 else ny
            tx = x if (m // 2) % 2 == 0 else nx
            tc = c if m % 2 == 0 else nc
            vec[m] = remote(
                SV.at[ty, tx, tc], RSV.at[m - 1], v_s.at[m - 1], v_r.at[m - 1], (plane_index(m), z)
            )

    def norm_grads_final():
        total = SV[y, x, c]
        for m in range(1, 8):
            vec[m].wait_recv()
            total = total + RSV[m - 1]
        gaing_ref[...] = total[0:2, 0:BLK]
        shiftg_ref[...] = total[2:4, 0:BLK]
        crossg_ref[0] = total[4:6, 0:BLK]
        crossg_ref[1] = total[6:8, 0:BLK]

    def turn_to_attention():
        norm_one_back()
        norm_grads_start()
        transpose_into(FDLT, FDL)
        for table in (a1, b1, a2, b2, cc):
            for i in range(9):
                table[i].wait_send()
                waited.append(id(table[i]))
        for condition, copy in passed:

            @pl.when(condition)
            def _(copy=copy):
                copy.wait_send()

    for name in ("wqk", "wv", "wo"):
        loads[name].wait()
    z_own(ATT)
    z_own(UP)
    loads["x"].wait()
    token_one()
    attn_forward(0)
    gather_a(0)
    transpose_into(XT, XA, z * 256)
    gather_a(1)
    gather_b(0)
    token_two()
    gather_a(2)
    gather_b(1)
    z_own(DOWN)
    gather_c(0)
    cross_one()
    gather_b(2)
    attn_forward(1)
    gather_c(1)
    gather_a(3)
    gather_a(4)
    gather_a(5)
    cross_two()
    gather_c(2)
    gather_b(3)
    attn_forward(2)
    gather_b(4)
    gather_b(5)
    gather_a(6)
    gather_a(7)
    cross_three()
    gather_c(3)
    attn_forward(3)
    gather_c(4)
    gather_a(8)
    cross_four()
    gather_c(5)
    norm_one()
    ffn_forward(0)
    gather_b(6)
    ffn_down(0)
    gather_b(7)
    cross_five()
    ffn_forward(1)
    gather_b(8)
    factor_start()
    ffn_down(1)
    ffn_forward(2)
    transpose_into(FLT, FL)
    gather_c(6)
    ffn_forward(3)
    gather_c(7)
    ffn_down(2)
    gather_c(8)
    ffn_down(3)
    factor_two()
    norm_two()
    output_rows()
    loads["cot"].wait()
    norm_two_back()
    transpose_into(FDLT, FDL)
    ffn_back_one(3)
    grad_down(3)
    grad_up(3)
    ffn_back_two(3)
    ffn_back_one(2)
    sum_one(0)
    grad_down(2)
    sum_one(1)
    grad_up(2)
    ffn_back_two(2)
    ffn_back_one(1)
    sum_one(2)
    grad_down(1)
    sum_one(3)
    grad_up(1)
    sum_two(0)
    sum_z(0)
    ffn_back_two(1)
    sum_one(4)
    ffn_back_one(0)
    sum_one(5)
    grad_down(0)
    grad_up(0)
    sum_two(1)
    sum_z(1)
    ffn_back_two(0)
    turn_to_attention()
    sum_one(6)
    sum_one(7)
    sum_two(2)
    attn_backward(3)
    sum_two(3)
    sum_z(2)
    attn_backward(2)
    sum_two(4)
    sum_z(4)
    sum_one(8)
    attn_backward(1)
    sum_two(5)
    sum_z(3)
    sum_z(5)
    attn_backward(0)
    sum_two(6)
    factor_three()
    ing_ref[0] = (GF[...] + ACC[...]).astype(BF16)
    norm_grads_two()
    sum_two(7)
    sum_one(9)
    factor_final()
    sum_two(8)
    sum_z(6)
    sum_one(10)
    sum_two(9)
    sum_one(11)
    sum_three(8)
    sum_z(8)
    write_unit(0, DOWN, sum_final(DOWN))
    sum_two(10)
    sum_three(9)
    sum_z(9)
    sum_z(7)
    sum_two(11)
    sum_three(10)
    sum_z(10)
    write_unit(0, UP, sum_final(UP))
    sum_three(11)
    sum_z(11)
    norm_grads_final()
    write_unit(0, ATT, sum_final(ATT))
    for copy in sends:
        if id(copy) not in waited:
            copy.wait_send()


def settle_kernel(*refs):
    sources, targets, held, sems = refs[:9], refs[9:18], refs[18:27], refs[27]
    arrive = [pltpu.make_async_copy(sources[i], held[i], sems.at[0, i]) for i in range(9)]
    leave = [pltpu.make_async_copy(held[i], targets[i], sems.at[1, i]) for i in range(9)]
    for copy in arrive:
        copy.start()
    for i in range(9):
        arrive[i].wait()
        leave[i].start()
    for copy in leave:
        copy.wait()


def fused_body(
    inputs, doc_ids, qkv_weight, out_weight, up_weight, down_weight, norm_gain, norm_shift, cotangent
):
    wq = qkv_weight.swapaxes(2, 3).reshape(2, 3, 2, BLK, 768)
    wo = out_weight.reshape(2, 2, BLK, 768)
    wu = up_weight.reshape(2, 2, 2, 2, BLK, 768)
    wd = down_weight.reshape(2, 2, 2, 2, BLK, 768)
    whole = pl.BlockSpec(memory_space=pl.ANY)
    vmem = pl.BlockSpec(memory_space=pltpu.VMEM)
    blocks = (2, 2, 2, BLK, 768)
    sem = pltpu.SemaphoreType.DMA
    results = pl.pallas_call(
        fused_kernel,
        out_shape=(
            jax.ShapeDtypeStruct((1, 256, 768), BF16),
            jax.ShapeDtypeStruct((1, 256, 768), BF16),
            jax.ShapeDtypeStruct((2, 3, BLK, 192), F32),
            jax.ShapeDtypeStruct((2, 192, BLK), F32),
            jax.ShapeDtypeStruct((2, BLK, 768), F32),
            jax.ShapeDtypeStruct((2, BLK, 768), F32),
            jax.ShapeDtypeStruct((2, BLK), F32),
            jax.ShapeDtypeStruct((2, BLK), F32),
            jax.ShapeDtypeStruct((2, 2, BLK), F32),
        ),
        in_specs=[whole, whole, whole, vmem, whole, whole, whole, whole, vmem, vmem],
        out_specs=(vmem,) * 9,
        scratch_shapes=[
            pltpu.VMEM((3, 4) + blocks, BF16),
            pltpu.VMEM((2, 4) + blocks, BF16),
            pltpu.VMEM((12, 2, 2, BLK, 768), BF16),
            pltpu.VMEM((12, 2, HALF, 768), BF16),
            pltpu.VMEM((12, 2, HALF, 768), BF16),
            pltpu.VMEM((4, HALF, 768), BF16),
            pltpu.VMEM((4, HALF, 768), BF16),
            pltpu.VMEM((3, BLK, 768), BF16),
            pltpu.VMEM((2, 3, 2, 2, HALF, 768), BF16),
            pltpu.VMEM((2, 2, HALF, 768), BF16),
            pltpu.VMEM((3,) + blocks, BF16),
            pltpu.VMEM((1024, 768), BF16),
            pltpu.VMEM((256, 768), BF16),
            pltpu.VMEM((4, 256, 576), BF16),
            pltpu.VMEM((4, 3, 256, 128), F32),
            pltpu.VMEM((4, 256, 192), BF16),
            pltpu.VMEM((4, 256, 768), BF16),
            pltpu.VMEM((4, 256, 768), BF16),
            pltpu.VMEM((256, 768), BF16),
            pltpu.VMEM((256, 576), BF16),
            pltpu.VMEM((256, 768), F32),
            pltpu.VMEM((256, 768), F32),
            pltpu.VMEM((256, 768), F32),
            pltpu.VMEM((256, 768), F32),
            pltpu.VMEM((256, 768), BF16),
            pltpu.VMEM((768, 256), BF16),
            pltpu.VMEM((256, 768), BF16),
            pltpu.VMEM((768, 256), BF16),
            pltpu.VMEM((768, 256), BF16),
            pltpu.VMEM((256, 192), BF16),
            pltpu.VMEM((8, 16, 768), BF16),
            pltpu.VMEM((256, 128), F32),
            pltpu.VMEM((256, 128), F32),
            pltpu.VMEM((2, 2, 2, 64, 768), BF16),
            pltpu.VMEM((768, 256), BF16),
            pltpu.VMEM((2, 8, 768), F32),
            pltpu.VMEM((7, 4, 8, 768), F32),
            pltpu.VMEM((8, 768), F32),
            pltpu.VMEM((2, 2, 2, 8, 128), F32),
            pltpu.VMEM((7, 8, 128), F32),
            sem((13,)),
            sem((12, 2)),
            sem((12,)),
            sem((5, 9)),
            sem((5, 9)),
            sem((9, 12)),
            sem((9, 12)),
            sem((7, 3)),
            sem((7, 3)),
            sem((3,)),
            sem((3,)),
            sem((7,)),
            sem((7,)),
        ],
        compiler_params=pltpu.CompilerParams(
            collective_id=0, has_side_effects=True, vmem_limit_bytes=63 * 2**20
        ),
    )(
        inputs, cotangent, cotangent.reshape(8, SEG, 768), doc_ids, wq, wo, wu, wd, norm_gain, norm_shift
    )
    final = pl.pallas_call(
        settle_kernel,
        out_shape=tuple(jax.ShapeDtypeStruct(v.shape, v.dtype) for v in results),
        in_specs=[whole] * 9,
        out_specs=(whole,) * 9,
        scratch_shapes=[pltpu.VMEM(v.shape, v.dtype) for v in results] + [sem((2, 9))],
    )(*results)
    return final[:5] + (final[5].swapaxes(1, 2),) + final[6:]


def solution(mesh):
    in_specs = (
        P("dp", None, None),
        P("dp", None),
        P(None, None, None, "tensor"),
        P(None, "tensor", None),
        P(None, None, "tensor"),
        P(None, "tensor", None),
        P(),
        P(),
        P("dp", None, None),
    )
    out_specs = (
        P("dp", "tensor", None),
        P("dp", "tensor", None),
        P(None, None, "dp", "tensor"),
        P(None, "tensor", "dp"),
        P(None, "dp", "tensor"),
        P(None, "tensor", "dp"),
        P(None, "dp"),
        P(None, "dp"),
        P(None, None, "dp"),
    )
    fits = dict(mesh.shape) == {"dp": 8, "tensor": 4}
    chosen = fused_body if fits else body
    return jax.shard_map(chosen, mesh=mesh, in_specs=in_specs, out_specs=out_specs, check_vma=False)
```

```python
from functools import partial
import math

import jax
import jax.numpy as jnp
from jax import lax
from jax.experimental import pallas as pl
from jax.experimental.pallas import tpu as pltpu
from jax.sharding import PartitionSpec as P

HEAD_DIM = 64
SEG = 128


EPSILON = 1e-05
MASK_FILL = -1000000000.0


def layer_norm(values, gain_row, shift_row):
    center = jnp.mean(values, axis=-1, keepdims=True)
    offset = values - center
    spread = jnp.mean(offset * offset, axis=-1, keepdims=True)
    inverse = lax.rsqrt(spread + EPSILON)
    scaled = offset * inverse
    return (scaled * gain_row + shift_row, (scaled, inverse))


def norm_back(grad_out, saved, gain_row):
    scaled, inverse = saved
    weighted = grad_out * gain_row
    mean_one = jnp.mean(weighted, axis=-1, keepdims=True)
    mean_two = jnp.mean(weighted * scaled, axis=-1, keepdims=True)
    grad_in = inverse * (weighted - mean_one - scaled * mean_two)
    return (grad_in, jnp.sum(grad_out * scaled, axis=(0, 1)), jnp.sum(grad_out, axis=(0, 1)))


def score_block(head_split, allowed):
    scores = jnp.einsum(
        "bqhe,bkhe->bhqk", head_split[0], head_split[1], preferred_element_type=jnp.float32
    ) * (1.0 / math.sqrt(HEAD_DIM))
    if allowed is not None:
        scores = jnp.where(allowed, scores, MASK_FILL)
    return scores


def attend_forward(rows_low, qkv_local, allowed):
    batch_count = rows_low.shape[0]
    length = rows_low.shape[1]
    project = jnp.einsum(
        "brd,cde->cbre", rows_low, qkv_local, preferred_element_type=jnp.float32
    ).astype(jnp.bfloat16)
    head_split = project.reshape(3, batch_count, length, -1, HEAD_DIM)
    scores = score_block(head_split, allowed)
    log_total = jax.nn.logsumexp(scores, axis=-1)
    soft_low = jnp.exp(scores - log_total[..., None]).astype(jnp.bfloat16)
    mixture = jnp.einsum(
        "bhqk,bkhe->bqhe", soft_low, head_split[2], preferred_element_type=jnp.float32
    )
    return (project, log_total, mixture.astype(jnp.bfloat16).reshape(batch_count, length, -1))


def attend_backward(rows_low, qkv_local, out_local, project, log_total, mixture, grad_low, allowed):
    batch_count = rows_low.shape[0]
    length = rows_low.shape[1]
    head_split = project.reshape(3, batch_count, length, -1, HEAD_DIM)
    grad_mixture = jnp.einsum(
        "brd,fd->brf", grad_low, out_local, preferred_element_type=jnp.float32
    ).astype(jnp.bfloat16)
    out_local_grad = jnp.einsum(
        "brf,brd->fd", mixture, grad_low, preferred_element_type=jnp.float32
    )
    grad_heads = grad_mixture.reshape(batch_count, length, -1, HEAD_DIM)
    scores = score_block(head_split, allowed)
    soft_full = jnp.exp(scores - log_total[..., None])
    grad_soft = jnp.einsum(
        "bqhe,bkhe->bhqk", grad_heads, head_split[2], preferred_element_type=jnp.float32
    )
    row_inner = jnp.sum(grad_soft * soft_full, axis=-1, keepdims=True)
    grad_scores = (soft_full * (grad_soft - row_inner)).astype(jnp.bfloat16)
    scale_factor = 1.0 / math.sqrt(HEAD_DIM)
    grad_query = (
        jnp.einsum(
            "bhqk,bkhe->bqhe", grad_scores, head_split[1], preferred_element_type=jnp.float32
        )
        * scale_factor
    )
    grad_key = (
        jnp.einsum(
            "bhqk,bqhe->bkhe", grad_scores, head_split[0], preferred_element_type=jnp.float32
        )
        * scale_factor
    )
    grad_value = jnp.einsum(
        "bhqk,bqhe->bkhe",
        soft_full.astype(jnp.bfloat16),
        grad_heads,
        preferred_element_type=jnp.float32,
    )
    grad_project = (
        jnp.stack([grad_query, grad_key, grad_value])
        .reshape(3, batch_count, length, -1)
        .astype(jnp.bfloat16)
    )
    qkv_local_grad = jnp.einsum(
        "brd,cbre->cde", rows_low, grad_project, preferred_element_type=jnp.float32
    )
    input_part = jnp.einsum(
        "cbre,cde->brd", grad_project, qkv_local, preferred_element_type=jnp.float32
    )
    return (input_part, qkv_local_grad, out_local_grad)


def expand_forward(rows_low, up_local, down_local):
    upward = jnp.einsum("brd,df->brf", rows_low, up_local, preferred_element_type=jnp.float32)
    active = jax.nn.gelu(upward, approximate=False).astype(jnp.bfloat16)
    return (
        upward,
        active,
        jnp.einsum("brf,fd->brd", active, down_local, preferred_element_type=jnp.float32),
    )


def expand_backward(rows_low, up_local, down_local, upward, active, grad_low):
    grad_active = jnp.einsum(
        "brd,fd->brf", grad_low, down_local, preferred_element_type=jnp.float32
    )
    down_local_grad = jnp.einsum(
        "brf,brd->fd", active, grad_low, preferred_element_type=jnp.float32
    )
    gelu_pull = jax.vjp(partial(jax.nn.gelu, approximate=False), upward)[1]
    grad_upward = gelu_pull(grad_active)[0].astype(jnp.bfloat16)
    up_local_grad = jnp.einsum(
        "brd,brf->df", rows_low, grad_upward, preferred_element_type=jnp.float32
    )
    input_part = jnp.einsum(
        "brf,df->brd", grad_upward, up_local, preferred_element_type=jnp.float32
    )
    return (input_part, up_local_grad, down_local_grad)


def body(
    inputs,
    doc_ids,
    qkv_weight,
    out_weight,
    up_weight,
    down_weight,
    norm_gain,
    norm_shift,
    cotangent,
):
    groups = lax.axis_size("tensor")
    position = lax.axis_index("tensor")
    model_width = inputs.shape[2]
    segment_count = inputs.shape[1] // SEG
    own_count = segment_count // groups
    row_start = position * own_count

    def final_rows(values):
        return lax.dynamic_slice_in_dim(values, row_start, own_count, 0)

    def forward_sum(partial_term):
        return lax.psum(partial_term.astype(jnp.bfloat16), "tensor").astype(jnp.float32)

    def backward_sum(partial_term):
        return lax.psum(partial_term.astype(jnp.bfloat16), "tensor").astype(jnp.float32)

    def cross_sum(partial_term):
        return lax.psum(partial_term.astype(jnp.bfloat16), "tensor").astype(jnp.float32)

    def cross_grad_sum(partial_term):
        return lax.psum(partial_term, "tensor")

    tokens = inputs[0].reshape(segment_count, SEG, model_width)
    tokens_wide = tokens.astype(jnp.float32)
    lower_proj, lower_total, lower_mix = attend_forward(tokens, qkv_weight[0], None)
    attended = forward_sum(
        jnp.einsum("brf,fd->brd", lower_mix, out_weight[0], preferred_element_type=jnp.float32)
    )
    first_norm, first_saved = layer_norm(tokens_wide + attended, norm_gain[0, 0], norm_shift[0, 0])
    first_low = first_norm.astype(jnp.bfloat16)
    lower_up, lower_active, fed_term = expand_forward(first_low, up_weight[0], down_weight[0])
    second, second_saved = layer_norm(
        first_norm + forward_sum(fed_term), norm_gain[0, 1], norm_shift[0, 1]
    )
    summary = second[:, 0, :]
    summary = summary[None]
    same_doc = (doc_ids[0][:, None] == doc_ids[0][None, :])[None, None]
    summary_low = summary.astype(jnp.bfloat16)
    upper_proj, upper_total, upper_mix = attend_forward(summary_low, qkv_weight[1], same_doc)
    upper_att = cross_sum(
        jnp.einsum("brf,fd->brd", upper_mix, out_weight[1], preferred_element_type=jnp.float32)
    )
    upper_first, upper_saved_one = layer_norm(
        summary + upper_att, norm_gain[1, 0], norm_shift[1, 0]
    )
    upper_first_low = upper_first.astype(jnp.bfloat16)
    upper_up, upper_active, upper_fed = expand_forward(
        upper_first_low, up_weight[1], down_weight[1]
    )
    upper_out, upper_saved_two = layer_norm(
        upper_first + cross_sum(upper_fed), norm_gain[1, 1], norm_shift[1, 1]
    )
    joined = second.at[:, 0, :].set(upper_out[0])
    outputs_own = final_rows(joined).reshape(1, -1, model_width).astype(jnp.bfloat16)
    grad_full = cotangent[0].reshape(segment_count, SEG, model_width).astype(jnp.float32)
    grad_top = grad_full[:, 0, :][None]
    grad_upper_fed, gain_cross_two, shift_cross_two = norm_back(
        grad_top, upper_saved_two, norm_gain[1, 1]
    )
    cross_part, up_cross, down_cross = expand_backward(
        upper_first_low,
        up_weight[1],
        down_weight[1],
        upper_up,
        upper_active,
        grad_upper_fed.astype(jnp.bfloat16),
    )
    grad_upper_first = grad_upper_fed + cross_grad_sum(cross_part)
    grad_upper_att, gain_cross_one, shift_cross_one = norm_back(
        grad_upper_first, upper_saved_one, norm_gain[1, 0]
    )
    cross_input_part, qkv_cross, out_cross = attend_backward(
        summary_low,
        qkv_weight[1],
        out_weight[1],
        upper_proj,
        upper_total,
        upper_mix,
        grad_upper_att.astype(jnp.bfloat16),
        same_doc,
    )
    grad_summary = grad_upper_att + cross_grad_sum(cross_input_part)
    grad_second = grad_full.at[:, 0, :].set(grad_summary[0])
    grad_fed, gain_seg_two, shift_seg_two = norm_back(grad_second, second_saved, norm_gain[0, 1])
    fed_low = grad_fed.astype(jnp.bfloat16)
    seg_part, up_seg, down_seg = expand_backward(
        first_low, up_weight[0], down_weight[0], lower_up, lower_active, fed_low
    )
    grad_first = grad_fed + backward_sum(seg_part)
    grad_att, gain_seg_one, shift_seg_one = norm_back(grad_first, first_saved, norm_gain[0, 0])
    att_low = grad_att.astype(jnp.bfloat16)
    seg_input_part, qkv_seg, out_seg = attend_backward(
        tokens, qkv_weight[0], out_weight[0], lower_proj, lower_total, lower_mix, att_low, None
    )
    input_full = grad_att + backward_sum(seg_input_part)
    input_own = final_rows(input_full).reshape(1, -1, model_width).astype(jnp.bfloat16)
    seg_gain = jnp.stack([gain_seg_one, gain_seg_two])
    seg_shift = jnp.stack([shift_seg_one, shift_seg_two])
    cross_norm = jnp.stack(
        [jnp.stack([gain_cross_one, gain_cross_two]), jnp.stack([shift_cross_one, shift_cross_two])]
    )
    qkv_all = jnp.stack([qkv_seg, qkv_cross])
    out_all = jnp.stack([out_seg, out_cross])
    up_all = jnp.stack([up_seg, up_cross])
    down_all = jnp.stack([down_seg, down_cross])
    summed = (
        lax.psum_scatter(qkv_all, "dp", scatter_dimension=2, tiled=True),
        lax.psum_scatter(out_all, "dp", scatter_dimension=2, tiled=True),
        lax.psum_scatter(up_all, "dp", scatter_dimension=1, tiled=True),
        lax.psum_scatter(down_all, "dp", scatter_dimension=2, tiled=True),
        lax.psum_scatter(seg_gain, "dp", scatter_dimension=1, tiled=True),
        lax.psum_scatter(seg_shift, "dp", scatter_dimension=1, tiled=True),
        lax.psum_scatter(cross_norm, "dp", scatter_dimension=2, tiled=True),
    )
    return (
        outputs_own,
        input_own,
        summed[0],
        summed[1],
        summed[2],
        summed[3],
        summed[4],
        summed[5],
        summed[6],
    )


MESH = pl.DeviceIdType.MESH
F32 = jnp.float32
BF16 = jnp.bfloat16
SCALE = 1.0 / math.sqrt(HEAD_DIM)
ATT, UP, DOWN = 0, 1, 2
BLK = 96
HALF = 48


def mm(a, b):
    return lax.dot_general(a, b, (((1,), (0,)), ((), ())), preferred_element_type=F32)


def mm_nt(a, b):
    return lax.dot_general(a, b, (((1,), (1,)), ((), ())), preferred_element_type=F32)


def mm_tn(a, b):
    return lax.dot_general(a, b, (((0,), (0,)), ((), ())), preferred_element_type=F32)


def normalize(values):
    center = jnp.mean(values, axis=-1, keepdims=True)
    offset = values - center
    spread = jnp.mean(offset * offset, axis=-1, keepdims=True)
    inverse = lax.rsqrt(spread + EPSILON)
    return offset * inverse, inverse


def normalize_back(grad_out, scaled, inverse, gain_row):
    weighted = grad_out * gain_row
    mean_one = jnp.mean(weighted, axis=-1, keepdims=True)
    mean_two = jnp.mean(weighted * scaled, axis=-1, keepdims=True)
    return inverse * (weighted - mean_one - scaled * mean_two)


def gelu_pair(upward):
    cdf = 0.5 * (1.0 + lax.erf(upward * math.sqrt(0.5)))
    pdf = jnp.exp(upward * upward * -0.5) * (1.0 / math.sqrt(2.0 * math.pi))
    return upward * cdf, cdf + upward * pdf


def fused_kernel(
    tokens_hbm, cot_hbm, cot_seg, doc_ref, wq_hbm, wo_hbm, wu_hbm, wd_hbm, gain_ref, shift_ref,
    out_ref, ing_ref, qkvg_ref, outg_ref, upg_ref, downg_ref, gaing_ref, shiftg_ref, crossg_ref,
    W, G, RC, RA1, RB1, RA2, RB2, RZ, RZF, RF, L1, XA, COT, QKV, PR, MIX, ACT, DG, GU, GQ, ACC, SC1, SC2, GF,
    FL, FLT, FDL, FDLT, XT, GM, C8, INV1, INV2, FAC, LT, GS, E, NV, SV, RSV,
    sem_local, zg_s, zg_r, ag_s, ag_r, rs_s, rs_r, e_s, e_r, f_s, f_r, v_s, v_r,
):
    dp = lax.axis_index("dp")
    z = lax.axis_index("tensor")
    c = dp % 2
    x = (dp // 2) % 2
    y = dp // 4
    nc, nx, ny = 1 - c, 1 - x, 1 - y
    core_peer = (dp + 1 - 2 * c, z)
    x_peer = (dp + 2 - 4 * x, z)
    y_peer = (dp + 4 - 8 * y, z)
    left_peer, right_peer = (dp, jnp.maximum(z - 1, 0)), (dp, jnp.minimum(z + 1, 3))
    z_peer = [None, (dp, z + 1 - 2 * (z % 2)), (dp, z + 2 - 4 * (z // 2)), (dp, 3 - z)]
    z_of = [z, z + 1 - 2 * (z % 2), z + 2 - 4 * (z // 2), 3 - z]

    def plane_index(m):
        ty = y if m // 4 == 0 else ny
        tx = x if (m // 2) % 2 == 0 else nx
        tc = c if m % 2 == 0 else nc
        return ty * 4 + tx * 2 + tc

    sends = []
    waited = []

    def remote(src, dst, ssem, rsem, target):
        copy = pltpu.make_async_remote_copy(
            src_ref=src, dst_ref=dst, send_sem=ssem, recv_sem=rsem, device_id=target, device_id_type=MESH
        )
        copy.start()
        sends.append(copy)
        return copy

    loads = {}

    def load(name, index, src, dst):
        copy = pltpu.make_async_copy(src, dst, sem_local.at[index])
        copy.start()
        loads[name] = copy

    load("x", 0, tokens_hbm.at[0], XA)
    load("wqk", 1, wq_hbm.at[0, pl.ds(0, 2)], W.at[ATT, z, 0])
    load("wv", 9, wq_hbm.at[0, 2], W.at[ATT, z, 1, 0])
    load("wo", 10, wo_hbm.at[0], W.at[ATT, z, 1, 1])
    load("wu", 2, wu_hbm.at[0], W.at[UP, z])
    load("wd", 3, wd_hbm.at[0], W.at[DOWN, z])
    load("cot", 4, cot_hbm.at[0, pl.ds(pl.multiple_of(z * 256, 256), 256)], COT)
    load("l1qk", 5, wq_hbm.at[1, pl.ds(0, 2)], L1.at[ATT, 0])
    load("l1v", 11, wq_hbm.at[1, 2], L1.at[ATT, 1, 0])
    load("l1o", 12, wo_hbm.at[1], L1.at[ATT, 1, 1])
    load("l1u", 6, wu_hbm.at[1], L1.at[UP])
    load("l1d", 7, wd_hbm.at[1], L1.at[DOWN])
    load("c8", 8, cot_seg.at[:, pl.ds(0, 16)], C8)

    barrier = pltpu.get_barrier_semaphore()
    for m in range(1, 8):
        pl.semaphore_signal(barrier, inc=1, device_id=(plane_index(m), z), device_id_type=MESH)
    for r in range(1, 4):
        pl.semaphore_signal(barrier, inc=1, device_id=z_peer[r], device_id_type=MESH)
    pl.semaphore_wait(barrier, 10)

    own_unit = [W.at[ATT, z], wu_hbm.at[0], wd_hbm.at[0]]
    units = [(ATT, 1), (UP, 1), (ATT, 2), (ATT, 3), (DOWN, 1), (UP, 2), (UP, 3), (DOWN, 2), (DOWN, 3)]
    a1, b1, a2, b2, a3, b3, cc = {}, {}, {}, {}, {}, {}, {}
    passed = []

    def z_copy(src, k, shard, side):
        return pltpu.make_async_remote_copy(
            src_ref=src,
            dst_ref=W.at[k, shard, y, x, c],
            send_sem=zg_s.at[k * 4 + shard, side],
            recv_sem=zg_r.at[k * 4 + shard],
            device_id=(left_peer, right_peer)[side],
            device_id_type=MESH,
        )

    def pass_on(condition, copy):
        @pl.when(condition)
        def _():
            copy.start()

        passed.append((condition, copy))

    def z_own(k):
        src = own_unit[k].at[y, x, c]
        pass_on(z > 0, z_copy(src, k, z, 0))
        pass_on(z < 3, z_copy(src, k, z, 1))

    def z_step(k, step):
        for side in range(2):
            shard = z - 1 - step if side else z + 1 + step
            there = shard >= 0 if side else shard <= 3
            further = jnp.logical_and(there, z < 3 if side else z > 0)
            shard = jnp.clip(shard, 0, 3)
            copy = z_copy(W.at[k, shard, y, x, c], k, shard, side)

            @pl.when(there)
            def _():
                copy.wait_recv()

            pass_on(further, copy)

    def gather_a(i):
        k, r = units[i]
        z_step(k, r - 1)
        upper = W.at[k, z_of[r], y, x, c, pl.ds(0, HALF)]
        lower = W.at[k, z_of[r], y, x, c, pl.ds(HALF, HALF)]
        a1[i] = remote(upper, upper, ag_s.at[0, i], ag_r.at[0, i], x_peer)
        b1[i] = remote(lower, lower, ag_s.at[1, i], ag_r.at[1, i], y_peer)
        a2[i] = remote(upper, upper, ag_s.at[2, i], ag_r.at[2, i], y_peer)
        b2[i] = remote(lower, lower, ag_s.at[3, i], ag_r.at[3, i], x_peer)

    def gather_b(i):
        k, r = units[i]
        a1[i].wait_recv()
        part = W.at[k, z_of[r], y, nx, c, pl.ds(0, HALF)]
        a3[i] = remote(part, part, ag_s.at[4, i], ag_r.at[4, i], y_peer)
        b1[i].wait_recv()
        part = W.at[k, z_of[r], ny, x, c, pl.ds(HALF, HALF)]
        b3[i] = remote(part, part, ag_s.at[5, i], ag_r.at[5, i], x_peer)

    def gather_c(i):
        k, r = units[i]
        for table in (a2, b2, a3, b3):
            table[i].wait_recv()
        part = W.at[k, z_of[r], :, :, c]
        cc[i] = remote(part, part, ag_s.at[6, i], ag_r.at[6, i], core_peer)

    def arrived(k, r):
        if r:
            cc[units.index((k, r))].wait_recv()

    def unit_value(ref):
        return ref[...].reshape(768, ref.shape[-1])

    def cols(k, r, start, size):
        return unit_value(W.at[k, z_of[r], :, :, :, :, pl.ds(start, size)])

    def qkv_rows(ref):
        return jnp.concatenate([ref[0].reshape(384, 768), ref[1, 0].reshape(192, 768)], axis=0)

    def out_rows(ref):
        return ref[1, 1].reshape(192, 768)

    def accumulate(first, value):
        if first:
            ACC[...] = value
        else:
            ACC[...] += value

    def attn_forward(r):
        arrived(ATT, r)
        QKV[r] = mm_nt(XA[own_rows, :], qkv_rows(W.at[ATT, z_of[r]])).astype(BF16)

        def segment(s, carry):
            rows = pl.ds(pl.multiple_of(s * SEG, SEG), SEG)
            qkv = QKV[r, rows, :]
            mixes = []
            for h in range(3):
                q = qkv[:, h * 64 : h * 64 + 64]
                key = qkv[:, 192 + h * 64 : 256 + h * 64]
                val = qkv[:, 384 + h * 64 : 448 + h * 64]
                scores = mm_nt(q, key) * SCALE
                top = jnp.max(scores, axis=-1, keepdims=True)
                expd = jnp.exp(scores - top)
                prob = expd * (1.0 / jnp.sum(expd, axis=-1, keepdims=True))
                PR[r, h, rows, :] = prob
                mixes.append(mm(prob.astype(BF16), val))
            MIX[r, rows, :] = jnp.concatenate(mixes, axis=-1).astype(BF16)
            return carry

        lax.fori_loop(0, 2, segment, 0)
        accumulate(r == 0, mm(MIX[r], out_rows(W.at[ATT, z_of[r]])))

    own_rows = pl.ds(pl.multiple_of(z * 256, 256), 256)

    def row_chunks(body, init=0):
        def one(i, carry):
            return body(i, pl.ds(pl.multiple_of(i * 64, 64), 64), carry)

        return lax.fori_loop(0, 4, one, init)

    g00, g01 = gain_ref[0, 0:1, :], gain_ref[0, 1:2, :]
    b00, b01 = shift_ref[0, 0:1, :], shift_ref[0, 1:2, :]
    g10, g11 = gain_ref[1, 0:1, :], gain_ref[1, 1:2, :]
    b10, b11 = shift_ref[1, 0:1, :], shift_ref[1, 1:2, :]

    def norm_one():
        def chunk(i, rows, carry):
            mine = XA[pl.ds(pl.multiple_of(z * 256 + i * 64, 64), 64), :]
            scaled, inverse = normalize(mine.astype(F32) + ACC[rows, :])
            SC1[rows, :] = scaled
            INV1[rows, :] = jnp.broadcast_to(inverse, (64, 128))
            FL[rows, :] = (scaled * g00 + b00).astype(BF16)
            return carry

        row_chunks(chunk)

    def ffn_forward(r):
        arrived(UP, r)
        def block(n, carry):
            part = pl.ds(pl.multiple_of(n * 256, 256), 256)
            upward = mm(FL[...], unit_value(W.at[UP, z_of[r], :, :, :, :, part]))
            active, slope = gelu_pair(upward)
            ACT[r, :, part] = active.astype(BF16)
            DG[r, :, part] = slope.astype(DG.dtype)
            return carry

        lax.fori_loop(0, 3, block, 0)

    def ffn_down(r):
        arrived(DOWN, r)
        accumulate(r == 0, mm(ACT[r], cols(DOWN, r, 0, 768)))

    def norm_two():
        def chunk(i, rows, carry):
            first = SC1[rows, :] * g00 + b00
            scaled, inverse = normalize(first + ACC[rows, :])
            SC2[rows, :] = scaled
            INV2[rows, :] = jnp.broadcast_to(inverse, (64, 128))
            out_ref[0, rows, :] = (scaled * g01 + b01).astype(BF16)
            return carry

        row_chunks(chunk)

    def transpose_into(dst, src, start=0):
        for i in range(2):
            dst[:, i * 128 : i * 128 + 128] = src[pl.ds(pl.multiple_of(start + i * 128, 128), 128), :].T

    exch = {}

    def exchange(e, value):
        E[e, 0] = value
        for r in range(1, 4):
            exch[e, r] = remote(E.at[e, 0], E.at[e, r], e_s.at[e, r - 1], e_r.at[e, r - 1], z_peer[r])

    def exchange_wait(e):
        for r in range(1, 4):
            exch[e, r].wait_recv()

    def exchange_sum(e):
        exchange_wait(e)
        return (E[e, 0] + E[e, 1]) + (E[e, 2] + E[e, 3])

    row_of = lax.broadcasted_iota(jnp.int32, (8, 768), 0)
    pair_of = row_of // 2

    def own_row(value, j):
        return jnp.sum(jnp.where(row_of == 2 * z + j, value, 0.0), axis=0, keepdims=True)


    def norm_two_back():
        def chunk(i, rows, carry):
            gains, shifts = carry
            which = lax.broadcasted_iota(jnp.int32, (64, 768), 0) + i * 64
            grad = jnp.where(which % SEG == 0, GS[i // 2][0:1, :], COT[rows, :].astype(F32))
            scaled = SC2[rows, :]
            fed = normalize_back(grad, scaled, INV2[rows, 0:1], g01)
            GF[rows, :] = fed
            FDL[rows, :] = fed.astype(BF16)
            return (
                gains + jnp.sum(grad * scaled, axis=0, keepdims=True),
                shifts + jnp.sum(grad, axis=0, keepdims=True),
            )

        zero = jnp.zeros((1, 768), F32)
        gains, shifts = row_chunks(chunk, (zero, zero))
        NV[1:2, :] = gains
        NV[3:4, :] = shifts

    def grad_unit(k, r):
        return W.at[UP, r] if k == ATT else G.at[k - 1, r]

    turn = (3, 2, 1, 0)
    order = [(k, r) for r in turn for k in (DOWN, UP)] + [(ATT, r) for r in turn]
    s0, sa1, sb1, sa2, sb2, sza, szb, sfa, sfb = {}, {}, {}, {}, {}, {}, {}, {}, {}

    def sum_start(i):
        k, r = order[i]
        g = grad_unit(k, r)
        s0[i] = remote(g.at[:, :, nc], RC.at[i], rs_s.at[0, i], rs_r.at[0, i], core_peer)

    def add_low(a, b):
        return (a.astype(F32) + b.astype(F32)).astype(BF16)

    top, low = pl.ds(0, HALF), pl.ds(HALF, HALF)

    def sum_one(i):
        k, r = order[i]
        g = grad_unit(k, r)
        s0[i].wait_recv()

        def block(j, carry):
            jy, jx = j // 2, j % 2
            g[jy, jx, c] = add_low(g[jy, jx, c], RC[i, jy, jx])
            return carry

        lax.fori_loop(0, 4, block, 0)
        if k == ATT:
            part_a, part_b = g.at[:, nx, c, top], g.at[ny, :, c, low]
            peer_a, peer_b = x_peer, y_peer
        else:
            part_a, part_b = g.at[ny, :, c, top], g.at[:, nx, c, low]
            peer_a, peer_b = y_peer, x_peer
        sa1[i] = remote(part_a, RA1.at[i], rs_s.at[1, i], rs_r.at[1, i], peer_a)
        sb1[i] = remote(part_b, RB1.at[i], rs_s.at[2, i], rs_r.at[2, i], peer_b)

    def sum_two(i):
        k, r = order[i]
        g = grad_unit(k, r)
        sa1[i].wait_recv()
        if k == ATT:
            for j in range(2):
                g[j, x, c, 0:HALF, :] = add_low(g[j, x, c, 0:HALF, :], RA1[i, j])
            sa2[i] = remote(g.at[ny, x, c, top], RA2.at[i - 8], rs_s.at[3, i], rs_r.at[3, i], y_peer)
            sb1[i].wait_recv()
            for j in range(2):
                g[y, j, c, HALF:BLK, :] = add_low(g[y, j, c, HALF:BLK, :], RB1[i, j])
            sb2[i] = remote(g.at[y, nx, c, low], RB2.at[i - 8], rs_s.at[4, i], rs_r.at[4, i], x_peer)
        else:
            sb1[i].wait_recv()
            for j in range(2):
                g[y, j, c, 0:HALF, :] = add_low(g[y, j, c, 0:HALF, :], RA1[i, j])
                g[j, x, c, HALF:BLK, :] = add_low(g[j, x, c, HALF:BLK, :], RB1[i, j])

    def sum_three(i):
        g = grad_unit(*order[i])
        sa2[i].wait_recv()
        g[y, x, c, 0:HALF, :] = add_low(g[y, x, c, 0:HALF, :], RA2[i - 8])
        sb2[i].wait_recv()
        g[y, x, c, HALF:BLK, :] = add_low(g[y, x, c, HALF:BLK, :], RB2[i - 8])

    landing = {1: 0, 3: 1, 2: 2}

    def z_wait(k, r):
        i = order.index((k, r))
        sza[i].wait_recv()
        if k != ATT:
            szb[i].wait_recv()

    def z_add(k, g, slot):
        if k == ATT:
            g[y, x, c] = add_low(g[y, x, c], RZ[slot])
        else:
            for j in range(2):
                g[y, j, c, 0:HALF, :] = add_low(g[y, j, c, 0:HALF, :], RZF[k - 1, slot, 0, j])
                g[j, x, c, HALF:BLK, :] = add_low(g[j, x, c, HALF:BLK, :], RZF[k - 1, slot, 1, j])

    def sum_z(i):
        k, r = order[i]
        g = grad_unit(k, r)
        if r == 2:
            z_wait(k, 3)
            z_add(k, g, landing[3])
        if r:
            peer = z_peer[2] if r == 2 else z_peer[1]
            if k == ATT:
                sza[i] = remote(g.at[y, x, c], RZ.at[landing[r]], rs_s.at[5, i], rs_r.at[5, i], peer)
            else:
                land = RZF.at[k - 1, landing[r]]
                sza[i] = remote(g.at[y, :, c, top], land.at[0], rs_s.at[5, i], rs_r.at[5, i], peer)
                szb[i] = remote(g.at[:, x, c, low], land.at[1], rs_s.at[6, i], rs_r.at[6, i], peer)
        else:
            z_wait(k, 1)
            z_wait(k, 2)
            if k != ATT:
                for j in range(2):
                    a, b = RZF[k - 1, 0, 0, j].astype(F32), RZF[k - 1, 2, 0, j].astype(F32)
                    g[y, j, c, 0:HALF, :] = add_low(g[y, j, c, 0:HALF, :], a + b)
                    a, b = RZF[k - 1, 0, 1, j].astype(F32), RZF[k - 1, 2, 1, j].astype(F32)
                    g[j, x, c, HALF:BLK, :] = add_low(g[j, x, c, HALF:BLK, :], a + b)
                sfa[k] = remote(g.at[y, nx, c, top], RF.at[k - 1, 0], rs_s.at[7, k], rs_r.at[7, k], x_peer)
                sfb[k] = remote(g.at[ny, x, c, low], RF.at[k - 1, 1], rs_s.at[8, k], rs_r.at[8, k], y_peer)

    def sum_final(k):
        own = grad_unit(k, 0)[y, x, c].astype(F32)
        if k == ATT:
            return own + (RZ[0].astype(F32) + RZ[2].astype(F32))
        sfa[k].wait_recv()
        sfb[k].wait_recv()
        return own + jnp.concatenate([RF[k - 1, 0], RF[k - 1, 1]], axis=0).astype(F32)

    def store_unit(ref, parts):
        for start, size, value in parts:
            ref[:, :, :, :, start : start + size] = value().astype(BF16).reshape(2, 2, 2, BLK, size)

    def store_ffn(k, r, lhs_t, rhs):
        ref = grad_unit(k, r)

        def block(n, carry):
            part = pl.ds(pl.multiple_of(n * 256, 256), 256)
            value = mm(lhs_t[...], rhs[:, part])
            ref[:, :, :, :, part] = value.astype(BF16).reshape(2, 2, 2, BLK, 256)
            return carry

        lax.fori_loop(0, 3, block, 0)

    def ffn_back_one(r):
        ga = mm_nt(FDL[...], cols(DOWN, r, 0, 768))
        GU[...] = (ga * DG[r].astype(F32)).astype(BF16)

    def ffn_back_two(r):
        accumulate(r == turn[0], mm_nt(GU[...], cols(UP, r, 0, 768)))

    def grad_down(r):
        store_ffn(DOWN, r, FDLT, ACT.at[r])
        sum_start(order.index((DOWN, r)))

    def grad_up(r):
        store_ffn(UP, r, FLT, GU)
        sum_start(order.index((UP, r)))

    def l1(k, start, size):
        return unit_value(L1.at[k, :, :, :, :, pl.ds(start, size)])

    live = {}

    def token_one():
        unit = W.at[ATT, z]
        kv_weight = jnp.concatenate([unit[0, 1].reshape(192, 768), unit[1, 0].reshape(192, 768)], axis=0)

        def rows_of(i, carry):
            rows = pl.ds(pl.multiple_of(i * 256, 256), 256)
            ACT[i, :, 0:384] = mm_nt(XA[rows, :], kv_weight).astype(BF16)
            return carry

        lax.fori_loop(0, 4, rows_of, 0)
        x8 = jnp.concatenate([XA[i * SEG : i * SEG + 16, :].astype(F32)[0:1] for i in range(8)], axis=0)
        live["x8"] = x8
        q8 = mm_nt(x8.astype(BF16), unit[0, 0].reshape(192, 768)).astype(BF16).astype(F32)
        row = lax.broadcasted_iota(jnp.int32, (8, 1024), 0)
        keep = lax.broadcasted_iota(jnp.int32, (8, 1024), 1) // SEG == row
        mixes = []
        for h in range(3):
            q = q8[:, h * 64 : h * 64 + 64].astype(BF16)
            parts = [mm_nt(q, ACT[i, :, h * 64 : h * 64 + 64]) for i in range(4)]
            scores = jnp.where(keep, jnp.concatenate(parts, axis=1) * SCALE, -3.0e38)
            top = jnp.max(scores, axis=-1, keepdims=True)
            expd = jnp.exp(scores - top)
            prob = (expd * (1.0 / jnp.sum(expd, axis=-1, keepdims=True))).astype(BF16)
            mix = None
            for i in range(4):
                val = ACT[i, :, 192 + h * 64 : 256 + h * 64]
                part = mm(prob[:, i * 256 : i * 256 + 256], val)
                mix = part if mix is None else mix + part
            mixes.append(mix)
        exchange(0, mm(jnp.concatenate(mixes, axis=-1).astype(BF16), out_rows(unit)))

    def token_two():
        attended = exchange_sum(0)
        scaled, _ = normalize(live["x8"] + attended)
        first = scaled * g00 + b00
        live["first8"] = first
        loads["wu"].wait()
        loads["wd"].wait()
        active, _ = gelu_pair(mm(first.astype(BF16), cols(UP, 0, 0, 768)))
        exchange(1, mm(active.astype(BF16), cols(DOWN, 0, 0, 768)))

    def cross_one():
        fed = exchange_sum(1)
        scaled, _ = normalize(live["first8"] + fed)
        summary = scaled * g01 + b01
        live["summary"] = summary
        live["summary_low"] = summary.astype(BF16)
        for name in ("l1qk", "l1v", "l1o"):
            loads[name].wait()
        qkv = mm_nt(live["summary_low"], qkv_rows(L1.at[ATT])).astype(BF16).astype(F32)
        pad = jnp.zeros((120, 64), F32)
        ids = jnp.broadcast_to(doc_ref[...].astype(F32), (8, 8))
        eye = lax.broadcasted_iota(jnp.int32, (8, 8), 0) == lax.broadcasted_iota(jnp.int32, (8, 8), 1)
        same = ids == jnp.sum(jnp.where(eye, ids, 0.0), axis=1, keepdims=True)
        keep = jnp.concatenate([jnp.where(same, 1.0, 0.0), jnp.zeros((8, 120), F32)], axis=1) > 0.5
        mixes = []
        for h in range(3):
            q = qkv[:, h * 64 : h * 64 + 64].astype(BF16)
            key = jnp.concatenate([qkv[:, 192 + h * 64 : 256 + h * 64], pad], axis=0).astype(BF16)
            val = jnp.concatenate([qkv[:, 384 + h * 64 : 448 + h * 64], pad], axis=0).astype(BF16)
            scores = jnp.where(keep, mm_nt(q, key) * SCALE, MASK_FILL)
            top = jnp.max(scores, axis=-1, keepdims=True)
            expd = jnp.exp(scores - top)
            prob = expd * (1.0 / jnp.sum(expd, axis=-1, keepdims=True))
            live["prob", h], live["q", h], live["key", h], live["val", h] = prob, q, key, val
            mixes.append(mm(prob.astype(BF16), val))
        mix = jnp.concatenate(mixes, axis=-1).astype(BF16)
        live["mix"] = mix
        exchange(2, mm(mix, out_rows(L1.at[ATT])))

    def cross_two():
        attended = exchange_sum(2)
        live["xs1"], live["xi1"] = normalize(live["summary"] + attended)
        first = live["xs1"] * g10 + b10
        live["xfirst"] = first
        live["xfirst_low"] = first.astype(BF16)
        loads["l1u"].wait()
        loads["l1d"].wait()
        active, live["xdg"] = gelu_pair(mm(live["xfirst_low"], l1(UP, 0, 768)))
        live["xact"] = active.astype(BF16)
        exchange(3, mm(live["xact"], l1(DOWN, 0, 768)))

    def cross_three():
        fed = exchange_sum(3)
        xs2, xi2 = normalize(live["xfirst"] + fed)
        upper = xs2 * g11 + b11
        for j in range(2):
            GS[j, 1:2, :] = own_row(upper, j)
        loads["c8"].wait()
        grad_top = C8[...].astype(F32)[:, 0, :]
        live["xs2"], live["xi2"] = xs2, xi2
        grad_fed = normalize_back(grad_top, live["xs2"], live["xi2"], g11)
        NV[5:6, :] = jnp.sum(grad_top * live["xs2"], axis=0, keepdims=True)
        NV[7:8, :] = jnp.sum(grad_top, axis=0, keepdims=True)
        live["xgf"] = grad_fed
        live["xfed_low"] = grad_fed.astype(BF16)
        ga = mm_nt(live["xfed_low"], l1(DOWN, 0, 768))
        live["xgu"] = (ga * live["xdg"]).astype(BF16)
        exchange(4, mm_nt(live["xgu"], l1(UP, 0, 768)))

    def cross_four():
        grad_first = live["xgf"] + exchange_sum(4)
        grad_att = normalize_back(grad_first, live["xs1"], live["xi1"], g10)
        NV[4:5, :] = jnp.sum(grad_first * live["xs1"], axis=0, keepdims=True)
        NV[6:7, :] = jnp.sum(grad_first, axis=0, keepdims=True)
        live["xga"] = grad_att
        att_low = grad_att.astype(BF16)
        live["xatt_low"] = att_low
        gm = mm_nt(att_low, out_rows(L1.at[ATT])).astype(BF16)
        gqs, gks, gvs = [], [], []
        for h in range(3):
            gmh = gm[:, h * 64 : h * 64 + 64]
            prob = live["prob", h]
            gp = mm_nt(gmh, live["val", h])
            inner = jnp.sum(gp * prob, axis=-1, keepdims=True)
            gs = (prob * (gp - inner)).astype(BF16)
            gqs.append(mm(gs, live["key", h]) * SCALE)
            gks.append(mm_tn(gs, live["q", h])[0:8, :] * SCALE)
            gvs.append(mm_tn(prob.astype(BF16), gmh)[0:8, :])
        gqkv = jnp.concatenate(gqs + gks + gvs, axis=-1).astype(BF16)
        live["xgqkv"] = gqkv
        exchange(5, mm(gqkv, qkv_rows(L1.at[ATT])))

    def cross_five():
        grad_summary = live["xga"] + exchange_sum(5)
        for j in range(2):
            GS[j, 0:1, :] = own_row(grad_summary, j)

    def output_rows():
        for j in range(2):
            out_ref[0, j * 128 : j * 128 + 1, :] = GS[j, 1:2, :].astype(BF16)

    def norm_one_back():
        def chunk(i, rows, carry):
            gains, shifts = carry
            grad = GF[rows, :] + ACC[rows, :]
            scaled = SC1[rows, :]
            att = normalize_back(grad, scaled, INV1[rows, 0:1], g00)
            GF[rows, :] = att
            FDL[rows, :] = att.astype(BF16)
            return (
                gains + jnp.sum(grad * scaled, axis=0, keepdims=True),
                shifts + jnp.sum(grad, axis=0, keepdims=True),
            )

        zero = jnp.zeros((1, 768), F32)
        gains, shifts = row_chunks(chunk, (zero, zero))
        NV[0:1, :] = gains
        NV[2:3, :] = shifts

    def attn_backward(r):
        GM[...] = mm_nt(FDL[...], out_rows(W.at[ATT, z_of[r]])).astype(BF16)

        def segment(s, carry):
            rows = pl.ds(pl.multiple_of(s * SEG, SEG), SEG)
            qkv = QKV[r, rows, :]
            gm = GM[rows, :]
            gqs, gks, gvs = [], [], []
            for h in range(3):
                q = qkv[:, h * 64 : h * 64 + 64]
                key = qkv[:, 192 + h * 64 : 256 + h * 64]
                val = qkv[:, 384 + h * 64 : 448 + h * 64]
                gmh = gm[:, h * 64 : h * 64 + 64]
                prob = PR[r, h, rows, :]
                gp = mm_nt(gmh, val)
                inner = jnp.sum(gp * prob, axis=-1, keepdims=True)
                gs = (prob * (gp - inner)).astype(BF16)
                gqs.append(mm(gs, key) * SCALE)
                gks.append(mm_tn(gs, q) * SCALE)
                gvs.append(mm_tn(prob.astype(BF16), gmh))
            GQ[rows, :] = jnp.concatenate(gqs + gks + gvs, axis=-1).astype(BF16)
            return carry

        lax.fori_loop(0, 2, segment, 0)
        store_unit(
            grad_unit(ATT, r),
            [
                (0, 576, lambda: mm(XT[...], GQ[...])),
                (576, 192, lambda: mm(FDLT[...], MIX[r])),
            ],
        )
        sum_start(order.index((ATT, r)))
        accumulate(r == turn[0], mm(GQ[...], qkv_rows(W.at[ATT, z_of[r]])))

    fac = {}

    def factor_start():
        wide = lambda v: v.astype(F32)
        zero_a, zero_b = jnp.zeros((8, 192), F32), jnp.zeros((8, 576), F32)
        att_left = jnp.concatenate([wide(live["xgqkv"]), zero_a], axis=-1)
        att_right = jnp.concatenate([zero_b, wide(live["mix"])], axis=-1)
        right = jnp.concatenate([wide(live["xact"]), wide(live["xgu"]), att_left, att_right], axis=0)
        left = jnp.concatenate(
            [wide(live["xfed_low"]), wide(live["xfirst_low"]), wide(live["summary_low"]), wide(live["xatt_low"])],
            axis=0,
        )
        FAC[y, x, c, 0:32, :] = right.astype(BF16)
        FAC[y, x, c, 32:64, :] = left.astype(BF16)
        part = FAC.at[y, x, c]
        fac[0] = remote(part, part, f_s.at[0], f_r.at[0], x_peer)

    def factor_two():
        fac[0].wait_recv()
        part = FAC.at[y, :, c]
        fac[1] = remote(part, part, f_s.at[1], f_r.at[1], y_peer)

    def factor_three():
        fac[1].wait_recv()
        part = FAC.at[:, :, c]
        fac[2] = remote(part, part, f_s.at[2], f_r.at[2], core_peer)

    def turn_rows(value):
        rows = value.shape[0]
        full = jnp.concatenate([value, jnp.zeros((128 - rows, value.shape[1]), F32)], axis=0)
        return full.T[:, 0:rows]

    def write_unit(layer, k, value):
        if k == ATT:
            for i in range(3):
                qkvg_ref[layer, i] = value[:, i * 192 : i * 192 + 192]
            outg_ref[layer] = turn_rows(value[:, 576:768])
        elif k == UP:
            upg_ref[layer] = value
        else:
            downg_ref[layer] = value

    def factor_final():
        fac[2].wait_recv()
        left = FAC[:, :, :, 32:64, :].reshape(256, 768)
        for i in range(2):
            LT[:, i * 128 : i * 128 + 128] = left[i * 128 : i * 128 + 128, :].T
        mine = LT[pl.ds(pl.multiple_of(dp * BLK, BLK), BLK), :].astype(F32)
        kind = (lax.broadcasted_iota(jnp.int32, (BLK, 256), 1) // 8) % 4
        right = FAC[:, :, :, 0:32, :].reshape(256, 768)
        write_unit(1, DOWN, mm(jnp.where(kind == 0, mine, 0.0).astype(BF16), right))
        write_unit(1, UP, mm(jnp.where(kind == 1, mine, 0.0).astype(BF16), right))
        write_unit(1, ATT, mm(jnp.where(kind >= 2, mine, 0.0).astype(BF16), right))

    vec = {}

    def norm_grads_start():
        exchange(6, NV[...])

    def norm_grads_two():
        total = jnp.where(row_of < 4, exchange_sum(6), NV[...])
        pad = jnp.zeros((8, 32), F32)
        for p in range(8):
            SV[p // 4, (p // 2) % 2, p % 2] = jnp.concatenate([total[:, p * BLK : p * BLK + BLK], pad], axis=-1)
        for m in range(1, 8):
            ty = y if m // 4 == 0 else ny
            tx = x if (m // 2) % 2 == 0 else nx
            tc = c if m % 2 == 0 else nc
            vec[m] = remote(
                SV.at[ty, tx, tc], RSV.at[m - 1], v_s.at[m - 1], v_r.at[m - 1], (plane_index(m), z)
            )

    def norm_grads_final():
        total = SV[y, x, c]
        for m in range(1, 8):
            vec[m].wait_recv()
            total = total + RSV[m - 1]
        gaing_ref[...] = total[0:2, 0:BLK]
        shiftg_ref[...] = total[2:4, 0:BLK]
        crossg_ref[0] = total[4:6, 0:BLK]
        crossg_ref[1] = total[6:8, 0:BLK]

    def turn_to_attention():
        norm_one_back()
        norm_grads_start()
        transpose_into(FDLT, FDL)
        for table in (a1, b1, a2, b2, a3, b3, cc):
            for i in range(9):
                table[i].wait_send()
                waited.append(id(table[i]))
        for condition, copy in passed:

            @pl.when(condition)
            def _(copy=copy):
                copy.wait_send()

    for name in ("wqk", "wv", "wo"):
        loads[name].wait()
    z_own(ATT)
    loads["x"].wait()
    token_one()
    z_own(UP)
    attn_forward(0)
    transpose_into(XT, XA, z * 256)
    gather_a(0)
    gather_a(1)
    token_two()
    gather_b(0)
    gather_a(2)
    z_own(DOWN)
    gather_b(1)
    gather_c(0)
    gather_b(2)
    gather_a(3)
    cross_one()
    gather_c(1)
    gather_a(4)
    gather_a(5)
    attn_forward(1)
    gather_b(3)
    gather_c(2)
    gather_b(4)
    cross_two()
    attn_forward(2)
    gather_b(5)
    gather_a(6)
    gather_a(7)
    gather_c(3)
    gather_c(4)
    cross_three()
    gather_c(5)
    attn_forward(3)
    gather_a(8)
    gather_b(6)
    norm_one()
    ffn_forward(1)
    gather_b(7)
    ffn_forward(0)
    ffn_down(0)
    ffn_down(1)
    cross_four()
    gather_b(8)
    ffn_forward(2)
    gather_c(6)
    transpose_into(FLT, FL)
    gather_c(7)
    gather_c(8)
    factor_start()
    ffn_forward(3)
    ffn_down(2)
    cross_five()
    ffn_down(3)
    norm_two()
    output_rows()
    loads["cot"].wait()
    norm_two_back()
    transpose_into(FDLT, FDL)
    factor_two()
    ffn_back_one(3)
    grad_down(3)
    grad_up(3)
    ffn_back_two(3)
    ffn_back_one(2)
    sum_one(0)
    grad_down(2)
    sum_one(1)
    grad_up(2)
    ffn_back_two(2)
    ffn_back_one(1)
    sum_one(2)
    grad_down(1)
    sum_one(3)
    grad_up(1)
    sum_two(0)
    sum_z(0)
    ffn_back_two(1)
    sum_one(4)
    ffn_back_one(0)
    sum_one(5)
    grad_down(0)
    grad_up(0)
    sum_two(1)
    sum_z(1)
    ffn_back_two(0)
    turn_to_attention()
    sum_one(6)
    sum_one(7)
    sum_two(2)
    attn_backward(3)
    sum_two(3)
    sum_z(2)
    attn_backward(2)
    sum_two(4)
    sum_z(4)
    sum_one(8)
    attn_backward(1)
    sum_two(5)
    sum_z(3)
    sum_z(5)
    attn_backward(0)
    sum_two(6)
    factor_three()
    ing_ref[0] = (GF[...] + ACC[...]).astype(BF16)
    norm_grads_two()
    sum_two(7)
    sum_one(9)
    factor_final()
    sum_two(8)
    sum_z(6)
    sum_one(10)
    sum_two(9)
    sum_one(11)
    sum_three(8)
    sum_z(8)
    write_unit(0, DOWN, sum_final(DOWN))
    sum_two(10)
    sum_three(9)
    sum_z(9)
    sum_z(7)
    sum_two(11)
    sum_three(10)
    sum_z(10)
    write_unit(0, UP, sum_final(UP))
    sum_three(11)
    sum_z(11)
    norm_grads_final()
    write_unit(0, ATT, sum_final(ATT))
    for copy in sends:
        if id(copy) not in waited:
            copy.wait_send()


def settle_kernel(*refs):
    sources, targets, sems = refs[:9], refs[9:18], refs[18]
    copies = [pltpu.make_async_copy(sources[i], targets[i], sems.at[i]) for i in range(9)]
    for copy in copies:
        copy.start()
    for copy in copies:
        copy.wait()


def fused_body(
    inputs, doc_ids, qkv_weight, out_weight, up_weight, down_weight, norm_gain, norm_shift, cotangent
):
    wq = qkv_weight.swapaxes(2, 3).reshape(2, 3, 2, BLK, 768)
    wo = out_weight.reshape(2, 2, BLK, 768)
    wu = up_weight.reshape(2, 2, 2, 2, BLK, 768)
    wd = down_weight.reshape(2, 2, 2, 2, BLK, 768)
    whole = pl.BlockSpec(memory_space=pl.ANY)
    vmem = pl.BlockSpec(memory_space=pltpu.VMEM)
    blocks = (2, 2, 2, BLK, 768)
    sem = pltpu.SemaphoreType.DMA
    results = pl.pallas_call(
        fused_kernel,
        out_shape=(
            pltpu.VMEM((1, 256, 768), BF16),
            pltpu.VMEM((1, 256, 768), BF16),
            pltpu.VMEM((2, 3, BLK, 192), F32),
            pltpu.VMEM((2, 192, BLK), F32),
            pltpu.VMEM((2, BLK, 768), F32),
            pltpu.VMEM((2, BLK, 768), F32),
            pltpu.VMEM((2, BLK), F32),
            pltpu.VMEM((2, BLK), F32),
            pltpu.VMEM((2, 2, BLK), F32),
        ),
        in_specs=[whole, whole, whole, vmem, whole, whole, whole, whole, vmem, vmem],
        out_specs=(vmem,) * 9,
        scratch_shapes=[
            pltpu.VMEM((3, 4) + blocks, BF16),
            pltpu.VMEM((2, 4) + blocks, BF16),
            pltpu.VMEM((12, 2, 2, BLK, 768), BF16),
            pltpu.VMEM((12, 2, HALF, 768), BF16),
            pltpu.VMEM((12, 2, HALF, 768), BF16),
            pltpu.VMEM((4, HALF, 768), BF16),
            pltpu.VMEM((4, HALF, 768), BF16),
            pltpu.VMEM((3, BLK, 768), BF16),
            pltpu.VMEM((2, 3, 2, 2, HALF, 768), BF16),
            pltpu.VMEM((2, 2, HALF, 768), BF16),
            pltpu.VMEM((3,) + blocks, BF16),
            pltpu.VMEM((1024, 768), BF16),
            pltpu.VMEM((256, 768), BF16),
            pltpu.VMEM((4, 256, 576), BF16),
            pltpu.VMEM((4, 3, 256, 128), F32),
            pltpu.VMEM((4, 256, 192), BF16),
            pltpu.VMEM((4, 256, 768), BF16),
            pltpu.VMEM((4, 256, 768), BF16),
            pltpu.VMEM((256, 768), BF16),
            pltpu.VMEM((256, 576), BF16),
            pltpu.VMEM((256, 768), F32),
            pltpu.VMEM((256, 768), F32),
            pltpu.VMEM((256, 768), F32),
            pltpu.VMEM((256, 768), F32),
            pltpu.VMEM((256, 768), BF16),
            pltpu.VMEM((768, 256), BF16),
            pltpu.VMEM((256, 768), BF16),
            pltpu.VMEM((768, 256), BF16),
            pltpu.VMEM((768, 256), BF16),
            pltpu.VMEM((256, 192), BF16),
            pltpu.VMEM((8, 16, 768), BF16),
            pltpu.VMEM((256, 128), F32),
            pltpu.VMEM((256, 128), F32),
            pltpu.VMEM((2, 2, 2, 64, 768), BF16),
            pltpu.VMEM((768, 256), BF16),
            pltpu.VMEM((2, 8, 768), F32),
            pltpu.VMEM((7, 4, 8, 768), F32),
            pltpu.VMEM((8, 768), F32),
            pltpu.VMEM((2, 2, 2, 8, 128), F32),
            pltpu.VMEM((7, 8, 128), F32),
            sem((13,)),
            sem((12, 2)),
            sem((12,)),
            sem((7, 9)),
            sem((7, 9)),
            sem((9, 12)),
            sem((9, 12)),
            sem((7, 3)),
            sem((7, 3)),
            sem((3,)),
            sem((3,)),
            sem((7,)),
            sem((7,)),
        ],
        compiler_params=pltpu.CompilerParams(
            collective_id=0, has_side_effects=True, vmem_limit_bytes=59 * 2**20
        ),
    )(
        inputs, cotangent, cotangent.reshape(8, SEG, 768), doc_ids, wq, wo, wu, wd, norm_gain, norm_shift
    )
    final = pl.pallas_call(
        settle_kernel,
        out_shape=tuple(jax.ShapeDtypeStruct(v.shape, v.dtype) for v in results),
        in_specs=[whole] * 9,
        out_specs=(whole,) * 9,
        scratch_shapes=[sem((9,))],
    )(*[pltpu.with_memory_space_constraint(v, pltpu.VMEM) for v in results])
    return final[:5] + (final[5].swapaxes(1, 2),) + final[6:]


def solution(mesh):
    in_specs = (
        P("dp", None, None),
        P("dp", None),
        P(None, None, None, "tensor"),
        P(None, "tensor", None),
        P(None, None, "tensor"),
        P(None, "tensor", None),
        P(),
        P(),
        P("dp", None, None),
    )
    out_specs = (
        P("dp", "tensor", None),
        P("dp", "tensor", None),
        P(None, None, "dp", "tensor"),
        P(None, "tensor", "dp"),
        P(None, "dp", "tensor"),
        P(None, "tensor", "dp"),
        P(None, "dp"),
        P(None, "dp"),
        P(None, None, "dp"),
    )
    fits = dict(mesh.shape) == {"dp": 8, "tensor": 4}
    chosen = fused_body if fits else body
    return jax.shard_map(chosen, mesh=mesh, in_specs=in_specs, out_specs=out_specs, check_vma=False)
```

```python
from functools import partial
import math

import jax
import jax.numpy as jnp
from jax import lax
from jax.experimental import pallas as pl
from jax.experimental.pallas import tpu as pltpu
from jax.sharding import PartitionSpec as P

HEAD_DIM = 64
SEG = 128


EPSILON = 1e-05
MASK_FILL = -1000000000.0


def layer_norm(values, gain_row, shift_row):
    center = jnp.mean(values, axis=-1, keepdims=True)
    offset = values - center
    spread = jnp.mean(offset * offset, axis=-1, keepdims=True)
    inverse = lax.rsqrt(spread + EPSILON)
    scaled = offset * inverse
    return (scaled * gain_row + shift_row, (scaled, inverse))


def norm_back(grad_out, saved, gain_row):
    scaled, inverse = saved
    weighted = grad_out * gain_row
    mean_one = jnp.mean(weighted, axis=-1, keepdims=True)
    mean_two = jnp.mean(weighted * scaled, axis=-1, keepdims=True)
    grad_in = inverse * (weighted - mean_one - scaled * mean_two)
    return (grad_in, jnp.sum(grad_out * scaled, axis=(0, 1)), jnp.sum(grad_out, axis=(0, 1)))


def score_block(head_split, allowed):
    scores = jnp.einsum(
        "bqhe,bkhe->bhqk", head_split[0], head_split[1], preferred_element_type=jnp.float32
    ) * (1.0 / math.sqrt(HEAD_DIM))
    if allowed is not None:
        scores = jnp.where(allowed, scores, MASK_FILL)
    return scores


def attend_forward(rows_low, qkv_local, allowed):
    batch_count = rows_low.shape[0]
    length = rows_low.shape[1]
    project = jnp.einsum(
        "brd,cde->cbre", rows_low, qkv_local, preferred_element_type=jnp.float32
    ).astype(jnp.bfloat16)
    head_split = project.reshape(3, batch_count, length, -1, HEAD_DIM)
    scores = score_block(head_split, allowed)
    log_total = jax.nn.logsumexp(scores, axis=-1)
    soft_low = jnp.exp(scores - log_total[..., None]).astype(jnp.bfloat16)
    mixture = jnp.einsum(
        "bhqk,bkhe->bqhe", soft_low, head_split[2], preferred_element_type=jnp.float32
    )
    return (project, log_total, mixture.astype(jnp.bfloat16).reshape(batch_count, length, -1))


def attend_backward(rows_low, qkv_local, out_local, project, log_total, mixture, grad_low, allowed):
    batch_count = rows_low.shape[0]
    length = rows_low.shape[1]
    head_split = project.reshape(3, batch_count, length, -1, HEAD_DIM)
    grad_mixture = jnp.einsum(
        "brd,fd->brf", grad_low, out_local, preferred_element_type=jnp.float32
    ).astype(jnp.bfloat16)
    out_local_grad = jnp.einsum(
        "brf,brd->fd", mixture, grad_low, preferred_element_type=jnp.float32
    )
    grad_heads = grad_mixture.reshape(batch_count, length, -1, HEAD_DIM)
    scores = score_block(head_split, allowed)
    soft_full = jnp.exp(scores - log_total[..., None])
    grad_soft = jnp.einsum(
        "bqhe,bkhe->bhqk", grad_heads, head_split[2], preferred_element_type=jnp.float32
    )
    row_inner = jnp.sum(grad_soft * soft_full, axis=-1, keepdims=True)
    grad_scores = (soft_full * (grad_soft - row_inner)).astype(jnp.bfloat16)
    scale_factor = 1.0 / math.sqrt(HEAD_DIM)
    grad_query = (
        jnp.einsum(
            "bhqk,bkhe->bqhe", grad_scores, head_split[1], preferred_element_type=jnp.float32
        )
        * scale_factor
    )
    grad_key = (
        jnp.einsum(
            "bhqk,bqhe->bkhe", grad_scores, head_split[0], preferred_element_type=jnp.float32
        )
        * scale_factor
    )
    grad_value = jnp.einsum(
        "bhqk,bqhe->bkhe",
        soft_full.astype(jnp.bfloat16),
        grad_heads,
        preferred_element_type=jnp.float32,
    )
    grad_project = (
        jnp.stack([grad_query, grad_key, grad_value])
        .reshape(3, batch_count, length, -1)
        .astype(jnp.bfloat16)
    )
    qkv_local_grad = jnp.einsum(
        "brd,cbre->cde", rows_low, grad_project, preferred_element_type=jnp.float32
    )
    input_part = jnp.einsum(
        "cbre,cde->brd", grad_project, qkv_local, preferred_element_type=jnp.float32
    )
    return (input_part, qkv_local_grad, out_local_grad)


def expand_forward(rows_low, up_local, down_local):
    upward = jnp.einsum("brd,df->brf", rows_low, up_local, preferred_element_type=jnp.float32)
    active = jax.nn.gelu(upward, approximate=False).astype(jnp.bfloat16)
    return (
        upward,
        active,
        jnp.einsum("brf,fd->brd", active, down_local, preferred_element_type=jnp.float32),
    )


def expand_backward(rows_low, up_local, down_local, upward, active, grad_low):
    grad_active = jnp.einsum(
        "brd,fd->brf", grad_low, down_local, preferred_element_type=jnp.float32
    )
    down_local_grad = jnp.einsum(
        "brf,brd->fd", active, grad_low, preferred_element_type=jnp.float32
    )
    gelu_pull = jax.vjp(partial(jax.nn.gelu, approximate=False), upward)[1]
    grad_upward = gelu_pull(grad_active)[0].astype(jnp.bfloat16)
    up_local_grad = jnp.einsum(
        "brd,brf->df", rows_low, grad_upward, preferred_element_type=jnp.float32
    )
    input_part = jnp.einsum(
        "brf,df->brd", grad_upward, up_local, preferred_element_type=jnp.float32
    )
    return (input_part, up_local_grad, down_local_grad)


def body(
    inputs,
    doc_ids,
    qkv_weight,
    out_weight,
    up_weight,
    down_weight,
    norm_gain,
    norm_shift,
    cotangent,
):
    groups = lax.axis_size("tensor")
    position = lax.axis_index("tensor")
    model_width = inputs.shape[2]
    segment_count = inputs.shape[1] // SEG
    own_count = segment_count // groups
    row_start = position * own_count

    def final_rows(values):
        return lax.dynamic_slice_in_dim(values, row_start, own_count, 0)

    def forward_sum(partial_term):
        return lax.psum(partial_term.astype(jnp.bfloat16), "tensor").astype(jnp.float32)

    def backward_sum(partial_term):
        return lax.psum(partial_term.astype(jnp.bfloat16), "tensor").astype(jnp.float32)

    def cross_sum(partial_term):
        return lax.psum(partial_term.astype(jnp.bfloat16), "tensor").astype(jnp.float32)

    def cross_grad_sum(partial_term):
        return lax.psum(partial_term, "tensor")

    tokens = inputs[0].reshape(segment_count, SEG, model_width)
    tokens_wide = tokens.astype(jnp.float32)
    lower_proj, lower_total, lower_mix = attend_forward(tokens, qkv_weight[0], None)
    attended = forward_sum(
        jnp.einsum("brf,fd->brd", lower_mix, out_weight[0], preferred_element_type=jnp.float32)
    )
    first_norm, first_saved = layer_norm(tokens_wide + attended, norm_gain[0, 0], norm_shift[0, 0])
    first_low = first_norm.astype(jnp.bfloat16)
    lower_up, lower_active, fed_term = expand_forward(first_low, up_weight[0], down_weight[0])
    second, second_saved = layer_norm(
        first_norm + forward_sum(fed_term), norm_gain[0, 1], norm_shift[0, 1]
    )
    summary = second[:, 0, :]
    summary = summary[None]
    same_doc = (doc_ids[0][:, None] == doc_ids[0][None, :])[None, None]
    summary_low = summary.astype(jnp.bfloat16)
    upper_proj, upper_total, upper_mix = attend_forward(summary_low, qkv_weight[1], same_doc)
    upper_att = cross_sum(
        jnp.einsum("brf,fd->brd", upper_mix, out_weight[1], preferred_element_type=jnp.float32)
    )
    upper_first, upper_saved_one = layer_norm(
        summary + upper_att, norm_gain[1, 0], norm_shift[1, 0]
    )
    upper_first_low = upper_first.astype(jnp.bfloat16)
    upper_up, upper_active, upper_fed = expand_forward(
        upper_first_low, up_weight[1], down_weight[1]
    )
    upper_out, upper_saved_two = layer_norm(
        upper_first + cross_sum(upper_fed), norm_gain[1, 1], norm_shift[1, 1]
    )
    joined = second.at[:, 0, :].set(upper_out[0])
    outputs_own = final_rows(joined).reshape(1, -1, model_width).astype(jnp.bfloat16)
    grad_full = cotangent[0].reshape(segment_count, SEG, model_width).astype(jnp.float32)
    grad_top = grad_full[:, 0, :][None]
    grad_upper_fed, gain_cross_two, shift_cross_two = norm_back(
        grad_top, upper_saved_two, norm_gain[1, 1]
    )
    cross_part, up_cross, down_cross = expand_backward(
        upper_first_low,
        up_weight[1],
        down_weight[1],
        upper_up,
        upper_active,
        grad_upper_fed.astype(jnp.bfloat16),
    )
    grad_upper_first = grad_upper_fed + cross_grad_sum(cross_part)
    grad_upper_att, gain_cross_one, shift_cross_one = norm_back(
        grad_upper_first, upper_saved_one, norm_gain[1, 0]
    )
    cross_input_part, qkv_cross, out_cross = attend_backward(
        summary_low,
        qkv_weight[1],
        out_weight[1],
        upper_proj,
        upper_total,
        upper_mix,
        grad_upper_att.astype(jnp.bfloat16),
        same_doc,
    )
    grad_summary = grad_upper_att + cross_grad_sum(cross_input_part)
    grad_second = grad_full.at[:, 0, :].set(grad_summary[0])
    grad_fed, gain_seg_two, shift_seg_two = norm_back(grad_second, second_saved, norm_gain[0, 1])
    fed_low = grad_fed.astype(jnp.bfloat16)
    seg_part, up_seg, down_seg = expand_backward(
        first_low, up_weight[0], down_weight[0], lower_up, lower_active, fed_low
    )
    grad_first = grad_fed + backward_sum(seg_part)
    grad_att, gain_seg_one, shift_seg_one = norm_back(grad_first, first_saved, norm_gain[0, 0])
    att_low = grad_att.astype(jnp.bfloat16)
    seg_input_part, qkv_seg, out_seg = attend_backward(
        tokens, qkv_weight[0], out_weight[0], lower_proj, lower_total, lower_mix, att_low, None
    )
    input_full = grad_att + backward_sum(seg_input_part)
    input_own = final_rows(input_full).reshape(1, -1, model_width).astype(jnp.bfloat16)
    seg_gain = jnp.stack([gain_seg_one, gain_seg_two])
    seg_shift = jnp.stack([shift_seg_one, shift_seg_two])
    cross_norm = jnp.stack(
        [jnp.stack([gain_cross_one, gain_cross_two]), jnp.stack([shift_cross_one, shift_cross_two])]
    )
    qkv_all = jnp.stack([qkv_seg, qkv_cross])
    out_all = jnp.stack([out_seg, out_cross])
    up_all = jnp.stack([up_seg, up_cross])
    down_all = jnp.stack([down_seg, down_cross])
    summed = (
        lax.psum_scatter(qkv_all, "dp", scatter_dimension=2, tiled=True),
        lax.psum_scatter(out_all, "dp", scatter_dimension=2, tiled=True),
        lax.psum_scatter(up_all, "dp", scatter_dimension=1, tiled=True),
        lax.psum_scatter(down_all, "dp", scatter_dimension=2, tiled=True),
        lax.psum_scatter(seg_gain, "dp", scatter_dimension=1, tiled=True),
        lax.psum_scatter(seg_shift, "dp", scatter_dimension=1, tiled=True),
        lax.psum_scatter(cross_norm, "dp", scatter_dimension=2, tiled=True),
    )
    return (
        outputs_own,
        input_own,
        summed[0],
        summed[1],
        summed[2],
        summed[3],
        summed[4],
        summed[5],
        summed[6],
    )


MESH = pl.DeviceIdType.MESH
F32 = jnp.float32
BF16 = jnp.bfloat16
SCALE = 1.0 / math.sqrt(HEAD_DIM)
ATT, UP, DOWN = 0, 1, 2
BLK = 96
HALF = 48


def mm(a, b):
    return lax.dot_general(a, b, (((1,), (0,)), ((), ())), preferred_element_type=F32)


def mm_nt(a, b):
    return lax.dot_general(a, b, (((1,), (1,)), ((), ())), preferred_element_type=F32)


def mm_tn(a, b):
    return lax.dot_general(a, b, (((0,), (0,)), ((), ())), preferred_element_type=F32)


def normalize(values):
    center = jnp.mean(values, axis=-1, keepdims=True)
    offset = values - center
    spread = jnp.mean(offset * offset, axis=-1, keepdims=True)
    inverse = lax.rsqrt(spread + EPSILON)
    return offset * inverse, inverse


def normalize_back(grad_out, scaled, inverse, gain_row):
    weighted = grad_out * gain_row
    mean_one = jnp.mean(weighted, axis=-1, keepdims=True)
    mean_two = jnp.mean(weighted * scaled, axis=-1, keepdims=True)
    return inverse * (weighted - mean_one - scaled * mean_two)


def gelu_pair(upward):
    cdf = 0.5 * (1.0 + lax.erf(upward * math.sqrt(0.5)))
    pdf = jnp.exp(upward * upward * -0.5) * (1.0 / math.sqrt(2.0 * math.pi))
    return upward * cdf, cdf + upward * pdf


def fused_kernel(
    tokens_hbm, cot_hbm, cot_seg, doc_ref, wq_hbm, wo_hbm, wu_hbm, wd_hbm, gain_ref, shift_ref,
    out_ref, ing_ref, qkvg_ref, outg_ref, upg_ref, downg_ref, gaing_ref, shiftg_ref, crossg_ref,
    W, G, RC, RA1, RB1, RA2, RB2, RZ, RZF, RF, L1, XA, COT, QKV, PR, MIX, ACT, DG, GU, GQ, ACC, SC1, SC2, GF,
    FL, FLT, FDL, FDLT, XT, GM, C8, INV1, INV2, FAC, LT, GS, E, NV, SV, RSV,
    sem_local, zg_s, zg_r, ag_s, ag_r, rs_s, rs_r, e_s, e_r, f_s, f_r, v_s, v_r,
):
    dp = lax.axis_index("dp")
    z = lax.axis_index("tensor")
    c = dp % 2
    x = (dp // 2) % 2
    y = dp // 4
    nc, nx, ny = 1 - c, 1 - x, 1 - y
    core_peer = (dp + 1 - 2 * c, z)
    x_peer = (dp + 2 - 4 * x, z)
    y_peer = (dp + 4 - 8 * y, z)
    left_peer, right_peer = (dp, jnp.maximum(z - 1, 0)), (dp, jnp.minimum(z + 1, 3))
    z_peer = [None, (dp, z + 1 - 2 * (z % 2)), (dp, z + 2 - 4 * (z // 2)), (dp, 3 - z)]
    z_of = [z, z + 1 - 2 * (z % 2), z + 2 - 4 * (z // 2), 3 - z]

    def plane_index(m):
        ty = y if m // 4 == 0 else ny
        tx = x if (m // 2) % 2 == 0 else nx
        tc = c if m % 2 == 0 else nc
        return ty * 4 + tx * 2 + tc

    sends = []
    waited = []

    def remote(src, dst, ssem, rsem, target):
        copy = pltpu.make_async_remote_copy(
            src_ref=src, dst_ref=dst, send_sem=ssem, recv_sem=rsem, device_id=target, device_id_type=MESH
        )
        copy.start()
        sends.append(copy)
        return copy

    barrier = pltpu.get_barrier_semaphore()
    for m in range(1, 8):
        pl.semaphore_signal(barrier, inc=1, device_id=(plane_index(m), z), device_id_type=MESH)
    for r in range(1, 4):
        pl.semaphore_signal(barrier, inc=1, device_id=z_peer[r], device_id_type=MESH)

    loads = {}

    def load(name, index, src, dst):
        copy = pltpu.make_async_copy(src, dst, sem_local.at[index])
        copy.start()
        loads[name] = copy

    load("wqk", 1, wq_hbm.at[0, pl.ds(0, 2)], W.at[ATT, z, 0])
    load("wv", 9, wq_hbm.at[0, 2], W.at[ATT, z, 1, 0])
    load("wo", 10, wo_hbm.at[0], W.at[ATT, z, 1, 1])
    load("x", 0, tokens_hbm.at[0], XA)
    load("wu", 2, wu_hbm.at[0], W.at[UP, z])
    load("wd", 3, wd_hbm.at[0], W.at[DOWN, z])
    load("cot", 4, cot_hbm.at[0, pl.ds(pl.multiple_of(z * 256, 256), 256)], COT)
    load("l1qk", 5, wq_hbm.at[1, pl.ds(0, 2)], L1.at[ATT, 0])
    load("l1v", 11, wq_hbm.at[1, 2], L1.at[ATT, 1, 0])
    load("l1o", 12, wo_hbm.at[1], L1.at[ATT, 1, 1])
    load("l1u", 6, wu_hbm.at[1], L1.at[UP])
    load("l1d", 7, wd_hbm.at[1], L1.at[DOWN])
    load("c8", 8, cot_seg.at[:, pl.ds(0, 16)], C8)

    pl.semaphore_wait(barrier, 10)

    own_unit = [W.at[ATT, z], wu_hbm.at[0], wd_hbm.at[0]]
    units = [(ATT, 1), (UP, 1), (ATT, 2), (ATT, 3), (DOWN, 1), (UP, 2), (UP, 3), (DOWN, 2), (DOWN, 3)]
    a1, b1, a2, b2, a3, b3, cc = {}, {}, {}, {}, {}, {}, {}
    passed = []

    def z_copy(src, k, shard, side):
        return pltpu.make_async_remote_copy(
            src_ref=src,
            dst_ref=W.at[k, shard, y, x, c],
            send_sem=zg_s.at[k * 4 + shard, side],
            recv_sem=zg_r.at[k * 4 + shard],
            device_id=(left_peer, right_peer)[side],
            device_id_type=MESH,
        )

    def pass_on(condition, copy):
        @pl.when(condition)
        def _():
            copy.start()

        passed.append((condition, copy))

    def z_own(k):
        src = own_unit[k].at[y, x, c]
        pass_on(z > 0, z_copy(src, k, z, 0))
        pass_on(z < 3, z_copy(src, k, z, 1))

    def z_step(k, step):
        for side in range(2):
            shard = z - 1 - step if side else z + 1 + step
            there = shard >= 0 if side else shard <= 3
            further = jnp.logical_and(there, z < 3 if side else z > 0)
            shard = jnp.clip(shard, 0, 3)
            copy = z_copy(W.at[k, shard, y, x, c], k, shard, side)

            @pl.when(there)
            def _():
                copy.wait_recv()

            pass_on(further, copy)

    def gather_a(i):
        k, r = units[i]
        z_step(k, r - 1)
        upper = W.at[k, z_of[r], y, x, c, pl.ds(0, HALF)]
        lower = W.at[k, z_of[r], y, x, c, pl.ds(HALF, HALF)]
        a1[i] = remote(upper, upper, ag_s.at[0, i], ag_r.at[0, i], x_peer)
        b1[i] = remote(lower, lower, ag_s.at[1, i], ag_r.at[1, i], y_peer)
        a2[i] = remote(upper, upper, ag_s.at[2, i], ag_r.at[2, i], y_peer)
        b2[i] = remote(lower, lower, ag_s.at[3, i], ag_r.at[3, i], x_peer)

    def gather_b(i):
        k, r = units[i]
        a1[i].wait_recv()
        part = W.at[k, z_of[r], y, nx, c, pl.ds(0, HALF)]
        a3[i] = remote(part, part, ag_s.at[4, i], ag_r.at[4, i], y_peer)
        b1[i].wait_recv()
        part = W.at[k, z_of[r], ny, x, c, pl.ds(HALF, HALF)]
        b3[i] = remote(part, part, ag_s.at[5, i], ag_r.at[5, i], x_peer)

    def gather_c(i):
        k, r = units[i]
        for table in (a2, b2, a3, b3):
            table[i].wait_recv()
        part = W.at[k, z_of[r], :, :, c]
        cc[i] = remote(part, part, ag_s.at[6, i], ag_r.at[6, i], core_peer)

    def arrived(k, r):
        if r:
            cc[units.index((k, r))].wait_recv()

    def unit_value(ref):
        return ref[...].reshape(768, ref.shape[-1])

    def cols(k, r, start, size):
        return unit_value(W.at[k, z_of[r], :, :, :, :, pl.ds(start, size)])

    def qkv_rows(ref):
        return jnp.concatenate([ref[0].reshape(384, 768), ref[1, 0].reshape(192, 768)], axis=0)

    def out_rows(ref):
        return ref[1, 1].reshape(192, 768)

    def accumulate(first, value):
        if first:
            ACC[...] = value
        else:
            ACC[...] += value

    def attn_forward(r):
        arrived(ATT, r)
        QKV[r] = mm_nt(XA[own_rows, :], qkv_rows(W.at[ATT, z_of[r]])).astype(BF16)

        def segment(s, carry):
            rows = pl.ds(pl.multiple_of(s * SEG, SEG), SEG)
            qkv = QKV[r, rows, :]
            mixes = []
            for h in range(3):
                q = qkv[:, h * 64 : h * 64 + 64]
                key = qkv[:, 192 + h * 64 : 256 + h * 64]
                val = qkv[:, 384 + h * 64 : 448 + h * 64]
                scores = mm_nt(q, key) * SCALE
                top = jnp.max(scores, axis=-1, keepdims=True)
                expd = jnp.exp(scores - top)
                prob = expd * (1.0 / jnp.sum(expd, axis=-1, keepdims=True))
                PR[r, h, rows, :] = prob
                mixes.append(mm(prob.astype(BF16), val))
            MIX[r, rows, :] = jnp.concatenate(mixes, axis=-1).astype(BF16)
            return carry

        lax.fori_loop(0, 2, segment, 0, unroll=True)
        accumulate(r == 0, mm(MIX[r], out_rows(W.at[ATT, z_of[r]])))

    own_rows = pl.ds(pl.multiple_of(z * 256, 256), 256)

    def row_chunks(body, init=0):
        def one(i, carry):
            return body(i, pl.ds(pl.multiple_of(i * 64, 64), 64), carry)

        return lax.fori_loop(0, 4, one, init, unroll=True)

    g00, g01 = gain_ref[0, 0:1, :], gain_ref[0, 1:2, :]
    b00, b01 = shift_ref[0, 0:1, :], shift_ref[0, 1:2, :]
    g10, g11 = gain_ref[1, 0:1, :], gain_ref[1, 1:2, :]
    b10, b11 = shift_ref[1, 0:1, :], shift_ref[1, 1:2, :]

    def norm_one():
        def chunk(i, rows, carry):
            mine = XA[pl.ds(pl.multiple_of(z * 256 + i * 64, 64), 64), :]
            scaled, inverse = normalize(mine.astype(F32) + ACC[rows, :])
            SC1[rows, :] = scaled
            INV1[rows, :] = jnp.broadcast_to(inverse, (64, 128))
            FL[rows, :] = (scaled * g00 + b00).astype(BF16)
            return carry

        row_chunks(chunk)

    def ffn_forward(r):
        arrived(UP, r)
        def block(n, carry):
            part = pl.ds(pl.multiple_of(n * 256, 256), 256)
            upward = mm(FL[...], unit_value(W.at[UP, z_of[r], :, :, :, :, part]))
            active, slope = gelu_pair(upward)
            ACT[r, :, part] = active.astype(BF16)
            DG[r, :, part] = slope.astype(DG.dtype)
            return carry

        lax.fori_loop(0, 3, block, 0, unroll=True)

    def ffn_down(r):
        arrived(DOWN, r)
        accumulate(r == 0, mm(ACT[r], cols(DOWN, r, 0, 768)))

    def norm_two():
        def chunk(i, rows, carry):
            first = SC1[rows, :] * g00 + b00
            scaled, inverse = normalize(first + ACC[rows, :])
            SC2[rows, :] = scaled
            INV2[rows, :] = jnp.broadcast_to(inverse, (64, 128))
            out_ref[0, rows, :] = (scaled * g01 + b01).astype(BF16)
            return carry

        row_chunks(chunk)

    def transpose_into(dst, src, start=0):
        for i in range(2):
            dst[:, i * 128 : i * 128 + 128] = src[pl.ds(pl.multiple_of(start + i * 128, 128), 128), :].T

    exch = {}

    def exchange(e, value):
        E[e, 0] = value
        for r in range(1, 4):
            exch[e, r] = remote(E.at[e, 0], E.at[e, r], e_s.at[e, r - 1], e_r.at[e, r - 1], z_peer[r])

    def exchange_wait(e):
        for r in range(1, 4):
            exch[e, r].wait_recv()

    def exchange_sum(e):
        exchange_wait(e)
        return (E[e, 0] + E[e, 1]) + (E[e, 2] + E[e, 3])

    row_of = lax.broadcasted_iota(jnp.int32, (8, 768), 0)
    pair_of = row_of // 2

    def own_row(value, j):
        return jnp.sum(jnp.where(row_of == 2 * z + j, value, 0.0), axis=0, keepdims=True)


    def norm_two_back():
        def chunk(i, rows, carry):
            gains, shifts = carry
            which = lax.broadcasted_iota(jnp.int32, (64, 768), 0) + i * 64
            grad = jnp.where(which % SEG == 0, GS[i // 2][0:1, :], COT[rows, :].astype(F32))
            scaled = SC2[rows, :]
            fed = normalize_back(grad, scaled, INV2[rows, 0:1], g01)
            GF[rows, :] = fed
            FDL[rows, :] = fed.astype(BF16)
            return (
                gains + jnp.sum(grad * scaled, axis=0, keepdims=True),
                shifts + jnp.sum(grad, axis=0, keepdims=True),
            )

        zero = jnp.zeros((1, 768), F32)
        gains, shifts = row_chunks(chunk, (zero, zero))
        NV[1:2, :] = gains
        NV[3:4, :] = shifts

    def grad_unit(k, r):
        return W.at[UP, r] if k == ATT else G.at[k - 1, r]

    turn = (3, 2, 1, 0)
    order = [(k, r) for r in turn for k in (DOWN, UP)] + [(ATT, r) for r in turn]
    s0, sa1, sb1, sa2, sb2, sza, szb, sfa, sfb = {}, {}, {}, {}, {}, {}, {}, {}, {}

    def sum_start(i):
        k, r = order[i]
        g = grad_unit(k, r)
        s0[i] = remote(g.at[:, :, nc], RC.at[i], rs_s.at[0, i], rs_r.at[0, i], core_peer)

    def add_low(a, b):
        return (a.astype(F32) + b.astype(F32)).astype(BF16)

    top, low = pl.ds(0, HALF), pl.ds(HALF, HALF)

    def sum_one(i):
        k, r = order[i]
        g = grad_unit(k, r)
        s0[i].wait_recv()

        def block(j, carry):
            jy, jx = j // 2, j % 2
            g[jy, jx, c] = add_low(g[jy, jx, c], RC[i, jy, jx])
            return carry

        lax.fori_loop(0, 4, block, 0, unroll=True)
        if k == ATT:
            part_a, part_b = g.at[:, nx, c, top], g.at[ny, :, c, low]
            peer_a, peer_b = x_peer, y_peer
        else:
            part_a, part_b = g.at[ny, :, c, top], g.at[:, nx, c, low]
            peer_a, peer_b = y_peer, x_peer
        sa1[i] = remote(part_a, RA1.at[i], rs_s.at[1, i], rs_r.at[1, i], peer_a)
        sb1[i] = remote(part_b, RB1.at[i], rs_s.at[2, i], rs_r.at[2, i], peer_b)

    def sum_two(i):
        k, r = order[i]
        g = grad_unit(k, r)
        sa1[i].wait_recv()
        if k == ATT:
            for j in range(2):
                g[j, x, c, 0:HALF, :] = add_low(g[j, x, c, 0:HALF, :], RA1[i, j])
            sa2[i] = remote(g.at[ny, x, c, top], RA2.at[i - 8], rs_s.at[3, i], rs_r.at[3, i], y_peer)
            sb1[i].wait_recv()
            for j in range(2):
                g[y, j, c, HALF:BLK, :] = add_low(g[y, j, c, HALF:BLK, :], RB1[i, j])
            sb2[i] = remote(g.at[y, nx, c, low], RB2.at[i - 8], rs_s.at[4, i], rs_r.at[4, i], x_peer)
        else:
            sb1[i].wait_recv()
            for j in range(2):
                g[y, j, c, 0:HALF, :] = add_low(g[y, j, c, 0:HALF, :], RA1[i, j])
                g[j, x, c, HALF:BLK, :] = add_low(g[j, x, c, HALF:BLK, :], RB1[i, j])

    def sum_three(i):
        g = grad_unit(*order[i])
        sa2[i].wait_recv()
        g[y, x, c, 0:HALF, :] = add_low(g[y, x, c, 0:HALF, :], RA2[i - 8])
        sb2[i].wait_recv()
        g[y, x, c, HALF:BLK, :] = add_low(g[y, x, c, HALF:BLK, :], RB2[i - 8])

    landing = {1: 0, 3: 1, 2: 2}

    def z_wait(k, r):
        i = order.index((k, r))
        sza[i].wait_recv()
        if k != ATT:
            szb[i].wait_recv()

    def z_add(k, g, slot):
        if k == ATT:
            g[y, x, c] = add_low(g[y, x, c], RZ[slot])
        else:
            for j in range(2):
                g[y, j, c, 0:HALF, :] = add_low(g[y, j, c, 0:HALF, :], RZF[k - 1, slot, 0, j])
                g[j, x, c, HALF:BLK, :] = add_low(g[j, x, c, HALF:BLK, :], RZF[k - 1, slot, 1, j])

    def sum_z(i):
        k, r = order[i]
        g = grad_unit(k, r)
        if r == 2:
            z_wait(k, 3)
            z_add(k, g, landing[3])
        if r:
            peer = z_peer[2] if r == 2 else z_peer[1]
            if k == ATT:
                sza[i] = remote(g.at[y, x, c], RZ.at[landing[r]], rs_s.at[5, i], rs_r.at[5, i], peer)
            else:
                land = RZF.at[k - 1, landing[r]]
                sza[i] = remote(g.at[y, :, c, top], land.at[0], rs_s.at[5, i], rs_r.at[5, i], peer)
                szb[i] = remote(g.at[:, x, c, low], land.at[1], rs_s.at[6, i], rs_r.at[6, i], peer)
        else:
            z_wait(k, 1)
            z_wait(k, 2)
            if k != ATT:
                for j in range(2):
                    a, b = RZF[k - 1, 0, 0, j].astype(F32), RZF[k - 1, 2, 0, j].astype(F32)
                    g[y, j, c, 0:HALF, :] = add_low(g[y, j, c, 0:HALF, :], a + b)
                    a, b = RZF[k - 1, 0, 1, j].astype(F32), RZF[k - 1, 2, 1, j].astype(F32)
                    g[j, x, c, HALF:BLK, :] = add_low(g[j, x, c, HALF:BLK, :], a + b)
                sfa[k] = remote(g.at[y, nx, c, top], RF.at[k - 1, 0], rs_s.at[7, k], rs_r.at[7, k], x_peer)
                sfb[k] = remote(g.at[ny, x, c, low], RF.at[k - 1, 1], rs_s.at[8, k], rs_r.at[8, k], y_peer)

    def sum_final(k):
        own = grad_unit(k, 0)[y, x, c].astype(F32)
        if k == ATT:
            return own + (RZ[0].astype(F32) + RZ[2].astype(F32))
        sfa[k].wait_recv()
        sfb[k].wait_recv()
        return own + jnp.concatenate([RF[k - 1, 0], RF[k - 1, 1]], axis=0).astype(F32)

    def store_unit(ref, parts):
        for start, size, value in parts:
            ref[:, :, :, :, start : start + size] = value().astype(BF16).reshape(2, 2, 2, BLK, size)

    def store_ffn(k, r, lhs_t, rhs):
        ref = grad_unit(k, r)

        def block(n, carry):
            part = pl.ds(pl.multiple_of(n * 256, 256), 256)
            value = mm(lhs_t[...], rhs[:, part])
            ref[:, :, :, :, part] = value.astype(BF16).reshape(2, 2, 2, BLK, 256)
            return carry

        lax.fori_loop(0, 3, block, 0, unroll=True)

    def ffn_back_one(r):
        ga = mm_nt(FDL[...], cols(DOWN, r, 0, 768))
        GU[...] = (ga * DG[r].astype(F32)).astype(BF16)

    def ffn_back_two(r):
        accumulate(r == turn[0], mm_nt(GU[...], cols(UP, r, 0, 768)))

    def grad_down(r):
        store_ffn(DOWN, r, FDLT, ACT.at[r])
        sum_start(order.index((DOWN, r)))

    def grad_up(r):
        store_ffn(UP, r, FLT, GU)
        sum_start(order.index((UP, r)))

    def l1(k, start, size):
        return unit_value(L1.at[k, :, :, :, :, pl.ds(start, size)])

    live = {}

    def token_one():
        unit = W.at[ATT, z]
        kv_weight = jnp.concatenate([unit[0, 1].reshape(192, 768), unit[1, 0].reshape(192, 768)], axis=0)

        def rows_of(i, carry):
            rows = pl.ds(pl.multiple_of(i * 256, 256), 256)
            ACT[i, :, 0:384] = mm_nt(XA[rows, :], kv_weight).astype(BF16)
            return carry

        lax.fori_loop(0, 4, rows_of, 0)
        x8 = jnp.concatenate([XA[i * SEG : i * SEG + 16, :].astype(F32)[0:1] for i in range(8)], axis=0)
        live["x8"] = x8
        q8 = mm_nt(x8.astype(BF16), unit[0, 0].reshape(192, 768)).astype(BF16).astype(F32)
        row = lax.broadcasted_iota(jnp.int32, (8, 1024), 0)
        keep = lax.broadcasted_iota(jnp.int32, (8, 1024), 1) // SEG == row
        mixes = []
        for h in range(3):
            q = q8[:, h * 64 : h * 64 + 64].astype(BF16)
            parts = [mm_nt(q, ACT[i, :, h * 64 : h * 64 + 64]) for i in range(4)]
            scores = jnp.where(keep, jnp.concatenate(parts, axis=1) * SCALE, -3.0e38)
            top = jnp.max(scores, axis=-1, keepdims=True)
            expd = jnp.exp(scores - top)
            prob = (expd * (1.0 / jnp.sum(expd, axis=-1, keepdims=True))).astype(BF16)
            mix = None
            for i in range(4):
                val = ACT[i, :, 192 + h * 64 : 256 + h * 64]
                part = mm(prob[:, i * 256 : i * 256 + 256], val)
                mix = part if mix is None else mix + part
            mixes.append(mix)
        exchange(0, mm(jnp.concatenate(mixes, axis=-1).astype(BF16), out_rows(unit)))

    def token_two():
        attended = exchange_sum(0)
        scaled, _ = normalize(live["x8"] + attended)
        first = scaled * g00 + b00
        live["first8"] = first
        loads["wu"].wait()
        loads["wd"].wait()
        active, _ = gelu_pair(mm(first.astype(BF16), cols(UP, 0, 0, 768)))
        exchange(1, mm(active.astype(BF16), cols(DOWN, 0, 0, 768)))

    def cross_one():
        fed = exchange_sum(1)
        scaled, _ = normalize(live["first8"] + fed)
        summary = scaled * g01 + b01
        live["summary"] = summary
        live["summary_low"] = summary.astype(BF16)
        for name in ("l1qk", "l1v", "l1o"):
            loads[name].wait()
        qkv = mm_nt(live["summary_low"], qkv_rows(L1.at[ATT])).astype(BF16).astype(F32)
        pad = jnp.zeros((120, 64), F32)
        ids = jnp.broadcast_to(doc_ref[...].astype(F32), (8, 8))
        eye = lax.broadcasted_iota(jnp.int32, (8, 8), 0) == lax.broadcasted_iota(jnp.int32, (8, 8), 1)
        same = ids == jnp.sum(jnp.where(eye, ids, 0.0), axis=1, keepdims=True)
        keep = jnp.concatenate([jnp.where(same, 1.0, 0.0), jnp.zeros((8, 120), F32)], axis=1) > 0.5
        mixes = []
        for h in range(3):
            q = qkv[:, h * 64 : h * 64 + 64].astype(BF16)
            key = jnp.concatenate([qkv[:, 192 + h * 64 : 256 + h * 64], pad], axis=0).astype(BF16)
            val = jnp.concatenate([qkv[:, 384 + h * 64 : 448 + h * 64], pad], axis=0).astype(BF16)
            scores = jnp.where(keep, mm_nt(q, key) * SCALE, MASK_FILL)
            top = jnp.max(scores, axis=-1, keepdims=True)
            expd = jnp.exp(scores - top)
            prob = expd * (1.0 / jnp.sum(expd, axis=-1, keepdims=True))
            live["prob", h], live["q", h], live["key", h], live["val", h] = prob, q, key, val
            mixes.append(mm(prob.astype(BF16), val))
        mix = jnp.concatenate(mixes, axis=-1).astype(BF16)
        live["mix"] = mix
        exchange(2, mm(mix, out_rows(L1.at[ATT])))

    def cross_two():
        attended = exchange_sum(2)
        live["xs1"], live["xi1"] = normalize(live["summary"] + attended)
        first = live["xs1"] * g10 + b10
        live["xfirst"] = first
        live["xfirst_low"] = first.astype(BF16)
        loads["l1u"].wait()
        loads["l1d"].wait()
        active, live["xdg"] = gelu_pair(mm(live["xfirst_low"], l1(UP, 0, 768)))
        live["xact"] = active.astype(BF16)
        exchange(3, mm(live["xact"], l1(DOWN, 0, 768)))

    def cross_three():
        fed = exchange_sum(3)
        xs2, xi2 = normalize(live["xfirst"] + fed)
        upper = xs2 * g11 + b11
        for j in range(2):
            GS[j, 1:2, :] = own_row(upper, j)
        loads["c8"].wait()
        grad_top = C8[...].astype(F32)[:, 0, :]
        live["xs2"], live["xi2"] = xs2, xi2
        grad_fed = normalize_back(grad_top, live["xs2"], live["xi2"], g11)
        NV[5:6, :] = jnp.sum(grad_top * live["xs2"], axis=0, keepdims=True)
        NV[7:8, :] = jnp.sum(grad_top, axis=0, keepdims=True)
        live["xgf"] = grad_fed
        live["xfed_low"] = grad_fed.astype(BF16)
        ga = mm_nt(live["xfed_low"], l1(DOWN, 0, 768))
        live["xgu"] = (ga * live["xdg"]).astype(BF16)
        exchange(4, mm_nt(live["xgu"], l1(UP, 0, 768)))

    def cross_four():
        grad_first = live["xgf"] + exchange_sum(4)
        grad_att = normalize_back(grad_first, live["xs1"], live["xi1"], g10)
        NV[4:5, :] = jnp.sum(grad_first * live["xs1"], axis=0, keepdims=True)
        NV[6:7, :] = jnp.sum(grad_first, axis=0, keepdims=True)
        live["xga"] = grad_att
        att_low = grad_att.astype(BF16)
        live["xatt_low"] = att_low
        gm = mm_nt(att_low, out_rows(L1.at[ATT])).astype(BF16)
        gqs, gks, gvs = [], [], []
        for h in range(3):
            gmh = gm[:, h * 64 : h * 64 + 64]
            prob = live["prob", h]
            gp = mm_nt(gmh, live["val", h])
            inner = jnp.sum(gp * prob, axis=-1, keepdims=True)
            gs = (prob * (gp - inner)).astype(BF16)
            gqs.append(mm(gs, live["key", h]) * SCALE)
            gks.append(mm_tn(gs, live["q", h])[0:8, :] * SCALE)
            gvs.append(mm_tn(prob.astype(BF16), gmh)[0:8, :])
        gqkv = jnp.concatenate(gqs + gks + gvs, axis=-1).astype(BF16)
        live["xgqkv"] = gqkv
        exchange(5, mm(gqkv, qkv_rows(L1.at[ATT])))

    def cross_five():
        grad_summary = live["xga"] + exchange_sum(5)
        for j in range(2):
            GS[j, 0:1, :] = own_row(grad_summary, j)

    def output_rows():
        for j in range(2):
            out_ref[0, j * 128 : j * 128 + 1, :] = GS[j, 1:2, :].astype(BF16)

    def norm_one_back():
        def chunk(i, rows, carry):
            gains, shifts = carry
            grad = GF[rows, :] + ACC[rows, :]
            scaled = SC1[rows, :]
            att = normalize_back(grad, scaled, INV1[rows, 0:1], g00)
            GF[rows, :] = att
            FDL[rows, :] = att.astype(BF16)
            return (
                gains + jnp.sum(grad * scaled, axis=0, keepdims=True),
                shifts + jnp.sum(grad, axis=0, keepdims=True),
            )

        zero = jnp.zeros((1, 768), F32)
        gains, shifts = row_chunks(chunk, (zero, zero))
        NV[0:1, :] = gains
        NV[2:3, :] = shifts

    def attn_backward(r):
        GM[...] = mm_nt(FDL[...], out_rows(W.at[ATT, z_of[r]])).astype(BF16)

        def segment(s, carry):
            rows = pl.ds(pl.multiple_of(s * SEG, SEG), SEG)
            qkv = QKV[r, rows, :]
            gm = GM[rows, :]
            gqs, gks, gvs = [], [], []
            for h in range(3):
                q = qkv[:, h * 64 : h * 64 + 64]
                key = qkv[:, 192 + h * 64 : 256 + h * 64]
                val = qkv[:, 384 + h * 64 : 448 + h * 64]
                gmh = gm[:, h * 64 : h * 64 + 64]
                prob = PR[r, h, rows, :]
                gp = mm_nt(gmh, val)
                inner = jnp.sum(gp * prob, axis=-1, keepdims=True)
                gs = (prob * (gp - inner)).astype(BF16)
                gqs.append(mm(gs, key) * SCALE)
                gks.append(mm_tn(gs, q) * SCALE)
                gvs.append(mm_tn(prob.astype(BF16), gmh))
            GQ[rows, :] = jnp.concatenate(gqs + gks + gvs, axis=-1).astype(BF16)
            return carry

        lax.fori_loop(0, 2, segment, 0, unroll=True)
        store_unit(
            grad_unit(ATT, r),
            [
                (0, 576, lambda: mm(XT[...], GQ[...])),
                (576, 192, lambda: mm(FDLT[...], MIX[r])),
            ],
        )
        sum_start(order.index((ATT, r)))
        accumulate(r == turn[0], mm(GQ[...], qkv_rows(W.at[ATT, z_of[r]])))

    fac = {}

    def factor_start():
        wide = lambda v: v.astype(F32)
        zero_a, zero_b = jnp.zeros((8, 192), F32), jnp.zeros((8, 576), F32)
        att_left = jnp.concatenate([wide(live["xgqkv"]), zero_a], axis=-1)
        att_right = jnp.concatenate([zero_b, wide(live["mix"])], axis=-1)
        right = jnp.concatenate([wide(live["xact"]), wide(live["xgu"]), att_left, att_right], axis=0)
        left = jnp.concatenate(
            [wide(live["xfed_low"]), wide(live["xfirst_low"]), wide(live["summary_low"]), wide(live["xatt_low"])],
            axis=0,
        )
        FAC[y, x, c, 0:32, :] = right.astype(BF16)
        FAC[y, x, c, 32:64, :] = left.astype(BF16)
        part = FAC.at[y, x, c]
        fac[0] = remote(part, part, f_s.at[0], f_r.at[0], x_peer)

    def factor_two():
        fac[0].wait_recv()
        part = FAC.at[y, :, c]
        fac[1] = remote(part, part, f_s.at[1], f_r.at[1], y_peer)

    def factor_three():
        fac[1].wait_recv()
        part = FAC.at[:, :, c]
        fac[2] = remote(part, part, f_s.at[2], f_r.at[2], core_peer)

    def turn_rows(value):
        rows = value.shape[0]
        full = jnp.concatenate([value, jnp.zeros((128 - rows, value.shape[1]), F32)], axis=0)
        return full.T[:, 0:rows]

    def write_unit(layer, k, value):
        if k == ATT:
            for i in range(3):
                qkvg_ref[layer, i] = value[:, i * 192 : i * 192 + 192]
            outg_ref[layer] = turn_rows(value[:, 576:768])
        elif k == UP:
            upg_ref[layer] = value
        else:
            downg_ref[layer] = value

    def factor_final():
        fac[2].wait_recv()
        left = FAC[:, :, :, 32:64, :].reshape(256, 768)
        for i in range(2):
            LT[:, i * 128 : i * 128 + 128] = left[i * 128 : i * 128 + 128, :].T
        mine = LT[pl.ds(pl.multiple_of(dp * BLK, BLK), BLK), :].astype(F32)
        kind = (lax.broadcasted_iota(jnp.int32, (BLK, 256), 1) // 8) % 4
        right = FAC[:, :, :, 0:32, :].reshape(256, 768)
        write_unit(1, DOWN, mm(jnp.where(kind == 0, mine, 0.0).astype(BF16), right))
        write_unit(1, UP, mm(jnp.where(kind == 1, mine, 0.0).astype(BF16), right))
        write_unit(1, ATT, mm(jnp.where(kind >= 2, mine, 0.0).astype(BF16), right))

    vec = {}

    def norm_grads_start():
        exchange(6, NV[...])

    def norm_grads_two():
        total = jnp.where(row_of < 4, exchange_sum(6), NV[...])
        pad = jnp.zeros((8, 32), F32)
        for p in range(8):
            SV[p // 4, (p // 2) % 2, p % 2] = jnp.concatenate([total[:, p * BLK : p * BLK + BLK], pad], axis=-1)
        for m in range(1, 8):
            ty = y if m // 4 == 0 else ny
            tx = x if (m // 2) % 2 == 0 else nx
            tc = c if m % 2 == 0 else nc
            vec[m] = remote(
                SV.at[ty, tx, tc], RSV.at[m - 1], v_s.at[m - 1], v_r.at[m - 1], (plane_index(m), z)
            )

    def norm_grads_final():
        total = SV[y, x, c]
        for m in range(1, 8):
            vec[m].wait_recv()
            total = total + RSV[m - 1]
        gaing_ref[...] = total[0:2, 0:BLK]
        shiftg_ref[...] = total[2:4, 0:BLK]
        crossg_ref[0] = total[4:6, 0:BLK]
        crossg_ref[1] = total[6:8, 0:BLK]

    def turn_to_attention():
        norm_one_back()
        norm_grads_start()
        transpose_into(FDLT, FDL)
        for table in (a1, b1, a2, b2, a3, b3, cc):
            for i in range(9):
                table[i].wait_send()
                waited.append(id(table[i]))
        for condition, copy in passed:

            @pl.when(condition)
            def _(copy=copy):
                copy.wait_send()

    for name in ("wqk", "wv", "wo"):
        loads[name].wait()
    z_own(ATT)
    loads["x"].wait()
    token_one()
    z_own(UP)
    attn_forward(0)
    transpose_into(XT, XA, z * 256)
    gather_a(0)
    gather_a(1)
    token_two()
    gather_b(0)
    gather_a(2)
    z_own(DOWN)
    gather_b(1)
    gather_c(0)
    gather_b(2)
    gather_a(3)
    cross_one()
    gather_c(1)
    gather_a(4)
    gather_a(5)
    attn_forward(1)
    gather_c(2)
    gather_b(3)
    gather_b(4)
    cross_two()
    attn_forward(2)
    gather_b(5)
    gather_a(6)
    gather_a(7)
    gather_c(3)
    gather_c(4)
    cross_three()
    gather_c(5)
    attn_forward(3)
    gather_b(6)
    gather_a(8)
    norm_one()
    ffn_forward(2)
    gather_b(7)
    ffn_forward(1)
    ffn_forward(0)
    ffn_down(0)
    gather_c(6)
    cross_four()
    gather_b(8)
    ffn_down(1)
    transpose_into(FLT, FL)
    ffn_forward(3)
    gather_c(7)
    gather_c(8)
    factor_start()
    ffn_down(2)
    cross_five()
    ffn_down(3)
    norm_two()
    output_rows()
    loads["cot"].wait()
    norm_two_back()
    transpose_into(FDLT, FDL)
    factor_two()
    grad_down(3)
    ffn_back_one(3)
    grad_up(3)
    ffn_back_two(3)
    ffn_back_one(2)
    grad_down(2)
    sum_one(0)
    grad_up(2)
    sum_one(1)
    ffn_back_two(2)
    ffn_back_one(1)
    sum_one(2)
    grad_down(1)
    sum_one(3)
    grad_up(1)
    grad_down(0)
    sum_two(0)
    sum_z(0)
    sum_one(4)
    ffn_back_two(1)
    ffn_back_one(0)
    sum_one(5)
    sum_two(1)
    sum_one(6)
    sum_z(1)
    grad_up(0)
    ffn_back_two(0)
    turn_to_attention()
    sum_two(2)
    attn_backward(3)
    sum_two(3)
    sum_one(7)
    sum_z(2)
    attn_backward(2)
    sum_two(4)
    sum_one(8)
    sum_z(4)
    attn_backward(1)
    sum_z(3)
    sum_one(9)
    sum_two(5)
    sum_z(5)
    sum_two(6)
    attn_backward(0)
    sum_two(7)
    factor_three()
    ing_ref[0] = (GF[...] + ACC[...]).astype(BF16)
    norm_grads_two()
    sum_two(8)
    sum_one(10)
    factor_final()
    sum_two(9)
    sum_z(6)
    sum_one(11)
    sum_three(8)
    sum_z(8)
    sum_two(10)
    sum_three(9)
    write_unit(0, DOWN, sum_final(DOWN))
    sum_z(9)
    sum_two(11)
    sum_z(7)
    sum_three(10)
    sum_z(10)
    sum_three(11)
    write_unit(0, UP, sum_final(UP))
    sum_z(11)
    norm_grads_final()
    write_unit(0, ATT, sum_final(ATT))
    for copy in sends:
        if id(copy) not in waited:
            copy.wait_send()


def settle_kernel(*refs):
    sources, targets, sems = refs[:9], refs[9:18], refs[18]
    copies = [pltpu.make_async_copy(sources[i], targets[i], sems.at[i]) for i in range(9)]
    for copy in copies:
        copy.start()
    for copy in copies:
        copy.wait()


def fused_body(
    inputs, doc_ids, qkv_weight, out_weight, up_weight, down_weight, norm_gain, norm_shift, cotangent
):
    wq = qkv_weight.swapaxes(2, 3).reshape(2, 3, 2, BLK, 768)
    wo = out_weight.reshape(2, 2, BLK, 768)
    wu = up_weight.reshape(2, 2, 2, 2, BLK, 768)
    wd = down_weight.reshape(2, 2, 2, 2, BLK, 768)
    whole = pl.BlockSpec(memory_space=pl.ANY)
    vmem = pl.BlockSpec(memory_space=pltpu.VMEM)
    blocks = (2, 2, 2, BLK, 768)
    sem = pltpu.SemaphoreType.DMA
    results = pl.pallas_call(
        fused_kernel,
        out_shape=(
            pltpu.VMEM((1, 256, 768), BF16),
            pltpu.VMEM((1, 256, 768), BF16),
            pltpu.VMEM((2, 3, BLK, 192), F32),
            pltpu.VMEM((2, 192, BLK), F32),
            pltpu.VMEM((2, BLK, 768), F32),
            pltpu.VMEM((2, BLK, 768), F32),
            pltpu.VMEM((2, BLK), F32),
            pltpu.VMEM((2, BLK), F32),
            pltpu.VMEM((2, 2, BLK), F32),
        ),
        in_specs=[whole, whole, whole, vmem, whole, whole, whole, whole, vmem, vmem],
        out_specs=(vmem,) * 9,
        scratch_shapes=[
            pltpu.VMEM((3, 4) + blocks, BF16),
            pltpu.VMEM((2, 4) + blocks, BF16),
            pltpu.VMEM((12, 2, 2, BLK, 768), BF16),
            pltpu.VMEM((12, 2, HALF, 768), BF16),
            pltpu.VMEM((12, 2, HALF, 768), BF16),
            pltpu.VMEM((4, HALF, 768), BF16),
            pltpu.VMEM((4, HALF, 768), BF16),
            pltpu.VMEM((3, BLK, 768), BF16),
            pltpu.VMEM((2, 3, 2, 2, HALF, 768), BF16),
            pltpu.VMEM((2, 2, HALF, 768), BF16),
            pltpu.VMEM((3,) + blocks, BF16),
            pltpu.VMEM((1024, 768), BF16),
            pltpu.VMEM((256, 768), BF16),
            pltpu.VMEM((4, 256, 576), BF16),
            pltpu.VMEM((4, 3, 256, 128), F32),
            pltpu.VMEM((4, 256, 192), BF16),
            pltpu.VMEM((4, 256, 768), BF16),
            pltpu.VMEM((4, 256, 768), BF16),
            pltpu.VMEM((256, 768), BF16),
            pltpu.VMEM((256, 576), BF16),
            pltpu.VMEM((256, 768), F32),
            pltpu.VMEM((256, 768), F32),
            pltpu.VMEM((256, 768), F32),
            pltpu.VMEM((256, 768), F32),
            pltpu.VMEM((256, 768), BF16),
            pltpu.VMEM((768, 256), BF16),
            pltpu.VMEM((256, 768), BF16),
            pltpu.VMEM((768, 256), BF16),
            pltpu.VMEM((768, 256), BF16),
            pltpu.VMEM((256, 192), BF16),
            pltpu.VMEM((8, 16, 768), BF16),
            pltpu.VMEM((256, 128), F32),
            pltpu.VMEM((256, 128), F32),
            pltpu.VMEM((2, 2, 2, 64, 768), BF16),
            pltpu.VMEM((768, 256), BF16),
            pltpu.VMEM((2, 8, 768), F32),
            pltpu.VMEM((7, 4, 8, 768), F32),
            pltpu.VMEM((8, 768), F32),
            pltpu.VMEM((2, 2, 2, 8, 128), F32),
            pltpu.VMEM((7, 8, 128), F32),
            sem((13,)),
            sem((12, 2)),
            sem((12,)),
            sem((7, 9)),
            sem((7, 9)),
            sem((9, 12)),
            sem((9, 12)),
            sem((7, 3)),
            sem((7, 3)),
            sem((3,)),
            sem((3,)),
            sem((7,)),
            sem((7,)),
        ],
        compiler_params=pltpu.CompilerParams(
            collective_id=0, has_side_effects=True, vmem_limit_bytes=59 * 2**20
        ),
    )(
        inputs, cotangent, cotangent.reshape(8, SEG, 768), doc_ids, wq, wo, wu, wd, norm_gain, norm_shift
    )
    final = pl.pallas_call(
        settle_kernel,
        out_shape=tuple(jax.ShapeDtypeStruct(v.shape, v.dtype) for v in results),
        in_specs=[whole] * 9,
        out_specs=(whole,) * 9,
        scratch_shapes=[sem((9,))],
    )(*[pltpu.with_memory_space_constraint(v, pltpu.VMEM) for v in results])
    return final[:5] + (final[5].swapaxes(1, 2),) + final[6:]


def solution(mesh):
    in_specs = (
        P("dp", None, None),
        P("dp", None),
        P(None, None, None, "tensor"),
        P(None, "tensor", None),
        P(None, None, "tensor"),
        P(None, "tensor", None),
        P(),
        P(),
        P("dp", None, None),
    )
    out_specs = (
        P("dp", "tensor", None),
        P("dp", "tensor", None),
        P(None, None, "dp", "tensor"),
        P(None, "tensor", "dp"),
        P(None, "dp", "tensor"),
        P(None, "tensor", "dp"),
        P(None, "dp"),
        P(None, "dp"),
        P(None, None, "dp"),
    )
    fits = dict(mesh.shape) == {"dp": 8, "tensor": 4}
    chosen = fused_body if fits else body
    return jax.shard_map(chosen, mesh=mesh, in_specs=in_specs, out_specs=out_specs, check_vma=False)
```

```python
from functools import partial
import math

import jax
import jax.numpy as jnp
from jax import lax
from jax.experimental import pallas as pl
from jax.experimental.pallas import tpu as pltpu
from jax.sharding import PartitionSpec as P

HEAD_DIM = 64
SEG = 128


EPSILON = 1e-05
MASK_FILL = -1000000000.0


def layer_norm(values, gain_row, shift_row):
    center = jnp.mean(values, axis=-1, keepdims=True)
    offset = values - center
    spread = jnp.mean(offset * offset, axis=-1, keepdims=True)
    inverse = lax.rsqrt(spread + EPSILON)
    scaled = offset * inverse
    return (scaled * gain_row + shift_row, (scaled, inverse))


def norm_back(grad_out, saved, gain_row):
    scaled, inverse = saved
    weighted = grad_out * gain_row
    mean_one = jnp.mean(weighted, axis=-1, keepdims=True)
    mean_two = jnp.mean(weighted * scaled, axis=-1, keepdims=True)
    grad_in = inverse * (weighted - mean_one - scaled * mean_two)
    return (grad_in, jnp.sum(grad_out * scaled, axis=(0, 1)), jnp.sum(grad_out, axis=(0, 1)))


def score_block(head_split, allowed):
    scores = jnp.einsum(
        "bqhe,bkhe->bhqk", head_split[0], head_split[1], preferred_element_type=jnp.float32
    ) * (1.0 / math.sqrt(HEAD_DIM))
    if allowed is not None:
        scores = jnp.where(allowed, scores, MASK_FILL)
    return scores


def attend_forward(rows_low, qkv_local, allowed):
    batch_count = rows_low.shape[0]
    length = rows_low.shape[1]
    project = jnp.einsum(
        "brd,cde->cbre", rows_low, qkv_local, preferred_element_type=jnp.float32
    ).astype(jnp.bfloat16)
    head_split = project.reshape(3, batch_count, length, -1, HEAD_DIM)
    scores = score_block(head_split, allowed)
    log_total = jax.nn.logsumexp(scores, axis=-1)
    soft_low = jnp.exp(scores - log_total[..., None]).astype(jnp.bfloat16)
    mixture = jnp.einsum(
        "bhqk,bkhe->bqhe", soft_low, head_split[2], preferred_element_type=jnp.float32
    )
    return (project, log_total, mixture.astype(jnp.bfloat16).reshape(batch_count, length, -1))


def attend_backward(rows_low, qkv_local, out_local, project, log_total, mixture, grad_low, allowed):
    batch_count = rows_low.shape[0]
    length = rows_low.shape[1]
    head_split = project.reshape(3, batch_count, length, -1, HEAD_DIM)
    grad_mixture = jnp.einsum(
        "brd,fd->brf", grad_low, out_local, preferred_element_type=jnp.float32
    ).astype(jnp.bfloat16)
    out_local_grad = jnp.einsum(
        "brf,brd->fd", mixture, grad_low, preferred_element_type=jnp.float32
    )
    grad_heads = grad_mixture.reshape(batch_count, length, -1, HEAD_DIM)
    scores = score_block(head_split, allowed)
    soft_full = jnp.exp(scores - log_total[..., None])
    grad_soft = jnp.einsum(
        "bqhe,bkhe->bhqk", grad_heads, head_split[2], preferred_element_type=jnp.float32
    )
    row_inner = jnp.sum(grad_soft * soft_full, axis=-1, keepdims=True)
    grad_scores = (soft_full * (grad_soft - row_inner)).astype(jnp.bfloat16)
    scale_factor = 1.0 / math.sqrt(HEAD_DIM)
    grad_query = (
        jnp.einsum(
            "bhqk,bkhe->bqhe", grad_scores, head_split[1], preferred_element_type=jnp.float32
        )
        * scale_factor
    )
    grad_key = (
        jnp.einsum(
            "bhqk,bqhe->bkhe", grad_scores, head_split[0], preferred_element_type=jnp.float32
        )
        * scale_factor
    )
    grad_value = jnp.einsum(
        "bhqk,bqhe->bkhe",
        soft_full.astype(jnp.bfloat16),
        grad_heads,
        preferred_element_type=jnp.float32,
    )
    grad_project = (
        jnp.stack([grad_query, grad_key, grad_value])
        .reshape(3, batch_count, length, -1)
        .astype(jnp.bfloat16)
    )
    qkv_local_grad = jnp.einsum(
        "brd,cbre->cde", rows_low, grad_project, preferred_element_type=jnp.float32
    )
    input_part = jnp.einsum(
        "cbre,cde->brd", grad_project, qkv_local, preferred_element_type=jnp.float32
    )
    return (input_part, qkv_local_grad, out_local_grad)


def expand_forward(rows_low, up_local, down_local):
    upward = jnp.einsum("brd,df->brf", rows_low, up_local, preferred_element_type=jnp.float32)
    active = jax.nn.gelu(upward, approximate=False).astype(jnp.bfloat16)
    return (
        upward,
        active,
        jnp.einsum("brf,fd->brd", active, down_local, preferred_element_type=jnp.float32),
    )


def expand_backward(rows_low, up_local, down_local, upward, active, grad_low):
    grad_active = jnp.einsum(
        "brd,fd->brf", grad_low, down_local, preferred_element_type=jnp.float32
    )
    down_local_grad = jnp.einsum(
        "brf,brd->fd", active, grad_low, preferred_element_type=jnp.float32
    )
    gelu_pull = jax.vjp(partial(jax.nn.gelu, approximate=False), upward)[1]
    grad_upward = gelu_pull(grad_active)[0].astype(jnp.bfloat16)
    up_local_grad = jnp.einsum(
        "brd,brf->df", rows_low, grad_upward, preferred_element_type=jnp.float32
    )
    input_part = jnp.einsum(
        "brf,df->brd", grad_upward, up_local, preferred_element_type=jnp.float32
    )
    return (input_part, up_local_grad, down_local_grad)


def body(
    inputs,
    doc_ids,
    qkv_weight,
    out_weight,
    up_weight,
    down_weight,
    norm_gain,
    norm_shift,
    cotangent,
):
    groups = lax.axis_size("tensor")
    position = lax.axis_index("tensor")
    model_width = inputs.shape[2]
    segment_count = inputs.shape[1] // SEG
    own_count = segment_count // groups
    row_start = position * own_count

    def final_rows(values):
        return lax.dynamic_slice_in_dim(values, row_start, own_count, 0)

    def forward_sum(partial_term):
        return lax.psum(partial_term.astype(jnp.bfloat16), "tensor").astype(jnp.float32)

    def backward_sum(partial_term):
        return lax.psum(partial_term.astype(jnp.bfloat16), "tensor").astype(jnp.float32)

    def cross_sum(partial_term):
        return lax.psum(partial_term.astype(jnp.bfloat16), "tensor").astype(jnp.float32)

    def cross_grad_sum(partial_term):
        return lax.psum(partial_term, "tensor")

    tokens = inputs[0].reshape(segment_count, SEG, model_width)
    tokens_wide = tokens.astype(jnp.float32)
    lower_proj, lower_total, lower_mix = attend_forward(tokens, qkv_weight[0], None)
    attended = forward_sum(
        jnp.einsum("brf,fd->brd", lower_mix, out_weight[0], preferred_element_type=jnp.float32)
    )
    first_norm, first_saved = layer_norm(tokens_wide + attended, norm_gain[0, 0], norm_shift[0, 0])
    first_low = first_norm.astype(jnp.bfloat16)
    lower_up, lower_active, fed_term = expand_forward(first_low, up_weight[0], down_weight[0])
    second, second_saved = layer_norm(
        first_norm + forward_sum(fed_term), norm_gain[0, 1], norm_shift[0, 1]
    )
    summary = second[:, 0, :]
    summary = summary[None]
    same_doc = (doc_ids[0][:, None] == doc_ids[0][None, :])[None, None]
    summary_low = summary.astype(jnp.bfloat16)
    upper_proj, upper_total, upper_mix = attend_forward(summary_low, qkv_weight[1], same_doc)
    upper_att = cross_sum(
        jnp.einsum("brf,fd->brd", upper_mix, out_weight[1], preferred_element_type=jnp.float32)
    )
    upper_first, upper_saved_one = layer_norm(
        summary + upper_att, norm_gain[1, 0], norm_shift[1, 0]
    )
    upper_first_low = upper_first.astype(jnp.bfloat16)
    upper_up, upper_active, upper_fed = expand_forward(
        upper_first_low, up_weight[1], down_weight[1]
    )
    upper_out, upper_saved_two = layer_norm(
        upper_first + cross_sum(upper_fed), norm_gain[1, 1], norm_shift[1, 1]
    )
    joined = second.at[:, 0, :].set(upper_out[0])
    outputs_own = final_rows(joined).reshape(1, -1, model_width).astype(jnp.bfloat16)
    grad_full = cotangent[0].reshape(segment_count, SEG, model_width).astype(jnp.float32)
    grad_top = grad_full[:, 0, :][None]
    grad_upper_fed, gain_cross_two, shift_cross_two = norm_back(
        grad_top, upper_saved_two, norm_gain[1, 1]
    )
    cross_part, up_cross, down_cross = expand_backward(
        upper_first_low,
        up_weight[1],
        down_weight[1],
        upper_up,
        upper_active,
        grad_upper_fed.astype(jnp.bfloat16),
    )
    grad_upper_first = grad_upper_fed + cross_grad_sum(cross_part)
    grad_upper_att, gain_cross_one, shift_cross_one = norm_back(
        grad_upper_first, upper_saved_one, norm_gain[1, 0]
    )
    cross_input_part, qkv_cross, out_cross = attend_backward(
        summary_low,
        qkv_weight[1],
        out_weight[1],
        upper_proj,
        upper_total,
        upper_mix,
        grad_upper_att.astype(jnp.bfloat16),
        same_doc,
    )
    grad_summary = grad_upper_att + cross_grad_sum(cross_input_part)
    grad_second = grad_full.at[:, 0, :].set(grad_summary[0])
    grad_fed, gain_seg_two, shift_seg_two = norm_back(grad_second, second_saved, norm_gain[0, 1])
    fed_low = grad_fed.astype(jnp.bfloat16)
    seg_part, up_seg, down_seg = expand_backward(
        first_low, up_weight[0], down_weight[0], lower_up, lower_active, fed_low
    )
    grad_first = grad_fed + backward_sum(seg_part)
    grad_att, gain_seg_one, shift_seg_one = norm_back(grad_first, first_saved, norm_gain[0, 0])
    att_low = grad_att.astype(jnp.bfloat16)
    seg_input_part, qkv_seg, out_seg = attend_backward(
        tokens, qkv_weight[0], out_weight[0], lower_proj, lower_total, lower_mix, att_low, None
    )
    input_full = grad_att + backward_sum(seg_input_part)
    input_own = final_rows(input_full).reshape(1, -1, model_width).astype(jnp.bfloat16)
    seg_gain = jnp.stack([gain_seg_one, gain_seg_two])
    seg_shift = jnp.stack([shift_seg_one, shift_seg_two])
    cross_norm = jnp.stack(
        [jnp.stack([gain_cross_one, gain_cross_two]), jnp.stack([shift_cross_one, shift_cross_two])]
    )
    qkv_all = jnp.stack([qkv_seg, qkv_cross])
    out_all = jnp.stack([out_seg, out_cross])
    up_all = jnp.stack([up_seg, up_cross])
    down_all = jnp.stack([down_seg, down_cross])
    summed = (
        lax.psum_scatter(qkv_all, "dp", scatter_dimension=2, tiled=True),
        lax.psum_scatter(out_all, "dp", scatter_dimension=2, tiled=True),
        lax.psum_scatter(up_all, "dp", scatter_dimension=1, tiled=True),
        lax.psum_scatter(down_all, "dp", scatter_dimension=2, tiled=True),
        lax.psum_scatter(seg_gain, "dp", scatter_dimension=1, tiled=True),
        lax.psum_scatter(seg_shift, "dp", scatter_dimension=1, tiled=True),
        lax.psum_scatter(cross_norm, "dp", scatter_dimension=2, tiled=True),
    )
    return (
        outputs_own,
        input_own,
        summed[0],
        summed[1],
        summed[2],
        summed[3],
        summed[4],
        summed[5],
        summed[6],
    )


MESH = pl.DeviceIdType.MESH
F32 = jnp.float32
BF16 = jnp.bfloat16
SCALE = 1.0 / math.sqrt(HEAD_DIM)
ATT, UP, DOWN = 0, 1, 2
BLK = 96
HALF = 48


def mm(a, b):
    return lax.dot_general(a, b, (((1,), (0,)), ((), ())), preferred_element_type=F32)


def mm_nt(a, b):
    return lax.dot_general(a, b, (((1,), (1,)), ((), ())), preferred_element_type=F32)


def mm_tn(a, b):
    return lax.dot_general(a, b, (((0,), (0,)), ((), ())), preferred_element_type=F32)


def normalize(values):
    center = jnp.mean(values, axis=-1, keepdims=True)
    offset = values - center
    spread = jnp.mean(offset * offset, axis=-1, keepdims=True)
    inverse = lax.rsqrt(spread + EPSILON)
    return offset * inverse, inverse


def normalize_back(grad_out, scaled, inverse, gain_row):
    weighted = grad_out * gain_row
    mean_one = jnp.mean(weighted, axis=-1, keepdims=True)
    mean_two = jnp.mean(weighted * scaled, axis=-1, keepdims=True)
    return inverse * (weighted - mean_one - scaled * mean_two)


def gelu_pair(upward):
    cdf = 0.5 * (1.0 + lax.erf(upward * math.sqrt(0.5)))
    pdf = jnp.exp(upward * upward * -0.5) * (1.0 / math.sqrt(2.0 * math.pi))
    return upward * cdf, cdf + upward * pdf


def fused_kernel(
    tokens_hbm, cot_hbm, cot_seg, doc_ref, wq_hbm, wo_hbm, wu_hbm, wd_hbm, gain_ref, shift_ref,
    out_ref, ing_ref, qkvg_ref, outg_ref, upg_ref, downg_ref, gaing_ref, shiftg_ref, crossg_ref,
    W, G, RC, RA1, RB1, RA2, RB2, RZ, RZF, RF, L1, XA, COT, QKV, PR, MIX, ACT, DG, GU, GQ, ACC, SC1, GF,
    FL, FLT, FDL, FDLT, XT, GM, C8, INV1, FAC, LT, GS, E, NV, SV, RSV,
    sem_local, zg_s, zg_r, ag_s, ag_r, rs_s, rs_r, e_s, e_r, f_s, f_r, v_s, v_r,
):
    dp = lax.axis_index("dp")
    z = lax.axis_index("tensor")
    c = dp % 2
    x = (dp // 2) % 2
    y = dp // 4
    nc, nx, ny = 1 - c, 1 - x, 1 - y
    core_peer = (dp + 1 - 2 * c, z)
    x_peer = (dp + 2 - 4 * x, z)
    y_peer = (dp + 4 - 8 * y, z)
    left_peer, right_peer = (dp, jnp.maximum(z - 1, 0)), (dp, jnp.minimum(z + 1, 3))
    z_peer = [None, (dp, z + 1 - 2 * (z % 2)), (dp, z + 2 - 4 * (z // 2)), (dp, 3 - z)]
    z_of = [z, z + 1 - 2 * (z % 2), z + 2 - 4 * (z // 2), 3 - z]

    def plane_index(m):
        ty = y if m // 4 == 0 else ny
        tx = x if (m // 2) % 2 == 0 else nx
        tc = c if m % 2 == 0 else nc
        return ty * 4 + tx * 2 + tc

    sends = []
    waited = []

    def remote(src, dst, ssem, rsem, target):
        copy = pltpu.make_async_remote_copy(
            src_ref=src, dst_ref=dst, send_sem=ssem, recv_sem=rsem, device_id=target, device_id_type=MESH
        )
        copy.start()
        sends.append(copy)
        return copy

    barrier = pltpu.get_barrier_semaphore()
    for m in range(1, 8):
        pl.semaphore_signal(barrier, inc=1, device_id=(plane_index(m), z), device_id_type=MESH)
    for r in range(1, 4):
        pl.semaphore_signal(barrier, inc=1, device_id=z_peer[r], device_id_type=MESH)

    loads = {}

    def load(name, index, src, dst):
        copy = pltpu.make_async_copy(src, dst, sem_local.at[index])
        copy.start()
        loads[name] = copy

    load("wqk", 1, wq_hbm.at[0, pl.ds(0, 2)], W.at[ATT, z, 0])
    load("wv", 9, wq_hbm.at[0, 2], W.at[ATT, z, 1, 0])
    load("wo", 10, wo_hbm.at[0], W.at[ATT, z, 1, 1])
    load("x", 0, tokens_hbm.at[0], XA)
    load("wu", 2, wu_hbm.at[0], W.at[UP, z])
    load("wd", 3, wd_hbm.at[0], W.at[DOWN, z])
    load("cot", 4, cot_hbm.at[0, pl.ds(pl.multiple_of(z * 256, 256), 256)], COT)
    load("l1qk", 5, wq_hbm.at[1, pl.ds(0, 2)], L1.at[ATT, 0])
    load("l1v", 11, wq_hbm.at[1, 2], L1.at[ATT, 1, 0])
    load("l1o", 12, wo_hbm.at[1], L1.at[ATT, 1, 1])
    load("l1u", 6, wu_hbm.at[1], L1.at[UP])
    load("l1d", 7, wd_hbm.at[1], L1.at[DOWN])
    load("c8", 8, cot_seg.at[:, pl.ds(0, 16)], C8)

    pl.semaphore_wait(barrier, 10)

    own_unit = [W.at[ATT, z], wu_hbm.at[0], wd_hbm.at[0]]
    units = [(ATT, 1), (UP, 1), (ATT, 2), (ATT, 3), (DOWN, 1), (UP, 2), (UP, 3), (DOWN, 2), (DOWN, 3)]
    a1, b1, a2, b2, a3, b3, cc = {}, {}, {}, {}, {}, {}, {}
    passed = []

    def z_copy(src, k, shard, side):
        return pltpu.make_async_remote_copy(
            src_ref=src,
            dst_ref=W.at[k, shard, y, x, c],
            send_sem=zg_s.at[k * 4 + shard, side],
            recv_sem=zg_r.at[k * 4 + shard],
            device_id=(left_peer, right_peer)[side],
            device_id_type=MESH,
        )

    def pass_on(condition, copy):
        @pl.when(condition)
        def _():
            copy.start()

        passed.append((condition, copy))

    def z_own(k):
        src = own_unit[k].at[y, x, c]
        pass_on(z > 0, z_copy(src, k, z, 0))
        pass_on(z < 3, z_copy(src, k, z, 1))

    def z_step(k, step):
        for side in range(2):
            shard = z - 1 - step if side else z + 1 + step
            there = shard >= 0 if side else shard <= 3
            further = jnp.logical_and(there, z < 3 if side else z > 0)
            shard = jnp.clip(shard, 0, 3)
            copy = z_copy(W.at[k, shard, y, x, c], k, shard, side)

            @pl.when(there)
            def _():
                copy.wait_recv()

            pass_on(further, copy)

    def gather_a(i):
        k, r = units[i]
        z_step(k, r - 1)
        upper = W.at[k, z_of[r], y, x, c, pl.ds(0, HALF)]
        lower = W.at[k, z_of[r], y, x, c, pl.ds(HALF, HALF)]
        a1[i] = remote(upper, upper, ag_s.at[0, i], ag_r.at[0, i], x_peer)
        b1[i] = remote(lower, lower, ag_s.at[1, i], ag_r.at[1, i], y_peer)
        a2[i] = remote(upper, upper, ag_s.at[2, i], ag_r.at[2, i], y_peer)
        b2[i] = remote(lower, lower, ag_s.at[3, i], ag_r.at[3, i], x_peer)

    def gather_b(i):
        k, r = units[i]
        a1[i].wait_recv()
        part = W.at[k, z_of[r], y, nx, c, pl.ds(0, HALF)]
        a3[i] = remote(part, part, ag_s.at[4, i], ag_r.at[4, i], y_peer)
        b1[i].wait_recv()
        part = W.at[k, z_of[r], ny, x, c, pl.ds(HALF, HALF)]
        b3[i] = remote(part, part, ag_s.at[5, i], ag_r.at[5, i], x_peer)

    def gather_c(i):
        k, r = units[i]
        for table in (a2, b2, a3, b3):
            table[i].wait_recv()
        part = W.at[k, z_of[r], :, :, c]
        cc[i] = remote(part, part, ag_s.at[6, i], ag_r.at[6, i], core_peer)

    def arrived(k, r):
        if r:
            cc[units.index((k, r))].wait_recv()

    def unit_value(ref):
        return ref[...].reshape(768, ref.shape[-1])

    def cols(k, r, start, size):
        return unit_value(W.at[k, z_of[r], :, :, :, :, pl.ds(start, size)])

    def qkv_rows(ref):
        return jnp.concatenate([ref[0].reshape(384, 768), ref[1, 0].reshape(192, 768)], axis=0)

    def out_rows(ref):
        return ref[1, 1].reshape(192, 768)

    def accumulate(first, value):
        if first:
            ACC[...] = value
        else:
            ACC[...] += value

    def attn_forward(r):
        arrived(ATT, r)
        QKV[r] = mm_nt(XA[own_rows, :], qkv_rows(W.at[ATT, z_of[r]])).astype(BF16)

        def segment(s, carry):
            rows = pl.ds(pl.multiple_of(s * SEG, SEG), SEG)
            qkv = QKV[r, rows, :]
            mixes = []
            for h in range(3):
                q = qkv[:, h * 64 : h * 64 + 64]
                key = qkv[:, 192 + h * 64 : 256 + h * 64]
                val = qkv[:, 384 + h * 64 : 448 + h * 64]
                scores = mm_nt(q, key) * SCALE
                top = jnp.max(scores, axis=-1, keepdims=True)
                expd = jnp.exp(scores - top)
                prob = expd * (1.0 / jnp.sum(expd, axis=-1, keepdims=True))
                PR[r, h, rows, :] = prob
                mixes.append(mm(prob.astype(BF16), val))
            MIX[r, rows, :] = jnp.concatenate(mixes, axis=-1).astype(BF16)
            return carry

        lax.fori_loop(0, 2, segment, 0, unroll=True)
        accumulate(r == 0, mm(MIX[r], out_rows(W.at[ATT, z_of[r]])))

    own_rows = pl.ds(pl.multiple_of(z * 256, 256), 256)

    def row_chunks(body, init=0):
        def one(i, carry):
            return body(i, pl.ds(pl.multiple_of(i * 64, 64), 64), carry)

        return lax.fori_loop(0, 4, one, init, unroll=True)

    g00, g01 = gain_ref[0, 0:1, :], gain_ref[0, 1:2, :]
    b00, b01 = shift_ref[0, 0:1, :], shift_ref[0, 1:2, :]
    g10, g11 = gain_ref[1, 0:1, :], gain_ref[1, 1:2, :]
    b10, b11 = shift_ref[1, 0:1, :], shift_ref[1, 1:2, :]

    def norm_one():
        def chunk(i, rows, carry):
            mine = XA[pl.ds(pl.multiple_of(z * 256 + i * 64, 64), 64), :]
            scaled, inverse = normalize(mine.astype(F32) + ACC[rows, :])
            SC1[rows, :] = scaled
            INV1[rows, :] = jnp.broadcast_to(inverse, (64, 128))
            FL[rows, :] = (scaled * g00 + b00).astype(BF16)
            return carry

        row_chunks(chunk)

    def ffn_forward(r):
        arrived(UP, r)
        def block(n, carry):
            part = pl.ds(pl.multiple_of(n * 256, 256), 256)
            upward = mm(FL[...], unit_value(W.at[UP, z_of[r], :, :, :, :, part]))
            active, slope = gelu_pair(upward)
            ACT[r, :, part] = active.astype(BF16)
            DG[r, :, part] = slope.astype(DG.dtype)
            return carry

        lax.fori_loop(0, 3, block, 0, unroll=True)

    def ffn_down(r):
        arrived(DOWN, r)
        accumulate(r == 0, mm(ACT[r], cols(DOWN, r, 0, 768)))

    def norm_two():
        loads["cot"].wait()

        def chunk(i, rows, carry):
            gains, shifts = carry
            first = SC1[rows, :] * g00 + b00
            scaled, inverse = normalize(first + ACC[rows, :])
            out_ref[0, rows, :] = (scaled * g01 + b01).astype(BF16)
            which = lax.broadcasted_iota(jnp.int32, (64, 768), 0) + i * 64
            grad = jnp.where(which % SEG == 0, GS[i // 2][0:1, :], COT[rows, :].astype(F32))
            fed = normalize_back(grad, scaled, inverse, g01)
            GF[rows, :] = fed
            FDL[rows, :] = fed.astype(BF16)
            return (
                gains + jnp.sum(grad * scaled, axis=0, keepdims=True),
                shifts + jnp.sum(grad, axis=0, keepdims=True),
            )

        zero = jnp.zeros((1, 768), F32)
        gains, shifts = row_chunks(chunk, (zero, zero))
        NV[1:2, :] = gains
        NV[3:4, :] = shifts

    def transpose_into(dst, src, start=0):
        for i in range(2):
            dst[:, i * 128 : i * 128 + 128] = src[pl.ds(pl.multiple_of(start + i * 128, 128), 128), :].T

    exch = {}

    def exchange(e, value):
        E[e, 0] = value
        for r in range(1, 4):
            exch[e, r] = remote(E.at[e, 0], E.at[e, r], e_s.at[e, r - 1], e_r.at[e, r - 1], z_peer[r])

    def exchange_wait(e):
        for r in range(1, 4):
            exch[e, r].wait_recv()

    def exchange_sum(e):
        exchange_wait(e)
        return (E[e, 0] + E[e, 1]) + (E[e, 2] + E[e, 3])

    row_of = lax.broadcasted_iota(jnp.int32, (8, 768), 0)
    pair_of = row_of // 2

    def own_row(value, j):
        return jnp.sum(jnp.where(row_of == 2 * z + j, value, 0.0), axis=0, keepdims=True)

    def grad_unit(k, r):
        return W.at[UP, r] if k == ATT else G.at[k - 1, r]

    turn = (3, 2, 1, 0)
    order = [(k, r) for r in turn for k in (DOWN, UP)] + [(ATT, r) for r in turn]
    s0, sa1, sb1, sa2, sb2, sza, szb, sfa, sfb = {}, {}, {}, {}, {}, {}, {}, {}, {}

    def sum_start(i):
        k, r = order[i]
        g = grad_unit(k, r)
        s0[i] = remote(g.at[:, :, nc], RC.at[i], rs_s.at[0, i], rs_r.at[0, i], core_peer)

    def add_low(a, b):
        return (a.astype(F32) + b.astype(F32)).astype(BF16)

    top, low = pl.ds(0, HALF), pl.ds(HALF, HALF)

    def sum_one(i):
        k, r = order[i]
        g = grad_unit(k, r)
        s0[i].wait_recv()

        def block(j, carry):
            jy, jx = j // 2, j % 2
            g[jy, jx, c] = add_low(g[jy, jx, c], RC[i, jy, jx])
            return carry

        lax.fori_loop(0, 4, block, 0, unroll=True)
        if k == ATT:
            part_a, part_b = g.at[:, nx, c, top], g.at[ny, :, c, low]
            peer_a, peer_b = x_peer, y_peer
        else:
            part_a, part_b = g.at[ny, :, c, top], g.at[:, nx, c, low]
            peer_a, peer_b = y_peer, x_peer
        sa1[i] = remote(part_a, RA1.at[i], rs_s.at[1, i], rs_r.at[1, i], peer_a)
        sb1[i] = remote(part_b, RB1.at[i], rs_s.at[2, i], rs_r.at[2, i], peer_b)

    def sum_two(i):
        k, r = order[i]
        g = grad_unit(k, r)
        sa1[i].wait_recv()
        if k == ATT:
            for j in range(2):
                g[j, x, c, 0:HALF, :] = add_low(g[j, x, c, 0:HALF, :], RA1[i, j])
            sa2[i] = remote(g.at[ny, x, c, top], RA2.at[i - 8], rs_s.at[3, i], rs_r.at[3, i], y_peer)
            sb1[i].wait_recv()
            for j in range(2):
                g[y, j, c, HALF:BLK, :] = add_low(g[y, j, c, HALF:BLK, :], RB1[i, j])
            sb2[i] = remote(g.at[y, nx, c, low], RB2.at[i - 8], rs_s.at[4, i], rs_r.at[4, i], x_peer)
        else:
            sb1[i].wait_recv()
            for j in range(2):
                g[y, j, c, 0:HALF, :] = add_low(g[y, j, c, 0:HALF, :], RA1[i, j])
                g[j, x, c, HALF:BLK, :] = add_low(g[j, x, c, HALF:BLK, :], RB1[i, j])

    def sum_three(i):
        g = grad_unit(*order[i])
        sa2[i].wait_recv()
        g[y, x, c, 0:HALF, :] = add_low(g[y, x, c, 0:HALF, :], RA2[i - 8])
        sb2[i].wait_recv()
        g[y, x, c, HALF:BLK, :] = add_low(g[y, x, c, HALF:BLK, :], RB2[i - 8])

    landing = {1: 0, 3: 1, 2: 2}

    def z_wait(k, r):
        i = order.index((k, r))
        sza[i].wait_recv()
        if k != ATT:
            szb[i].wait_recv()

    def z_add(k, g, slot):
        if k == ATT:
            g[y, x, c] = add_low(g[y, x, c], RZ[slot])
        else:
            for j in range(2):
                g[y, j, c, 0:HALF, :] = add_low(g[y, j, c, 0:HALF, :], RZF[k - 1, slot, 0, j])
                g[j, x, c, HALF:BLK, :] = add_low(g[j, x, c, HALF:BLK, :], RZF[k - 1, slot, 1, j])

    def sum_z(i):
        k, r = order[i]
        g = grad_unit(k, r)
        if r == 2:
            z_wait(k, 3)
            z_add(k, g, landing[3])
        if r:
            peer = z_peer[2] if r == 2 else z_peer[1]
            if k == ATT:
                sza[i] = remote(g.at[y, x, c], RZ.at[landing[r]], rs_s.at[5, i], rs_r.at[5, i], peer)
            else:
                land = RZF.at[k - 1, landing[r]]
                sza[i] = remote(g.at[y, :, c, top], land.at[0], rs_s.at[5, i], rs_r.at[5, i], peer)
                szb[i] = remote(g.at[:, x, c, low], land.at[1], rs_s.at[6, i], rs_r.at[6, i], peer)
        else:
            z_wait(k, 1)
            z_wait(k, 2)
            if k != ATT:
                for j in range(2):
                    a, b = RZF[k - 1, 0, 0, j].astype(F32), RZF[k - 1, 2, 0, j].astype(F32)
                    g[y, j, c, 0:HALF, :] = add_low(g[y, j, c, 0:HALF, :], a + b)
                    a, b = RZF[k - 1, 0, 1, j].astype(F32), RZF[k - 1, 2, 1, j].astype(F32)
                    g[j, x, c, HALF:BLK, :] = add_low(g[j, x, c, HALF:BLK, :], a + b)
                sfa[k] = remote(g.at[y, nx, c, top], RF.at[k - 1, 0], rs_s.at[7, k], rs_r.at[7, k], x_peer)
                sfb[k] = remote(g.at[ny, x, c, low], RF.at[k - 1, 1], rs_s.at[8, k], rs_r.at[8, k], y_peer)

    def sum_final(k):
        own = grad_unit(k, 0)[y, x, c].astype(F32)
        if k == ATT:
            return own + (RZ[0].astype(F32) + RZ[2].astype(F32))
        sfa[k].wait_recv()
        sfb[k].wait_recv()
        return own + jnp.concatenate([RF[k - 1, 0], RF[k - 1, 1]], axis=0).astype(F32)

    def store_unit(ref, parts):
        for start, size, value in parts:
            ref[:, :, :, :, start : start + size] = value().astype(BF16).reshape(2, 2, 2, BLK, size)

    def store_ffn(k, r, lhs_t, rhs):
        ref = grad_unit(k, r)

        def block(n, carry):
            part = pl.ds(pl.multiple_of(n * 256, 256), 256)
            value = mm(lhs_t[...], rhs[:, part])
            ref[:, :, :, :, part] = value.astype(BF16).reshape(2, 2, 2, BLK, 256)
            return carry

        lax.fori_loop(0, 3, block, 0, unroll=True)

    def ffn_back_one(r):
        ga = mm_nt(FDL[...], cols(DOWN, r, 0, 768))
        GU[...] = (ga * DG[r].astype(F32)).astype(BF16)

    def ffn_back_two(r):
        accumulate(r == turn[0], mm_nt(GU[...], cols(UP, r, 0, 768)))

    def grad_down(r):
        store_ffn(DOWN, r, FDLT, ACT.at[r])
        sum_start(order.index((DOWN, r)))

    def grad_up(r):
        store_ffn(UP, r, FLT, GU)
        sum_start(order.index((UP, r)))

    def l1(k, start, size):
        return unit_value(L1.at[k, :, :, :, :, pl.ds(start, size)])

    live = {}

    def token_one():
        unit = W.at[ATT, z]
        kv_weight = jnp.concatenate([unit[0, 1].reshape(192, 768), unit[1, 0].reshape(192, 768)], axis=0)

        def rows_of(i, carry):
            rows = pl.ds(pl.multiple_of(i * 256, 256), 256)
            ACT[i, :, 0:384] = mm_nt(XA[rows, :], kv_weight).astype(BF16)
            return carry

        lax.fori_loop(0, 4, rows_of, 0)
        x8 = jnp.concatenate([XA[i * SEG : i * SEG + 16, :].astype(F32)[0:1] for i in range(8)], axis=0)
        live["x8"] = x8
        q8 = mm_nt(x8.astype(BF16), unit[0, 0].reshape(192, 768)).astype(BF16).astype(F32)
        row = lax.broadcasted_iota(jnp.int32, (8, 1024), 0)
        keep = lax.broadcasted_iota(jnp.int32, (8, 1024), 1) // SEG == row
        mixes = []
        for h in range(3):
            q = q8[:, h * 64 : h * 64 + 64].astype(BF16)
            parts = [mm_nt(q, ACT[i, :, h * 64 : h * 64 + 64]) for i in range(4)]
            scores = jnp.where(keep, jnp.concatenate(parts, axis=1) * SCALE, -3.0e38)
            top = jnp.max(scores, axis=-1, keepdims=True)
            expd = jnp.exp(scores - top)
            prob = (expd * (1.0 / jnp.sum(expd, axis=-1, keepdims=True))).astype(BF16)
            mix = None
            for i in range(4):
                val = ACT[i, :, 192 + h * 64 : 256 + h * 64]
                part = mm(prob[:, i * 256 : i * 256 + 256], val)
                mix = part if mix is None else mix + part
            mixes.append(mix)
        exchange(0, mm(jnp.concatenate(mixes, axis=-1).astype(BF16), out_rows(unit)))

    def token_two():
        attended = exchange_sum(0)
        scaled, _ = normalize(live["x8"] + attended)
        first = scaled * g00 + b00
        live["first8"] = first
        loads["wu"].wait()
        loads["wd"].wait()
        active, _ = gelu_pair(mm(first.astype(BF16), cols(UP, 0, 0, 768)))
        exchange(1, mm(active.astype(BF16), cols(DOWN, 0, 0, 768)))

    def cross_one():
        fed = exchange_sum(1)
        scaled, _ = normalize(live["first8"] + fed)
        summary = scaled * g01 + b01
        live["summary"] = summary
        live["summary_low"] = summary.astype(BF16)
        for name in ("l1qk", "l1v", "l1o"):
            loads[name].wait()
        qkv = mm_nt(live["summary_low"], qkv_rows(L1.at[ATT])).astype(BF16).astype(F32)
        pad = jnp.zeros((120, 64), F32)
        ids = jnp.broadcast_to(doc_ref[...].astype(F32), (8, 8))
        eye = lax.broadcasted_iota(jnp.int32, (8, 8), 0) == lax.broadcasted_iota(jnp.int32, (8, 8), 1)
        same = ids == jnp.sum(jnp.where(eye, ids, 0.0), axis=1, keepdims=True)
        keep = jnp.concatenate([jnp.where(same, 1.0, 0.0), jnp.zeros((8, 120), F32)], axis=1) > 0.5
        mixes = []
        for h in range(3):
            q = qkv[:, h * 64 : h * 64 + 64].astype(BF16)
            key = jnp.concatenate([qkv[:, 192 + h * 64 : 256 + h * 64], pad], axis=0).astype(BF16)
            val = jnp.concatenate([qkv[:, 384 + h * 64 : 448 + h * 64], pad], axis=0).astype(BF16)
            scores = jnp.where(keep, mm_nt(q, key) * SCALE, MASK_FILL)
            top = jnp.max(scores, axis=-1, keepdims=True)
            expd = jnp.exp(scores - top)
            prob = expd * (1.0 / jnp.sum(expd, axis=-1, keepdims=True))
            live["prob", h], live["q", h], live["key", h], live["val", h] = prob, q, key, val
            mixes.append(mm(prob.astype(BF16), val))
        mix = jnp.concatenate(mixes, axis=-1).astype(BF16)
        live["mix"] = mix
        exchange(2, mm(mix, out_rows(L1.at[ATT])))

    def cross_two():
        attended = exchange_sum(2)
        live["xs1"], live["xi1"] = normalize(live["summary"] + attended)
        first = live["xs1"] * g10 + b10
        live["xfirst"] = first
        live["xfirst_low"] = first.astype(BF16)
        loads["l1u"].wait()
        loads["l1d"].wait()
        active, live["xdg"] = gelu_pair(mm(live["xfirst_low"], l1(UP, 0, 768)))
        live["xact"] = active.astype(BF16)
        exchange(3, mm(live["xact"], l1(DOWN, 0, 768)))

    def cross_three():
        fed = exchange_sum(3)
        xs2, xi2 = normalize(live["xfirst"] + fed)
        upper = xs2 * g11 + b11
        for j in range(2):
            GS[j, 1:2, :] = own_row(upper, j)
        loads["c8"].wait()
        grad_top = C8[...].astype(F32)[:, 0, :]
        live["xs2"], live["xi2"] = xs2, xi2
        grad_fed = normalize_back(grad_top, live["xs2"], live["xi2"], g11)
        NV[5:6, :] = jnp.sum(grad_top * live["xs2"], axis=0, keepdims=True)
        NV[7:8, :] = jnp.sum(grad_top, axis=0, keepdims=True)
        live["xgf"] = grad_fed
        live["xfed_low"] = grad_fed.astype(BF16)
        ga = mm_nt(live["xfed_low"], l1(DOWN, 0, 768))
        live["xgu"] = (ga * live["xdg"]).astype(BF16)
        exchange(4, mm_nt(live["xgu"], l1(UP, 0, 768)))

    def cross_four():
        grad_first = live["xgf"] + exchange_sum(4)
        grad_att = normalize_back(grad_first, live["xs1"], live["xi1"], g10)
        NV[4:5, :] = jnp.sum(grad_first * live["xs1"], axis=0, keepdims=True)
        NV[6:7, :] = jnp.sum(grad_first, axis=0, keepdims=True)
        live["xga"] = grad_att
        att_low = grad_att.astype(BF16)
        live["xatt_low"] = att_low
        gm = mm_nt(att_low, out_rows(L1.at[ATT])).astype(BF16)
        gqs, gks, gvs = [], [], []
        for h in range(3):
            gmh = gm[:, h * 64 : h * 64 + 64]
            prob = live["prob", h]
            gp = mm_nt(gmh, live["val", h])
            inner = jnp.sum(gp * prob, axis=-1, keepdims=True)
            gs = (prob * (gp - inner)).astype(BF16)
            gqs.append(mm(gs, live["key", h]) * SCALE)
            gks.append(mm_tn(gs, live["q", h])[0:8, :] * SCALE)
            gvs.append(mm_tn(prob.astype(BF16), gmh)[0:8, :])
        gqkv = jnp.concatenate(gqs + gks + gvs, axis=-1).astype(BF16)
        live["xgqkv"] = gqkv
        exchange(5, mm(gqkv, qkv_rows(L1.at[ATT])))

    def cross_five():
        grad_summary = live["xga"] + exchange_sum(5)
        for j in range(2):
            GS[j, 0:1, :] = own_row(grad_summary, j)

    def output_rows():
        for j in range(2):
            out_ref[0, j * 128 : j * 128 + 1, :] = GS[j, 1:2, :].astype(BF16)

    def norm_one_back():
        def chunk(i, rows, carry):
            gains, shifts = carry
            grad = GF[rows, :] + ACC[rows, :]
            scaled = SC1[rows, :]
            att = normalize_back(grad, scaled, INV1[rows, 0:1], g00)
            GF[rows, :] = att
            FDL[rows, :] = att.astype(BF16)
            return (
                gains + jnp.sum(grad * scaled, axis=0, keepdims=True),
                shifts + jnp.sum(grad, axis=0, keepdims=True),
            )

        zero = jnp.zeros((1, 768), F32)
        gains, shifts = row_chunks(chunk, (zero, zero))
        NV[0:1, :] = gains
        NV[2:3, :] = shifts

    def attn_backward(r):
        GM[...] = mm_nt(FDL[...], out_rows(W.at[ATT, z_of[r]])).astype(BF16)

        def segment(s, carry):
            rows = pl.ds(pl.multiple_of(s * SEG, SEG), SEG)
            qkv = QKV[r, rows, :]
            gm = GM[rows, :]
            gqs, gks, gvs = [], [], []
            for h in range(3):
                q = qkv[:, h * 64 : h * 64 + 64]
                key = qkv[:, 192 + h * 64 : 256 + h * 64]
                val = qkv[:, 384 + h * 64 : 448 + h * 64]
                gmh = gm[:, h * 64 : h * 64 + 64]
                prob = PR[r, h, rows, :]
                gp = mm_nt(gmh, val)
                inner = jnp.sum(gp * prob, axis=-1, keepdims=True)
                gs = (prob * (gp - inner)).astype(BF16)
                gqs.append(mm(gs, key) * SCALE)
                gks.append(mm_tn(gs, q) * SCALE)
                gvs.append(mm_tn(prob.astype(BF16), gmh))
            GQ[rows, :] = jnp.concatenate(gqs + gks + gvs, axis=-1).astype(BF16)
            return carry

        lax.fori_loop(0, 2, segment, 0, unroll=True)
        store_unit(
            grad_unit(ATT, r),
            [
                (0, 576, lambda: mm(XT[...], GQ[...])),
                (576, 192, lambda: mm(FDLT[...], MIX[r])),
            ],
        )
        sum_start(order.index((ATT, r)))
        accumulate(r == turn[0], mm(GQ[...], qkv_rows(W.at[ATT, z_of[r]])))

    fac = {}

    def factor_start():
        wide = lambda v: v.astype(F32)
        zero_a, zero_b = jnp.zeros((8, 192), F32), jnp.zeros((8, 576), F32)
        att_left = jnp.concatenate([wide(live["xgqkv"]), zero_a], axis=-1)
        att_right = jnp.concatenate([zero_b, wide(live["mix"])], axis=-1)
        right = jnp.concatenate([wide(live["xact"]), wide(live["xgu"]), att_left, att_right], axis=0)
        left = jnp.concatenate(
            [wide(live["xfed_low"]), wide(live["xfirst_low"]), wide(live["summary_low"]), wide(live["xatt_low"])],
            axis=0,
        )
        FAC[y, x, c, 0:32, :] = right.astype(BF16)
        FAC[y, x, c, 32:64, :] = left.astype(BF16)
        part = FAC.at[y, x, c]
        fac[0] = remote(part, part, f_s.at[0], f_r.at[0], x_peer)

    def factor_two():
        fac[0].wait_recv()
        part = FAC.at[y, :, c]
        fac[1] = remote(part, part, f_s.at[1], f_r.at[1], y_peer)

    def factor_three():
        fac[1].wait_recv()
        part = FAC.at[:, :, c]
        fac[2] = remote(part, part, f_s.at[2], f_r.at[2], core_peer)

    def turn_rows(value):
        rows = value.shape[0]
        full = jnp.concatenate([value, jnp.zeros((128 - rows, value.shape[1]), F32)], axis=0)
        return full.T[:, 0:rows]

    def write_unit(layer, k, value):
        if k == ATT:
            for i in range(3):
                qkvg_ref[layer, i] = value[:, i * 192 : i * 192 + 192]
            outg_ref[layer] = turn_rows(value[:, 576:768])
        elif k == UP:
            upg_ref[layer] = value
        else:
            downg_ref[layer] = value

    def factor_final():
        fac[2].wait_recv()
        left = FAC[:, :, :, 32:64, :].reshape(256, 768)
        for i in range(2):
            LT[:, i * 128 : i * 128 + 128] = left[i * 128 : i * 128 + 128, :].T
        mine = LT[pl.ds(pl.multiple_of(dp * BLK, BLK), BLK), :].astype(F32)
        kind = (lax.broadcasted_iota(jnp.int32, (BLK, 256), 1) // 8) % 4
        right = FAC[:, :, :, 0:32, :].reshape(256, 768)
        write_unit(1, DOWN, mm(jnp.where(kind == 0, mine, 0.0).astype(BF16), right))
        write_unit(1, UP, mm(jnp.where(kind == 1, mine, 0.0).astype(BF16), right))
        write_unit(1, ATT, mm(jnp.where(kind >= 2, mine, 0.0).astype(BF16), right))

    vec = {}

    def norm_grads_start():
        exchange(6, NV[...])

    def norm_grads_two():
        total = jnp.where(row_of < 4, exchange_sum(6), NV[...])
        pad = jnp.zeros((8, 32), F32)
        for p in range(8):
            SV[p // 4, (p // 2) % 2, p % 2] = jnp.concatenate([total[:, p * BLK : p * BLK + BLK], pad], axis=-1)
        for m in range(1, 8):
            ty = y if m // 4 == 0 else ny
            tx = x if (m // 2) % 2 == 0 else nx
            tc = c if m % 2 == 0 else nc
            vec[m] = remote(
                SV.at[ty, tx, tc], RSV.at[m - 1], v_s.at[m - 1], v_r.at[m - 1], (plane_index(m), z)
            )

    def norm_grads_final():
        total = SV[y, x, c]
        for m in range(1, 8):
            vec[m].wait_recv()
            total = total + RSV[m - 1]
        gaing_ref[...] = total[0:2, 0:BLK]
        shiftg_ref[...] = total[2:4, 0:BLK]
        crossg_ref[0] = total[4:6, 0:BLK]
        crossg_ref[1] = total[6:8, 0:BLK]

    def turn_to_attention():
        norm_one_back()
        norm_grads_start()
        transpose_into(FDLT, FDL)
        for table in (a1, b1, a2, b2, a3, b3, cc):
            for i in range(9):
                table[i].wait_send()
                waited.append(id(table[i]))
        for condition, copy in passed:

            @pl.when(condition)
            def _(copy=copy):
                copy.wait_send()

    for name in ("wqk", "wv", "wo"):
        loads[name].wait()
    z_own(ATT)
    loads["x"].wait()
    token_one()
    z_own(UP)
    attn_forward(0)
    transpose_into(XT, XA, z * 256)
    gather_a(0)
    gather_a(1)
    token_two()
    gather_b(0)
    gather_a(2)
    z_own(DOWN)
    gather_b(1)
    gather_c(0)
    gather_b(2)
    gather_a(3)
    cross_one()
    gather_c(1)
    gather_a(4)
    gather_a(5)
    attn_forward(1)
    gather_c(2)
    gather_b(3)
    gather_b(4)
    cross_two()
    attn_forward(2)
    gather_b(5)
    gather_a(6)
    gather_a(7)
    gather_c(3)
    gather_c(4)
    cross_three()
    gather_c(5)
    attn_forward(3)
    gather_b(6)
    gather_a(8)
    norm_one()
    ffn_forward(2)
    gather_b(7)
    ffn_forward(1)
    ffn_forward(0)
    ffn_down(0)
    gather_c(6)
    cross_four()
    gather_b(8)
    ffn_down(1)
    transpose_into(FLT, FL)
    ffn_forward(3)
    gather_c(7)
    gather_c(8)
    factor_start()
    ffn_down(2)
    cross_five()
    ffn_down(3)
    norm_two()
    output_rows()
    transpose_into(FDLT, FDL)
    factor_two()
    grad_down(3)
    ffn_back_one(3)
    grad_up(3)
    ffn_back_two(3)
    ffn_back_one(2)
    grad_down(2)
    sum_one(0)
    grad_up(2)
    sum_one(1)
    ffn_back_two(2)
    ffn_back_one(1)
    sum_one(2)
    grad_down(1)
    sum_one(3)
    grad_up(1)
    grad_down(0)
    sum_two(0)
    sum_z(0)
    sum_one(4)
    ffn_back_two(1)
    ffn_back_one(0)
    sum_one(5)
    sum_two(1)
    sum_one(6)
    sum_z(1)
    grad_up(0)
    ffn_back_two(0)
    turn_to_attention()
    sum_two(2)
    attn_backward(3)
    sum_two(3)
    sum_one(7)
    sum_z(2)
    attn_backward(2)
    sum_two(4)
    sum_one(8)
    sum_z(4)
    attn_backward(1)
    sum_z(3)
    sum_one(9)
    sum_two(5)
    sum_z(5)
    sum_two(6)
    attn_backward(0)
    sum_two(7)
    factor_three()
    ing_ref[0] = (GF[...] + ACC[...]).astype(BF16)
    norm_grads_two()
    sum_two(8)
    sum_one(10)
    factor_final()
    sum_two(9)
    sum_z(6)
    sum_one(11)
    sum_three(8)
    sum_z(8)
    sum_two(10)
    sum_three(9)
    write_unit(0, DOWN, sum_final(DOWN))
    sum_z(9)
    sum_two(11)
    sum_z(7)
    sum_three(10)
    sum_z(10)
    sum_three(11)
    write_unit(0, UP, sum_final(UP))
    sum_z(11)
    norm_grads_final()
    write_unit(0, ATT, sum_final(ATT))
    for copy in sends:
        if id(copy) not in waited:
            copy.wait_send()


def settle_kernel(*refs):
    sources, targets, sems = refs[:9], refs[9:18], refs[18]
    copies = [pltpu.make_async_copy(sources[i], targets[i], sems.at[i]) for i in range(9)]
    for copy in copies:
        copy.start()
    for copy in copies:
        copy.wait()


def fused_body(
    inputs, doc_ids, qkv_weight, out_weight, up_weight, down_weight, norm_gain, norm_shift, cotangent
):
    wq = qkv_weight.swapaxes(2, 3).reshape(2, 3, 2, BLK, 768)
    wo = out_weight.reshape(2, 2, BLK, 768)
    wu = up_weight.reshape(2, 2, 2, 2, BLK, 768)
    wd = down_weight.reshape(2, 2, 2, 2, BLK, 768)
    whole = pl.BlockSpec(memory_space=pl.ANY)
    vmem = pl.BlockSpec(memory_space=pltpu.VMEM)
    blocks = (2, 2, 2, BLK, 768)
    sem = pltpu.SemaphoreType.DMA
    results = pl.pallas_call(
        fused_kernel,
        out_shape=(
            pltpu.VMEM((1, 256, 768), BF16),
            pltpu.VMEM((1, 256, 768), BF16),
            pltpu.VMEM((2, 3, BLK, 192), F32),
            pltpu.VMEM((2, 192, BLK), F32),
            pltpu.VMEM((2, BLK, 768), F32),
            pltpu.VMEM((2, BLK, 768), F32),
            pltpu.VMEM((2, BLK), F32),
            pltpu.VMEM((2, BLK), F32),
            pltpu.VMEM((2, 2, BLK), F32),
        ),
        in_specs=[whole, whole, whole, vmem, whole, whole, whole, whole, vmem, vmem],
        out_specs=(vmem,) * 9,
        scratch_shapes=[
            pltpu.VMEM((3, 4) + blocks, BF16),
            pltpu.VMEM((2, 4) + blocks, BF16),
            pltpu.VMEM((12, 2, 2, BLK, 768), BF16),
            pltpu.VMEM((12, 2, HALF, 768), BF16),
            pltpu.VMEM((12, 2, HALF, 768), BF16),
            pltpu.VMEM((4, HALF, 768), BF16),
            pltpu.VMEM((4, HALF, 768), BF16),
            pltpu.VMEM((3, BLK, 768), BF16),
            pltpu.VMEM((2, 3, 2, 2, HALF, 768), BF16),
            pltpu.VMEM((2, 2, HALF, 768), BF16),
            pltpu.VMEM((3,) + blocks, BF16),
            pltpu.VMEM((1024, 768), BF16),
            pltpu.VMEM((256, 768), BF16),
            pltpu.VMEM((4, 256, 576), BF16),
            pltpu.VMEM((4, 3, 256, 128), F32),
            pltpu.VMEM((4, 256, 192), BF16),
            pltpu.VMEM((4, 256, 768), BF16),
            pltpu.VMEM((4, 256, 768), BF16),
            pltpu.VMEM((256, 768), BF16),
            pltpu.VMEM((256, 576), BF16),
            pltpu.VMEM((256, 768), F32),
            pltpu.VMEM((256, 768), F32),
            pltpu.VMEM((256, 768), F32),
            pltpu.VMEM((256, 768), BF16),
            pltpu.VMEM((768, 256), BF16),
            pltpu.VMEM((256, 768), BF16),
            pltpu.VMEM((768, 256), BF16),
            pltpu.VMEM((768, 256), BF16),
            pltpu.VMEM((256, 192), BF16),
            pltpu.VMEM((8, 16, 768), BF16),
            pltpu.VMEM((256, 128), F32),
            pltpu.VMEM((2, 2, 2, 64, 768), BF16),
            pltpu.VMEM((768, 256), BF16),
            pltpu.VMEM((2, 8, 768), F32),
            pltpu.VMEM((7, 4, 8, 768), F32),
            pltpu.VMEM((8, 768), F32),
            pltpu.VMEM((2, 2, 2, 8, 128), F32),
            pltpu.VMEM((7, 8, 128), F32),
            sem((13,)),
            sem((12, 2)),
            sem((12,)),
            sem((7, 9)),
            sem((7, 9)),
            sem((9, 12)),
            sem((9, 12)),
            sem((7, 3)),
            sem((7, 3)),
            sem((3,)),
            sem((3,)),
            sem((7,)),
            sem((7,)),
        ],
        compiler_params=pltpu.CompilerParams(
            collective_id=0, has_side_effects=True, vmem_limit_bytes=59 * 2**20
        ),
    )(
        inputs, cotangent, cotangent.reshape(8, SEG, 768), doc_ids, wq, wo, wu, wd, norm_gain, norm_shift
    )
    final = pl.pallas_call(
        settle_kernel,
        out_shape=tuple(jax.ShapeDtypeStruct(v.shape, v.dtype) for v in results),
        in_specs=[whole] * 9,
        out_specs=(whole,) * 9,
        scratch_shapes=[sem((9,))],
    )(*[pltpu.with_memory_space_constraint(v, pltpu.VMEM) for v in results])
    return final[:5] + (final[5].swapaxes(1, 2),) + final[6:]


def solution(mesh):
    in_specs = (
        P("dp", None, None),
        P("dp", None),
        P(None, None, None, "tensor"),
        P(None, "tensor", None),
        P(None, None, "tensor"),
        P(None, "tensor", None),
        P(),
        P(),
        P("dp", None, None),
    )
    out_specs = (
        P("dp", "tensor", None),
        P("dp", "tensor", None),
        P(None, None, "dp", "tensor"),
        P(None, "tensor", "dp"),
        P(None, "dp", "tensor"),
        P(None, "tensor", "dp"),
        P(None, "dp"),
        P(None, "dp"),
        P(None, None, "dp"),
    )
    fits = dict(mesh.shape) == {"dp": 8, "tensor": 4}
    chosen = fused_body if fits else body
    return jax.shard_map(chosen, mesh=mesh, in_specs=in_specs, out_specs=out_specs, check_vma=False)
```

```python
from functools import partial
import math

import jax
import jax.numpy as jnp
from jax import lax
from jax.experimental import pallas as pl
from jax.experimental.pallas import tpu as pltpu
from jax.sharding import PartitionSpec as P

HEAD_DIM = 64
SEG = 128


EPSILON = 1e-05
MASK_FILL = -1000000000.0


def layer_norm(values, gain_row, shift_row):
    center = jnp.mean(values, axis=-1, keepdims=True)
    offset = values - center
    spread = jnp.mean(offset * offset, axis=-1, keepdims=True)
    inverse = lax.rsqrt(spread + EPSILON)
    scaled = offset * inverse
    return (scaled * gain_row + shift_row, (scaled, inverse))


def norm_back(grad_out, saved, gain_row):
    scaled, inverse = saved
    weighted = grad_out * gain_row
    mean_one = jnp.mean(weighted, axis=-1, keepdims=True)
    mean_two = jnp.mean(weighted * scaled, axis=-1, keepdims=True)
    grad_in = inverse * (weighted - mean_one - scaled * mean_two)
    return (grad_in, jnp.sum(grad_out * scaled, axis=(0, 1)), jnp.sum(grad_out, axis=(0, 1)))


def score_block(head_split, allowed):
    scores = jnp.einsum(
        "bqhe,bkhe->bhqk", head_split[0], head_split[1], preferred_element_type=jnp.float32
    ) * (1.0 / math.sqrt(HEAD_DIM))
    if allowed is not None:
        scores = jnp.where(allowed, scores, MASK_FILL)
    return scores


def attend_forward(rows_low, qkv_local, allowed):
    batch_count = rows_low.shape[0]
    length = rows_low.shape[1]
    project = jnp.einsum(
        "brd,cde->cbre", rows_low, qkv_local, preferred_element_type=jnp.float32
    ).astype(jnp.bfloat16)
    head_split = project.reshape(3, batch_count, length, -1, HEAD_DIM)
    scores = score_block(head_split, allowed)
    log_total = jax.nn.logsumexp(scores, axis=-1)
    soft_low = jnp.exp(scores - log_total[..., None]).astype(jnp.bfloat16)
    mixture = jnp.einsum(
        "bhqk,bkhe->bqhe", soft_low, head_split[2], preferred_element_type=jnp.float32
    )
    return (project, log_total, mixture.astype(jnp.bfloat16).reshape(batch_count, length, -1))


def attend_backward(rows_low, qkv_local, out_local, project, log_total, mixture, grad_low, allowed):
    batch_count = rows_low.shape[0]
    length = rows_low.shape[1]
    head_split = project.reshape(3, batch_count, length, -1, HEAD_DIM)
    grad_mixture = jnp.einsum(
        "brd,fd->brf", grad_low, out_local, preferred_element_type=jnp.float32
    ).astype(jnp.bfloat16)
    out_local_grad = jnp.einsum(
        "brf,brd->fd", mixture, grad_low, preferred_element_type=jnp.float32
    )
    grad_heads = grad_mixture.reshape(batch_count, length, -1, HEAD_DIM)
    scores = score_block(head_split, allowed)
    soft_full = jnp.exp(scores - log_total[..., None])
    grad_soft = jnp.einsum(
        "bqhe,bkhe->bhqk", grad_heads, head_split[2], preferred_element_type=jnp.float32
    )
    row_inner = jnp.sum(grad_soft * soft_full, axis=-1, keepdims=True)
    grad_scores = (soft_full * (grad_soft - row_inner)).astype(jnp.bfloat16)
    scale_factor = 1.0 / math.sqrt(HEAD_DIM)
    grad_query = (
        jnp.einsum(
            "bhqk,bkhe->bqhe", grad_scores, head_split[1], preferred_element_type=jnp.float32
        )
        * scale_factor
    )
    grad_key = (
        jnp.einsum(
            "bhqk,bqhe->bkhe", grad_scores, head_split[0], preferred_element_type=jnp.float32
        )
        * scale_factor
    )
    grad_value = jnp.einsum(
        "bhqk,bqhe->bkhe",
        soft_full.astype(jnp.bfloat16),
        grad_heads,
        preferred_element_type=jnp.float32,
    )
    grad_project = (
        jnp.stack([grad_query, grad_key, grad_value])
        .reshape(3, batch_count, length, -1)
        .astype(jnp.bfloat16)
    )
    qkv_local_grad = jnp.einsum(
        "brd,cbre->cde", rows_low, grad_project, preferred_element_type=jnp.float32
    )
    input_part = jnp.einsum(
        "cbre,cde->brd", grad_project, qkv_local, preferred_element_type=jnp.float32
    )
    return (input_part, qkv_local_grad, out_local_grad)


def expand_forward(rows_low, up_local, down_local):
    upward = jnp.einsum("brd,df->brf", rows_low, up_local, preferred_element_type=jnp.float32)
    active = jax.nn.gelu(upward, approximate=False).astype(jnp.bfloat16)
    return (
        upward,
        active,
        jnp.einsum("brf,fd->brd", active, down_local, preferred_element_type=jnp.float32),
    )


def expand_backward(rows_low, up_local, down_local, upward, active, grad_low):
    grad_active = jnp.einsum(
        "brd,fd->brf", grad_low, down_local, preferred_element_type=jnp.float32
    )
    down_local_grad = jnp.einsum(
        "brf,brd->fd", active, grad_low, preferred_element_type=jnp.float32
    )
    gelu_pull = jax.vjp(partial(jax.nn.gelu, approximate=False), upward)[1]
    grad_upward = gelu_pull(grad_active)[0].astype(jnp.bfloat16)
    up_local_grad = jnp.einsum(
        "brd,brf->df", rows_low, grad_upward, preferred_element_type=jnp.float32
    )
    input_part = jnp.einsum(
        "brf,df->brd", grad_upward, up_local, preferred_element_type=jnp.float32
    )
    return (input_part, up_local_grad, down_local_grad)


def body(
    inputs,
    doc_ids,
    qkv_weight,
    out_weight,
    up_weight,
    down_weight,
    norm_gain,
    norm_shift,
    cotangent,
):
    groups = lax.axis_size("tensor")
    position = lax.axis_index("tensor")
    model_width = inputs.shape[2]
    segment_count = inputs.shape[1] // SEG
    own_count = segment_count // groups
    row_start = position * own_count

    def final_rows(values):
        return lax.dynamic_slice_in_dim(values, row_start, own_count, 0)

    def forward_sum(partial_term):
        return lax.psum(partial_term.astype(jnp.bfloat16), "tensor").astype(jnp.float32)

    def backward_sum(partial_term):
        return lax.psum(partial_term.astype(jnp.bfloat16), "tensor").astype(jnp.float32)

    def cross_sum(partial_term):
        return lax.psum(partial_term.astype(jnp.bfloat16), "tensor").astype(jnp.float32)

    def cross_grad_sum(partial_term):
        return lax.psum(partial_term, "tensor")

    tokens = inputs[0].reshape(segment_count, SEG, model_width)
    tokens_wide = tokens.astype(jnp.float32)
    lower_proj, lower_total, lower_mix = attend_forward(tokens, qkv_weight[0], None)
    attended = forward_sum(
        jnp.einsum("brf,fd->brd", lower_mix, out_weight[0], preferred_element_type=jnp.float32)
    )
    first_norm, first_saved = layer_norm(tokens_wide + attended, norm_gain[0, 0], norm_shift[0, 0])
    first_low = first_norm.astype(jnp.bfloat16)
    lower_up, lower_active, fed_term = expand_forward(first_low, up_weight[0], down_weight[0])
    second, second_saved = layer_norm(
        first_norm + forward_sum(fed_term), norm_gain[0, 1], norm_shift[0, 1]
    )
    summary = second[:, 0, :]
    summary = summary[None]
    same_doc = (doc_ids[0][:, None] == doc_ids[0][None, :])[None, None]
    summary_low = summary.astype(jnp.bfloat16)
    upper_proj, upper_total, upper_mix = attend_forward(summary_low, qkv_weight[1], same_doc)
    upper_att = cross_sum(
        jnp.einsum("brf,fd->brd", upper_mix, out_weight[1], preferred_element_type=jnp.float32)
    )
    upper_first, upper_saved_one = layer_norm(
        summary + upper_att, norm_gain[1, 0], norm_shift[1, 0]
    )
    upper_first_low = upper_first.astype(jnp.bfloat16)
    upper_up, upper_active, upper_fed = expand_forward(
        upper_first_low, up_weight[1], down_weight[1]
    )
    upper_out, upper_saved_two = layer_norm(
        upper_first + cross_sum(upper_fed), norm_gain[1, 1], norm_shift[1, 1]
    )
    joined = second.at[:, 0, :].set(upper_out[0])
    outputs_own = final_rows(joined).reshape(1, -1, model_width).astype(jnp.bfloat16)
    grad_full = cotangent[0].reshape(segment_count, SEG, model_width).astype(jnp.float32)
    grad_top = grad_full[:, 0, :][None]
    grad_upper_fed, gain_cross_two, shift_cross_two = norm_back(
        grad_top, upper_saved_two, norm_gain[1, 1]
    )
    cross_part, up_cross, down_cross = expand_backward(
        upper_first_low,
        up_weight[1],
        down_weight[1],
        upper_up,
        upper_active,
        grad_upper_fed.astype(jnp.bfloat16),
    )
    grad_upper_first = grad_upper_fed + cross_grad_sum(cross_part)
    grad_upper_att, gain_cross_one, shift_cross_one = norm_back(
        grad_upper_first, upper_saved_one, norm_gain[1, 0]
    )
    cross_input_part, qkv_cross, out_cross = attend_backward(
        summary_low,
        qkv_weight[1],
        out_weight[1],
        upper_proj,
        upper_total,
        upper_mix,
        grad_upper_att.astype(jnp.bfloat16),
        same_doc,
    )
    grad_summary = grad_upper_att + cross_grad_sum(cross_input_part)
    grad_second = grad_full.at[:, 0, :].set(grad_summary[0])
    grad_fed, gain_seg_two, shift_seg_two = norm_back(grad_second, second_saved, norm_gain[0, 1])
    fed_low = grad_fed.astype(jnp.bfloat16)
    seg_part, up_seg, down_seg = expand_backward(
        first_low, up_weight[0], down_weight[0], lower_up, lower_active, fed_low
    )
    grad_first = grad_fed + backward_sum(seg_part)
    grad_att, gain_seg_one, shift_seg_one = norm_back(grad_first, first_saved, norm_gain[0, 0])
    att_low = grad_att.astype(jnp.bfloat16)
    seg_input_part, qkv_seg, out_seg = attend_backward(
        tokens, qkv_weight[0], out_weight[0], lower_proj, lower_total, lower_mix, att_low, None
    )
    input_full = grad_att + backward_sum(seg_input_part)
    input_own = final_rows(input_full).reshape(1, -1, model_width).astype(jnp.bfloat16)
    seg_gain = jnp.stack([gain_seg_one, gain_seg_two])
    seg_shift = jnp.stack([shift_seg_one, shift_seg_two])
    cross_norm = jnp.stack(
        [jnp.stack([gain_cross_one, gain_cross_two]), jnp.stack([shift_cross_one, shift_cross_two])]
    )
    qkv_all = jnp.stack([qkv_seg, qkv_cross])
    out_all = jnp.stack([out_seg, out_cross])
    up_all = jnp.stack([up_seg, up_cross])
    down_all = jnp.stack([down_seg, down_cross])
    summed = (
        lax.psum_scatter(qkv_all, "dp", scatter_dimension=2, tiled=True),
        lax.psum_scatter(out_all, "dp", scatter_dimension=2, tiled=True),
        lax.psum_scatter(up_all, "dp", scatter_dimension=1, tiled=True),
        lax.psum_scatter(down_all, "dp", scatter_dimension=2, tiled=True),
        lax.psum_scatter(seg_gain, "dp", scatter_dimension=1, tiled=True),
        lax.psum_scatter(seg_shift, "dp", scatter_dimension=1, tiled=True),
        lax.psum_scatter(cross_norm, "dp", scatter_dimension=2, tiled=True),
    )
    return (
        outputs_own,
        input_own,
        summed[0],
        summed[1],
        summed[2],
        summed[3],
        summed[4],
        summed[5],
        summed[6],
    )


MESH = pl.DeviceIdType.MESH
F32 = jnp.float32
BF16 = jnp.bfloat16
SCALE = 1.0 / math.sqrt(HEAD_DIM)
ATT, UP, DOWN = 0, 1, 2
BLK = 96
HALF = 48


def mm(a, b):
    return lax.dot_general(a, b, (((1,), (0,)), ((), ())), preferred_element_type=F32)


def mm_nt(a, b):
    return lax.dot_general(a, b, (((1,), (1,)), ((), ())), preferred_element_type=F32)


def mm_tn(a, b):
    return lax.dot_general(a, b, (((0,), (0,)), ((), ())), preferred_element_type=F32)


def normalize(values):
    center = jnp.mean(values, axis=-1, keepdims=True)
    offset = values - center
    spread = jnp.mean(offset * offset, axis=-1, keepdims=True)
    inverse = lax.rsqrt(spread + EPSILON)
    return offset * inverse, inverse


def normalize_back(grad_out, scaled, inverse, gain_row):
    weighted = grad_out * gain_row
    mean_one = jnp.mean(weighted, axis=-1, keepdims=True)
    mean_two = jnp.mean(weighted * scaled, axis=-1, keepdims=True)
    return inverse * (weighted - mean_one - scaled * mean_two)


def gelu_pair(upward):
    cdf = 0.5 * (1.0 + lax.erf(upward * math.sqrt(0.5)))
    pdf = jnp.exp(upward * upward * -0.5) * (1.0 / math.sqrt(2.0 * math.pi))
    return upward * cdf, cdf + upward * pdf


def fused_kernel(
    tokens_hbm, cot_hbm, cot_seg, doc_ref, wq_hbm, wo_hbm, wu_hbm, wd_hbm, gain_ref, shift_ref,
    out_ref, ing_ref, qkvg_ref, outg_ref, upg_ref, downg_ref, gaing_ref, shiftg_ref, crossg_ref,
    W, G, RC, RA1, RB1, RA2, RB2, RZ, RZF, RF, L1, XA, COT, QKV, PR, MIX, ACT, DG, GU, GQ, ACC, SC1, GF,
    FL, FLT, FDL, FDLT, XT, GM, C8, INV1, FAC, LT, GS, E, NV, SV, RSV,
    sem_local, zg_s, zg_r, ag_s, ag_r, rs_s, rs_r, e_s, e_r, f_s, f_r, v_s, v_r,
):
    dp = lax.axis_index("dp")
    z = lax.axis_index("tensor")
    c = dp % 2
    x = (dp // 2) % 2
    y = dp // 4
    nc, nx, ny = 1 - c, 1 - x, 1 - y
    core_peer = (dp + 1 - 2 * c, z)
    x_peer = (dp + 2 - 4 * x, z)
    y_peer = (dp + 4 - 8 * y, z)
    left_peer, right_peer = (dp, jnp.maximum(z - 1, 0)), (dp, jnp.minimum(z + 1, 3))
    z_peer = [None, (dp, z + 1 - 2 * (z % 2)), (dp, z + 2 - 4 * (z // 2)), (dp, 3 - z)]
    z_of = [z, z + 1 - 2 * (z % 2), z + 2 - 4 * (z // 2), 3 - z]

    def plane_index(m):
        ty = y if m // 4 == 0 else ny
        tx = x if (m // 2) % 2 == 0 else nx
        tc = c if m % 2 == 0 else nc
        return ty * 4 + tx * 2 + tc

    sends = []
    waited = []

    def remote(src, dst, ssem, rsem, target):
        copy = pltpu.make_async_remote_copy(
            src_ref=src, dst_ref=dst, send_sem=ssem, recv_sem=rsem, device_id=target, device_id_type=MESH
        )
        copy.start()
        sends.append(copy)
        return copy

    barrier = pltpu.get_barrier_semaphore()
    for m in range(1, 8):
        pl.semaphore_signal(barrier, inc=1, device_id=(plane_index(m), z), device_id_type=MESH)
    for r in range(1, 4):
        pl.semaphore_signal(barrier, inc=1, device_id=z_peer[r], device_id_type=MESH)

    loads = {}

    def load(name, index, src, dst):
        copy = pltpu.make_async_copy(src, dst, sem_local.at[index])
        copy.start()
        loads[name] = copy

    load("wqk", 1, wq_hbm.at[0, pl.ds(0, 2)], W.at[ATT, z, 0])
    load("wv", 9, wq_hbm.at[0, 2], W.at[ATT, z, 1, 0])
    load("wo", 10, wo_hbm.at[0], W.at[ATT, z, 1, 1])
    load("x", 0, tokens_hbm.at[0], XA)
    load("wu", 2, wu_hbm.at[0], W.at[UP, z])
    load("wd", 3, wd_hbm.at[0], W.at[DOWN, z])
    load("cot", 4, cot_hbm.at[0, pl.ds(pl.multiple_of(z * 256, 256), 256)], COT)
    load("l1qk", 5, wq_hbm.at[1, pl.ds(0, 2)], L1.at[ATT, 0])
    load("l1v", 11, wq_hbm.at[1, 2], L1.at[ATT, 1, 0])
    load("l1o", 12, wo_hbm.at[1], L1.at[ATT, 1, 1])
    load("l1u", 6, wu_hbm.at[1], L1.at[UP])
    load("l1d", 7, wd_hbm.at[1], L1.at[DOWN])
    load("c8", 8, cot_seg.at[:, pl.ds(0, 16)], C8)

    pl.semaphore_wait(barrier, 10)

    own_unit = [W.at[ATT, z], wu_hbm.at[0], wd_hbm.at[0]]
    units = [(ATT, 1), (UP, 1), (ATT, 2), (ATT, 3), (DOWN, 1), (UP, 2), (UP, 3), (DOWN, 2), (DOWN, 3)]
    a1, b1, a2, b2, a3, b3, cc = {}, {}, {}, {}, {}, {}, {}
    passed = []

    def z_copy(src, k, shard, side):
        return pltpu.make_async_remote_copy(
            src_ref=src,
            dst_ref=W.at[k, shard, y, x, c],
            send_sem=zg_s.at[k * 4 + shard, side],
            recv_sem=zg_r.at[k * 4 + shard],
            device_id=(left_peer, right_peer)[side],
            device_id_type=MESH,
        )

    def pass_on(condition, copy):
        @pl.when(condition)
        def _():
            copy.start()

        passed.append((condition, copy))

    def z_own(k):
        src = own_unit[k].at[y, x, c]
        pass_on(z > 0, z_copy(src, k, z, 0))
        pass_on(z < 3, z_copy(src, k, z, 1))

    def z_step(k, step):
        for side in range(2):
            shard = z - 1 - step if side else z + 1 + step
            there = shard >= 0 if side else shard <= 3
            further = jnp.logical_and(there, z < 3 if side else z > 0)
            shard = jnp.clip(shard, 0, 3)
            copy = z_copy(W.at[k, shard, y, x, c], k, shard, side)

            @pl.when(there)
            def _():
                copy.wait_recv()

            pass_on(further, copy)

    def gather_a(i):
        k, r = units[i]
        z_step(k, r - 1)
        upper = W.at[k, z_of[r], y, x, c, pl.ds(0, HALF)]
        lower = W.at[k, z_of[r], y, x, c, pl.ds(HALF, HALF)]
        a1[i] = remote(upper, upper, ag_s.at[0, i], ag_r.at[0, i], x_peer)
        b1[i] = remote(lower, lower, ag_s.at[1, i], ag_r.at[1, i], y_peer)
        a2[i] = remote(upper, upper, ag_s.at[2, i], ag_r.at[2, i], y_peer)
        b2[i] = remote(lower, lower, ag_s.at[3, i], ag_r.at[3, i], x_peer)

    def gather_b(i):
        k, r = units[i]
        a1[i].wait_recv()
        part = W.at[k, z_of[r], y, nx, c, pl.ds(0, HALF)]
        a3[i] = remote(part, part, ag_s.at[4, i], ag_r.at[4, i], y_peer)
        b1[i].wait_recv()
        part = W.at[k, z_of[r], ny, x, c, pl.ds(HALF, HALF)]
        b3[i] = remote(part, part, ag_s.at[5, i], ag_r.at[5, i], x_peer)

    def gather_c(i):
        k, r = units[i]
        for table in (a2, b2, a3, b3):
            table[i].wait_recv()
        part = W.at[k, z_of[r], :, :, c]
        cc[i] = remote(part, part, ag_s.at[6, i], ag_r.at[6, i], core_peer)

    def arrived(k, r):
        if r:
            cc[units.index((k, r))].wait_recv()

    def unit_value(ref):
        return ref[...].reshape(768, ref.shape[-1])

    def cols(k, r, start, size):
        return unit_value(W.at[k, z_of[r], :, :, :, :, pl.ds(start, size)])

    def qkv_rows(ref):
        return jnp.concatenate([ref[0].reshape(384, 768), ref[1, 0].reshape(192, 768)], axis=0)

    def out_rows(ref):
        return ref[1, 1].reshape(192, 768)

    def accumulate(first, value):
        if first:
            ACC[...] = value
        else:
            ACC[...] += value

    def attn_forward(r):
        arrived(ATT, r)
        QKV[r] = mm_nt(XA[own_rows, :], qkv_rows(W.at[ATT, z_of[r]])).astype(BF16)

        def segment(s, carry):
            rows = pl.ds(pl.multiple_of(s * SEG, SEG), SEG)
            qkv = QKV[r, rows, :]
            mixes = []
            for h in range(3):
                q = qkv[:, h * 64 : h * 64 + 64]
                key = qkv[:, 192 + h * 64 : 256 + h * 64]
                val = qkv[:, 384 + h * 64 : 448 + h * 64]
                scores = mm_nt(q, key) * SCALE
                top = jnp.max(scores, axis=-1, keepdims=True)
                expd = jnp.exp(scores - top)
                prob = expd * (1.0 / jnp.sum(expd, axis=-1, keepdims=True))
                PR[r, h, rows, :] = prob
                mixes.append(mm(prob.astype(BF16), val))
            MIX[r, rows, :] = jnp.concatenate(mixes, axis=-1).astype(BF16)
            return carry

        lax.fori_loop(0, 2, segment, 0, unroll=True)
        accumulate(r == 0, mm(MIX[r], out_rows(W.at[ATT, z_of[r]])))

    own_rows = pl.ds(pl.multiple_of(z * 256, 256), 256)

    def row_chunks(body, init=0):
        def one(i, carry):
            return body(i, pl.ds(pl.multiple_of(i * 64, 64), 64), carry)

        return lax.fori_loop(0, 4, one, init, unroll=True)

    g00, g01 = gain_ref[0, 0:1, :], gain_ref[0, 1:2, :]
    b00, b01 = shift_ref[0, 0:1, :], shift_ref[0, 1:2, :]
    g10, g11 = gain_ref[1, 0:1, :], gain_ref[1, 1:2, :]
    b10, b11 = shift_ref[1, 0:1, :], shift_ref[1, 1:2, :]

    def norm_one():
        def chunk(i, rows, carry):
            mine = XA[pl.ds(pl.multiple_of(z * 256 + i * 64, 64), 64), :]
            scaled, inverse = normalize(mine.astype(F32) + ACC[rows, :])
            SC1[rows, :] = scaled
            INV1[rows, :] = jnp.broadcast_to(inverse, (64, 128))
            FL[rows, :] = (scaled * g00 + b00).astype(BF16)
            return carry

        row_chunks(chunk)

    def ffn_forward(r):
        arrived(UP, r)
        def block(n, carry):
            part = pl.ds(pl.multiple_of(n * 256, 256), 256)
            upward = mm(FL[...], unit_value(W.at[UP, z_of[r], :, :, :, :, part]))
            active, slope = gelu_pair(upward)
            ACT[r, :, part] = active.astype(BF16)
            DG[r, :, part] = slope.astype(DG.dtype)
            return carry

        lax.fori_loop(0, 3, block, 0, unroll=True)

    def ffn_down(r):
        arrived(DOWN, r)
        accumulate(r == 0, mm(ACT[r], cols(DOWN, r, 0, 768)))

    def norm_two():
        loads["cot"].wait()

        def chunk(i, rows, carry):
            gains, shifts = carry
            first = SC1[rows, :] * g00 + b00
            scaled, inverse = normalize(first + ACC[rows, :])
            out_ref[0, rows, :] = (scaled * g01 + b01).astype(BF16)
            which = lax.broadcasted_iota(jnp.int32, (64, 768), 0) + i * 64
            grad = jnp.where(which % SEG == 0, GS[i // 2][0:1, :], COT[rows, :].astype(F32))
            fed = normalize_back(grad, scaled, inverse, g01)
            GF[rows, :] = fed
            FDL[rows, :] = fed.astype(BF16)
            return (
                gains + jnp.sum(grad * scaled, axis=0, keepdims=True),
                shifts + jnp.sum(grad, axis=0, keepdims=True),
            )

        zero = jnp.zeros((1, 768), F32)
        gains, shifts = row_chunks(chunk, (zero, zero))
        NV[1:2, :] = gains
        NV[3:4, :] = shifts

    def transpose_into(dst, src, start=0):
        for i in range(2):
            dst[:, i * 128 : i * 128 + 128] = src[pl.ds(pl.multiple_of(start + i * 128, 128), 128), :].T

    exch = {}

    def exchange(e, value):
        E[e, 0] = value
        for r in range(1, 4):
            exch[e, r] = remote(E.at[e, 0], E.at[e, r], e_s.at[e, r - 1], e_r.at[e, r - 1], z_peer[r])

    def exchange_wait(e):
        for r in range(1, 4):
            exch[e, r].wait_recv()

    def exchange_sum(e):
        exchange_wait(e)
        return (E[e, 0] + E[e, 1]) + (E[e, 2] + E[e, 3])

    row_of = lax.broadcasted_iota(jnp.int32, (8, 768), 0)
    pair_of = row_of // 2

    def own_row(value, j):
        return jnp.sum(jnp.where(row_of == 2 * z + j, value, 0.0), axis=0, keepdims=True)

    def grad_unit(k, r):
        return W.at[UP, r] if k == ATT else G.at[k - 1, r]

    turn = (3, 2, 1, 0)
    order = [(k, r) for r in turn for k in (DOWN, UP)] + [(ATT, r) for r in turn]
    s0, sa1, sb1, sa2, sb2, sza, szb, sfa, sfb = {}, {}, {}, {}, {}, {}, {}, {}, {}

    def sum_start(i):
        k, r = order[i]
        g = grad_unit(k, r)
        s0[i] = remote(g.at[:, :, nc], RC.at[i], rs_s.at[0, i], rs_r.at[0, i], core_peer)

    def add_low(a, b):
        return (a.astype(F32) + b.astype(F32)).astype(BF16)

    top, low = pl.ds(0, HALF), pl.ds(HALF, HALF)

    def sum_one(i):
        k, r = order[i]
        g = grad_unit(k, r)
        s0[i].wait_recv()

        def block(j, carry):
            jy, jx = j // 2, j % 2
            g[jy, jx, c] = add_low(g[jy, jx, c], RC[i, jy, jx])
            return carry

        lax.fori_loop(0, 4, block, 0, unroll=True)
        if k == ATT:
            part_a, part_b = g.at[:, nx, c, top], g.at[ny, :, c, low]
            peer_a, peer_b = x_peer, y_peer
        else:
            part_a, part_b = g.at[ny, :, c, top], g.at[:, nx, c, low]
            peer_a, peer_b = y_peer, x_peer
        sa1[i] = remote(part_a, RA1.at[i], rs_s.at[1, i], rs_r.at[1, i], peer_a)
        sb1[i] = remote(part_b, RB1.at[i], rs_s.at[2, i], rs_r.at[2, i], peer_b)

    def sum_two(i):
        k, r = order[i]
        g = grad_unit(k, r)
        sa1[i].wait_recv()
        if k == ATT:
            for j in range(2):
                g[j, x, c, 0:HALF, :] = add_low(g[j, x, c, 0:HALF, :], RA1[i, j])
            sa2[i] = remote(g.at[ny, x, c, top], RA2.at[i - 8], rs_s.at[3, i], rs_r.at[3, i], y_peer)
            sb1[i].wait_recv()
            for j in range(2):
                g[y, j, c, HALF:BLK, :] = add_low(g[y, j, c, HALF:BLK, :], RB1[i, j])
            sb2[i] = remote(g.at[y, nx, c, low], RB2.at[i - 8], rs_s.at[4, i], rs_r.at[4, i], x_peer)
        else:
            sb1[i].wait_recv()
            for j in range(2):
                g[y, j, c, 0:HALF, :] = add_low(g[y, j, c, 0:HALF, :], RA1[i, j])
                g[j, x, c, HALF:BLK, :] = add_low(g[j, x, c, HALF:BLK, :], RB1[i, j])

    def sum_three(i):
        g = grad_unit(*order[i])
        sa2[i].wait_recv()
        g[y, x, c, 0:HALF, :] = add_low(g[y, x, c, 0:HALF, :], RA2[i - 8])
        sb2[i].wait_recv()
        g[y, x, c, HALF:BLK, :] = add_low(g[y, x, c, HALF:BLK, :], RB2[i - 8])

    landing = {1: 0, 3: 1, 2: 2}

    def z_wait(k, r):
        i = order.index((k, r))
        sza[i].wait_recv()
        if k != ATT:
            szb[i].wait_recv()

    def z_add(k, g, slot):
        if k == ATT:
            g[y, x, c] = add_low(g[y, x, c], RZ[slot])
        else:
            for j in range(2):
                g[y, j, c, 0:HALF, :] = add_low(g[y, j, c, 0:HALF, :], RZF[k - 1, slot, 0, j])
                g[j, x, c, HALF:BLK, :] = add_low(g[j, x, c, HALF:BLK, :], RZF[k - 1, slot, 1, j])

    def sum_z(i):
        k, r = order[i]
        g = grad_unit(k, r)
        if r == 2:
            z_wait(k, 3)
            z_add(k, g, landing[3])
        if r:
            peer = z_peer[2] if r == 2 else z_peer[1]
            if k == ATT:
                sza[i] = remote(g.at[y, x, c], RZ.at[landing[r]], rs_s.at[5, i], rs_r.at[5, i], peer)
            else:
                land = RZF.at[k - 1, landing[r]]
                sza[i] = remote(g.at[y, :, c, top], land.at[0], rs_s.at[5, i], rs_r.at[5, i], peer)
                szb[i] = remote(g.at[:, x, c, low], land.at[1], rs_s.at[6, i], rs_r.at[6, i], peer)
        else:
            z_wait(k, 1)
            z_wait(k, 2)
            if k != ATT:
                for j in range(2):
                    a, b = RZF[k - 1, 0, 0, j].astype(F32), RZF[k - 1, 2, 0, j].astype(F32)
                    g[y, j, c, 0:HALF, :] = add_low(g[y, j, c, 0:HALF, :], a + b)
                    a, b = RZF[k - 1, 0, 1, j].astype(F32), RZF[k - 1, 2, 1, j].astype(F32)
                    g[j, x, c, HALF:BLK, :] = add_low(g[j, x, c, HALF:BLK, :], a + b)
                sfa[k] = remote(g.at[y, nx, c, top], RF.at[k - 1, 0], rs_s.at[7, k], rs_r.at[7, k], x_peer)
                sfb[k] = remote(g.at[ny, x, c, low], RF.at[k - 1, 1], rs_s.at[8, k], rs_r.at[8, k], y_peer)

    def sum_final(k):
        own = grad_unit(k, 0)[y, x, c].astype(F32)
        if k == ATT:
            return own + (RZ[0].astype(F32) + RZ[2].astype(F32))
        sfa[k].wait_recv()
        sfb[k].wait_recv()
        return own + jnp.concatenate([RF[k - 1, 0], RF[k - 1, 1]], axis=0).astype(F32)

    def store_unit(ref, parts):
        for start, size, value in parts:
            ref[:, :, :, :, start : start + size] = value().astype(BF16).reshape(2, 2, 2, BLK, size)

    def store_ffn(k, r, lhs_t, rhs):
        ref = grad_unit(k, r)

        def block(n, carry):
            part = pl.ds(pl.multiple_of(n * 256, 256), 256)
            value = mm(lhs_t[...], rhs[:, part])
            ref[:, :, :, :, part] = value.astype(BF16).reshape(2, 2, 2, BLK, 256)
            return carry

        lax.fori_loop(0, 3, block, 0, unroll=True)

    def ffn_back_one(r):
        ga = mm_nt(FDL[...], cols(DOWN, r, 0, 768))
        GU[...] = (ga * DG[r].astype(F32)).astype(BF16)

    def ffn_back_two(r):
        accumulate(r == turn[0], mm_nt(GU[...], cols(UP, r, 0, 768)))

    def grad_down(r):
        store_ffn(DOWN, r, FDLT, ACT.at[r])
        sum_start(order.index((DOWN, r)))

    def grad_up(r):
        store_ffn(UP, r, FLT, GU)
        sum_start(order.index((UP, r)))

    def l1(k, start, size):
        return unit_value(L1.at[k, :, :, :, :, pl.ds(start, size)])

    live = {}

    def token_one():
        unit = W.at[ATT, z]
        kv_weight = jnp.concatenate([unit[0, 1].reshape(192, 768), unit[1, 0].reshape(192, 768)], axis=0)

        def rows_of(i, carry):
            rows = pl.ds(pl.multiple_of(i * 256, 256), 256)
            ACT[i, :, 0:384] = mm_nt(XA[rows, :], kv_weight).astype(BF16)
            return carry

        lax.fori_loop(0, 4, rows_of, 0)
        x8 = jnp.concatenate([XA[i * SEG : i * SEG + 16, :].astype(F32)[0:1] for i in range(8)], axis=0)
        live["x8"] = x8
        q8 = mm_nt(x8.astype(BF16), unit[0, 0].reshape(192, 768)).astype(BF16).astype(F32)
        row = lax.broadcasted_iota(jnp.int32, (8, 1024), 0)
        keep = lax.broadcasted_iota(jnp.int32, (8, 1024), 1) // SEG == row
        mixes = []
        for h in range(3):
            q = q8[:, h * 64 : h * 64 + 64].astype(BF16)
            parts = [mm_nt(q, ACT[i, :, h * 64 : h * 64 + 64]) for i in range(4)]
            scores = jnp.where(keep, jnp.concatenate(parts, axis=1) * SCALE, -3.0e38)
            top = jnp.max(scores, axis=-1, keepdims=True)
            expd = jnp.exp(scores - top)
            prob = (expd * (1.0 / jnp.sum(expd, axis=-1, keepdims=True))).astype(BF16)
            mix = None
            for i in range(4):
                val = ACT[i, :, 192 + h * 64 : 256 + h * 64]
                part = mm(prob[:, i * 256 : i * 256 + 256], val)
                mix = part if mix is None else mix + part
            mixes.append(mix)
        exchange(0, mm(jnp.concatenate(mixes, axis=-1).astype(BF16), out_rows(unit)))

    def token_two():
        attended = exchange_sum(0)
        scaled, _ = normalize(live["x8"] + attended)
        first = scaled * g00 + b00
        live["first8"] = first
        loads["wu"].wait()
        loads["wd"].wait()
        active, _ = gelu_pair(mm(first.astype(BF16), cols(UP, 0, 0, 768)))
        exchange(1, mm(active.astype(BF16), cols(DOWN, 0, 0, 768)))

    def cross_one():
        fed = exchange_sum(1)
        scaled, _ = normalize(live["first8"] + fed)
        summary = scaled * g01 + b01
        live["summary"] = summary
        live["summary_low"] = summary.astype(BF16)
        for name in ("l1qk", "l1v", "l1o"):
            loads[name].wait()
        qkv = mm_nt(live["summary_low"], qkv_rows(L1.at[ATT])).astype(BF16).astype(F32)
        pad = jnp.zeros((120, 64), F32)
        ids = jnp.broadcast_to(doc_ref[...].astype(F32), (8, 8))
        eye = lax.broadcasted_iota(jnp.int32, (8, 8), 0) == lax.broadcasted_iota(jnp.int32, (8, 8), 1)
        same = ids == jnp.sum(jnp.where(eye, ids, 0.0), axis=1, keepdims=True)
        keep = jnp.concatenate([jnp.where(same, 1.0, 0.0), jnp.zeros((8, 120), F32)], axis=1) > 0.5
        mixes = []
        for h in range(3):
            q = qkv[:, h * 64 : h * 64 + 64].astype(BF16)
            key = jnp.concatenate([qkv[:, 192 + h * 64 : 256 + h * 64], pad], axis=0).astype(BF16)
            val = jnp.concatenate([qkv[:, 384 + h * 64 : 448 + h * 64], pad], axis=0).astype(BF16)
            scores = jnp.where(keep, mm_nt(q, key) * SCALE, MASK_FILL)
            top = jnp.max(scores, axis=-1, keepdims=True)
            expd = jnp.exp(scores - top)
            prob = expd * (1.0 / jnp.sum(expd, axis=-1, keepdims=True))
            live["prob", h], live["q", h], live["key", h], live["val", h] = prob, q, key, val
            mixes.append(mm(prob.astype(BF16), val))
        mix = jnp.concatenate(mixes, axis=-1).astype(BF16)
        live["mix"] = mix
        exchange(2, mm(mix, out_rows(L1.at[ATT])))

    def cross_two():
        attended = exchange_sum(2)
        live["xs1"], live["xi1"] = normalize(live["summary"] + attended)
        first = live["xs1"] * g10 + b10
        live["xfirst"] = first
        live["xfirst_low"] = first.astype(BF16)
        loads["l1u"].wait()
        loads["l1d"].wait()
        active, live["xdg"] = gelu_pair(mm(live["xfirst_low"], l1(UP, 0, 768)))
        live["xact"] = active.astype(BF16)
        exchange(3, mm(live["xact"], l1(DOWN, 0, 768)))

    def cross_three():
        fed = exchange_sum(3)
        xs2, xi2 = normalize(live["xfirst"] + fed)
        upper = xs2 * g11 + b11
        for j in range(2):
            GS[j, 1:2, :] = own_row(upper, j)
        loads["c8"].wait()
        grad_top = C8[...].astype(F32)[:, 0, :]
        live["xs2"], live["xi2"] = xs2, xi2
        grad_fed = normalize_back(grad_top, live["xs2"], live["xi2"], g11)
        NV[5:6, :] = jnp.sum(grad_top * live["xs2"], axis=0, keepdims=True)
        NV[7:8, :] = jnp.sum(grad_top, axis=0, keepdims=True)
        live["xgf"] = grad_fed
        live["xfed_low"] = grad_fed.astype(BF16)
        ga = mm_nt(live["xfed_low"], l1(DOWN, 0, 768))
        live["xgu"] = (ga * live["xdg"]).astype(BF16)
        exchange(4, mm_nt(live["xgu"], l1(UP, 0, 768)))

    def cross_four():
        grad_first = live["xgf"] + exchange_sum(4)
        grad_att = normalize_back(grad_first, live["xs1"], live["xi1"], g10)
        NV[4:5, :] = jnp.sum(grad_first * live["xs1"], axis=0, keepdims=True)
        NV[6:7, :] = jnp.sum(grad_first, axis=0, keepdims=True)
        live["xga"] = grad_att
        att_low = grad_att.astype(BF16)
        live["xatt_low"] = att_low
        gm = mm_nt(att_low, out_rows(L1.at[ATT])).astype(BF16)
        gqs, gks, gvs = [], [], []
        for h in range(3):
            gmh = gm[:, h * 64 : h * 64 + 64]
            prob = live["prob", h]
            gp = mm_nt(gmh, live["val", h])
            inner = jnp.sum(gp * prob, axis=-1, keepdims=True)
            gs = (prob * (gp - inner)).astype(BF16)
            gqs.append(mm(gs, live["key", h]) * SCALE)
            gks.append(mm_tn(gs, live["q", h])[0:8, :] * SCALE)
            gvs.append(mm_tn(prob.astype(BF16), gmh)[0:8, :])
        gqkv = jnp.concatenate(gqs + gks + gvs, axis=-1).astype(BF16)
        live["xgqkv"] = gqkv
        exchange(5, mm(gqkv, qkv_rows(L1.at[ATT])))

    def cross_five():
        grad_summary = live["xga"] + exchange_sum(5)
        for j in range(2):
            GS[j, 0:1, :] = own_row(grad_summary, j)

    def output_rows():
        for j in range(2):
            out_ref[0, j * 128 : j * 128 + 1, :] = GS[j, 1:2, :].astype(BF16)

    def norm_one_back():
        def chunk(i, rows, carry):
            gains, shifts = carry
            grad = GF[rows, :] + ACC[rows, :]
            scaled = SC1[rows, :]
            att = normalize_back(grad, scaled, INV1[rows, 0:1], g00)
            GF[rows, :] = att
            FDL[rows, :] = att.astype(BF16)
            return (
                gains + jnp.sum(grad * scaled, axis=0, keepdims=True),
                shifts + jnp.sum(grad, axis=0, keepdims=True),
            )

        zero = jnp.zeros((1, 768), F32)
        gains, shifts = row_chunks(chunk, (zero, zero))
        NV[0:1, :] = gains
        NV[2:3, :] = shifts

    def attn_backward(r):
        GM[...] = mm_nt(FDL[...], out_rows(W.at[ATT, z_of[r]])).astype(BF16)

        def segment(s, carry):
            rows = pl.ds(pl.multiple_of(s * SEG, SEG), SEG)
            qkv = QKV[r, rows, :]
            gm = GM[rows, :]
            gqs, gks, gvs = [], [], []
            for h in range(3):
                q = qkv[:, h * 64 : h * 64 + 64]
                key = qkv[:, 192 + h * 64 : 256 + h * 64]
                val = qkv[:, 384 + h * 64 : 448 + h * 64]
                gmh = gm[:, h * 64 : h * 64 + 64]
                prob = PR[r, h, rows, :]
                gp = mm_nt(gmh, val)
                inner = jnp.sum(gp * prob, axis=-1, keepdims=True)
                gs = (prob * (gp - inner)).astype(BF16)
                gqs.append(mm(gs, key) * SCALE)
                gks.append(mm_tn(gs, q) * SCALE)
                gvs.append(mm_tn(prob.astype(BF16), gmh))
            GQ[rows, :] = jnp.concatenate(gqs + gks + gvs, axis=-1).astype(BF16)
            return carry

        lax.fori_loop(0, 2, segment, 0, unroll=True)
        store_unit(
            grad_unit(ATT, r),
            [
                (0, 576, lambda: mm(XT[...], GQ[...])),
                (576, 192, lambda: mm(FDLT[...], MIX[r])),
            ],
        )
        sum_start(order.index((ATT, r)))
        accumulate(r == turn[0], mm(GQ[...], qkv_rows(W.at[ATT, z_of[r]])))

    fac = {}

    def factor_start():
        wide = lambda v: v.astype(F32)
        zero_a, zero_b = jnp.zeros((8, 192), F32), jnp.zeros((8, 576), F32)
        att_left = jnp.concatenate([wide(live["xgqkv"]), zero_a], axis=-1)
        att_right = jnp.concatenate([zero_b, wide(live["mix"])], axis=-1)
        right = jnp.concatenate([wide(live["xact"]), wide(live["xgu"]), att_left, att_right], axis=0)
        left = jnp.concatenate(
            [wide(live["xfed_low"]), wide(live["xfirst_low"]), wide(live["summary_low"]), wide(live["xatt_low"])],
            axis=0,
        )
        FAC[y, x, c, 0:32, :] = right.astype(BF16)
        FAC[y, x, c, 32:64, :] = left.astype(BF16)
        part = FAC.at[y, x, c]
        fac[0] = remote(part, part, f_s.at[0], f_r.at[0], x_peer)

    def factor_two():
        fac[0].wait_recv()
        part = FAC.at[y, :, c]
        fac[1] = remote(part, part, f_s.at[1], f_r.at[1], y_peer)

    def factor_three():
        fac[1].wait_recv()
        part = FAC.at[:, :, c]
        fac[2] = remote(part, part, f_s.at[2], f_r.at[2], core_peer)

    def turn_rows(value):
        rows = value.shape[0]
        full = jnp.concatenate([value, jnp.zeros((128 - rows, value.shape[1]), F32)], axis=0)
        return full.T[:, 0:rows]

    def write_unit(layer, k, value):
        if k == ATT:
            for i in range(3):
                qkvg_ref[layer, i] = value[:, i * 192 : i * 192 + 192]
            outg_ref[layer] = turn_rows(value[:, 576:768])
        elif k == UP:
            upg_ref[layer] = value
        else:
            downg_ref[layer] = value

    def factor_final():
        fac[2].wait_recv()
        left = FAC[:, :, :, 32:64, :].reshape(256, 768)
        for i in range(2):
            LT[:, i * 128 : i * 128 + 128] = left[i * 128 : i * 128 + 128, :].T
        mine = LT[pl.ds(pl.multiple_of(dp * BLK, BLK), BLK), :].astype(F32)
        kind = (lax.broadcasted_iota(jnp.int32, (BLK, 256), 1) // 8) % 4
        right = FAC[:, :, :, 0:32, :].reshape(256, 768)
        write_unit(1, DOWN, mm(jnp.where(kind == 0, mine, 0.0).astype(BF16), right))
        write_unit(1, UP, mm(jnp.where(kind == 1, mine, 0.0).astype(BF16), right))
        write_unit(1, ATT, mm(jnp.where(kind >= 2, mine, 0.0).astype(BF16), right))

    vec = {}

    def norm_grads_start():
        exchange(6, NV[...])

    def norm_grads_two():
        total = jnp.where(row_of < 4, exchange_sum(6), NV[...])
        pad = jnp.zeros((8, 32), F32)
        for p in range(8):
            SV[p // 4, (p // 2) % 2, p % 2] = jnp.concatenate([total[:, p * BLK : p * BLK + BLK], pad], axis=-1)
        for m in range(1, 8):
            ty = y if m // 4 == 0 else ny
            tx = x if (m // 2) % 2 == 0 else nx
            tc = c if m % 2 == 0 else nc
            vec[m] = remote(
                SV.at[ty, tx, tc], RSV.at[m - 1], v_s.at[m - 1], v_r.at[m - 1], (plane_index(m), z)
            )

    def norm_grads_final():
        total = SV[y, x, c]
        for m in range(1, 8):
            vec[m].wait_recv()
            total = total + RSV[m - 1]
        gaing_ref[...] = total[0:2, 0:BLK]
        shiftg_ref[...] = total[2:4, 0:BLK]
        crossg_ref[0] = total[4:6, 0:BLK]
        crossg_ref[1] = total[6:8, 0:BLK]

    def turn_to_attention():
        norm_one_back()
        norm_grads_start()
        transpose_into(FDLT, FDL)
        for table in (a1, b1, a2, b2, a3, b3, cc):
            for i in range(9):
                table[i].wait_send()
                waited.append(id(table[i]))
        for condition, copy in passed:

            @pl.when(condition)
            def _(copy=copy):
                copy.wait_send()

    def settle_sends(keep):
        for copy in sends[: len(sends) - keep]:
            if id(copy) not in waited:
                copy.wait_send()
                waited.append(id(copy))

    for name in ("wqk", "wv", "wo"):
        loads[name].wait()
    z_own(ATT)
    loads["x"].wait()
    token_one()
    z_own(UP)
    attn_forward(0)
    transpose_into(XT, XA, z * 256)
    gather_a(0)
    gather_a(1)
    token_two()
    gather_b(0)
    gather_a(2)
    z_own(DOWN)
    gather_b(1)
    gather_c(0)
    gather_b(2)
    gather_a(3)
    cross_one()
    gather_c(1)
    gather_a(4)
    gather_a(5)
    attn_forward(1)
    gather_c(2)
    gather_b(3)
    gather_b(4)
    cross_two()
    attn_forward(2)
    gather_b(5)
    gather_a(6)
    gather_a(7)
    gather_c(3)
    gather_c(4)
    cross_three()
    gather_c(5)
    attn_forward(3)
    gather_b(6)
    gather_a(8)
    norm_one()
    ffn_forward(2)
    gather_b(7)
    ffn_forward(1)
    ffn_forward(0)
    ffn_down(0)
    gather_c(6)
    cross_four()
    gather_b(8)
    ffn_down(1)
    transpose_into(FLT, FL)
    ffn_forward(3)
    gather_c(7)
    gather_c(8)
    factor_start()
    ffn_down(2)
    cross_five()
    ffn_down(3)
    norm_two()
    output_rows()
    transpose_into(FDLT, FDL)
    factor_two()
    grad_down(3)
    ffn_back_one(3)
    grad_up(3)
    ffn_back_two(3)
    ffn_back_one(2)
    grad_down(2)
    sum_one(0)
    grad_up(2)
    sum_one(1)
    ffn_back_two(2)
    ffn_back_one(1)
    sum_one(2)
    grad_down(1)
    sum_one(3)
    grad_up(1)
    grad_down(0)
    sum_two(0)
    sum_z(0)
    sum_one(4)
    ffn_back_two(1)
    ffn_back_one(0)
    sum_one(5)
    sum_two(1)
    sum_one(6)
    sum_z(1)
    grad_up(0)
    ffn_back_two(0)
    turn_to_attention()
    sum_two(2)
    attn_backward(3)
    sum_two(3)
    sum_one(7)
    sum_z(2)
    attn_backward(2)
    sum_two(4)
    sum_one(8)
    sum_z(4)
    attn_backward(1)
    sum_z(3)
    sum_one(9)
    sum_two(5)
    sum_z(5)
    sum_two(6)
    attn_backward(0)
    sum_two(7)
    factor_three()
    ing_ref[0] = (GF[...] + ACC[...]).astype(BF16)
    norm_grads_two()
    sum_two(8)
    sum_one(10)
    factor_final()
    sum_two(9)
    sum_z(6)
    sum_one(11)
    sum_three(8)
    sum_z(8)
    sum_two(10)
    sum_three(9)
    write_unit(0, DOWN, sum_final(DOWN))
    sum_z(9)
    sum_two(11)
    sum_z(7)
    sum_three(10)
    sum_z(10)
    settle_sends(8)
    sum_three(11)
    write_unit(0, UP, sum_final(UP))
    sum_z(11)
    norm_grads_final()
    write_unit(0, ATT, sum_final(ATT))
    for copy in sends:
        if id(copy) not in waited:
            copy.wait_send()


def settle_kernel(*refs):
    sources, targets, sems = refs[:9], refs[9:18], refs[18]
    copies = [pltpu.make_async_copy(sources[i], targets[i], sems.at[i]) for i in range(9)]
    for copy in copies:
        copy.start()
    for copy in copies:
        copy.wait()


def fused_body(
    inputs, doc_ids, qkv_weight, out_weight, up_weight, down_weight, norm_gain, norm_shift, cotangent
):
    wq = qkv_weight.swapaxes(2, 3).reshape(2, 3, 2, BLK, 768)
    wo = out_weight.reshape(2, 2, BLK, 768)
    wu = up_weight.reshape(2, 2, 2, 2, BLK, 768)
    wd = down_weight.reshape(2, 2, 2, 2, BLK, 768)
    whole = pl.BlockSpec(memory_space=pl.ANY)
    vmem = pl.BlockSpec(memory_space=pltpu.VMEM)
    blocks = (2, 2, 2, BLK, 768)
    sem = pltpu.SemaphoreType.DMA
    results = pl.pallas_call(
        fused_kernel,
        out_shape=(
            pltpu.VMEM((1, 256, 768), BF16),
            pltpu.VMEM((1, 256, 768), BF16),
            pltpu.VMEM((2, 3, BLK, 192), F32),
            pltpu.VMEM((2, 192, BLK), F32),
            pltpu.VMEM((2, BLK, 768), F32),
            pltpu.VMEM((2, BLK, 768), F32),
            pltpu.VMEM((2, BLK), F32),
            pltpu.VMEM((2, BLK), F32),
            pltpu.VMEM((2, 2, BLK), F32),
        ),
        in_specs=[whole, whole, whole, vmem, whole, whole, whole, whole, vmem, vmem],
        out_specs=(vmem,) * 9,
        scratch_shapes=[
            pltpu.VMEM((3, 4) + blocks, BF16),
            pltpu.VMEM((2, 4) + blocks, BF16),
            pltpu.VMEM((12, 2, 2, BLK, 768), BF16),
            pltpu.VMEM((12, 2, HALF, 768), BF16),
            pltpu.VMEM((12, 2, HALF, 768), BF16),
            pltpu.VMEM((4, HALF, 768), BF16),
            pltpu.VMEM((4, HALF, 768), BF16),
            pltpu.VMEM((3, BLK, 768), BF16),
            pltpu.VMEM((2, 3, 2, 2, HALF, 768), BF16),
            pltpu.VMEM((2, 2, HALF, 768), BF16),
            pltpu.VMEM((3,) + blocks, BF16),
            pltpu.VMEM((1024, 768), BF16),
            pltpu.VMEM((256, 768), BF16),
            pltpu.VMEM((4, 256, 576), BF16),
            pltpu.VMEM((4, 3, 256, 128), F32),
            pltpu.VMEM((4, 256, 192), BF16),
            pltpu.VMEM((4, 256, 768), BF16),
            pltpu.VMEM((4, 256, 768), BF16),
            pltpu.VMEM((256, 768), BF16),
            pltpu.VMEM((256, 576), BF16),
            pltpu.VMEM((256, 768), F32),
            pltpu.VMEM((256, 768), F32),
            pltpu.VMEM((256, 768), F32),
            pltpu.VMEM((256, 768), BF16),
            pltpu.VMEM((768, 256), BF16),
            pltpu.VMEM((256, 768), BF16),
            pltpu.VMEM((768, 256), BF16),
            pltpu.VMEM((768, 256), BF16),
            pltpu.VMEM((256, 192), BF16),
            pltpu.VMEM((8, 16, 768), BF16),
            pltpu.VMEM((256, 128), F32),
            pltpu.VMEM((2, 2, 2, 64, 768), BF16),
            pltpu.VMEM((768, 256), BF16),
            pltpu.VMEM((2, 8, 768), F32),
            pltpu.VMEM((7, 4, 8, 768), F32),
            pltpu.VMEM((8, 768), F32),
            pltpu.VMEM((2, 2, 2, 8, 128), F32),
            pltpu.VMEM((7, 8, 128), F32),
            sem((13,)),
            sem((12, 2)),
            sem((12,)),
            sem((7, 9)),
            sem((7, 9)),
            sem((9, 12)),
            sem((9, 12)),
            sem((7, 3)),
            sem((7, 3)),
            sem((3,)),
            sem((3,)),
            sem((7,)),
            sem((7,)),
        ],
        compiler_params=pltpu.CompilerParams(
            collective_id=0, has_side_effects=True, vmem_limit_bytes=59 * 2**20
        ),
    )(
        inputs, cotangent, cotangent.reshape(8, SEG, 768), doc_ids, wq, wo, wu, wd, norm_gain, norm_shift
    )
    final = pl.pallas_call(
        settle_kernel,
        out_shape=tuple(jax.ShapeDtypeStruct(v.shape, v.dtype) for v in results),
        in_specs=[whole] * 9,
        out_specs=(whole,) * 9,
        scratch_shapes=[sem((9,))],
    )(*[pltpu.with_memory_space_constraint(v, pltpu.VMEM) for v in results])
    return final[:5] + (final[5].swapaxes(1, 2),) + final[6:]


def solution(mesh):
    in_specs = (
        P("dp", None, None),
        P("dp", None),
        P(None, None, None, "tensor"),
        P(None, "tensor", None),
        P(None, None, "tensor"),
        P(None, "tensor", None),
        P(),
        P(),
        P("dp", None, None),
    )
    out_specs = (
        P("dp", "tensor", None),
        P("dp", "tensor", None),
        P(None, None, "dp", "tensor"),
        P(None, "tensor", "dp"),
        P(None, "dp", "tensor"),
        P(None, "tensor", "dp"),
        P(None, "dp"),
        P(None, "dp"),
        P(None, None, "dp"),
    )
    fits = dict(mesh.shape) == {"dp": 8, "tensor": 4}
    chosen = fused_body if fits else body
    return jax.shard_map(chosen, mesh=mesh, in_specs=in_specs, out_specs=out_specs, check_vma=False)
```
